32 devices in a mesh: dp: 4 (over x, core), seq: 8 (over z, y).
Axes of the slice: x: 2, y: 2, z: 4, core: 2. Of those that a mesh axis runs over, the one named last changes fastest.
Arguments:
- tokens: float32 [8, 1024, 1024], P('dp', 'seq'), may hold values from -6 to 6
- encoder: float32 [8, 512, 1024], P('dp'), may hold values from -6 to 6
- cotangent: float32 [8, 1024, 1024], P('dp', 'seq'), may hold values from -6 to 6
- adapter_pick: int32 [8], P('dp'), may hold values from 0 to 7, as said below
- segment_order: int32 [8, 8], P('dp'), may hold values from 0 to 7, each once within a row
- parents: int32 [8, 8], P('dp'), may hold values from -1 to 3, as said below
- norm_gains: float32 [3, 1024], replicated, may hold values from 0.5 to 1.5
- w_qkv: float32 [1024, 3072], P(None, 'seq'), may hold values from -0.1875 to 0.1875
- w_self_out: float32 [1024, 1024], P('seq'), may hold values from -1.5 to 1.5
- w_cross_q: float32 [1024, 1024], P(None, 'seq'), may hold values from -0.1875 to 0.1875
- w_cross_kv: float32 [1024, 2048], P(None, 'seq'), may hold values from -0.1875 to 0.1875
- w_cross_out: float32 [1024, 1024], P('seq'), may hold values from -1.5 to 1.5
- w_fc_in: float32 [1024, 8192], P(None, 'seq'), may hold values from -0.1875 to 0.1875
- w_fc_out: float32 [8192, 1024], P('seq'), may hold values from -0.0625 to 0.0625
- attn_down: bfloat16 [8, 8, 1024, 16], replicated, may hold values from -0.1875 to 0.1875
- attn_up: bfloat16 [8, 8, 16, 1024], replicated, may hold values from -0.375 to 0.375
- fc_in_down: bfloat16 [8, 1024, 16], replicated, may hold values from -0.1875 to 0.1875
- fc_in_up: bfloat16 [8, 16, 8192], replicated, may hold values from -0.375 to 0.375
- fc_out_down: bfloat16 [8, 8192, 16], replicated, may hold values from -0.0625 to 0.0625
- fc_out_up: bfloat16 [8, 16, 1024], replicated, may hold values from -0.375 to 0.375
Outputs:
- layer_out: float32 [8, 1024, 1024], P('dp', 'seq')
- grad_tokens: float32 [8, 1024, 1024], P('dp', 'seq')
- grad_encoder: float32 [8, 512, 1024], P('dp', 'seq')
- grad_attn_down: float32 [8, 8, 1024, 16], replicated
- grad_attn_up: float32 [8, 8, 16, 1024], replicated
- grad_fc_in_down: float32 [8, 1024, 16], replicated
- grad_fc_in_up: float32 [8, 16, 8192], replicated
- grad_fc_out_down: float32 [8, 8192, 16], replicated
- grad_fc_out_up: float32 [8, 16, 1024], replicated
The draws below stay inside these ranges and needn't reach their ends.
Inputs may be any that keep to these rules, and one draw needn't show every extreme that they name: `parents`: logical segments of the first quarter of the 8 form the trunk, each the child of the one before, segment 0 the root with parent -1; the second quarter are branch segments, the first four (all, if fewer) children of the trunk's last segment and each later one the child of the branch segment four before it; the other half are leaves, each the child of a branch segment, the last leaf that of the last branch segment. `adapter_pick`: every adapter is chosen by at least one tree.
All inputs are finite; a program needn't handle non-finite values.
Results may differ from the reference program's by a relative error of at most 0.0003.
Values sent between devices are 32-bit elements; how exact they have to be, the bound alone decides.
A program may use at most 512 MiB of HBM per device.

```python
import jax
import jax.numpy as jnp
from jax import lax

D = 1024
HEADS = 16
HD = 64
FF = 8192
RANK = 16
ADAPTERS = 8
SEG = 128
ENC = 512
NSEG = 8
TREE_LEN = 1024
TREES = 8


def draw_adapter_pick(key, part):
    key = jax.random.fold_in(key, 12)
    shuffled = jax.random.permutation(key, jnp.arange(TREES, dtype=jnp.int32))
    return (shuffled % ADAPTERS).astype(jnp.int32)


def draw_parents(key, part):
    key = jax.random.fold_in(key, 11)
    index = jnp.broadcast_to(jnp.arange(NSEG, dtype=jnp.int32)[None, :], (TREES, NSEG))
    trunk_end = NSEG // 4
    branch_end = trunk_end + NSEG // 4
    trunk_parent = index - 1
    branch_parent = jnp.where(index - trunk_end < 4, trunk_end - 1, index - 4)
    random_branch = trunk_end + jax.random.randint(key, (TREES, NSEG), 0, NSEG // 4, dtype=jnp.int32)
    leaf_parent = jnp.where(index == NSEG - 1, branch_end - 1, random_branch)
    return jnp.where(index < trunk_end, trunk_parent, jnp.where(index < branch_end, branch_parent, leaf_parent))


def block_levels(stream_key, extent, pieces, least, largest):
    def one(position, shards_of):
        steps = jax.random.uniform(jax.random.fold_in(jax.random.fold_in(stream_key, 6), position), (shards_of,), jnp.float32, least / len(pieces), largest / len(pieces))
        return jnp.repeat(jnp.exp(steps), extent[position] // shards_of).reshape((-1,) + (1,) * (len(extent) - position - 1))

    loudness = one(*pieces[0])
    for cut in pieces[1:]:
        loudness = loudness * one(*cut)
    return loudness


def gaussian(stream_key, extent, scale, limit, shards=(), held_as=jnp.bfloat16):
    result = jax.random.normal(stream_key, extent, jnp.float32) * scale
    if len(shards) > 0:
        result = block_levels(stream_key, extent, shards, -0.22, 0.18) * result
    return jnp.clip(result, min=-limit, max=limit).astype(held_as)


def setup_inputs(seed: int = 0) -> dict:
    key_of = jax.random.split(jax.random.key(seed), 21)
    return {
        "tokens": gaussian(key_of[0], (TREES, TREE_LEN, D), 1.0, 6.0, ((0, 4), (1, 8)), jnp.float32),
        "encoder": gaussian(key_of[1], (TREES, ENC, D), 1.0, 6.0, ((0, 4),), jnp.float32),
        "cotangent": gaussian(key_of[2], (TREES, TREE_LEN, D), 1.0, 6.0, ((0, 4), (1, 8)), jnp.float32),
        "adapter_pick": draw_adapter_pick(jax.random.fold_in(key_of[20], 71), 0),
        "segment_order": jax.vmap(lambda own: jax.random.permutation(own, NSEG))(jax.random.split(key_of[4], TREES)).reshape((TREES, NSEG)).astype(jnp.int32),
        "parents": draw_parents(jax.random.fold_in(key_of[20], 71), 0),
        "norm_gains": jnp.clip(1.0 + 0.1 * jax.random.normal(key_of[6], (3, D), jnp.float32), 0.5, 1.5),
        "w_qkv": gaussian(key_of[7], (D, 3 * D), D ** -0.5, 0.1875, ((1, 8),), jnp.float32),
        "w_self_out": gaussian(key_of[8], (D, D), (D // 64) ** -0.5, 1.5, ((0, 8),), jnp.float32),
        "w_cross_q": gaussian(key_of[9], (D, D), D ** -0.5, 0.1875, ((1, 8),), jnp.float32),
        "w_cross_kv": gaussian(key_of[10], (D, 2 * D), D ** -0.5, 0.1875, ((1, 8),), jnp.float32),
        "w_cross_out": gaussian(key_of[11], (D, D), (D // 64) ** -0.5, 1.5, ((0, 8),), jnp.float32),
        "w_fc_in": gaussian(key_of[12], (D, FF), D ** -0.5, 0.1875, ((1, 8),), jnp.float32),
        "w_fc_out": gaussian(key_of[13], (FF, D), FF ** -0.5, 0.0625, ((0, 8),), jnp.float32),
        "attn_down": gaussian(key_of[14], (ADAPTERS, 8, D, RANK), D ** -0.5, 0.1875),
        "attn_up": gaussian(key_of[15], (ADAPTERS, 8, RANK, D), (RANK * 16) ** -0.5, 0.375),
        "fc_in_down": gaussian(key_of[16], (ADAPTERS, D, RANK), D ** -0.5, 0.1875),
        "fc_in_up": gaussian(key_of[17], (ADAPTERS, RANK, FF), (RANK * 16) ** -0.5, 0.375),
        "fc_out_down": gaussian(key_of[18], (ADAPTERS, FF, RANK), FF ** -0.5, 0.0625),
        "fc_out_up": gaussian(key_of[19], (ADAPTERS, RANK, D), (RANK * 16) ** -0.5, 0.375),
    }


PRECISE = lax.Precision.HIGHEST
ADAPT_SCALE = 2.0
NORM_EPS = 1e-05
MASK_FILL = -1e+30

def matmul(left_side, right_side):
    return jnp.dot(left_side, right_side, precision=PRECISE)

def reach_table(segment_order, parents):
    segment_count = parents.shape[-1]
    column = lax.broadcasted_iota(jnp.int32, (segment_count, segment_count), 1)
    identity = (lax.broadcasted_iota(jnp.int32, (segment_count, segment_count), 0) == column).astype(jnp.int32)
    parent_hot = (parents[..., :, None] == column).astype(jnp.int32)

    def extend(sweep_index, reach_rows):
        through = lax.optimization_barrier(jnp.max(parent_hot[..., :, :, None] * reach_rows[..., None, :, :], axis=-2))
        return jnp.maximum(identity, through)
    initial = jnp.broadcast_to(identity, parent_hot.shape)
    reach_rows = lax.fori_loop(0, segment_count, extend, initial)
    order_rows = jnp.take_along_axis(reach_rows, segment_order[..., :, None].astype(jnp.int32), axis=1)
    return jnp.take_along_axis(order_rows, segment_order[..., None, :].astype(jnp.int32), axis=2)

def layer_norm(values, gain_row):
    center = values - lax.optimization_barrier(jnp.mean(values, -1, keepdims=True))
    variance = lax.optimization_barrier(jnp.mean(center * center, -1, keepdims=True))
    return center * lax.rsqrt(variance + NORM_EPS) * gain_row

def project(inputs, weight, down_map, up_map):
    return matmul(inputs, weight) + ADAPT_SCALE * matmul(matmul(inputs, down_map), up_map)

def attention(queries, key_rows, value_rows, reach_rows):
    length = queries.shape[0]
    key_count = key_rows.shape[0]
    block_rows = min(length, 512)
    query_heads = queries.reshape(length, HEADS, HD)
    key_heads = key_rows.reshape(key_count, HEADS, HD)
    value_heads = value_rows.reshape(key_count, HEADS, HD)
    key_index = jnp.arange(key_count, dtype=jnp.int32)

    def one_block(first_row):
        row_index = first_row + jnp.arange(block_rows, dtype=jnp.int32)
        query_part = lax.dynamic_slice_in_dim(query_heads, first_row, block_rows, 0)
        scores = jnp.einsum('qhd,khd->hqk', query_part, key_heads, precision=PRECISE) * HD ** (-0.5)
        if reach_rows is not None:
            query_slot = row_index // SEG
            key_slot = key_index // SEG
            path_ok = reach_rows[query_slot][:, key_slot] > 0
            causal_ok = (query_slot[:, None] != key_slot[None, :]) | (key_index[None, :] <= row_index[:, None])
            scores = jnp.where((path_ok & causal_ok)[None], scores, MASK_FILL)
        weights = jax.nn.softmax(scores, axis=-1)
        return jnp.einsum('hqk,khd->qhd', weights, value_heads, precision=PRECISE)
    firsts = jnp.arange(length // block_rows, dtype=jnp.int32) * block_rows
    blocks = lax.map(jax.checkpoint(one_block), firsts)
    return blocks.reshape(length, HEADS * HD)

def tree_forward(tokens, encoder, adapters, chosen_index, reach_rows, frozen):
    norm_gains, w_qkv, w_self_out, w_cross_q, w_cross_kv, w_cross_out, w_fc_in, w_fc_out = frozen
    chosen = (jnp.arange(adapters[0].shape[0], dtype=jnp.int32) == chosen_index).astype(jnp.float32)
    picked = [jnp.tensordot(chosen, adapter_table, axes=1, precision=PRECISE) for adapter_table in adapters]
    attn_down, attn_up, in_down, in_up, out_down, out_up = picked
    width = tokens.shape[1]
    normed_one = layer_norm(tokens, norm_gains[0])
    adapter_parts = [matmul(matmul(normed_one, attn_down[index]), attn_up[index]) for index in range(3)]
    stacked = matmul(normed_one, w_qkv) + ADAPT_SCALE * jnp.concatenate(adapter_parts, axis=1)
    context = attention(stacked[:, :width], stacked[:, width:2 * width], stacked[:, 2 * width:], reach_rows)
    middle = tokens + project(context, w_self_out, attn_down[3], attn_up[3])
    normed_two = layer_norm(middle, norm_gains[1])
    cross_queries = project(normed_two, w_cross_q, attn_down[4], attn_up[4])
    memory_parts = [matmul(matmul(encoder, attn_down[index]), attn_up[index]) for index in (5, 6)]
    memory = matmul(encoder, w_cross_kv) + ADAPT_SCALE * jnp.concatenate(memory_parts, axis=1)
    cross_context = attention(cross_queries, memory[:, :width], memory[:, width:], None)
    after_cross = middle + project(cross_context, w_cross_out, attn_down[7], attn_up[7])
    normed_three = layer_norm(after_cross, norm_gains[2])
    hidden = jax.nn.gelu(project(normed_three, w_fc_in, in_down, in_up), approximate=True)
    return after_cross + project(hidden, w_fc_out, out_down, out_up)

def reference(tokens, encoder, cotangent, adapter_pick, segment_order, parents, norm_gains, w_qkv, w_self_out, w_cross_q, w_cross_kv, w_cross_out, w_fc_in, w_fc_out, attn_down, attn_up, fc_in_down, fc_in_up, fc_out_down, fc_out_up):
    reach_all = reach_table(segment_order, parents)
    tables = tuple((adapter_table.astype(jnp.float32) for adapter_table in (attn_down, attn_up, fc_in_down, fc_in_up, fc_out_down, fc_out_up)))
    frozen = (norm_gains, w_qkv, w_self_out, w_cross_q, w_cross_kv, w_cross_out, w_fc_in, w_fc_out)

    def one_tree(running, tree_items):
        tree_tokens, tree_encoder, tree_cotangent, chosen_index, reach_rows = tree_items

        def forward(inputs, memory, adapters):
            return tree_forward(inputs, memory, adapters, chosen_index, reach_rows, frozen)
        output, pullback = jax.vjp(forward, tree_tokens, tree_encoder, tables)
        grad_inputs, grad_memory, grad_tables = pullback(tree_cotangent)
        running = tuple((old_sum + grad_part for old_sum, grad_part in zip(running, grad_tables)))
        return (running, (output, grad_inputs, grad_memory))
    zero_sums = tuple((jnp.zeros_like(adapter_table) for adapter_table in tables))
    running, outputs = lax.scan(one_tree, zero_sums, (tokens, encoder, cotangent, adapter_pick, reach_all))
    return (outputs[0], outputs[1], outputs[2], running[0], running[1], running[2], running[3], running[4], running[5])
```

```python
import functools
import math

import jax
import jax.numpy as jnp
from jax import lax
from jax.experimental import pallas as pl
from jax.experimental.pallas import tpu as pltpu
from jax.sharding import PartitionSpec as P

HEADS = 16
HD = 64


PRECISE = lax.Precision.HIGHEST
ADAPT_SCALE = 2.0
NORM_EPS = 1e-05
MASK_FILL = -1e30


def matmul(left_side, right_side):
    return jnp.dot(left_side, right_side, precision=PRECISE, preferred_element_type=jnp.float32)


def product(formula, first_operand, second_operand):
    return jnp.einsum(
        formula,
        first_operand,
        second_operand,
        precision=PRECISE,
        preferred_element_type=jnp.float32,
    )


def reach_table(segment_order, parents):
    segment_count = parents.shape[-1]
    column = lax.broadcasted_iota(jnp.int32, (segment_count, segment_count), 1)
    identity = (
        lax.broadcasted_iota(jnp.int32, (segment_count, segment_count), 0) == column
    ).astype(jnp.int32)
    parent_hot = (parents[..., :, None] == column).astype(jnp.int32)

    def extend(sweep_index, reach_rows):
        return jnp.minimum(identity + jnp.einsum("gab,gbc->gac", parent_hot, reach_rows), 1)

    initial = jnp.broadcast_to(identity, parent_hot.shape)
    reach_rows = lax.fori_loop(0, segment_count, extend, initial)
    order_hot = (segment_order[..., :, None] == column).astype(jnp.int32)
    return jnp.einsum("gsa,gab,gtb->gst", order_hot, reach_rows, order_hot)


def layer_norm(values, gain_row):
    center = values - jnp.mean(values, -1, keepdims=True)
    inverse = lax.rsqrt(jnp.mean(center * center, -1, keepdims=True) + NORM_EPS)
    normal = center * inverse
    return (normal * gain_row, normal, inverse)


def norm_back(normal, inverse, gain_row, grads):
    scaled = grads * gain_row
    mean_one = jnp.mean(scaled, -1, keepdims=True)
    mean_two = jnp.mean(scaled * normal, -1, keepdims=True)
    return inverse * (scaled - mean_one - normal * mean_two)


def gelu_back(pre_act, d_hidden):

    def activate(values):
        return jax.nn.gelu(values, approximate=True)

    return jax.vjp(activate, pre_act)[1](d_hidden)[0]


def cols_forward(inputs, shard):
    flat_rows = inputs.reshape(-1, inputs.shape[-1])
    result = matmul(flat_rows, lax.all_gather(shard, "seq", axis=1, tiled=True))
    return result.reshape(inputs.shape[:-1] + (result.shape[-1],))


def cols_back(grads, shard):
    flat_grads = grads.reshape(-1, grads.shape[-1])
    result = matmul(flat_grads, lax.all_gather(shard, "seq", axis=1, tiled=True).T)
    return result.reshape(grads.shape[:-1] + (shard.shape[0],))


def rows_forward(inputs, shard):
    flat_rows = inputs.reshape(-1, inputs.shape[-1])
    result = matmul(flat_rows, lax.all_gather(shard, "seq", axis=0, tiled=True))
    return result.reshape(inputs.shape[:-1] + (shard.shape[1],))


def rows_back(grads, shard):
    flat_grads = grads.reshape(-1, grads.shape[-1])
    result = matmul(flat_grads, lax.all_gather(shard, "seq", axis=0, tiled=True).T)
    return result.reshape(grads.shape[:-1] + (result.shape[-1],))


def adapter_apply(inputs, down_map, up_map):
    inner = product("gsd,gdr->gsr", inputs, down_map)
    return (ADAPT_SCALE * product("gsr,gro->gso", inner, up_map), inner)


def adapter_back(inputs, inner, down_map, up_map, grads):
    d_inner = ADAPT_SCALE * product("gso,gro->gsr", grads, up_map)
    grad_up = ADAPT_SCALE * product("gsr,gso->gro", inner, grads)
    grad_down = product("gsd,gsr->gdr", inputs, d_inner)
    return (product("gsr,gdr->gsd", d_inner, down_map), grad_down, grad_up)


def key_mask(my_reach, my_slot, query_index, first_key, key_count, seg_len):
    slot_count = my_reach.shape[1]
    key_index = first_key + lax.broadcasted_iota(jnp.int32, (1, key_count), 1)
    key_slot = key_index // seg_len
    slot_hot = (key_slot[0][:, None] == lax.broadcasted_iota(jnp.int32, (1, slot_count), 1)).astype(
        jnp.int32
    )
    key_allowed = jnp.einsum("gc,nc->gn", my_reach, slot_hot)
    causal_ok = (key_slot != my_slot) | (key_index <= query_index)
    allowed = (key_allowed[:, None, :] > 0) & causal_ok[None]
    return (allowed, jnp.any(key_allowed > 0))


def self_forward(queries, key_rows, value_rows, my_reach, my_slot):
    groups, seg_len, width = queries.shape
    query_heads = queries.reshape(groups, seg_len, HEADS, HD) * HD ** (-0.5)
    query_index = my_slot * seg_len + lax.broadcasted_iota(jnp.int32, (seg_len, 1), 0)
    start_state = (
        jnp.full((groups, HEADS, seg_len), MASK_FILL, jnp.float32),
        jnp.zeros((groups, HEADS, seg_len), jnp.float32),
        jnp.zeros((groups, HEADS, seg_len, HD), jnp.float32),
    )
    key_part = lax.all_gather(key_rows, "seq", axis=1, tiled=True)
    value_part = lax.all_gather(value_rows, "seq", axis=1, tiled=True)
    key_count = key_part.shape[1]
    allowed, any_allowed = key_mask(
        my_reach, my_slot, query_index, jnp.int32(0), key_count, seg_len
    )

    def attend(state):
        peak, mass, accum = state
        key_heads = key_part.reshape(groups, key_count, HEADS, HD)
        value_heads = value_part.reshape(groups, key_count, HEADS, HD)
        scores = product("gshd,gnhd->ghsn", query_heads, key_heads)
        masked = jnp.where(allowed[:, None], scores, MASK_FILL)
        new_peak = jnp.maximum(peak, jnp.max(masked, -1))
        probs = jnp.where(allowed[:, None], jnp.exp(masked - new_peak[..., None]), 0.0)
        mass = jnp.sum(probs, -1)
        accum = product("ghsn,gnhd->ghsd", probs, value_heads)
        return (new_peak, mass, accum)

    peak, mass, accum = lax.cond(any_allowed, attend, lambda state: state, start_state)
    context = (accum / mass[..., None]).transpose(0, 2, 1, 3).reshape(groups, seg_len, width)
    return (context, peak + jnp.log(mass))


def self_backward(queries, key_all, value_all, log_mass, delta, d_context, my_reach, my_slot):
    groups, seg_len, width = queries.shape
    scale = HD ** (-0.5)
    query_heads = queries.reshape(groups, seg_len, HEADS, HD) * scale
    out_heads = d_context.reshape(groups, seg_len, HEADS, HD)
    query_index = my_slot * seg_len + lax.broadcasted_iota(jnp.int32, (seg_len, 1), 0)
    total_keys = key_all.shape[1]
    block_keys = seg_len * math.gcd(total_keys // seg_len, max(1, 512 // seg_len))
    firsts = jnp.arange(total_keys // block_keys, dtype=jnp.int32) * block_keys

    def block_step(state, first_key):
        allowed, any_allowed = key_mask(
            my_reach, my_slot, query_index, first_key, block_keys, seg_len
        )

        def gradients(inner_state):
            key_heads = lax.dynamic_slice_in_dim(key_all, first_key, block_keys, 1).reshape(
                groups, block_keys, HEADS, HD
            )
            value_heads = lax.dynamic_slice_in_dim(value_all, first_key, block_keys, 1).reshape(
                groups, block_keys, HEADS, HD
            )
            scores = product("gshd,gnhd->ghsn", query_heads, key_heads)
            masked = jnp.where(allowed[:, None], scores, MASK_FILL)
            probs = jnp.where(allowed[:, None], jnp.exp(masked - log_mass[..., None]), 0.0)
            d_probs = product("gshd,gnhd->ghsn", out_heads, value_heads)
            d_scores = probs * (d_probs - delta[..., None])
            d_query = inner_state[0] + product("ghsn,gnhd->gshd", d_scores, key_heads)
            d_value_part = product("ghsn,gshd->gnhd", probs, out_heads)
            d_key_part = product("ghsn,gshd->gnhd", d_scores, query_heads)
            d_key_all = lax.dynamic_update_slice_in_dim(
                inner_state[1], d_key_part.reshape(groups, block_keys, width), first_key, 1
            )
            d_value_all = lax.dynamic_update_slice_in_dim(
                inner_state[2], d_value_part.reshape(groups, block_keys, width), first_key, 1
            )
            return (d_query, d_key_all, d_value_all)

        return (lax.cond(any_allowed, gradients, lambda inner_state: inner_state, state), None)

    zero_query = jnp.zeros((groups, seg_len, HEADS, HD), jnp.float32)
    initial = (zero_query, jnp.zeros_like(key_all), jnp.zeros_like(value_all))
    final_state, unused = lax.scan(block_step, initial, firsts)
    d_query = final_state[0].reshape(groups, seg_len, width) * scale
    return (d_query, final_state[1], final_state[2])


def cross_forward(queries, key_rows, value_rows):
    groups, seg_len, width = queries.shape
    enc_rows = key_rows.shape[1]
    query_heads = queries.reshape(groups, seg_len, HEADS, HD) * HD ** (-0.5)
    scores = product("gshd,gehd->ghse", query_heads, key_rows.reshape(groups, enc_rows, HEADS, HD))
    probs = jax.nn.softmax(scores, axis=-1)
    context = product("ghse,gehd->gshd", probs, value_rows.reshape(groups, enc_rows, HEADS, HD))
    return (context.reshape(groups, seg_len, width), probs)


def cross_backward(queries, key_rows, value_rows, probs, d_context):
    groups, seg_len, width = queries.shape
    enc_rows = key_rows.shape[1]
    scale = HD ** (-0.5)
    query_heads = queries.reshape(groups, seg_len, HEADS, HD) * scale
    key_heads = key_rows.reshape(groups, enc_rows, HEADS, HD)
    value_heads = value_rows.reshape(groups, enc_rows, HEADS, HD)
    out_heads = d_context.reshape(groups, seg_len, HEADS, HD)
    d_values = product("ghse,gshd->gehd", probs, out_heads)
    d_probs = product("gshd,gehd->ghse", out_heads, value_heads)
    d_scores = probs * (d_probs - jnp.sum(probs * d_probs, -1, keepdims=True))
    d_queries = product("ghse,gehd->gshd", d_scores, key_heads) * scale
    d_keys = product("ghse,gshd->gehd", d_scores, query_heads)
    return (
        d_queries.reshape(groups, seg_len, width),
        d_keys.reshape(groups, enc_rows, width),
        d_values.reshape(groups, enc_rows, width),
    )


def shards(
    tokens,
    encoder,
    cotangent,
    adapter_pick,
    segment_order,
    parents,
    norm_gains,
    w_qkv,
    w_self_out,
    w_cross_q,
    w_cross_kv,
    w_cross_out,
    w_fc_in,
    w_fc_out,
    attn_down,
    attn_up,
    fc_in_down,
    fc_in_up,
    fc_out_down,
    fc_out_up,
):
    groups, seg_len, width = tokens.shape
    enc_rows = encoder.shape[1]
    my_slot = lax.axis_index("seq")
    reach_rows = reach_table(segment_order, parents)
    my_reach = lax.dynamic_index_in_dim(reach_rows, my_slot, 1, keepdims=False)
    adapter_count = attn_down.shape[0]
    chosen = (
        adapter_pick[:, None] == lax.broadcasted_iota(jnp.int32, (1, adapter_count), 1)
    ).astype(jnp.float32)
    chosen_low = chosen.astype(jnp.bfloat16)

    def select(adapter_table):
        return jnp.einsum(
            "ga,a...->g...", chosen_low, adapter_table, preferred_element_type=jnp.float32
        )

    sel_down = select(attn_down)
    sel_up = select(attn_up)
    in_down = select(fc_in_down)
    in_up = select(fc_in_up)
    out_down = select(fc_out_down)
    out_up = select(fc_out_up)
    normed_one, normal_one, inverse_one = layer_norm(tokens, norm_gains[0])
    inner_qkv = product("gsd,gpdr->gspr", normed_one, sel_down[:, 0:3])
    stacked = cols_forward(normed_one, w_qkv) + ADAPT_SCALE * product(
        "gspr,gpro->gspo", inner_qkv, sel_up[:, 0:3]
    ).reshape(groups, seg_len, 3 * width)
    queries = stacked[..., :width]
    key_rows = stacked[..., width : 2 * width]
    value_rows = stacked[..., 2 * width :]
    context, log_mass = self_forward(queries, key_rows, value_rows, my_reach, my_slot)
    self_term, inner_self = adapter_apply(context, sel_down[:, 3], sel_up[:, 3])
    middle = tokens + rows_forward(context, w_self_out) + self_term
    normed_two, normal_two, inverse_two = layer_norm(middle, norm_gains[1])
    query_term, inner_cross_q = adapter_apply(normed_two, sel_down[:, 4], sel_up[:, 4])
    cross_queries = cols_forward(normed_two, w_cross_q) + query_term
    inner_memory = product("ged,gpdr->gepr", encoder, sel_down[:, 5:7])
    memory = cols_forward(encoder, w_cross_kv) + ADAPT_SCALE * product(
        "gepr,gpro->gepo", inner_memory, sel_up[:, 5:7]
    ).reshape(groups, enc_rows, 2 * width)
    cross_keys = memory[..., :width]
    cross_values = memory[..., width:]
    cross_context, cross_probs = cross_forward(cross_queries, cross_keys, cross_values)
    cross_term, inner_cross_out = adapter_apply(cross_context, sel_down[:, 7], sel_up[:, 7])
    after_cross = middle + rows_forward(cross_context, w_cross_out) + cross_term
    normed_three, normal_three, inverse_three = layer_norm(after_cross, norm_gains[2])
    inner_in = product("gsd,gdr->gsr", normed_three, in_down)
    pre_act = cols_forward(normed_three, w_fc_in) + ADAPT_SCALE * product(
        "gsr,grf->gsf", inner_in, in_up
    )
    hidden = jax.nn.gelu(pre_act, approximate=True)
    inner_out = product("gsf,gfr->gsr", hidden, out_down)
    mlp_out = rows_forward(hidden, w_fc_out) + ADAPT_SCALE * product(
        "gsr,grd->gsd", inner_out, out_up
    )
    layer_out = after_cross + mlp_out
    d_inner_out = ADAPT_SCALE * product("gsd,grd->gsr", cotangent, out_up)
    grad_out_up_tree = ADAPT_SCALE * product("gsr,gsd->grd", inner_out, cotangent)
    d_hidden = rows_back(cotangent, w_fc_out) + product("gsr,gfr->gsf", d_inner_out, out_down)
    grad_out_down_tree = product("gsf,gsr->gfr", hidden, d_inner_out)
    d_pre = gelu_back(pre_act, d_hidden)
    d_inner_in = ADAPT_SCALE * product("gsf,grf->gsr", d_pre, in_up)
    grad_in_up_tree = ADAPT_SCALE * product("gsr,gsf->grf", inner_in, d_pre)
    d_normed_three = cols_back(d_pre, w_fc_in) + product("gsr,gdr->gsd", d_inner_in, in_down)
    grad_in_down_tree = product("gsd,gsr->gdr", normed_three, d_inner_in)
    d_after = cotangent + norm_back(normal_three, inverse_three, norm_gains[2], d_normed_three)
    d_cross_ctx, grad_down_seven, grad_up_seven = adapter_back(
        cross_context, inner_cross_out, sel_down[:, 7], sel_up[:, 7], d_after
    )
    d_cross_ctx = d_cross_ctx + rows_back(d_after, w_cross_out)
    d_cross_q, d_cross_k, d_cross_v = cross_backward(
        cross_queries, cross_keys, cross_values, cross_probs, d_cross_ctx
    )
    d_normed_two, grad_down_four, grad_up_four = adapter_back(
        normed_two, inner_cross_q, sel_down[:, 4], sel_up[:, 4], d_cross_q
    )
    d_normed_two = d_normed_two + cols_back(d_cross_q, w_cross_q)
    d_middle = d_after + norm_back(normal_two, inverse_two, norm_gains[1], d_normed_two)
    d_memory = jnp.concatenate([d_cross_k, d_cross_v], axis=-1)
    d_memory_split = d_memory.reshape(groups, enc_rows, 2, width)
    d_inner_memory = ADAPT_SCALE * product("gepo,gpro->gepr", d_memory_split, sel_up[:, 5:7])
    grad_up_memory = ADAPT_SCALE * product("gepr,gepo->gpro", inner_memory, d_memory_split)
    grad_down_memory = product("ged,gepr->gpdr", encoder, d_inner_memory)
    d_encoder_local = cols_back(d_memory, w_cross_kv) + product(
        "gepr,gpdr->ged", d_inner_memory, sel_down[:, 5:7]
    )
    grad_encoder = lax.psum_scatter(d_encoder_local, "seq", scatter_dimension=1, tiled=True)
    d_context, grad_down_three, grad_up_three = adapter_back(
        context, inner_self, sel_down[:, 3], sel_up[:, 3], d_middle
    )
    d_context = d_context + rows_back(d_middle, w_self_out)
    delta = jnp.sum(
        d_context.reshape(groups, seg_len, HEADS, HD) * context.reshape(groups, seg_len, HEADS, HD),
        -1,
    ).transpose(0, 2, 1)
    key_all, value_all = (
        lax.all_gather(key_rows, "seq", axis=1, tiled=True),
        lax.all_gather(value_rows, "seq", axis=1, tiled=True),
    )
    d_queries, d_key_all, d_value_all = self_backward(
        queries, key_all, value_all, log_mass, delta, d_context, my_reach, my_slot
    )
    d_keys, d_values = (
        lax.psum_scatter(d_key_all, "seq", scatter_dimension=1, tiled=True),
        lax.psum_scatter(d_value_all, "seq", scatter_dimension=1, tiled=True),
    )
    d_stacked = jnp.concatenate([d_queries, d_keys, d_values], axis=-1)
    d_split = d_stacked.reshape(groups, seg_len, 3, width)
    d_inner_qkv = ADAPT_SCALE * product("gspo,gpro->gspr", d_split, sel_up[:, 0:3])
    grad_up_qkv = ADAPT_SCALE * product("gspr,gspo->gpro", inner_qkv, d_split)
    grad_down_qkv = product("gsd,gspr->gpdr", normed_one, d_inner_qkv)
    d_normed_one = cols_back(d_stacked, w_qkv) + product(
        "gspr,gpdr->gsd", d_inner_qkv, sel_down[:, 0:3]
    )
    grad_tokens = d_middle + norm_back(normal_one, inverse_one, norm_gains[0], d_normed_one)
    down_stack = jnp.concatenate(
        [
            grad_down_qkv,
            grad_down_three[:, None],
            grad_down_four[:, None],
            grad_down_memory,
            grad_down_seven[:, None],
        ],
        axis=1,
    )
    up_stack = jnp.concatenate(
        [
            grad_up_qkv,
            grad_up_three[:, None],
            grad_up_four[:, None],
            grad_up_memory,
            grad_up_seven[:, None],
        ],
        axis=1,
    )
    tree_parts = (
        down_stack,
        up_stack,
        grad_in_down_tree,
        grad_in_up_tree,
        grad_out_down_tree,
        grad_out_up_tree,
    )
    shapes = (
        attn_down.shape,
        attn_up.shape,
        fc_in_down.shape,
        fc_in_up.shape,
        fc_out_down.shape,
        fc_out_up.shape,
    )
    local_sums = tuple(
        (product("ga,gx->ax", chosen, part.reshape(groups, -1)).reshape(-1) for part in tree_parts)
    )
    owned = lax.psum_scatter(local_sums, ("dp", "seq"), scatter_dimension=0, tiled=True)
    full_sums = lax.all_gather(owned, ("dp", "seq"), axis=0, tiled=True)
    results = [summed.reshape(shape) for summed, shape in zip(full_sums, shapes)]
    return (
        layer_out,
        grad_tokens,
        grad_encoder,
        results[0],
        results[1],
        results[2],
        results[3],
        results[4],
        results[5],
    )


ROWS = ("z", "y")
COPIES = ("x", "c")
EVERY = ROWS + COPIES
F32 = jnp.float32
BF16 = jnp.bfloat16
MIB = 1 << 20
SWAP = [(0, 1), (1, 0)]
NN = (((1,), (0,)), ((), ()))
NT = (((1,), (1,)), ((), ()))
TN = (((0,), (0,)), ((), ()))


def split(values):
    high = values.astype(BF16)
    return high, (values - high.astype(F32)).astype(BF16)


def dot(left, right, dims=NN):
    return lax.dot_general(left, right, dims, preferred_element_type=F32)


def dot3(left, right, dims=NN):
    (left_high, left_low), (right_high, right_low) = left, right
    return (
        dot(left_high, right_high, dims)
        + dot(left_high, right_low, dims)
        + dot(left_low, right_high, dims)
    )


def dot2(left, right, dims=NN):
    return dot(left[0], right, dims) + dot(left[1], right, dims)


def adapted(rows, down, up):
    inner = dot2(rows, down, NT)
    return dot2(split(ADAPT_SCALE * inner), up), inner


def adapted_back(rows, grads, down, up):
    inner = split(ADAPT_SCALE * dot2(rows, down, NT))
    d_inner = split(ADAPT_SCALE * dot2(grads, up, NT))
    return dot2(d_inner, down), dot3(d_inner, rows, TN), dot3(inner, grads, TN)


def both(parts, where):
    return parts[0][where], parts[1][where]


def vmem(limit):
    return pltpu.CompilerParams(vmem_limit_bytes=limit * MIB)


def shaped(*shape):
    return jax.ShapeDtypeStruct(shape, F32)


def whole_spec(shape):
    return pl.BlockSpec(shape, lambda *_: (0,) * len(shape))


def heads_kernel(
    tokens_ref,
    gains_ref,
    weight_ref,
    down_ref,
    up_ref,
    normed_ref,
    inner_ref,
    qkv_ref,
    rows_ref,
    w_high,
    w_low,
    out_sem,
    up_sem,
    down_sem,
    across_sem,
    here_sem,
):
    z, y = lax.axis_index("z"), lax.axis_index("y")
    last = lax.axis_size("z") - 1
    trees, seg_len, width = tokens_ref.shape
    lanes = weight_ref.shape[2]
    rank = up_ref.shape[2]

    def place(level, side):
        return level * 2 + side

    def move(slot, sems, index, target):
        return pltpu.make_async_remote_copy(
            src_ref=rows_ref.at[slot],
            dst_ref=rows_ref.at[slot],
            send_sem=sems.at[index],
            recv_sem=here_sem.at[slot],
            device_id=target,
            device_id_type=pl.DeviceIdType.MESH,
        )

    def upward(hop):
        return move(place(z - hop, y), up_sem, hop, {"z": z + 1})

    def downward(hop):
        return move(place(z + hop, y), down_sem, hop, {"z": z - 1})

    def across(level, index):
        return move(place(level, y), across_sem, index, {"y": 1 - y})

    def arrived(slot):
        move(slot, across_sem, 0, {"y": 1 - y}).wait_recv()

    barrier = pltpu.get_barrier_semaphore()
    pl.semaphore_signal(barrier, 1, device_id={"y": 1 - y}, device_id_type=pl.DeviceIdType.MESH)

    @pl.when(z > 0)
    def _():
        pl.semaphore_signal(
            barrier, 1, device_id={"z": z - 1}, device_id_type=pl.DeviceIdType.MESH
        )

    @pl.when(z < last)
    def _():
        pl.semaphore_signal(
            barrier, 1, device_id={"z": z + 1}, device_id_type=pl.DeviceIdType.MESH
        )

    own = place(z, y)
    for tree in range(trees):
        normed = layer_norm(tokens_ref[tree], gains_ref[0:1])[0]
        rows_ref[own, tree * seg_len : (tree + 1) * seg_len] = normed
    pl.semaphore_wait(
        barrier, 1 + (z > 0).astype(jnp.int32) + (z < last).astype(jnp.int32)
    )

    @pl.when(z < last)
    def _():
        upward(0).start()

    @pl.when(z > 0)
    def _():
        downward(0).start()

    across(z, 0).start()
    for kind in range(3):
        high, low = split(weight_ref[kind])
        w_high[:, kind * lanes : (kind + 1) * lanes] = high
        w_low[:, kind * lanes : (kind + 1) * lanes] = low

    def keep(slot):
        return pltpu.make_async_copy(rows_ref.at[slot], normed_ref.at[slot], out_sem.at[slot])

    def work(slot):
        keep(slot).start()
        parts = split(rows_ref[slot])
        product = dot3(parts, (w_high[...], w_low[...]))
        for tree in range(trees):
            rows = slice(tree * seg_len, (tree + 1) * seg_len)
            inner = dot2(both(parts, rows), down_ref[tree], NT)
            inner_ref[slot, tree] = inner
            inner_parts = split(ADAPT_SCALE * inner)
            for kind in range(3):
                term = dot2(
                    both(inner_parts, (slice(None), slice(kind * rank, (kind + 1) * rank))),
                    up_ref[tree, kind],
                )
                qkv_ref[slot, kind, tree] = (
                    product[rows, kind * lanes : (kind + 1) * lanes] + term
                )

    work(own)
    for hop in range(1, last + 1):

        @pl.when(z - hop >= 0)
        def _(hop=hop):
            arrived(place(z - hop, y))

            @pl.when(z < last)
            def _():
                upward(hop).start()

            across(z - hop, hop).start()

        @pl.when(z + hop <= last)
        def _(hop=hop):
            arrived(place(z + hop, y))

            @pl.when(z > 0)
            def _():
                downward(hop).start()

            across(z + hop, last + hop).start()

        for step in (-1, 1):
            level = z + step * hop
            before = level - step

            @pl.when(jnp.logical_and(level >= 0, level <= last))
            def _(level=level):
                work(place(level, y))

            if hop == 1 and step == 1:
                continue

            @pl.when(jnp.logical_and(before >= 0, before <= last))
            def _(before=before):
                arrived(place(before, 1 - y))
                work(place(before, 1 - y))

    for level in (z - last, z + last):

        @pl.when(jnp.logical_and(level >= 0, level <= last))
        def _(level=level):
            arrived(place(level, 1 - y))
            work(place(level, 1 - y))

    across(z, 0).wait_send()
    for hop in range(0, last + 1):

        @pl.when(jnp.logical_and(z - hop >= 0, z < last))
        def _(hop=hop):
            upward(hop).wait_send()

        @pl.when(jnp.logical_and(z + hop <= last, z > 0))
        def _(hop=hop):
            downward(hop).wait_send()

        if hop:

            @pl.when(z - hop >= 0)
            def _(hop=hop):
                across(z - hop, hop).wait_send()

            @pl.when(z + hop <= last)
            def _(hop=hop):
                across(z + hop, last + hop).wait_send()

    for slot in range(normed_ref.shape[0]):
        keep(slot).wait()


def heads_call(tokens, gains, weight, down, up):
    trees, seg_len, width = tokens.shape
    slots = lax.axis_size(ROWS)
    levels = lax.axis_size("z")
    lanes = weight.shape[2]
    inner = down.shape[1]
    dma = pltpu.SemaphoreType.DMA
    here = pl.BlockSpec(memory_space=pltpu.VMEM)
    return pl.pallas_call(
        heads_kernel,
        out_shape=[
            shaped(slots, trees * seg_len, width),
            shaped(slots, trees, seg_len, inner),
            shaped(slots, 3, trees, seg_len, lanes),
        ],
        in_specs=[here] * 5,
        out_specs=[pl.BlockSpec(memory_space=pl.ANY), here, here],
        scratch_shapes=[
            pltpu.VMEM((slots, trees * seg_len, width), F32),
            pltpu.VMEM((width, 3 * lanes), BF16),
            pltpu.VMEM((width, 3 * lanes), BF16),
            dma((slots,)),
            dma((levels,)),
            dma((levels,)),
            dma((2 * levels - 1,)),
            dma((slots,)),
        ],
        compiler_params=pltpu.CompilerParams(
            vmem_limit_bytes=48 * MIB, collective_id=0, has_side_effects=True
        ),
    )(tokens, gains, weight, down, up)


def ancestor_slots(order_ref, parents_ref, slot_of, tree, slot, depth):
    segment = order_ref[tree, slot]
    chain = [(slot, None)]
    there = None
    for _ in range(depth - 1):
        parent = parents_ref[tree, segment]
        there = parent >= 0 if there is None else jnp.logical_and(there, parent >= 0)
        segment = jnp.maximum(parent, 0)
        chain.append((slot_of[segment], there))
    return chain


def fill_slot_of(order_ref, slot_of, tree, slots):
    for slot in range(slots):
        slot_of[order_ref[tree, slot]] = slot


def chain_mask(chain, seg_len):
    row = lax.broadcasted_iota(jnp.int32, (seg_len, seg_len), 0)
    column = lax.broadcasted_iota(jnp.int32, (seg_len, seg_len), 1)
    masks = [(column <= row).astype(jnp.int32)]
    for _, there in chain[1:]:
        masks.append(jnp.full((seg_len, seg_len), there.astype(jnp.int32)))
    return jnp.concatenate(masks, axis=1) > 0


def attend(queries, keys, values, mask):
    scores = dot3(split(queries), split(keys), NT)
    if mask is not None:
        scores = jnp.where(mask, scores, MASK_FILL)
    weights = jnp.exp(scores - jnp.max(scores, -1, keepdims=True))
    mass = jnp.sum(weights, -1, keepdims=True)
    return dot3(split(weights), split(values)) / mass


def attend_back(queries, keys, values, d_context, mask):
    query_parts, key_parts = split(queries), split(keys)
    value_parts, out_parts = split(values), split(d_context)
    scores = dot3(query_parts, key_parts, NT)
    if mask is not None:
        scores = jnp.where(mask, scores, MASK_FILL)
    weights = jnp.exp(scores - jnp.max(scores, -1, keepdims=True))
    weights = weights / jnp.sum(weights, -1, keepdims=True)
    d_weights = dot3(out_parts, value_parts, NT)
    shared = jnp.sum(weights * d_weights, -1, keepdims=True)
    score_parts = split(weights * (d_weights - shared))
    return (
        dot3(score_parts, key_parts) * HD ** (-0.5),
        dot3(score_parts, query_parts, TN),
        dot3(split(weights), out_parts, TN),
    )


def by_head(formula, *arrays, mask=None):
    results = []
    for head in range(arrays[0].shape[1] // HD):
        lanes = slice(head * HD, (head + 1) * HD)
        results.append(formula(*[array[:, lanes] for array in arrays], mask))
    if isinstance(results[0], tuple):
        return [jnp.concatenate(parts, axis=1) for parts in zip(*results)]
    return jnp.concatenate(results, axis=1)


def self_forward_kernel(depth, order_ref, parents_ref, qkv_ref, context_ref, slot_of):
    tree = pl.program_id(0)
    slots, seg_len = qkv_ref.shape[0], qkv_ref.shape[3]
    fill_slot_of(order_ref, slot_of, tree, slots)

    def one_slot(slot, carry):
        chain = ancestor_slots(order_ref, parents_ref, slot_of, tree, slot, depth)
        keys = jnp.concatenate([qkv_ref[where, 1, 0] for where, _ in chain], axis=0)
        values = jnp.concatenate([qkv_ref[where, 2, 0] for where, _ in chain], axis=0)
        context_ref[slot, 0] = by_head(
            attend,
            qkv_ref[slot, 0, 0] * HD ** (-0.5),
            keys,
            values,
            mask=chain_mask(chain, seg_len),
        )
        return carry

    lax.fori_loop(0, slots, one_slot, 0)


def self_backward_kernel(
    depth,
    order_ref,
    parents_ref,
    qkv_ref,
    d_context_ref,
    normed_ref,
    inner_ref,
    up_ref,
    d_qkv_ref,
    g_down_ref,
    g_up_ref,
    slot_of,
):
    tree = pl.program_id(0)
    slots, seg_len, pair = qkv_ref.shape[0], qkv_ref.shape[3], qkv_ref.shape[4]
    rank = up_ref.shape[2]
    fill_slot_of(order_ref, slot_of, tree, slots)
    d_qkv_ref[...] = jnp.zeros_like(d_qkv_ref)

    def one_slot(slot, carry):
        chain = ancestor_slots(order_ref, parents_ref, slot_of, tree, slot, depth)
        keys = jnp.concatenate([qkv_ref[where, 1, 0] for where, _ in chain], axis=0)
        values = jnp.concatenate([qkv_ref[where, 2, 0] for where, _ in chain], axis=0)
        d_queries, d_keys, d_values = by_head(
            attend_back,
            qkv_ref[slot, 0, 0] * HD ** (-0.5),
            keys,
            values,
            d_context_ref[slot, 0],
            mask=chain_mask(chain, seg_len),
        )
        d_qkv_ref[slot, 0, 0] += d_queries
        for entry, (where, _) in enumerate(chain):
            rows = slice(entry * seg_len, (entry + 1) * seg_len)
            d_qkv_ref[where, 1, 0] += d_keys[rows]
            d_qkv_ref[where, 2, 0] += d_values[rows]
        return carry

    lax.fori_loop(0, slots, one_slot, 0)

    normed = split(normed_ref[...].reshape(slots * seg_len, -1))
    inner = split(ADAPT_SCALE * inner_ref[...].reshape(slots * seg_len, 3 * rank))
    for kind in range(3):
        grads = split(d_qkv_ref[:, kind, 0].reshape(slots * seg_len, pair))
        ranks = slice(kind * rank, (kind + 1) * rank)
        d_inner = split(ADAPT_SCALE * dot2(grads, up_ref[0, kind], NT))
        g_down_ref[0, kind] = dot3(d_inner, normed, TN)
        g_up_ref[0, kind] = dot3(both(inner, (slice(None), ranks)), grads, TN)


def slots_spec(shape):
    lead = len(shape) - 3
    return pl.BlockSpec(
        shape[:lead] + (1,) + shape[lead + 1 :],
        lambda tree, *_: (0,) * lead + (tree, 0, 0),
    )


def tree_spec(shape):
    return pl.BlockSpec((1,) + shape[1:], lambda tree, *_: (tree,) + (0,) * (len(shape) - 1))


def self_call(kernel, depth, order, parents, operands, in_specs, out_shape, out_specs):
    trees, slots = order.shape
    return pl.pallas_call(
        functools.partial(kernel, depth),
        out_shape=out_shape,
        grid_spec=pltpu.PrefetchScalarGridSpec(
            num_scalar_prefetch=2,
            grid=(trees,),
            in_specs=in_specs,
            out_specs=out_specs,
            scratch_shapes=[pltpu.SMEM((slots,), jnp.int32)],
        ),
        compiler_params=vmem(56),
    )(order, parents, *operands)


def cross_forward_kernel(query_ref, key_ref, value_ref, context_ref):
    context_ref[0] = by_head(
        attend, query_ref[0] * HD ** (-0.5), key_ref[0], value_ref[0]
    )


def cross_backward_kernel(
    query_ref, key_ref, value_ref, d_context_ref, d_query_ref, d_key_ref, d_value_ref
):
    d_query_ref[0], d_key_ref[0], d_value_ref[0] = by_head(
        attend_back,
        query_ref[0] * HD ** (-0.5),
        key_ref[0],
        value_ref[0],
        d_context_ref[0],
    )


def cross_call(kernel, queries, memory, rest, long_outs):
    trees, seg_len, width = queries.shape
    enc_rows = memory.shape[1]
    lanes = 2 * HD
    steps = width // lanes
    short = pl.BlockSpec((1, seg_len, lanes), lambda tree, step: (tree, 0, step))
    keys = pl.BlockSpec((1, enc_rows, lanes), lambda tree, step: (tree, 0, step))
    values = pl.BlockSpec((1, enc_rows, lanes), lambda tree, step: (tree, 0, steps + step))
    return pl.pallas_call(
        kernel,
        out_shape=[shaped(trees, seg_len, width)] + [shaped(trees, enc_rows, width)] * long_outs,
        grid=(trees, steps),
        in_specs=[short, keys, values] + [short] * len(rest),
        out_specs=[short] + [keys] * long_outs,
        compiler_params=vmem(48),
    )(queries, memory, memory, *rest)


def square(ref):
    return ref[...].reshape(-1, ref.shape[-1])


def joined(ref):
    slots, trees = ref.shape[:2]
    return jnp.concatenate(
        [
            jnp.concatenate([ref[slot, tree] for slot in range(slots)], axis=1)
            for tree in range(trees)
        ],
        axis=0,
    )


def rows_of(ref):
    return ref[...].reshape(-1, ref.shape[-1])


def tree_rows(trees, count):
    return [slice(tree * count, (tree + 1) * count) for tree in range(trees)]


def with_adapters(parts, down_ref, up_ref, entry, trees):
    count = parts[0].shape[0] // trees
    return jnp.concatenate(
        [
            adapted(both(parts, rows), down_ref[tree, entry], up_ref[tree, entry])[0]
            for tree, rows in enumerate(tree_rows(trees, count))
        ],
        axis=0,
    )


def with_adapters_back(parts, grads, down_ref, up_ref, entry, trees, g_down_ref, g_up_ref, place):
    count = parts[0].shape[0] // trees
    terms = []
    for tree, rows in enumerate(tree_rows(trees, count)):
        term, g_down_ref[tree, place], g_up_ref[tree, place] = adapted_back(
            both(parts, rows), both(grads, rows), down_ref[tree, entry], up_ref[tree, entry]
        )
        terms.append(term)
    return jnp.concatenate(terms, axis=0)


def after_self_kernel(
    context_ref, tokens_ref, gains_ref, out_ref, query_ref, down_ref, up_ref, middle_ref, cross_ref
):
    trees = tokens_ref.shape[0]
    context = split(joined(context_ref))
    middle = rows_of(tokens_ref) + dot3(context, split(square(out_ref)))
    middle = middle + with_adapters(context, down_ref, up_ref, 3, trees)
    middle_ref[...] = middle.reshape(middle_ref.shape)
    normed = split(layer_norm(middle, gains_ref[1:2])[0])
    queries = dot3(normed, split(square(query_ref)), NT)
    queries = queries + with_adapters(normed, down_ref, up_ref, 4, trees)
    cross_ref[...] = queries.reshape(cross_ref.shape)


def after_cross_kernel(
    context_ref, middle_ref, gains_ref, out_ref, down_ref, up_ref, after_ref, normed_ref
):
    trees = context_ref.shape[0]
    context = split(rows_of(context_ref))
    after = rows_of(middle_ref) + dot3(context, split(square(out_ref)))
    after = after + with_adapters(context, down_ref, up_ref, 7, trees)
    after_ref[...] = after.reshape(after_ref.shape)
    normed = layer_norm(after, gains_ref[2:3])[0]
    normed_ref[...] = normed.reshape(normed_ref.shape)


def into_cross_kernel(
    own_ref,
    other_ref,
    after_ref,
    cotangent_ref,
    context_ref,
    gains_ref,
    out_ref,
    down_ref,
    up_ref,
    d_after_ref,
    d_context_ref,
    g_down_ref,
    g_up_ref,
):
    trees = after_ref.shape[0]
    _, normal, inverse = layer_norm(rows_of(after_ref), gains_ref[2:3])
    d_normed = rows_of(own_ref) + rows_of(other_ref)
    d_after = rows_of(cotangent_ref) + norm_back(normal, inverse, gains_ref[2:3], d_normed)
    d_after_ref[...] = d_after.reshape(d_after_ref.shape)
    grads = split(d_after)
    context = split(rows_of(context_ref))
    d_context = dot3(grads, split(square(out_ref)), NT)
    d_context = d_context + with_adapters_back(
        context, grads, down_ref, up_ref, 7, trees, g_down_ref, g_up_ref, 0
    )
    d_context_ref[...] = d_context.reshape(d_context_ref.shape)


def into_self_kernel(
    d_query_ref,
    d_after_ref,
    middle_ref,
    context_ref,
    gains_ref,
    query_ref,
    out_ref,
    down_ref,
    up_ref,
    d_middle_ref,
    d_context_ref,
    g_down_ref,
    g_up_ref,
):
    slots, trees, seg_len, lanes = context_ref.shape
    rows, normal, inverse = layer_norm(rows_of(middle_ref), gains_ref[1:2])
    grads = split(rows_of(d_query_ref))
    d_normed = dot3(grads, split(square(query_ref)))
    d_normed = d_normed + with_adapters_back(
        split(rows), grads, down_ref, up_ref, 4, trees, g_down_ref, g_up_ref, 1
    )
    d_middle = rows_of(d_after_ref) + norm_back(normal, inverse, gains_ref[1:2], d_normed)
    d_middle_ref[...] = d_middle.reshape(d_middle_ref.shape)
    grads = split(d_middle)
    context = split(joined(context_ref))
    d_context = dot3(grads, split(square(out_ref)), NT)
    d_context = d_context + with_adapters_back(
        context, grads, down_ref, up_ref, 3, trees, g_down_ref, g_up_ref, 0
    )
    for slot in range(slots):
        for tree in range(trees):
            d_context_ref[slot, tree] = d_context[
                tree * seg_len : (tree + 1) * seg_len, slot * lanes : (slot + 1) * lanes
            ]


def packed_spec(packed, first, count):
    return pl.BlockSpec(
        packed.shape[:2] + (count, packed.shape[3]), lambda *_: (0, 0, first // count, 0)
    )


def rows_call(kernel, operands, specs, out_shape):
    return pl.pallas_call(
        kernel,
        out_shape=out_shape,
        grid=(1,),
        in_specs=[
            whole_spec(operand.shape) if spec is None else spec
            for operand, spec in zip(operands, specs)
        ],
        out_specs=[whole_spec(out.shape) for out in out_shape],
        compiler_params=vmem(56),
    )(*operands)


def memory_kernel(encoder_ref, weight_ref, down_ref, up_ref, memory_ref, row_high, row_low, inner):
    trees, rank = down_ref.shape[0], down_ref.shape[2]
    step = pl.program_id(0)
    half = pl.num_programs(0) // 2
    lanes = memory_ref.shape[2]
    count = encoder_ref.shape[1]

    @pl.when(step == 0)
    def _():
        row_high[...], row_low[...] = split(rows_of(encoder_ref))
        for tree, rows in enumerate(tree_rows(trees, count)):
            for kind in range(2):
                parts = (row_high[rows], row_low[rows])
                inner[kind, rows] = jnp.concatenate(
                    split(ADAPT_SCALE * dot2(parts, down_ref[tree, 5 + kind], NT)), axis=1
                )

    result = dot3((row_high[...], row_low[...]), split(square(weight_ref)), NT)
    kind = step // half
    for tree, rows in enumerate(tree_rows(trees, count)):
        up = up_ref[tree, 0]
        term = dot(inner[kind, rows], jnp.concatenate([up, up], axis=0))
        memory_ref[tree] = result[rows] + term


def memory_call(encoder, packed, down, up):
    trees, count, width = encoder.shape
    rank = down.shape[2]
    slots, copies = packed.shape[:2]
    lanes = 2 * width // slots
    half = slots // 2
    return pl.pallas_call(
        memory_kernel,
        out_shape=shaped(trees, count, 2 * width),
        grid=(slots,),
        in_specs=[
            whole_spec(encoder.shape),
            pl.BlockSpec((1, copies, lanes // copies, width), lambda step: (step, 0, 0, 0)),
            whole_spec(down.shape),
            pl.BlockSpec((trees, 1, rank, lanes), lambda step: (0, 5 + step // half, 0, step % half)),
        ],
        out_specs=pl.BlockSpec((trees, count, lanes), lambda step: (0, 0, step)),
        scratch_shapes=[
            pltpu.VMEM((trees * count, width), BF16),
            pltpu.VMEM((trees * count, width), BF16),
            pltpu.VMEM((2, trees * count, 2 * rank), BF16),
        ],
        compiler_params=vmem(56),
    )(encoder, packed, down, up)


def memory_back_kernel(
    encoder_ref,
    d_key_ref,
    d_value_ref,
    weight_ref,
    down_ref,
    up_ref,
    d_encoder_ref,
    g_down_ref,
    g_up_ref,
    row_high,
    row_low,
    inner,
    d_inner,
):
    trees, rank = down_ref.shape[0], down_ref.shape[2]
    step = pl.program_id(0)
    half = pl.num_programs(0) // 2
    count = encoder_ref.shape[1]
    spans = tree_rows(trees, count)

    @pl.when(step == 0)
    def _():
        row_high[...], row_low[...] = split(rows_of(encoder_ref))
        d_encoder_ref[...] = jnp.zeros_like(d_encoder_ref)
        d_inner[...] = jnp.zeros_like(d_inner)
        for tree, rows in enumerate(spans):
            for kind in range(2):
                parts = (row_high[rows], row_low[rows])
                inner[kind, rows] = jnp.concatenate(
                    split(ADAPT_SCALE * dot2(parts, down_ref[tree, 5 + kind], NT)), axis=1
                )

    kind = step // half
    grads = split(jnp.where(kind == 0, rows_of(d_key_ref), rows_of(d_value_ref)))
    d_encoder_ref[...] += dot3(grads, split(square(weight_ref))).reshape(d_encoder_ref.shape)
    for tree, rows in enumerate(spans):
        own = both(grads, rows)
        d_inner[kind, rows] += dot2(own, up_ref[tree, 0], NT)
        high, low = inner[kind, rows, :rank], inner[kind, rows, rank:]
        g_up_ref[tree, 0] = dot3((high, low), own, TN)

    @pl.when(step == 2 * half - 1)
    def _():
        for tree, rows in enumerate(spans):
            parts = (row_high[rows], row_low[rows])
            for kind in range(2):
                own = split(ADAPT_SCALE * d_inner[kind, rows])
                d_encoder_ref[tree] += dot2(own, down_ref[tree, 5 + kind])
                g_down_ref[tree, kind] = dot3(own, parts, TN)


def memory_back_call(encoder, d_keys, d_values, packed, down, up):
    trees, count, width = encoder.shape
    rank = down.shape[2]
    slots, copies = packed.shape[:2]
    lanes = 2 * width // slots
    half = slots // 2
    kind_spec = pl.BlockSpec((trees, 1, rank, lanes), lambda step: (0, step // half, 0, step % half))
    return pl.pallas_call(
        memory_back_kernel,
        out_shape=[
            shaped(trees, count, width),
            shaped(trees, 2, rank, width),
            shaped(trees, 2, rank, width),
        ],
        grid=(slots,),
        in_specs=[
            whole_spec(encoder.shape),
            pl.BlockSpec((trees, count, lanes), lambda step: (0, 0, jnp.minimum(step, half - 1))),
            pl.BlockSpec((trees, count, lanes), lambda step: (0, 0, jnp.maximum(step - half, 0))),
            pl.BlockSpec((1, copies, lanes // copies, width), lambda step: (step, 0, 0, 0)),
            whole_spec(down.shape),
            pl.BlockSpec((trees, 1, rank, lanes), lambda step: (0, 5 + step // half, 0, step % half)),
        ],
        out_specs=[
            whole_spec((trees, count, width)),
            whole_spec((trees, 2, rank, width)),
            kind_spec,
        ],
        scratch_shapes=[
            pltpu.VMEM((trees * count, width), BF16),
            pltpu.VMEM((trees * count, width), BF16),
            pltpu.VMEM((2, trees * count, 2 * rank), BF16),
            pltpu.VMEM((2, trees * count, rank), F32),
        ],
        compiler_params=vmem(56),
    )(encoder, d_keys, d_values, packed, down, up)


def feed_forward_kernel(
    rows_ref,
    cot_ref,
    w_in_ref,
    w_out_ref,
    in_up_ref,
    out_down_ref,
    in_down_ref,
    out_up_ref,
    out_ref,
    d_rows_ref,
    g_in_up_ref,
    g_out_down_ref,
    g_in_down_ref,
    g_out_up_ref,
    row_high,
    row_low,
    cot_high,
    cot_low,
    inner_in,
    d_inner_out,
    inner_in_t,
    d_inner_out_t,
    inner_out,
    d_inner_in,
):
    trees, rank = in_up_ref.shape[0], in_up_ref.shape[1]
    step = pl.program_id(0) * pl.num_programs(1) + pl.program_id(1)
    last = pl.num_programs(0) * pl.num_programs(1) - 1
    spans = tree_rows(trees, rows_ref.shape[0] // trees)

    @pl.when(step == 0)
    def _():
        row_high[...], row_low[...] = split(rows_ref[...])
        cot_high[...], cot_low[...] = split(cot_ref[...])
        out_ref[...] = jnp.zeros_like(out_ref)
        d_rows_ref[...] = jnp.zeros_like(d_rows_ref)
        inner_out[...] = jnp.zeros_like(inner_out)
        d_inner_in[...] = jnp.zeros_like(d_inner_in)
        for tree, own in enumerate(spans):
            rows = (row_high[own], row_low[own])
            cots = (cot_high[own], cot_low[own])
            down, up = in_down_ref[tree], out_up_ref[tree]
            inner_in[own] = jnp.concatenate(
                split(ADAPT_SCALE * dot2(rows, down, NT)), axis=1
            )
            d_inner_out[own] = jnp.concatenate(
                split(ADAPT_SCALE * dot2(cots, up, NT)), axis=1
            )
            inner_in_t[tree] = jnp.concatenate(
                split(ADAPT_SCALE * (dot(down, rows[0], NT) + dot(down, rows[1], NT))), axis=0
            )
            d_inner_out_t[tree] = jnp.concatenate(
                split(ADAPT_SCALE * (dot(up, cots[0], NT) + dot(up, cots[1], NT))), axis=0
            )

    rows = (row_high[...], row_low[...])
    cots = (cot_high[...], cot_low[...])
    w_in = split(w_in_ref[0])
    w_out = split(w_out_ref[0])

    def per_tree(inner, maps):
        return jnp.concatenate(
            [
                dot(inner[own], jnp.concatenate([maps[tree], maps[tree]], axis=0))
                for tree, own in enumerate(spans)
            ],
            axis=0,
        )

    pre_act = dot3(rows, w_in) + per_tree(inner_in, in_up_ref)
    root = math.sqrt(2.0 / math.pi)
    squared = pre_act * pre_act
    bend = jnp.tanh(root * (pre_act + 0.044715 * (squared * pre_act)))
    hidden = 0.5 * pre_act * (1.0 + bend)
    slope = 0.5 * (1.0 + bend) + 0.5 * pre_act * (1.0 - bend * bend) * (
        root * (1.0 + 3 * 0.044715 * squared)
    )
    hidden_parts = split(hidden)
    out_ref[...] += dot3(hidden_parts, w_out)
    d_hidden = dot3(cots, w_out, NT) + per_tree(d_inner_out, out_down_ref)
    pre_parts = split(d_hidden * slope)
    d_rows_ref[...] += dot3(pre_parts, w_in, NT)

    for tree, own in enumerate(spans):
        hidden_own = both(hidden_parts, own)
        pre_own = both(pre_parts, own)
        inner_out[own] += dot2(hidden_own, out_down_ref[tree], NT)
        d_inner_in[own] += dot2(pre_own, in_up_ref[tree], NT)
        pair = dot(inner_in_t[tree], pre_own[0])
        g_in_up_ref[tree] = (
            pair[:rank] + pair[rank:] + dot(inner_in_t[tree, :rank], pre_own[1])
        )
        pair = dot(d_inner_out_t[tree], hidden_own[0])
        g_out_down_ref[tree] = (
            pair[:rank] + pair[rank:] + dot(d_inner_out_t[tree, :rank], hidden_own[1])
        )

    @pl.when(step == last)
    def _():
        for tree, own in enumerate(spans):
            inner = split(ADAPT_SCALE * inner_out[own])
            d_inner = split(ADAPT_SCALE * d_inner_in[own])
            out_ref[own] += dot2(inner, out_up_ref[tree])
            d_rows_ref[own] += dot2(d_inner, in_down_ref[tree])
            g_in_down_ref[tree] = dot3(d_inner, (row_high[own], row_low[own]), TN)
            g_out_up_ref[tree] = dot3(inner, (cot_high[own], cot_low[own]), TN)


def feed_forward(rows, cots, weights, in_up, out_down, in_down, out_up):
    count, width = rows.shape
    w_in, w_out = weights
    shards, units = w_in.shape[0], w_in.shape[2]
    trees, rank = in_up.shape[0], in_up.shape[1]
    block = min(units, 512)
    steps = units // block
    columns = pl.BlockSpec(
        (trees, rank, block), lambda shard, step: (0, 0, shard * steps + step)
    )
    maps = [whole_spec(in_down.shape), whole_spec(out_up.shape)]
    rows_spec = whole_spec((count, width))
    return pl.pallas_call(
        feed_forward_kernel,
        out_shape=[shaped(count, width)] * 2
        + [shaped(*in_up.shape), shaped(*out_down.shape)]
        + [shaped(*in_down.shape), shaped(*out_up.shape)],
        grid=(shards, steps),
        in_specs=[
            rows_spec,
            rows_spec,
            pl.BlockSpec((1, width, block), lambda shard, step: (shard, 0, step)),
            pl.BlockSpec((1, block, width), lambda shard, step: (shard, step, 0)),
            columns,
            columns,
        ]
        + maps,
        out_specs=[rows_spec, rows_spec, columns, columns] + maps,
        scratch_shapes=[pltpu.VMEM((count, width), BF16)] * 4
        + [pltpu.VMEM((count, 2 * rank), BF16)] * 2
        + [pltpu.VMEM((trees, 2 * rank, count // trees), BF16)] * 2
        + [pltpu.VMEM((count, rank), F32)] * 2,
        compiler_params=vmem(56),
    )(rows, cots, w_in, w_out, in_up, out_down, in_down, out_up)


def into_tokens_kernel(
    d_qkv_ref, weight_ref, tokens_ref, d_middle_ref, gains_ref, down_ref, up_ref, out_ref, total
):
    slots, trees, seg_len = d_qkv_ref.shape[0], d_qkv_ref.shape[2], d_qkv_ref.shape[3]
    kind = pl.program_id(0)
    spans = tree_rows(trees, seg_len)

    @pl.when(kind == 0)
    def _():
        total[...] = jnp.zeros_like(total)

    grads = split(joined(d_qkv_ref.at[:, 0]))
    total[...] += dot3(grads, split(weight_ref[...]))
    for tree, rows in enumerate(spans):
        inner = split(ADAPT_SCALE * dot2(both(grads, rows), up_ref[tree, 0], NT))
        total[rows] += dot2(inner, down_ref[tree, 0])

    @pl.when(kind == pl.num_programs(0) - 1)
    def _():
        _, normal, inverse = layer_norm(rows_of(tokens_ref), gains_ref[0:1])
        grad = rows_of(d_middle_ref) + norm_back(normal, inverse, gains_ref[0:1], total[...])
        out_ref[...] = grad.reshape(out_ref.shape)


def into_tokens_call(d_qkv, weight, tokens, d_middle, gains, down, up):
    slots, kinds, trees, seg_len, lanes = d_qkv.shape
    width = tokens.shape[2]
    rank = up.shape[2]
    one = pl.BlockSpec((trees, 1, rank, width), lambda kind: (0, kind, 0, 0))
    return pl.pallas_call(
        into_tokens_kernel,
        out_shape=shaped(*tokens.shape),
        grid=(kinds,),
        in_specs=[
            pl.BlockSpec((slots, 1, trees, seg_len, lanes), lambda kind: (0, kind, 0, 0, 0)),
            pl.BlockSpec((width, width), lambda kind: (kind, 0)),
            whole_spec(tokens.shape),
            whole_spec(tokens.shape),
            whole_spec(gains.shape),
            one,
            one,
        ],
        out_specs=whole_spec(tokens.shape),
        scratch_shapes=[pltpu.VMEM((trees * seg_len, width), F32)],
        compiler_params=vmem(56),
    )(d_qkv, weight, tokens, d_middle, gains, down, up)


def place_kernel(source_ref, early_ref, late_ref, down_ref, up_ref, in_down_ref, out_up_ref):
    owners = early_ref.shape[1]
    late_count = late_ref.shape[3] // 2
    early_count = early_ref.shape[3] // 2 - 1
    for owner in range(owners):
        lanes = slice(owner * late_ref.shape[5], (owner + 1) * late_ref.shape[5])
        for entry in range(late_count):
            down_ref[0, entry, :, lanes] = late_ref[0, owner, 0, entry]
            up_ref[0, entry, :, lanes] = late_ref[0, owner, 0, late_count + entry]
        for entry in range(early_count):
            down_ref[0, late_count + entry, :, lanes] = early_ref[0, owner, 0, entry]
            up_ref[0, late_count + entry, :, lanes] = early_ref[0, owner, 0, early_count + entry]
        in_down_ref[0, :, lanes] = early_ref[0, owner, 0, 2 * early_count]
        out_up_ref[0, :, lanes] = early_ref[0, owner, 0, 2 * early_count + 1]


def place_hidden_kernel(source_ref, parts_ref, in_up_ref, out_down_ref):
    for owner in range(parts_ref.shape[1]):
        units = parts_ref.shape[5]
        lanes = slice(owner * units, (owner + 1) * units)
        in_up_ref[0, :, lanes] = parts_ref[0, owner, 0, 0]
        out_down_ref[0, :, lanes] = parts_ref[0, owner, 0, 1]


def place_call(kernel, source, arrays, out_shape):
    def chosen(array):
        groups = array.shape[2]
        return pl.BlockSpec(
            (1, array.shape[1], 1) + array.shape[3:],
            lambda entry, tree: (tree[entry] // groups, 0, tree[entry] % groups, 0, 0, 0),
        )

    return pl.pallas_call(
        kernel,
        out_shape=out_shape,
        grid_spec=pltpu.PrefetchScalarGridSpec(
            num_scalar_prefetch=1,
            grid=(out_shape[0].shape[0],),
            in_specs=[chosen(array) for array in arrays],
            out_specs=[tree_spec(out.shape) for out in out_shape],
        ),
        compiler_params=vmem(48),
    )(source, *arrays)


def my_quarter(shard):
    part = shard.shape[0] // lax.axis_size(COPIES)
    return lax.dynamic_slice_in_dim(shard, lax.axis_index(COPIES) * part, part, 0)


def gather_pair_half(shard):
    whole = lax.all_gather(my_quarter(shard), ("z",) + COPIES, axis=0, tiled=True)
    return whole.reshape((-1,) + shard.shape)


def pick(table, adapter_pick):
    return jnp.stack(
        [
            lax.dynamic_index_in_dim(table, adapter_pick[tree], 0, keepdims=False)
            for tree in range(adapter_pick.shape[0])
        ]
    )


def own_heads(w_qkv):
    slots = lax.axis_size(ROWS)
    lanes = w_qkv.shape[1] // 3
    me = lax.axis_index(ROWS)
    blocks = [
        lax.ppermute(
            w_qkv[:, i * lanes : (i + 1) * lanes],
            ROWS,
            [(s, (3 * s + i) % slots) for s in range(slots)],
        )
        for i in range(3)
    ]
    kinds = [0] * (3 * slots)
    for s in range(slots):
        for i in range(3):
            kinds[(3 * s + i) % slots * 3 + (3 * s + i) // slots] = i
    stacked = jnp.stack(blocks)
    table = jnp.array(kinds, jnp.int32)
    return jnp.stack(
        [
            lax.dynamic_index_in_dim(stacked, table[me * 3 + kind], 0, keepdims=False)
            for kind in range(3)
        ]
    )


def swap(array):
    return lax.ppermute(array, "y", SWAP)


def summed_to_owner(parts, axes):
    return jnp.sum(lax.all_to_all(parts, axes, split_axis=0, concat_axis=0, tiled=True), axis=0)


def to_everyone(array):
    everyone = lax.all_gather(array, COPIES + ROWS, axis=0, tiled=False)
    return everyone.reshape((-1, lax.axis_size(ROWS)) + array.shape)


def by_heads(
    tokens,
    encoder,
    cotangent,
    adapter_pick,
    segment_order,
    parents,
    norm_gains,
    w_qkv,
    w_self_out,
    w_cross_q,
    w_cross_kv,
    w_cross_out,
    w_fc_in,
    w_fc_out,
    attn_down,
    attn_up,
    fc_in_down,
    fc_in_up,
    fc_out_down,
    fc_out_up,
):
    trees, seg_len, width = tokens.shape
    slots = lax.axis_size(ROWS)
    copies = lax.axis_size(COPIES)
    adapters, projections, rank = attn_up.shape[:3]
    hidden_units = fc_in_up.shape[2]
    pairs = lax.axis_size("y")
    me, my_y = lax.axis_index(ROWS), lax.axis_index("y")
    lanes = width // slots
    depth = 4

    down = pick(attn_down.swapaxes(2, 3), adapter_pick)
    up = pick(attn_up, adapter_pick)
    in_down = pick(fc_in_down.swapaxes(1, 2), adapter_pick)
    out_up = pick(fc_out_up, adapter_pick)

    def half_columns(table):
        picked = pick(table, adapter_pick).reshape(
            trees, rank, slots // pairs, pairs, hidden_units // slots
        )
        return lax.dynamic_index_in_dim(picked, my_y, 3, keepdims=False).reshape(
            trees, rank, hidden_units // pairs
        )

    in_up = half_columns(fc_in_up)
    out_down = half_columns(fc_out_down.swapaxes(1, 2))
    down_qkv = down[:, 0:3].reshape(trees, 3 * rank, width)
    up_own = lax.dynamic_slice_in_dim(up[:, 0:3], me * lanes, lanes, 3)

    parts = [my_quarter(w) for w in (w_cross_kv.T, w_self_out, w_cross_out, w_cross_q.T)]
    packed = lax.all_gather(jnp.concatenate(parts, axis=0), EVERY, axis=0, tiled=False)
    packed = packed.reshape((slots, copies) + packed.shape[1:])
    row = width // (slots * copies)
    self_out_spec = packed_spec(packed, 2 * row, row)
    cross_out_spec = packed_spec(packed, 3 * row, row)
    cross_q_spec = packed_spec(packed, 4 * row, row)
    fc_in_half = gather_pair_half(w_fc_in)
    fc_out_half = gather_pair_half(w_fc_out)
    qkv_rows = lax.all_gather(my_quarter(w_qkv.T), EVERY, axis=0, tiled=True)

    normed_all, inner_all, qkv = heads_call(
        tokens, norm_gains, own_heads(w_qkv), down_qkv, up_own
    )
    own_context = self_call(
        self_forward_kernel,
        depth,
        segment_order,
        parents,
        (qkv,),
        [slots_spec(qkv.shape)],
        shaped(slots, trees, seg_len, lanes),
        slots_spec((slots, trees, seg_len, lanes)),
    )
    context = lax.all_to_all(own_context, ROWS, split_axis=0, concat_axis=0, tiled=True)

    memory = memory_call(encoder, packed, down, up)
    middle, cross_queries = rows_call(
        after_self_kernel,
        (context, tokens, norm_gains, packed, packed, down, up),
        (None, None, None, self_out_spec, cross_q_spec, None, None),
        [shaped(*tokens.shape)] * 2,
    )
    (cross_context,) = cross_call(cross_forward_kernel, cross_queries, memory, (), 0)
    after_cross, normed_three = rows_call(
        after_cross_kernel,
        (cross_context, middle, norm_gains, packed, down, up),
        (None, None, None, cross_out_spec, None, None),
        [shaped(*tokens.shape)] * 2,
    )

    def with_partner(rows):
        return jnp.stack([rows, swap(rows)], axis=1).reshape(-1, width)

    out_part, d_rows_part, g_in_up, g_out_down, g_in_down, g_out_up = feed_forward(
        with_partner(normed_three),
        with_partner(cotangent),
        (fc_in_half, fc_out_half),
        in_up,
        out_down,
        in_down,
        out_up,
    )
    d_rows_part = d_rows_part.reshape(trees, 2, seg_len, width)
    out_part = out_part.reshape(trees, 2, seg_len, width)
    d_rows_other = swap(d_rows_part[:, 1])
    layer_out = after_cross + out_part[:, 0] + swap(out_part[:, 1])

    pair_maps = [shaped(trees, 1, rank, width)] * 2
    d_after, d_cross_ctx, g_down_seven, g_up_seven = rows_call(
        into_cross_kernel,
        (
            d_rows_part[:, 0],
            d_rows_other,
            after_cross,
            cotangent,
            cross_context,
            norm_gains,
            packed,
            down,
            up,
        ),
        (None,) * 6 + (cross_out_spec, None, None),
        [shaped(*tokens.shape)] * 2 + pair_maps,
    )
    d_cross_q, d_cross_k, d_cross_v = cross_call(
        cross_backward_kernel, cross_queries, memory, (d_cross_ctx,), 2
    )
    d_middle, d_context, g_down_mid, g_up_mid = rows_call(
        into_self_kernel,
        (d_cross_q, d_after, middle, context, norm_gains, packed, packed, down, up),
        (None,) * 5 + (cross_q_spec, self_out_spec, None, None),
        [shaped(*tokens.shape), shaped(slots, trees, seg_len, lanes)]
        + [shaped(trees, 2, rank, width)] * 2,
    )
    d_own_context = lax.all_to_all(d_context, ROWS, split_axis=0, concat_axis=0, tiled=True)
    d_encoder, g_down_memory, g_up_memory = memory_back_call(
        encoder, d_cross_k, d_cross_v, packed, down, up
    )
    grad_encoder = lax.psum_scatter(d_encoder, ROWS, scatter_dimension=1, tiled=True)

    def columns(parts):
        stack = jnp.concatenate(parts, axis=1)
        return stack.reshape(stack.shape[:3] + (slots, lanes)).transpose(3, 0, 1, 2, 4)

    hidden_parts = jnp.stack([g_in_up, g_out_down], axis=1).reshape(
        trees, 2, rank, slots // pairs, hidden_units // slots
    )
    hidden_all = to_everyone(summed_to_owner(hidden_parts.transpose(3, 0, 1, 2, 4), "z"))
    early = columns(
        [
            g_down_mid,
            g_down_memory,
            g_down_seven,
            g_up_mid,
            g_up_memory,
            g_up_seven,
            g_in_down[:, None],
            g_out_up[:, None],
        ]
    )
    early_all = to_everyone(summed_to_owner(early, ROWS))

    normed_shape = (slots, trees, seg_len, width)
    d_qkv, g_down_part, g_up_qkv = self_call(
        self_backward_kernel,
        depth,
        segment_order,
        parents,
        (qkv, d_own_context, normed_all.reshape(normed_shape), inner_all, up_own),
        [
            slots_spec(qkv.shape),
            slots_spec(d_own_context.shape),
            slots_spec(normed_shape),
            slots_spec(inner_all.shape),
            tree_spec(up_own.shape),
        ],
        [
            shaped(*qkv.shape),
            shaped(trees, 3, rank, width),
            shaped(trees, 3, rank, lanes),
        ],
        [
            slots_spec(qkv.shape),
            tree_spec((trees, 3, rank, width)),
            tree_spec((trees, 3, rank, lanes)),
        ],
    )
    g_down_qkv = summed_to_owner(columns([g_down_part]), ROWS)
    late_all = to_everyone(jnp.concatenate([g_down_qkv, g_up_qkv], axis=1))
    d_split = lax.all_to_all(d_qkv, ROWS, split_axis=0, concat_axis=0, tiled=True)
    grad_tokens = into_tokens_call(
        d_split, qkv_rows, tokens, d_middle, norm_gains, down, up
    )

    all_picks = lax.all_gather(adapter_pick, COPIES, axis=0, tiled=True)
    entry = lax.broadcasted_iota(jnp.int32, (adapters, 1), 0)
    tree_index = lax.broadcasted_iota(jnp.int32, (1, all_picks.shape[0]), 1)
    source = jnp.sum(jnp.where(entry == all_picks[None, :], tree_index, 0), axis=1)
    wide = shaped(adapters, projections, rank, width)
    narrow = shaped(adapters, rank, width)
    grad_down, grad_up, grad_in_down, grad_out_up = place_call(
        place_kernel, source, (early_all, late_all), [wide, wide, narrow, narrow]
    )
    grad_in_up, grad_out_down = place_call(
        place_hidden_kernel, source, (hidden_all,), [shaped(adapters, rank, hidden_units)] * 2
    )
    return (
        layer_out,
        grad_tokens,
        grad_encoder,
        grad_down.swapaxes(2, 3),
        grad_up,
        grad_in_down.swapaxes(1, 2),
        grad_in_up,
        grad_out_down.swapaxes(1, 2),
        grad_out_up,
    )


def placements(rows, copies):
    spread = P(copies, rows, None)
    ins = (
        spread,
        P(copies, None, None),
        spread,
        P(copies),
        P(copies, None),
        P(copies, None),
        P(),
        P(None, rows),
        P(rows, None),
        P(None, rows),
        P(None, rows),
        P(rows, None),
        P(None, rows),
        P(rows, None),
    ) + (P(),) * 6
    return ins, (spread,) * 3 + (P(),) * 6


def solution(mesh):
    copies, rows = mesh.shape["dp"], mesh.shape["seq"]
    general = jax.shard_map(
        shards,
        mesh=mesh,
        in_specs=placements("seq", "dp")[0],
        out_specs=placements("seq", "dp")[1],
        check_vma=False,
    )
    if rows != 8 or copies % 2:
        return general
    fine = jax.sharding.Mesh(
        mesh.devices.reshape(copies // 2, 2, rows // 2, 2), ("x", "c", "z", "y")
    )
    ins, outs = placements(ROWS, COPIES)
    special = jax.shard_map(by_heads, mesh=fine, in_specs=ins, out_specs=outs, check_vma=False)

    def step(*arrays):
        one_each = arrays[0].shape[0] == arrays[14].shape[0]
        return (special if one_each else general)(*arrays)

    return step
```

```python
import functools
import math

import jax
import jax.numpy as jnp
from jax import lax
from jax.experimental import pallas as pl
from jax.experimental.pallas import tpu as pltpu
from jax.sharding import PartitionSpec as P

HEADS = 16
HD = 64


PRECISE = lax.Precision.HIGHEST
ADAPT_SCALE = 2.0
NORM_EPS = 1e-05
MASK_FILL = -1e30


def matmul(left_side, right_side):
    return jnp.dot(left_side, right_side, precision=PRECISE, preferred_element_type=jnp.float32)


def product(formula, first_operand, second_operand):
    return jnp.einsum(
        formula,
        first_operand,
        second_operand,
        precision=PRECISE,
        preferred_element_type=jnp.float32,
    )


def reach_table(segment_order, parents):
    segment_count = parents.shape[-1]
    column = lax.broadcasted_iota(jnp.int32, (segment_count, segment_count), 1)
    identity = (
        lax.broadcasted_iota(jnp.int32, (segment_count, segment_count), 0) == column
    ).astype(jnp.int32)
    parent_hot = (parents[..., :, None] == column).astype(jnp.int32)

    def extend(sweep_index, reach_rows):
        return jnp.minimum(identity + jnp.einsum("gab,gbc->gac", parent_hot, reach_rows), 1)

    initial = jnp.broadcast_to(identity, parent_hot.shape)
    reach_rows = lax.fori_loop(0, segment_count, extend, initial)
    order_hot = (segment_order[..., :, None] == column).astype(jnp.int32)
    return jnp.einsum("gsa,gab,gtb->gst", order_hot, reach_rows, order_hot)


def layer_norm(values, gain_row):
    center = values - jnp.mean(values, -1, keepdims=True)
    inverse = lax.rsqrt(jnp.mean(center * center, -1, keepdims=True) + NORM_EPS)
    normal = center * inverse
    return (normal * gain_row, normal, inverse)


def norm_back(normal, inverse, gain_row, grads):
    scaled = grads * gain_row
    mean_one = jnp.mean(scaled, -1, keepdims=True)
    mean_two = jnp.mean(scaled * normal, -1, keepdims=True)
    return inverse * (scaled - mean_one - normal * mean_two)


def gelu_back(pre_act, d_hidden):

    def activate(values):
        return jax.nn.gelu(values, approximate=True)

    return jax.vjp(activate, pre_act)[1](d_hidden)[0]


def cols_forward(inputs, shard):
    flat_rows = inputs.reshape(-1, inputs.shape[-1])
    result = matmul(flat_rows, lax.all_gather(shard, "seq", axis=1, tiled=True))
    return result.reshape(inputs.shape[:-1] + (result.shape[-1],))


def cols_back(grads, shard):
    flat_grads = grads.reshape(-1, grads.shape[-1])
    result = matmul(flat_grads, lax.all_gather(shard, "seq", axis=1, tiled=True).T)
    return result.reshape(grads.shape[:-1] + (shard.shape[0],))


def rows_forward(inputs, shard):
    flat_rows = inputs.reshape(-1, inputs.shape[-1])
    result = matmul(flat_rows, lax.all_gather(shard, "seq", axis=0, tiled=True))
    return result.reshape(inputs.shape[:-1] + (shard.shape[1],))


def rows_back(grads, shard):
    flat_grads = grads.reshape(-1, grads.shape[-1])
    result = matmul(flat_grads, lax.all_gather(shard, "seq", axis=0, tiled=True).T)
    return result.reshape(grads.shape[:-1] + (result.shape[-1],))


def adapter_apply(inputs, down_map, up_map):
    inner = product("gsd,gdr->gsr", inputs, down_map)
    return (ADAPT_SCALE * product("gsr,gro->gso", inner, up_map), inner)


def adapter_back(inputs, inner, down_map, up_map, grads):
    d_inner = ADAPT_SCALE * product("gso,gro->gsr", grads, up_map)
    grad_up = ADAPT_SCALE * product("gsr,gso->gro", inner, grads)
    grad_down = product("gsd,gsr->gdr", inputs, d_inner)
    return (product("gsr,gdr->gsd", d_inner, down_map), grad_down, grad_up)


def key_mask(my_reach, my_slot, query_index, first_key, key_count, seg_len):
    slot_count = my_reach.shape[1]
    key_index = first_key + lax.broadcasted_iota(jnp.int32, (1, key_count), 1)
    key_slot = key_index // seg_len
    slot_hot = (key_slot[0][:, None] == lax.broadcasted_iota(jnp.int32, (1, slot_count), 1)).astype(
        jnp.int32
    )
    key_allowed = jnp.einsum("gc,nc->gn", my_reach, slot_hot)
    causal_ok = (key_slot != my_slot) | (key_index <= query_index)
    allowed = (key_allowed[:, None, :] > 0) & causal_ok[None]
    return (allowed, jnp.any(key_allowed > 0))


def self_forward(queries, key_rows, value_rows, my_reach, my_slot):
    groups, seg_len, width = queries.shape
    query_heads = queries.reshape(groups, seg_len, HEADS, HD) * HD ** (-0.5)
    query_index = my_slot * seg_len + lax.broadcasted_iota(jnp.int32, (seg_len, 1), 0)
    start_state = (
        jnp.full((groups, HEADS, seg_len), MASK_FILL, jnp.float32),
        jnp.zeros((groups, HEADS, seg_len), jnp.float32),
        jnp.zeros((groups, HEADS, seg_len, HD), jnp.float32),
    )
    key_part = lax.all_gather(key_rows, "seq", axis=1, tiled=True)
    value_part = lax.all_gather(value_rows, "seq", axis=1, tiled=True)
    key_count = key_part.shape[1]
    allowed, any_allowed = key_mask(
        my_reach, my_slot, query_index, jnp.int32(0), key_count, seg_len
    )

    def attend(state):
        peak, mass, accum = state
        key_heads = key_part.reshape(groups, key_count, HEADS, HD)
        value_heads = value_part.reshape(groups, key_count, HEADS, HD)
        scores = product("gshd,gnhd->ghsn", query_heads, key_heads)
        masked = jnp.where(allowed[:, None], scores, MASK_FILL)
        new_peak = jnp.maximum(peak, jnp.max(masked, -1))
        probs = jnp.where(allowed[:, None], jnp.exp(masked - new_peak[..., None]), 0.0)
        mass = jnp.sum(probs, -1)
        accum = product("ghsn,gnhd->ghsd", probs, value_heads)
        return (new_peak, mass, accum)

    peak, mass, accum = lax.cond(any_allowed, attend, lambda state: state, start_state)
    context = (accum / mass[..., None]).transpose(0, 2, 1, 3).reshape(groups, seg_len, width)
    return (context, peak + jnp.log(mass))


def self_backward(queries, key_all, value_all, log_mass, delta, d_context, my_reach, my_slot):
    groups, seg_len, width = queries.shape
    scale = HD ** (-0.5)
    query_heads = queries.reshape(groups, seg_len, HEADS, HD) * scale
    out_heads = d_context.reshape(groups, seg_len, HEADS, HD)
    query_index = my_slot * seg_len + lax.broadcasted_iota(jnp.int32, (seg_len, 1), 0)
    total_keys = key_all.shape[1]
    block_keys = seg_len * math.gcd(total_keys // seg_len, max(1, 512 // seg_len))
    firsts = jnp.arange(total_keys // block_keys, dtype=jnp.int32) * block_keys

    def block_step(state, first_key):
        allowed, any_allowed = key_mask(
            my_reach, my_slot, query_index, first_key, block_keys, seg_len
        )

        def gradients(inner_state):
            key_heads = lax.dynamic_slice_in_dim(key_all, first_key, block_keys, 1).reshape(
                groups, block_keys, HEADS, HD
            )
            value_heads = lax.dynamic_slice_in_dim(value_all, first_key, block_keys, 1).reshape(
                groups, block_keys, HEADS, HD
            )
            scores = product("gshd,gnhd->ghsn", query_heads, key_heads)
            masked = jnp.where(allowed[:, None], scores, MASK_FILL)
            probs = jnp.where(allowed[:, None], jnp.exp(masked - log_mass[..., None]), 0.0)
            d_probs = product("gshd,gnhd->ghsn", out_heads, value_heads)
            d_scores = probs * (d_probs - delta[..., None])
            d_query = inner_state[0] + product("ghsn,gnhd->gshd", d_scores, key_heads)
            d_value_part = product("ghsn,gshd->gnhd", probs, out_heads)
            d_key_part = product("ghsn,gshd->gnhd", d_scores, query_heads)
            d_key_all = lax.dynamic_update_slice_in_dim(
                inner_state[1], d_key_part.reshape(groups, block_keys, width), first_key, 1
            )
            d_value_all = lax.dynamic_update_slice_in_dim(
                inner_state[2], d_value_part.reshape(groups, block_keys, width), first_key, 1
            )
            return (d_query, d_key_all, d_value_all)

        return (lax.cond(any_allowed, gradients, lambda inner_state: inner_state, state), None)

    zero_query = jnp.zeros((groups, seg_len, HEADS, HD), jnp.float32)
    initial = (zero_query, jnp.zeros_like(key_all), jnp.zeros_like(value_all))
    final_state, unused = lax.scan(block_step, initial, firsts)
    d_query = final_state[0].reshape(groups, seg_len, width) * scale
    return (d_query, final_state[1], final_state[2])


def cross_forward(queries, key_rows, value_rows):
    groups, seg_len, width = queries.shape
    enc_rows = key_rows.shape[1]
    query_heads = queries.reshape(groups, seg_len, HEADS, HD) * HD ** (-0.5)
    scores = product("gshd,gehd->ghse", query_heads, key_rows.reshape(groups, enc_rows, HEADS, HD))
    probs = jax.nn.softmax(scores, axis=-1)
    context = product("ghse,gehd->gshd", probs, value_rows.reshape(groups, enc_rows, HEADS, HD))
    return (context.reshape(groups, seg_len, width), probs)


def cross_backward(queries, key_rows, value_rows, probs, d_context):
    groups, seg_len, width = queries.shape
    enc_rows = key_rows.shape[1]
    scale = HD ** (-0.5)
    query_heads = queries.reshape(groups, seg_len, HEADS, HD) * scale
    key_heads = key_rows.reshape(groups, enc_rows, HEADS, HD)
    value_heads = value_rows.reshape(groups, enc_rows, HEADS, HD)
    out_heads = d_context.reshape(groups, seg_len, HEADS, HD)
    d_values = product("ghse,gshd->gehd", probs, out_heads)
    d_probs = product("gshd,gehd->ghse", out_heads, value_heads)
    d_scores = probs * (d_probs - jnp.sum(probs * d_probs, -1, keepdims=True))
    d_queries = product("ghse,gehd->gshd", d_scores, key_heads) * scale
    d_keys = product("ghse,gshd->gehd", d_scores, query_heads)
    return (
        d_queries.reshape(groups, seg_len, width),
        d_keys.reshape(groups, enc_rows, width),
        d_values.reshape(groups, enc_rows, width),
    )


def shards(
    tokens,
    encoder,
    cotangent,
    adapter_pick,
    segment_order,
    parents,
    norm_gains,
    w_qkv,
    w_self_out,
    w_cross_q,
    w_cross_kv,
    w_cross_out,
    w_fc_in,
    w_fc_out,
    attn_down,
    attn_up,
    fc_in_down,
    fc_in_up,
    fc_out_down,
    fc_out_up,
):
    groups, seg_len, width = tokens.shape
    enc_rows = encoder.shape[1]
    my_slot = lax.axis_index("seq")
    reach_rows = reach_table(segment_order, parents)
    my_reach = lax.dynamic_index_in_dim(reach_rows, my_slot, 1, keepdims=False)
    adapter_count = attn_down.shape[0]
    chosen = (
        adapter_pick[:, None] == lax.broadcasted_iota(jnp.int32, (1, adapter_count), 1)
    ).astype(jnp.float32)
    chosen_low = chosen.astype(jnp.bfloat16)

    def select(adapter_table):
        return jnp.einsum(
            "ga,a...->g...", chosen_low, adapter_table, preferred_element_type=jnp.float32
        )

    sel_down = select(attn_down)
    sel_up = select(attn_up)
    in_down = select(fc_in_down)
    in_up = select(fc_in_up)
    out_down = select(fc_out_down)
    out_up = select(fc_out_up)
    normed_one, normal_one, inverse_one = layer_norm(tokens, norm_gains[0])
    inner_qkv = product("gsd,gpdr->gspr", normed_one, sel_down[:, 0:3])
    stacked = cols_forward(normed_one, w_qkv) + ADAPT_SCALE * product(
        "gspr,gpro->gspo", inner_qkv, sel_up[:, 0:3]
    ).reshape(groups, seg_len, 3 * width)
    queries = stacked[..., :width]
    key_rows = stacked[..., width : 2 * width]
    value_rows = stacked[..., 2 * width :]
    context, log_mass = self_forward(queries, key_rows, value_rows, my_reach, my_slot)
    self_term, inner_self = adapter_apply(context, sel_down[:, 3], sel_up[:, 3])
    middle = tokens + rows_forward(context, w_self_out) + self_term
    normed_two, normal_two, inverse_two = layer_norm(middle, norm_gains[1])
    query_term, inner_cross_q = adapter_apply(normed_two, sel_down[:, 4], sel_up[:, 4])
    cross_queries = cols_forward(normed_two, w_cross_q) + query_term
    inner_memory = product("ged,gpdr->gepr", encoder, sel_down[:, 5:7])
    memory = cols_forward(encoder, w_cross_kv) + ADAPT_SCALE * product(
        "gepr,gpro->gepo", inner_memory, sel_up[:, 5:7]
    ).reshape(groups, enc_rows, 2 * width)
    cross_keys = memory[..., :width]
    cross_values = memory[..., width:]
    cross_context, cross_probs = cross_forward(cross_queries, cross_keys, cross_values)
    cross_term, inner_cross_out = adapter_apply(cross_context, sel_down[:, 7], sel_up[:, 7])
    after_cross = middle + rows_forward(cross_context, w_cross_out) + cross_term
    normed_three, normal_three, inverse_three = layer_norm(after_cross, norm_gains[2])
    inner_in = product("gsd,gdr->gsr", normed_three, in_down)
    pre_act = cols_forward(normed_three, w_fc_in) + ADAPT_SCALE * product(
        "gsr,grf->gsf", inner_in, in_up
    )
    hidden = jax.nn.gelu(pre_act, approximate=True)
    inner_out = product("gsf,gfr->gsr", hidden, out_down)
    mlp_out = rows_forward(hidden, w_fc_out) + ADAPT_SCALE * product(
        "gsr,grd->gsd", inner_out, out_up
    )
    layer_out = after_cross + mlp_out
    d_inner_out = ADAPT_SCALE * product("gsd,grd->gsr", cotangent, out_up)
    grad_out_up_tree = ADAPT_SCALE * product("gsr,gsd->grd", inner_out, cotangent)
    d_hidden = rows_back(cotangent, w_fc_out) + product("gsr,gfr->gsf", d_inner_out, out_down)
    grad_out_down_tree = product("gsf,gsr->gfr", hidden, d_inner_out)
    d_pre = gelu_back(pre_act, d_hidden)
    d_inner_in = ADAPT_SCALE * product("gsf,grf->gsr", d_pre, in_up)
    grad_in_up_tree = ADAPT_SCALE * product("gsr,gsf->grf", inner_in, d_pre)
    d_normed_three = cols_back(d_pre, w_fc_in) + product("gsr,gdr->gsd", d_inner_in, in_down)
    grad_in_down_tree = product("gsd,gsr->gdr", normed_three, d_inner_in)
    d_after = cotangent + norm_back(normal_three, inverse_three, norm_gains[2], d_normed_three)
    d_cross_ctx, grad_down_seven, grad_up_seven = adapter_back(
        cross_context, inner_cross_out, sel_down[:, 7], sel_up[:, 7], d_after
    )
    d_cross_ctx = d_cross_ctx + rows_back(d_after, w_cross_out)
    d_cross_q, d_cross_k, d_cross_v = cross_backward(
        cross_queries, cross_keys, cross_values, cross_probs, d_cross_ctx
    )
    d_normed_two, grad_down_four, grad_up_four = adapter_back(
        normed_two, inner_cross_q, sel_down[:, 4], sel_up[:, 4], d_cross_q
    )
    d_normed_two = d_normed_two + cols_back(d_cross_q, w_cross_q)
    d_middle = d_after + norm_back(normal_two, inverse_two, norm_gains[1], d_normed_two)
    d_memory = jnp.concatenate([d_cross_k, d_cross_v], axis=-1)
    d_memory_split = d_memory.reshape(groups, enc_rows, 2, width)
    d_inner_memory = ADAPT_SCALE * product("gepo,gpro->gepr", d_memory_split, sel_up[:, 5:7])
    grad_up_memory = ADAPT_SCALE * product("gepr,gepo->gpro", inner_memory, d_memory_split)
    grad_down_memory = product("ged,gepr->gpdr", encoder, d_inner_memory)
    d_encoder_local = cols_back(d_memory, w_cross_kv) + product(
        "gepr,gpdr->ged", d_inner_memory, sel_down[:, 5:7]
    )
    grad_encoder = lax.psum_scatter(d_encoder_local, "seq", scatter_dimension=1, tiled=True)
    d_context, grad_down_three, grad_up_three = adapter_back(
        context, inner_self, sel_down[:, 3], sel_up[:, 3], d_middle
    )
    d_context = d_context + rows_back(d_middle, w_self_out)
    delta = jnp.sum(
        d_context.reshape(groups, seg_len, HEADS, HD) * context.reshape(groups, seg_len, HEADS, HD),
        -1,
    ).transpose(0, 2, 1)
    key_all, value_all = (
        lax.all_gather(key_rows, "seq", axis=1, tiled=True),
        lax.all_gather(value_rows, "seq", axis=1, tiled=True),
    )
    d_queries, d_key_all, d_value_all = self_backward(
        queries, key_all, value_all, log_mass, delta, d_context, my_reach, my_slot
    )
    d_keys, d_values = (
        lax.psum_scatter(d_key_all, "seq", scatter_dimension=1, tiled=True),
        lax.psum_scatter(d_value_all, "seq", scatter_dimension=1, tiled=True),
    )
    d_stacked = jnp.concatenate([d_queries, d_keys, d_values], axis=-1)
    d_split = d_stacked.reshape(groups, seg_len, 3, width)
    d_inner_qkv = ADAPT_SCALE * product("gspo,gpro->gspr", d_split, sel_up[:, 0:3])
    grad_up_qkv = ADAPT_SCALE * product("gspr,gspo->gpro", inner_qkv, d_split)
    grad_down_qkv = product("gsd,gspr->gpdr", normed_one, d_inner_qkv)
    d_normed_one = cols_back(d_stacked, w_qkv) + product(
        "gspr,gpdr->gsd", d_inner_qkv, sel_down[:, 0:3]
    )
    grad_tokens = d_middle + norm_back(normal_one, inverse_one, norm_gains[0], d_normed_one)
    down_stack = jnp.concatenate(
        [
            grad_down_qkv,
            grad_down_three[:, None],
            grad_down_four[:, None],
            grad_down_memory,
            grad_down_seven[:, None],
        ],
        axis=1,
    )
    up_stack = jnp.concatenate(
        [
            grad_up_qkv,
            grad_up_three[:, None],
            grad_up_four[:, None],
            grad_up_memory,
            grad_up_seven[:, None],
        ],
        axis=1,
    )
    tree_parts = (
        down_stack,
        up_stack,
        grad_in_down_tree,
        grad_in_up_tree,
        grad_out_down_tree,
        grad_out_up_tree,
    )
    shapes = (
        attn_down.shape,
        attn_up.shape,
        fc_in_down.shape,
        fc_in_up.shape,
        fc_out_down.shape,
        fc_out_up.shape,
    )
    local_sums = tuple(
        (product("ga,gx->ax", chosen, part.reshape(groups, -1)).reshape(-1) for part in tree_parts)
    )
    owned = lax.psum_scatter(local_sums, ("dp", "seq"), scatter_dimension=0, tiled=True)
    full_sums = lax.all_gather(owned, ("dp", "seq"), axis=0, tiled=True)
    results = [summed.reshape(shape) for summed, shape in zip(full_sums, shapes)]
    return (
        layer_out,
        grad_tokens,
        grad_encoder,
        results[0],
        results[1],
        results[2],
        results[3],
        results[4],
        results[5],
    )


ROWS = ("z", "y")
COPIES = ("x", "c")
EVERY = ROWS + COPIES
F32 = jnp.float32
BF16 = jnp.bfloat16
MIB = 1 << 20
SWAP = [(0, 1), (1, 0)]
NN = (((1,), (0,)), ((), ()))
NT = (((1,), (1,)), ((), ()))
TN = (((0,), (0,)), ((), ()))


def split(values):
    high = values.astype(BF16)
    return high, (values - high.astype(F32)).astype(BF16)


def dot(left, right, dims=NN):
    return lax.dot_general(left, right, dims, preferred_element_type=F32)


def dot3(left, right, dims=NN):
    (left_high, left_low), (right_high, right_low) = left, right
    return (
        dot(left_high, right_high, dims)
        + dot(left_high, right_low, dims)
        + dot(left_low, right_high, dims)
    )


def dot2(left, right, dims=NN):
    return dot(left[0], right, dims) + dot(left[1], right, dims)


def adapted(rows, down, up):
    inner = dot2(rows, down, NT)
    return dot2(split(ADAPT_SCALE * inner), up), inner


def adapted_back(rows, grads, down, up):
    inner = split(ADAPT_SCALE * dot2(rows, down, NT))
    d_inner = split(ADAPT_SCALE * dot2(grads, up, NT))
    return dot2(d_inner, down), dot3(d_inner, rows, TN), dot3(inner, grads, TN)


def both(parts, where):
    return parts[0][where], parts[1][where]


def vmem(limit):
    return pltpu.CompilerParams(vmem_limit_bytes=limit * MIB)


def lasting(micros):
    return pl.CostEstimate(
        flops=int(micros * 1e9), bytes_accessed=int(micros * 3e6), transcendentals=0
    )


def shaped(*shape):
    return jax.ShapeDtypeStruct(shape, F32)


def whole_spec(shape):
    return pl.BlockSpec(shape, lambda *_: (0,) * len(shape))


def signal(target):
    pl.semaphore_signal(
        pltpu.get_barrier_semaphore(), 1, device_id=target, device_id_type=pl.DeviceIdType.MESH
    )


def greet(z, last, partners, more=0):
    for partner in partners:
        signal(partner)

    @pl.when(z > 0)
    def _():
        signal({"z": z - 1})

    @pl.when(z < last)
    def _():
        signal({"z": z + 1})

    def met():
        lines = (z > 0).astype(jnp.int32) + (z < last).astype(jnp.int32)
        pl.semaphore_wait(pltpu.get_barrier_semaphore(), len(partners) + lines + more)

    return met


def heads_kernel(
    tokens_ref,
    gains_ref,
    weight_ref,
    down_ref,
    up_ref,
    normed_ref,
    inner_ref,
    qkv_ref,
    own_weight_ref,
    rows_ref,
    blocks_ref,
    w_high,
    w_low,
    out_sem,
    up_sem,
    down_sem,
    across_sem,
    here_sem,
    block_sem,
    block_here_sem,
    keep_sem,
):
    z, y = lax.axis_index("z"), lax.axis_index("y")
    last = lax.axis_size("z") - 1
    trees, seg_len, width = tokens_ref.shape
    lanes = weight_ref.shape[1] // 3
    rank = up_ref.shape[2]
    slots = rows_ref.shape[0]

    def place(level, side):
        return level * 2 + side

    def move(slot, sems, index, target):
        return pltpu.make_async_remote_copy(
            src_ref=rows_ref.at[slot],
            dst_ref=rows_ref.at[slot],
            send_sem=sems.at[index],
            recv_sem=here_sem.at[slot],
            device_id=target,
            device_id_type=pl.DeviceIdType.MESH,
        )

    def upward(hop):
        return move(place(z - hop, y), up_sem, hop, {"z": z + 1})

    def downward(hop):
        return move(place(z + hop, y), down_sem, hop, {"z": z - 1})

    def across(level, index):
        return move(place(level, y), across_sem, index, {"y": 1 - y})

    def arrived(slot):
        move(slot, across_sem, 0, {"y": 1 - y}).wait_recv()

    own = place(z, y)

    def block_move(i):
        block = 3 * own + i
        target, kind = block % slots, block // slots
        source = weight_ref.at[:, i * lanes : (i + 1) * lanes]

        def sent():
            return pltpu.make_async_remote_copy(
                src_ref=source,
                dst_ref=blocks_ref.at[kind],
                send_sem=block_sem.at[i],
                recv_sem=block_here_sem.at[kind],
                device_id={"z": target // 2, "y": target % 2},
                device_id_type=pl.DeviceIdType.MESH,
            )

        def kept():
            return pltpu.make_async_copy(source, blocks_ref.at[kind], block_here_sem.at[kind])

        return target, sent, kept

    away = jnp.int32(0)
    for i in range(3):
        giver = (slots * i + own) // 3
        away = away + ((3 * own + i) % slots != own).astype(jnp.int32)

        @pl.when(giver != own)
        def _(giver=giver):
            signal({"z": giver // 2, "y": giver % 2})

    met = greet(z, last, [{"y": 1 - y}], away)
    for tree in range(trees):
        normed = layer_norm(tokens_ref[tree], gains_ref[0:1])[0]
        rows_ref[own, tree * seg_len : (tree + 1) * seg_len] = normed
    met()

    @pl.when(z < last)
    def _():
        upward(0).start()

    @pl.when(z > 0)
    def _():
        downward(0).start()

    across(z, 0).start()
    for i in range(3):
        target, sent, kept = block_move(i)

        @pl.when(target != own)
        def _(sent=sent):
            sent().start()

        @pl.when(target == own)
        def _(kept=kept):
            kept().start()

    def keep(slot):
        return pltpu.make_async_copy(rows_ref.at[slot], normed_ref.at[slot], out_sem.at[slot])

    def work(slot):
        keep(slot).start()
        parts = split(rows_ref[slot])
        product = dot3(parts, (w_high[...], w_low[...]))
        for tree in range(trees):
            rows = slice(tree * seg_len, (tree + 1) * seg_len)
            inner = dot2(both(parts, rows), down_ref[tree], NT)
            inner_ref[slot, tree] = inner
            inner_parts = split(ADAPT_SCALE * inner)
            for kind in range(3):
                term = dot2(
                    both(inner_parts, (slice(None), slice(kind * rank, (kind + 1) * rank))),
                    up_ref[tree, kind],
                )
                qkv_ref[slot, kind, tree] = (
                    product[rows, kind * lanes : (kind + 1) * lanes] + term
                )

    def keep_blocks():
        return pltpu.make_async_copy(blocks_ref, own_weight_ref, keep_sem)

    def take_blocks():
        for kind in range(3):
            block = blocks_ref.at[kind]
            pltpu.make_async_copy(block, block, block_here_sem.at[kind]).wait()
            where = slice(kind * lanes, (kind + 1) * lanes)
            w_high[:, where], w_low[:, where] = split(block[...])
        keep_blocks().start()

    for hop in range(1, last + 1):

        @pl.when(z - hop >= 0)
        def _(hop=hop):
            arrived(place(z - hop, y))

            @pl.when(z < last)
            def _():
                upward(hop).start()

            across(z - hop, hop).start()

        @pl.when(z + hop <= last)
        def _(hop=hop):
            arrived(place(z + hop, y))

            @pl.when(z > 0)
            def _():
                downward(hop).start()

            across(z + hop, last + hop).start()

        if hop == 1:
            take_blocks()
            work(own)
        for step in (-1, 1):
            level = z + step * hop
            before = level - step

            @pl.when(jnp.logical_and(level >= 0, level <= last))
            def _(level=level):
                work(place(level, y))

            if hop == 1 and step == 1:
                continue

            @pl.when(jnp.logical_and(before >= 0, before <= last))
            def _(before=before):
                arrived(place(before, 1 - y))
                work(place(before, 1 - y))

    for level in (z - last, z + last):

        @pl.when(jnp.logical_and(level >= 0, level <= last))
        def _(level=level):
            arrived(place(level, 1 - y))
            work(place(level, 1 - y))

    keep_blocks().wait()
    for i in range(3):
        target, sent, _ = block_move(i)

        @pl.when(target != own)
        def _(sent=sent):
            sent().wait_send()

    across(z, 0).wait_send()
    for hop in range(0, last + 1):

        @pl.when(jnp.logical_and(z - hop >= 0, z < last))
        def _(hop=hop):
            upward(hop).wait_send()

        @pl.when(jnp.logical_and(z + hop <= last, z > 0))
        def _(hop=hop):
            downward(hop).wait_send()

        if hop:

            @pl.when(z - hop >= 0)
            def _(hop=hop):
                across(z - hop, hop).wait_send()

            @pl.when(z + hop <= last)
            def _(hop=hop):
                across(z + hop, last + hop).wait_send()

    for slot in range(normed_ref.shape[0]):
        keep(slot).wait()


def heads_call(tokens, gains, weight, down, up):
    trees, seg_len, width = tokens.shape
    slots = lax.axis_size(ROWS)
    levels = lax.axis_size("z")
    lanes = weight.shape[1] // 3
    inner = down.shape[1]
    dma = pltpu.SemaphoreType.DMA
    here = pl.BlockSpec(memory_space=pltpu.VMEM)
    there = pl.BlockSpec(memory_space=pl.ANY)
    return pl.pallas_call(
        heads_kernel,
        out_shape=[
            shaped(slots, trees * seg_len, width),
            shaped(slots, trees, seg_len, inner),
            shaped(slots, 3, trees, seg_len, lanes),
            shaped(3, width, lanes),
        ],
        in_specs=[here, here, there, here, here],
        out_specs=[there, here, here, there],
        scratch_shapes=[
            pltpu.VMEM((slots, trees * seg_len, width), F32),
            pltpu.VMEM((3, width, lanes), F32),
            pltpu.VMEM((width, 3 * lanes), BF16),
            pltpu.VMEM((width, 3 * lanes), BF16),
            dma((slots,)),
            dma((levels,)),
            dma((levels,)),
            dma((2 * levels - 1,)),
            dma((slots,)),
            dma((3,)),
            dma((3,)),
            dma,
        ],
        compiler_params=pltpu.CompilerParams(
            vmem_limit_bytes=48 * MIB, collective_id=0, has_side_effects=True
        ),
        cost_estimate=lasting(110),
    )(tokens, gains, weight, down, up)


def ancestor_slots(order_ref, parents_ref, slot_of, tree, slot, depth):
    segment = order_ref[tree, slot]
    chain = [(slot, None)]
    there = None
    for _ in range(depth - 1):
        parent = parents_ref[tree, segment]
        there = parent >= 0 if there is None else jnp.logical_and(there, parent >= 0)
        segment = jnp.maximum(parent, 0)
        chain.append((slot_of[segment], there))
    return chain


def fill_slot_of(order_ref, slot_of, tree, slots):
    for slot in range(slots):
        slot_of[order_ref[tree, slot]] = slot


def chain_mask(chain, seg_len):
    row = lax.broadcasted_iota(jnp.int32, (seg_len, seg_len), 0)
    column = lax.broadcasted_iota(jnp.int32, (seg_len, seg_len), 1)
    masks = [(column <= row).astype(jnp.int32)]
    for _, there in chain[1:]:
        masks.append(jnp.full((seg_len, seg_len), there.astype(jnp.int32)))
    return jnp.concatenate(masks, axis=1) > 0


def attend(queries, keys, values, mask):
    scores = dot3(split(queries), split(keys), NT)
    if mask is not None:
        scores = jnp.where(mask, scores, MASK_FILL)
    weights = jnp.exp(scores - jnp.max(scores, -1, keepdims=True))
    mass = jnp.sum(weights, -1, keepdims=True)
    return dot3(split(weights), split(values)) / mass


def attend_back(queries, keys, values, d_context, mask):
    query_parts, key_parts = split(queries), split(keys)
    value_parts, out_parts = split(values), split(d_context)
    scores = dot3(query_parts, key_parts, NT)
    if mask is not None:
        scores = jnp.where(mask, scores, MASK_FILL)
    weights = jnp.exp(scores - jnp.max(scores, -1, keepdims=True))
    weights = weights / jnp.sum(weights, -1, keepdims=True)
    d_weights = dot3(out_parts, value_parts, NT)
    shared = jnp.sum(weights * d_weights, -1, keepdims=True)
    score_parts = split(weights * (d_weights - shared))
    return (
        dot3(score_parts, key_parts) * HD ** (-0.5),
        dot3(score_parts, query_parts, TN),
        dot3(split(weights), out_parts, TN),
    )


def by_head(formula, *arrays, mask=None):
    results = []
    for head in range(arrays[0].shape[1] // HD):
        lanes = slice(head * HD, (head + 1) * HD)
        results.append(formula(*[array[:, lanes] for array in arrays], mask))
    if isinstance(results[0], tuple):
        return [jnp.concatenate(parts, axis=1) for parts in zip(*results)]
    return jnp.concatenate(results, axis=1)


def self_forward_kernel(depth, order_ref, parents_ref, qkv_ref, context_ref, slot_of):
    tree = pl.program_id(0)
    slots, seg_len = qkv_ref.shape[0], qkv_ref.shape[3]
    fill_slot_of(order_ref, slot_of, tree, slots)

    def one_slot(slot, carry):
        chain = ancestor_slots(order_ref, parents_ref, slot_of, tree, slot, depth)
        keys = jnp.concatenate([qkv_ref[where, 1, 0] for where, _ in chain], axis=0)
        values = jnp.concatenate([qkv_ref[where, 2, 0] for where, _ in chain], axis=0)
        context_ref[slot, 0] = by_head(
            attend,
            qkv_ref[slot, 0, 0] * HD ** (-0.5),
            keys,
            values,
            mask=chain_mask(chain, seg_len),
        )
        return carry

    lax.fori_loop(0, slots, one_slot, 0)


def self_backward_kernel(
    depth,
    order_ref,
    parents_ref,
    qkv_ref,
    d_context_ref,
    normed_ref,
    inner_ref,
    up_ref,
    d_qkv_ref,
    g_down_ref,
    g_up_ref,
    slot_of,
):
    tree = pl.program_id(0)
    slots, seg_len, pair = qkv_ref.shape[0], qkv_ref.shape[3], qkv_ref.shape[4]
    rank = up_ref.shape[2]
    fill_slot_of(order_ref, slot_of, tree, slots)
    d_qkv_ref[...] = jnp.zeros_like(d_qkv_ref)

    def one_slot(slot, carry):
        chain = ancestor_slots(order_ref, parents_ref, slot_of, tree, slot, depth)
        keys = jnp.concatenate([qkv_ref[where, 1, 0] for where, _ in chain], axis=0)
        values = jnp.concatenate([qkv_ref[where, 2, 0] for where, _ in chain], axis=0)
        d_queries, d_keys, d_values = by_head(
            attend_back,
            qkv_ref[slot, 0, 0] * HD ** (-0.5),
            keys,
            values,
            d_context_ref[slot, 0],
            mask=chain_mask(chain, seg_len),
        )
        d_qkv_ref[slot, 0, 0] += d_queries
        for entry, (where, _) in enumerate(chain):
            rows = slice(entry * seg_len, (entry + 1) * seg_len)
            d_qkv_ref[where, 1, 0] += d_keys[rows]
            d_qkv_ref[where, 2, 0] += d_values[rows]
        return carry

    lax.fori_loop(0, slots, one_slot, 0)

    normed = split(normed_ref[...].reshape(slots * seg_len, -1))
    inner = split(ADAPT_SCALE * inner_ref[...].reshape(slots * seg_len, 3 * rank))
    for kind in range(3):
        grads = split(d_qkv_ref[:, kind, 0].reshape(slots * seg_len, pair))
        ranks = slice(kind * rank, (kind + 1) * rank)
        d_inner = split(ADAPT_SCALE * dot2(grads, up_ref[0, kind], NT))
        g_down_ref[0, kind] = dot3(d_inner, normed, TN)
        g_up_ref[0, kind] = dot3(both(inner, (slice(None), ranks)), grads, TN)


def slots_spec(shape):
    lead = len(shape) - 3
    return pl.BlockSpec(
        shape[:lead] + (1,) + shape[lead + 1 :],
        lambda tree, *_: (0,) * lead + (tree, 0, 0),
    )


def tree_spec(shape):
    return pl.BlockSpec((1,) + shape[1:], lambda tree, *_: (tree,) + (0,) * (len(shape) - 1))


def self_call(kernel, depth, order, parents, operands, in_specs, out_shape, out_specs, micros):
    trees, slots = order.shape
    return pl.pallas_call(
        functools.partial(kernel, depth),
        out_shape=out_shape,
        grid_spec=pltpu.PrefetchScalarGridSpec(
            num_scalar_prefetch=2,
            grid=(trees,),
            in_specs=in_specs,
            out_specs=out_specs,
            scratch_shapes=[pltpu.SMEM((slots,), jnp.int32)],
        ),
        compiler_params=vmem(56),
        cost_estimate=lasting(micros),
    )(order, parents, *operands)


def cross_forward_kernel(query_ref, key_ref, value_ref, context_ref):
    context_ref[0] = by_head(
        attend, query_ref[0] * HD ** (-0.5), key_ref[0], value_ref[0]
    )


def cross_backward_kernel(
    query_ref, key_ref, value_ref, d_context_ref, d_query_ref, d_key_ref, d_value_ref
):
    d_query_ref[0], d_key_ref[0], d_value_ref[0] = by_head(
        attend_back,
        query_ref[0] * HD ** (-0.5),
        key_ref[0],
        value_ref[0],
        d_context_ref[0],
    )


def cross_call(kernel, queries, memory, rest, long_outs):
    trees, seg_len, width = queries.shape
    enc_rows = memory.shape[1]
    lanes = 2 * HD
    steps = width // lanes
    short = pl.BlockSpec((1, seg_len, lanes), lambda tree, step: (tree, 0, step))
    keys = pl.BlockSpec((1, enc_rows, lanes), lambda tree, step: (tree, 0, step))
    values = pl.BlockSpec((1, enc_rows, lanes), lambda tree, step: (tree, 0, steps + step))
    return pl.pallas_call(
        kernel,
        out_shape=[shaped(trees, seg_len, width)] + [shaped(trees, enc_rows, width)] * long_outs,
        grid=(trees, steps),
        in_specs=[short, keys, values] + [short] * len(rest),
        out_specs=[short] + [keys] * long_outs,
        compiler_params=vmem(48),
        cost_estimate=lasting(32 if long_outs else 19),
    )(queries, memory, memory, *rest)


def square(ref):
    return ref[...].reshape(-1, ref.shape[-1])


def joined(ref):
    slots, trees = ref.shape[:2]
    return jnp.concatenate(
        [
            jnp.concatenate([ref[slot, tree] for slot in range(slots)], axis=1)
            for tree in range(trees)
        ],
        axis=0,
    )


def rows_of(ref):
    return ref[...].reshape(-1, ref.shape[-1])


def tree_rows(trees, count):
    return [slice(tree * count, (tree + 1) * count) for tree in range(trees)]


def with_adapters(parts, down_ref, up_ref, entry, trees):
    count = parts[0].shape[0] // trees
    return jnp.concatenate(
        [
            adapted(both(parts, rows), down_ref[tree, entry], up_ref[tree, entry])[0]
            for tree, rows in enumerate(tree_rows(trees, count))
        ],
        axis=0,
    )


def with_adapters_back(parts, grads, down_ref, up_ref, entry, trees, g_down_ref, g_up_ref, place):
    count = parts[0].shape[0] // trees
    terms = []
    for tree, rows in enumerate(tree_rows(trees, count)):
        term, g_down_ref[tree, place], g_up_ref[tree, place] = adapted_back(
            both(parts, rows), both(grads, rows), down_ref[tree, entry], up_ref[tree, entry]
        )
        terms.append(term)
    return jnp.concatenate(terms, axis=0)


def after_self_kernel(
    context_ref, tokens_ref, gains_ref, out_ref, query_ref, down_ref, up_ref, middle_ref, cross_ref
):
    trees = tokens_ref.shape[0]
    context = split(joined(context_ref))
    middle = rows_of(tokens_ref) + dot3(context, split(square(out_ref)))
    middle = middle + with_adapters(context, down_ref, up_ref, 3, trees)
    middle_ref[...] = middle.reshape(middle_ref.shape)
    normed = split(layer_norm(middle, gains_ref[1:2])[0])
    queries = dot3(normed, split(square(query_ref)), NT)
    queries = queries + with_adapters(normed, down_ref, up_ref, 4, trees)
    cross_ref[...] = queries.reshape(cross_ref.shape)


def after_cross_kernel(
    context_ref, middle_ref, gains_ref, out_ref, down_ref, up_ref, after_ref, normed_ref
):
    trees = context_ref.shape[0]
    context = split(rows_of(context_ref))
    after = rows_of(middle_ref) + dot3(context, split(square(out_ref)))
    after = after + with_adapters(context, down_ref, up_ref, 7, trees)
    after_ref[...] = after.reshape(after_ref.shape)
    normed = layer_norm(after, gains_ref[2:3])[0]
    normed_ref[...] = normed.reshape(normed_ref.shape)


def into_cross_kernel(
    own_ref,
    other_ref,
    after_ref,
    cotangent_ref,
    context_ref,
    gains_ref,
    out_ref,
    down_ref,
    up_ref,
    d_after_ref,
    d_context_ref,
    g_down_ref,
    g_up_ref,
):
    trees = after_ref.shape[0]
    _, normal, inverse = layer_norm(rows_of(after_ref), gains_ref[2:3])
    d_normed = rows_of(own_ref) + rows_of(other_ref)
    d_after = rows_of(cotangent_ref) + norm_back(normal, inverse, gains_ref[2:3], d_normed)
    d_after_ref[...] = d_after.reshape(d_after_ref.shape)
    grads = split(d_after)
    context = split(rows_of(context_ref))
    d_context = dot3(grads, split(square(out_ref)), NT)
    d_context = d_context + with_adapters_back(
        context, grads, down_ref, up_ref, 7, trees, g_down_ref, g_up_ref, 0
    )
    d_context_ref[...] = d_context.reshape(d_context_ref.shape)


def into_self_kernel(
    d_query_ref,
    d_after_ref,
    middle_ref,
    context_ref,
    gains_ref,
    query_ref,
    out_ref,
    down_ref,
    up_ref,
    d_middle_ref,
    d_context_ref,
    g_down_ref,
    g_up_ref,
):
    slots, trees, seg_len, lanes = context_ref.shape
    rows, normal, inverse = layer_norm(rows_of(middle_ref), gains_ref[1:2])
    grads = split(rows_of(d_query_ref))
    d_normed = dot3(grads, split(square(query_ref)))
    d_normed = d_normed + with_adapters_back(
        split(rows), grads, down_ref, up_ref, 4, trees, g_down_ref, g_up_ref, 1
    )
    d_middle = rows_of(d_after_ref) + norm_back(normal, inverse, gains_ref[1:2], d_normed)
    d_middle_ref[...] = d_middle.reshape(d_middle_ref.shape)
    grads = split(d_middle)
    context = split(joined(context_ref))
    d_context = dot3(grads, split(square(out_ref)), NT)
    d_context = d_context + with_adapters_back(
        context, grads, down_ref, up_ref, 3, trees, g_down_ref, g_up_ref, 0
    )
    for slot in range(slots):
        for tree in range(trees):
            d_context_ref[slot, tree] = d_context[
                tree * seg_len : (tree + 1) * seg_len, slot * lanes : (slot + 1) * lanes
            ]


def packed_spec(packed, first, count):
    return pl.BlockSpec(
        packed.shape[:2] + (count, packed.shape[3]), lambda *_: (0, 0, first // count, 0)
    )


def rows_call(kernel, operands, specs, out_shape):
    return pl.pallas_call(
        kernel,
        out_shape=out_shape,
        grid=(1,),
        in_specs=[
            whole_spec(operand.shape) if spec is None else spec
            for operand, spec in zip(operands, specs)
        ],
        out_specs=[whole_spec(out.shape) for out in out_shape],
        compiler_params=vmem(56),
        cost_estimate=lasting(10),
    )(*operands)


def memory_kernel(encoder_ref, weight_ref, down_ref, up_ref, memory_ref, row_high, row_low, inner):
    trees, rank = down_ref.shape[0], down_ref.shape[2]
    step = pl.program_id(0)
    half = pl.num_programs(0) // 2
    lanes = memory_ref.shape[2]
    count = encoder_ref.shape[1]

    @pl.when(step == 0)
    def _():
        row_high[...], row_low[...] = split(rows_of(encoder_ref))
        for tree, rows in enumerate(tree_rows(trees, count)):
            for kind in range(2):
                parts = (row_high[rows], row_low[rows])
                inner[kind, rows] = jnp.concatenate(
                    split(ADAPT_SCALE * dot2(parts, down_ref[tree, 5 + kind], NT)), axis=1
                )

    result = dot3((row_high[...], row_low[...]), split(square(weight_ref)), NT)
    kind = step // half
    for tree, rows in enumerate(tree_rows(trees, count)):
        up = up_ref[tree, 0]
        term = dot(inner[kind, rows], jnp.concatenate([up, up], axis=0))
        memory_ref[tree] = result[rows] + term


def memory_call(encoder, packed, down, up):
    trees, count, width = encoder.shape
    rank = down.shape[2]
    slots, copies = packed.shape[:2]
    lanes = 2 * width // slots
    half = slots // 2
    return pl.pallas_call(
        memory_kernel,
        out_shape=shaped(trees, count, 2 * width),
        grid=(slots,),
        in_specs=[
            whole_spec(encoder.shape),
            pl.BlockSpec((1, copies, lanes // copies, width), lambda step: (step, 0, 0, 0)),
            whole_spec(down.shape),
            pl.BlockSpec((trees, 1, rank, lanes), lambda step: (0, 5 + step // half, 0, step % half)),
        ],
        out_specs=pl.BlockSpec((trees, count, lanes), lambda step: (0, 0, step)),
        scratch_shapes=[
            pltpu.VMEM((trees * count, width), BF16),
            pltpu.VMEM((trees * count, width), BF16),
            pltpu.VMEM((2, trees * count, 2 * rank), BF16),
        ],
        compiler_params=vmem(56),
        cost_estimate=lasting(22),
    )(encoder, packed, down, up)


def memory_back_kernel(
    encoder_ref,
    d_key_ref,
    d_value_ref,
    weight_ref,
    down_ref,
    up_ref,
    d_encoder_ref,
    g_down_ref,
    g_up_ref,
    row_high,
    row_low,
    inner,
    d_inner,
):
    trees, rank = down_ref.shape[0], down_ref.shape[2]
    step = pl.program_id(0)
    half = pl.num_programs(0) // 2
    count = encoder_ref.shape[1]
    spans = tree_rows(trees, count)

    @pl.when(step == 0)
    def _():
        row_high[...], row_low[...] = split(rows_of(encoder_ref))
        d_encoder_ref[...] = jnp.zeros_like(d_encoder_ref)
        d_inner[...] = jnp.zeros_like(d_inner)
        for tree, rows in enumerate(spans):
            for kind in range(2):
                parts = (row_high[rows], row_low[rows])
                inner[kind, rows] = jnp.concatenate(
                    split(ADAPT_SCALE * dot2(parts, down_ref[tree, 5 + kind], NT)), axis=1
                )

    kind = step // half
    grads = split(jnp.where(kind == 0, rows_of(d_key_ref), rows_of(d_value_ref)))
    d_encoder_ref[...] += dot3(grads, split(square(weight_ref))).reshape(d_encoder_ref.shape)
    for tree, rows in enumerate(spans):
        own = both(grads, rows)
        d_inner[kind, rows] += dot2(own, up_ref[tree, 0], NT)
        high, low = inner[kind, rows, :rank], inner[kind, rows, rank:]
        g_up_ref[tree, 0] = dot3((high, low), own, TN)

    @pl.when(step == 2 * half - 1)
    def _():
        for tree, rows in enumerate(spans):
            parts = (row_high[rows], row_low[rows])
            for kind in range(2):
                own = split(ADAPT_SCALE * d_inner[kind, rows])
                d_encoder_ref[tree] += dot2(own, down_ref[tree, 5 + kind])
                g_down_ref[tree, kind] = dot3(own, parts, TN)


def memory_back_call(encoder, d_keys, d_values, packed, down, up):
    trees, count, width = encoder.shape
    rank = down.shape[2]
    slots, copies = packed.shape[:2]
    lanes = 2 * width // slots
    half = slots // 2
    kind_spec = pl.BlockSpec((trees, 1, rank, lanes), lambda step: (0, step // half, 0, step % half))
    return pl.pallas_call(
        memory_back_kernel,
        out_shape=[
            shaped(trees, count, width),
            shaped(trees, 2, rank, width),
            shaped(trees, 2, rank, width),
        ],
        grid=(slots,),
        in_specs=[
            whole_spec(encoder.shape),
            pl.BlockSpec((trees, count, lanes), lambda step: (0, 0, jnp.minimum(step, half - 1))),
            pl.BlockSpec((trees, count, lanes), lambda step: (0, 0, jnp.maximum(step - half, 0))),
            pl.BlockSpec((1, copies, lanes // copies, width), lambda step: (step, 0, 0, 0)),
            whole_spec(down.shape),
            pl.BlockSpec((trees, 1, rank, lanes), lambda step: (0, 5 + step // half, 0, step % half)),
        ],
        out_specs=[
            whole_spec((trees, count, width)),
            whole_spec((trees, 2, rank, width)),
            kind_spec,
        ],
        scratch_shapes=[
            pltpu.VMEM((trees * count, width), BF16),
            pltpu.VMEM((trees * count, width), BF16),
            pltpu.VMEM((2, trees * count, 2 * rank), BF16),
            pltpu.VMEM((2, trees * count, rank), F32),
        ],
        compiler_params=vmem(56),
        cost_estimate=lasting(31),
    )(encoder, d_keys, d_values, packed, down, up)


def nearest(z, last, turn):
    orders = [
        sorted((level for level in range(last + 1) if level != own), key=lambda level: abs(level - own))
        for own in range(last + 1)
    ]
    level = orders[0][turn]
    for own in range(1, last + 1):
        level = jnp.where(z == own, orders[own][turn], level)
    return level


def feed_forward_kernel(
    rows_ref,
    cot_ref,
    w_in_ref,
    w_out_ref,
    in_up_ref,
    out_down_ref,
    in_down_ref,
    out_up_ref,
    out_ref,
    d_rows_ref,
    g_in_up_ref,
    g_out_down_ref,
    g_in_down_ref,
    g_out_up_ref,
    shards_ref,
    w_in_buf,
    row_high,
    row_low,
    cot_high,
    cot_low,
    inner_in,
    d_inner_out,
    inner_in_t,
    d_inner_out_t,
    inner_out,
    d_inner_in,
    own_sem,
    w_in_sem,
    line_sem,
    line_here_sem,
    plane_sem,
    plane_here_sem,
    core_sem,
    core_here_sem,
):
    trees, rank = in_up_ref.shape[0], in_up_ref.shape[2]
    spans = tree_rows(trees, rows_ref.shape[0] // trees)
    x, c, z = lax.axis_index("x"), lax.axis_index("c"), lax.axis_index("z")
    last = lax.axis_size("z") - 1
    block = shards_ref.shape[2]
    part = block // 2
    levels = [nearest(z, last, turn) for turn in range(last)]

    def piece(level, plane, core):
        return shards_ref.at[level, plane, pl.ds(pl.multiple_of(core * part, part), part)]

    def move(source, target, sem, arrival, device):
        return pltpu.make_async_remote_copy(
            src_ref=source,
            dst_ref=target,
            send_sem=sem,
            recv_sem=arrival,
            device_id=device,
            device_id_type=pl.DeviceIdType.MESH,
        )

    mine = w_out_ref.at[pl.ds(pl.multiple_of(x * block + c * part, part), part)]

    def own_move(index, target):
        return move(
            mine, piece(z, x, c), line_sem.at[index], line_here_sem.at[z], {"z": target}
        )

    def line_move(turn, target):
        level = levels[turn]
        here = piece(level, x, c)
        return move(here, here, line_sem.at[2 + turn], line_here_sem.at[level], {"z": target})

    def plane_move(turn):
        here = piece(levels[turn], x, c)
        return move(here, here, plane_sem.at[turn], plane_here_sem.at[turn], {"x": 1 - x})

    def core_move(turn, kind):
        here = piece(levels[turn], x if kind == 0 else 1 - x, c)
        index = 2 * turn + kind
        return move(here, here, core_sem.at[index], core_here_sem.at[index], {"c": 1 - c})

    def wait_line(turn):
        line_move(turn, z).wait_recv()

    def passing(turn, action):
        level = levels[turn]

        @pl.when(jnp.logical_and(level < z, z < last))
        def _():
            action(line_move(turn, z + 1))

        @pl.when(jnp.logical_and(level > z, z > 0))
        def _():
            action(line_move(turn, z - 1))

    def relay(turn):
        wait_line(turn)
        passing(turn, lambda copy: copy.start())
        plane_move(turn).start()
        core_move(turn, 0).start()

    def relay_plane(turn):
        plane_move(turn).wait_recv()
        core_move(turn, 1).start()

    order = [(-1, 0), (-1, 1), (0, 0), (1, 0), (0, 1), (2, 0), (1, 1), (2, 1)]

    def chosen(step):
        level, plane = z, x
        for index, (turn, other) in enumerate(order):
            hit = step == index
            level = jnp.where(hit, z if turn < 0 else levels[turn], level)
            plane = jnp.where(hit, 1 - x if other else x, plane)
        return level, plane

    def w_in_copy(step):
        level, plane = chosen(step)
        columns = pl.ds(pl.multiple_of(plane * block, block), block)
        slot = lax.rem(step, 2)
        return pltpu.make_async_copy(
            w_in_ref.at[level, :, columns], w_in_buf.at[slot], w_in_sem.at[slot]
        )

    def own_copy(plane):
        return pltpu.make_async_copy(
            w_out_ref.at[pl.ds(plane * block, block)], shards_ref.at[z, plane], own_sem.at[plane]
        )

    met = greet(z, last, [{"x": 1 - x}, {"c": 1 - c}])
    for plane in range(2):
        own_copy(plane).start()
    w_in_copy(0).start()
    met()

    @pl.when(z < last)
    def _():
        own_move(0, z + 1).start()

    @pl.when(z > 0)
    def _():
        own_move(1, z - 1).start()

    row_high[...], row_low[...] = split(rows_ref[...])
    cot_high[...], cot_low[...] = split(cot_ref[...])
    out_ref[...] = jnp.zeros_like(out_ref)
    d_rows_ref[...] = jnp.zeros_like(d_rows_ref)
    inner_out[...] = jnp.zeros_like(inner_out)
    d_inner_in[...] = jnp.zeros_like(d_inner_in)
    for tree, own in enumerate(spans):
        rows = (row_high[own], row_low[own])
        cots = (cot_high[own], cot_low[own])
        down, up = in_down_ref[tree], out_up_ref[tree]
        inner_in[own] = jnp.concatenate(split(ADAPT_SCALE * dot2(rows, down, NT)), axis=1)
        d_inner_out[own] = jnp.concatenate(split(ADAPT_SCALE * dot2(cots, up, NT)), axis=1)
        inner_in_t[tree] = jnp.concatenate(
            split(ADAPT_SCALE * (dot(down, rows[0], NT) + dot(down, rows[1], NT))), axis=0
        )
        d_inner_out_t[tree] = jnp.concatenate(
            split(ADAPT_SCALE * (dot(up, cots[0], NT) + dot(up, cots[1], NT))), axis=0
        )
    for plane in range(2):
        own_copy(plane).wait()

    def work(step, carry):
        level, plane = chosen(step)
        entry = level * 2 + plane

        @pl.when(step + 1 < len(order))
        def _():
            w_in_copy(step + 1).start()

        @pl.when(step == 2)
        def _():
            relay(0)
            core_move(0, 0).wait_recv()

        @pl.when(step == 3)
        def _():
            relay(1)
            relay_plane(0)
            core_move(1, 0).wait_recv()

        @pl.when(step == 4)
        def _():
            core_move(0, 1).wait_recv()

        @pl.when(step == 5)
        def _():
            relay(2)
            relay_plane(1)
            core_move(2, 0).wait_recv()

        @pl.when(step == 6)
        def _():
            core_move(1, 1).wait_recv()

        @pl.when(step == 7)
        def _():
            relay_plane(2)
            core_move(2, 1).wait_recv()

        w_in_copy(step).wait()
        rows = (row_high[...], row_low[...])
        cots = (cot_high[...], cot_low[...])
        w_in = split(w_in_buf[lax.rem(step, 2)])
        w_out = split(shards_ref[level, plane])
        in_up = [in_up_ref[tree, entry] for tree in range(trees)]
        out_down = [out_down_ref[tree, entry] for tree in range(trees)]

        def per_tree(inner, maps):
            return jnp.concatenate(
                [
                    dot(inner[own], jnp.concatenate([maps[tree], maps[tree]], axis=0))
                    for tree, own in enumerate(spans)
                ],
                axis=0,
            )

        pre_act = dot3(rows, w_in) + per_tree(inner_in, in_up)
        root = math.sqrt(2.0 / math.pi)
        squared = pre_act * pre_act
        bend = jnp.tanh(root * (pre_act + 0.044715 * (squared * pre_act)))
        hidden = 0.5 * pre_act * (1.0 + bend)
        slope = 0.5 * (1.0 + bend) + 0.5 * pre_act * (1.0 - bend * bend) * (
            root * (1.0 + 3 * 0.044715 * squared)
        )
        hidden_parts = split(hidden)
        out_ref[...] += dot3(hidden_parts, w_out)
        d_hidden = dot3(cots, w_out, NT) + per_tree(d_inner_out, out_down)
        pre_parts = split(d_hidden * slope)
        d_rows_ref[...] += dot3(pre_parts, w_in, NT)

        for tree, own in enumerate(spans):
            hidden_own = both(hidden_parts, own)
            pre_own = both(pre_parts, own)
            inner_out[own] += dot2(hidden_own, out_down[tree], NT)
            d_inner_in[own] += dot2(pre_own, in_up[tree], NT)
            pair = dot(inner_in_t[tree], pre_own[0])
            g_in_up_ref[tree, entry] = (
                pair[:rank] + pair[rank:] + dot(inner_in_t[tree, :rank], pre_own[1])
            )
            pair = dot(d_inner_out_t[tree], hidden_own[0])
            g_out_down_ref[tree, entry] = (
                pair[:rank] + pair[rank:] + dot(d_inner_out_t[tree, :rank], hidden_own[1])
            )
        return carry

    lax.fori_loop(0, len(order), work, 0)

    for tree, own in enumerate(spans):
        inner = split(ADAPT_SCALE * inner_out[own])
        d_inner = split(ADAPT_SCALE * d_inner_in[own])
        out_ref[own] += dot2(inner, out_up_ref[tree])
        d_rows_ref[own] += dot2(d_inner, in_down_ref[tree])
        g_in_down_ref[tree] = dot3(d_inner, (row_high[own], row_low[own]), TN)
        g_out_up_ref[tree] = dot3(inner, (cot_high[own], cot_low[own]), TN)

    @pl.when(z < last)
    def _():
        own_move(0, z + 1).wait_send()

    @pl.when(z > 0)
    def _():
        own_move(1, z - 1).wait_send()

    for turn in range(last):
        passing(turn, lambda copy: copy.wait_send())
        plane_move(turn).wait_send()
        core_move(turn, 0).wait_send()
        core_move(turn, 1).wait_send()


def feed_forward(rows, cots, w_in, w_out, in_up, out_down, in_down, out_up):
    count, width = rows.shape
    levels, _, units = w_in.shape
    block = units // 2
    trees, entries, rank = in_up.shape[:3]
    dma = pltpu.SemaphoreType.DMA
    here = pl.BlockSpec(memory_space=pltpu.VMEM)
    there = pl.BlockSpec(memory_space=pl.ANY)
    return pl.pallas_call(
        feed_forward_kernel,
        out_shape=[shaped(count, width)] * 2
        + [shaped(*in_up.shape), shaped(*out_down.shape)]
        + [shaped(*in_down.shape), shaped(*out_up.shape)],
        in_specs=[here, here, there, there] + [here] * 4,
        out_specs=[here] * 6,
        scratch_shapes=[
            pltpu.VMEM((levels, 2, block, width), F32),
            pltpu.VMEM((2, width, block), F32),
        ]
        + [pltpu.VMEM((count, width), BF16)] * 4
        + [pltpu.VMEM((count, 2 * rank), BF16)] * 2
        + [pltpu.VMEM((trees, 2 * rank, count // trees), BF16)] * 2
        + [pltpu.VMEM((count, rank), F32)] * 2
        + [
            dma((2,)),
            dma((2,)),
            dma((levels + 1,)),
            dma((levels,)),
            dma((levels - 1,)),
            dma((levels - 1,)),
            dma((2 * levels - 2,)),
            dma((2 * levels - 2,)),
        ],
        compiler_params=pltpu.CompilerParams(
            vmem_limit_bytes=60 * MIB, collective_id=2, has_side_effects=True
        ),
        cost_estimate=lasting(110),
    )(rows, cots, w_in, w_out, in_up, out_down, in_down, out_up)


def by_distance(z, last, turn):
    orders = [sorted(range(last + 1), key=lambda level: -abs(level - own)) for own in range(last + 1)]
    level = orders[0][turn]
    for own in range(1, last + 1):
        level = jnp.where(z == own, orders[own][turn], level)
    return level


def into_tokens_kernel(
    d_qkv_ref,
    weight_ref,
    tokens_ref,
    d_middle_ref,
    gains_ref,
    down_ref,
    up_ref,
    out_ref,
    own_ref,
    sent_ref,
    across_ref,
    rising_ref,
    falling_ref,
    w_high,
    w_low,
    sent_sem,
    line_sem,
    across_sem,
    rising_sem,
    falling_sem,
):
    z, y = lax.axis_index("z"), lax.axis_index("y")
    last = lax.axis_size("z") - 1
    trees, rank = up_ref.shape[0], up_ref.shape[2]
    seg_len, lanes = d_qkv_ref.shape[3], d_qkv_ref.shape[4]
    met = greet(z, last, [{"y": 1 - y}])
    for kind in range(3):
        where = slice(kind * lanes, (kind + 1) * lanes)
        w_high[:, where], w_low[:, where] = split(weight_ref[kind])
    met()

    def partial(level, side, ref):
        slot = level * 2 + side
        grads = split(
            jnp.concatenate(
                [
                    jnp.concatenate([d_qkv_ref[slot, kind, tree] for kind in range(3)], axis=1)
                    for tree in range(trees)
                ],
                axis=0,
            )
        )
        total = dot3(grads, (w_high[...], w_low[...]), NT)
        for tree, rows in enumerate(tree_rows(trees, seg_len)):
            inner = jnp.concatenate(
                [
                    dot2(
                        both(grads, (rows, slice(kind * lanes, (kind + 1) * lanes))),
                        up_ref[tree, kind],
                        NT,
                    )
                    for kind in range(3)
                ],
                axis=1,
            )
            ref[level, rows] = total[rows] + dot2(split(ADAPT_SCALE * inner), down_ref[tree])

    def move(source, target, level, sem, arrival, device):
        return pltpu.make_async_remote_copy(
            src_ref=source.at[level],
            dst_ref=target.at[level],
            send_sem=sem,
            recv_sem=arrival.at[level],
            device_id=device,
            device_id_type=pl.DeviceIdType.MESH,
        )

    def across(turn, level):
        return move(sent_ref, across_ref, level, sent_sem.at[turn], across_sem, {"y": 1 - y})

    def rising(turn, level):
        return move(own_ref, rising_ref, level, line_sem.at[turn], rising_sem, {"z": z + 1})

    def falling(turn, level):
        return move(own_ref, falling_ref, level, line_sem.at[turn], falling_sem, {"z": z - 1})

    levels = [by_distance(z, last, turn) for turn in range(last + 1)]
    for turn, level in enumerate(levels):
        partial(level, 1 - y, sent_ref)
        across(turn, level).start()
    for level in levels:
        partial(level, y, own_ref)
    for turn, level in enumerate(levels):
        across(turn, level).wait_recv()
        own_ref[level] += across_ref[level]

        @pl.when(jnp.logical_and(level >= z, z > 0))
        def _(level=level):
            rising(0, level).wait_recv()
            own_ref[level] += rising_ref[level]

        @pl.when(jnp.logical_and(level <= z, z < last))
        def _(level=level):
            falling(0, level).wait_recv()
            own_ref[level] += falling_ref[level]

        @pl.when(level > z)
        def _(turn=turn, level=level):
            rising(turn, level).start()

        @pl.when(level < z)
        def _(turn=turn, level=level):
            falling(turn, level).start()

    _, normal, inverse = layer_norm(rows_of(tokens_ref), gains_ref[0:1])
    grad = rows_of(d_middle_ref) + norm_back(normal, inverse, gains_ref[0:1], own_ref[z])
    out_ref[...] = grad.reshape(out_ref.shape)
    for turn, level in enumerate(levels):
        across(turn, level).wait_send()

        @pl.when(level > z)
        def _(turn=turn, level=level):
            rising(turn, level).wait_send()

        @pl.when(level < z)
        def _(turn=turn, level=level):
            falling(turn, level).wait_send()


def into_tokens_call(d_qkv, weight, tokens, d_middle, gains, down, up):
    trees, seg_len, width = tokens.shape
    levels = lax.axis_size("z")
    lanes = weight.shape[2]
    dma = pltpu.SemaphoreType.DMA((levels,))
    here = pl.BlockSpec(memory_space=pltpu.VMEM)
    return pl.pallas_call(
        into_tokens_kernel,
        out_shape=shaped(*tokens.shape),
        in_specs=[here] * 7,
        out_specs=here,
        scratch_shapes=[pltpu.VMEM((levels, trees * seg_len, width), F32)] * 5
        + [pltpu.VMEM((width, 3 * lanes), BF16)] * 2
        + [dma] * 5,
        compiler_params=pltpu.CompilerParams(
            vmem_limit_bytes=56 * MIB, collective_id=1, has_side_effects=True
        ),
        cost_estimate=lasting(110),
    )(d_qkv, weight, tokens, d_middle, gains, down, up)


LATE_DOWN, LATE_UP = (0, 1, 2, 5, 6), (5, 6)
OWN_UP = (0, 1, 2)
EARLY = (3, 4, 7)


def place_kernel(source_ref, parts_ref, down_ref, up_ref, in_down_ref, out_up_ref):
    places = [(down_ref, entry) for entry in LATE_DOWN] + [(up_ref, entry) for entry in LATE_UP]
    places += [(up_ref, entry) for entry in OWN_UP]
    places += [(down_ref, entry) for entry in EARLY] + [(up_ref, entry) for entry in EARLY]
    span = parts_ref.shape[5]
    for owner in range(parts_ref.shape[1]):
        lanes = slice(owner * span, (owner + 1) * span)
        for part, (ref, entry) in enumerate(places):
            ref[0, entry, :, lanes] = parts_ref[0, owner, 0, part]
        in_down_ref[0, :, lanes] = parts_ref[0, owner, 0, len(places)]
        out_up_ref[0, :, lanes] = parts_ref[0, owner, 0, len(places) + 1]


def place_hidden_kernel(source_ref, parts_ref, in_up_ref, out_down_ref):
    for owner in range(parts_ref.shape[1]):
        units = parts_ref.shape[5]
        lanes = slice(owner * units, (owner + 1) * units)
        in_up_ref[0, :, lanes] = parts_ref[0, owner, 0, 0]
        out_down_ref[0, :, lanes] = parts_ref[0, owner, 0, 1]


def place_call(kernel, source, arrays, out_shape):
    def chosen(array):
        groups = array.shape[2]
        return pl.BlockSpec(
            (1, array.shape[1], 1) + array.shape[3:],
            lambda entry, tree: (tree[entry] // groups, 0, tree[entry] % groups, 0, 0, 0),
        )

    return pl.pallas_call(
        kernel,
        out_shape=out_shape,
        grid_spec=pltpu.PrefetchScalarGridSpec(
            num_scalar_prefetch=1,
            grid=(out_shape[0].shape[0],),
            in_specs=[chosen(array) for array in arrays],
            out_specs=[tree_spec(out.shape) for out in out_shape],
        ),
        compiler_params=vmem(48),
        cost_estimate=lasting(9),
    )(source, *arrays)


def my_quarter(shard):
    part = shard.shape[0] // lax.axis_size(COPIES)
    return lax.dynamic_slice_in_dim(shard, lax.axis_index(COPIES) * part, part, 0)


def gather_pair_half(shard):
    whole = lax.all_gather(my_quarter(shard), ("z",) + COPIES, axis=0, tiled=True)
    return whole.reshape((-1,) + shard.shape)


def pick(table, adapter_pick):
    return jnp.stack(
        [
            lax.dynamic_index_in_dim(table, adapter_pick[tree], 0, keepdims=False)
            for tree in range(adapter_pick.shape[0])
        ]
    )


def swap(array):
    return lax.ppermute(array, "y", SWAP)


def summed_to_owner(parts, axes):
    return jnp.sum(lax.all_to_all(parts, axes, split_axis=0, concat_axis=0, tiled=True), axis=0)


def to_everyone(array):
    everyone = lax.all_gather(array, COPIES + ROWS, axis=0, tiled=False)
    return everyone.reshape((-1, lax.axis_size(ROWS)) + array.shape)


def by_heads(
    tokens,
    encoder,
    cotangent,
    adapter_pick,
    segment_order,
    parents,
    norm_gains,
    w_qkv,
    w_self_out,
    w_cross_q,
    w_cross_kv,
    w_cross_out,
    w_fc_in,
    w_fc_out,
    attn_down,
    attn_up,
    fc_in_down,
    fc_in_up,
    fc_out_down,
    fc_out_up,
):
    trees, seg_len, width = tokens.shape
    slots = lax.axis_size(ROWS)
    copies = lax.axis_size(COPIES)
    adapters, projections, rank = attn_up.shape[:3]
    hidden_units = fc_in_up.shape[2]
    pairs = lax.axis_size("y")
    me, my_y = lax.axis_index(ROWS), lax.axis_index("y")
    lanes = width // slots
    depth = 4

    down = pick(attn_down.swapaxes(2, 3), adapter_pick)
    up = pick(attn_up, adapter_pick)
    in_down = pick(fc_in_down.swapaxes(1, 2), adapter_pick)
    out_up = pick(fc_out_up, adapter_pick)

    def half_columns(table):
        picked = pick(table, adapter_pick).reshape(
            trees, rank, slots // pairs, pairs, hidden_units // slots
        )
        half = lax.dynamic_index_in_dim(picked, my_y, 3, keepdims=False)
        return half.reshape(trees, rank, slots, -1).swapaxes(1, 2)

    in_up = half_columns(fc_in_up)
    out_down = half_columns(fc_out_down.swapaxes(1, 2))
    down_qkv = down[:, 0:3].reshape(trees, 3 * rank, width)
    up_own = lax.dynamic_slice_in_dim(up[:, 0:3], me * lanes, lanes, 3)

    parts = [my_quarter(w) for w in (w_cross_kv.T, w_self_out, w_cross_out, w_cross_q.T)]
    packed = lax.all_gather(jnp.concatenate(parts, axis=0), EVERY, axis=0, tiled=False)
    packed = packed.reshape((slots, copies) + packed.shape[1:])
    row = width // (slots * copies)
    self_out_spec = packed_spec(packed, 2 * row, row)
    cross_out_spec = packed_spec(packed, 3 * row, row)
    cross_q_spec = packed_spec(packed, 4 * row, row)
    fc_in_half = gather_pair_half(w_fc_in)

    normed_all, inner_all, qkv, qkv_own = heads_call(
        tokens, norm_gains, w_qkv, down_qkv, up_own
    )
    own_context = self_call(
        self_forward_kernel,
        depth,
        segment_order,
        parents,
        (qkv,),
        [slots_spec(qkv.shape)],
        shaped(slots, trees, seg_len, lanes),
        slots_spec((slots, trees, seg_len, lanes)),
        20,
    )
    context = lax.all_to_all(own_context, ROWS, split_axis=0, concat_axis=0, tiled=True)

    memory = memory_call(encoder, packed, down, up)
    middle, cross_queries = rows_call(
        after_self_kernel,
        (context, tokens, norm_gains, packed, packed, down, up),
        (None, None, None, self_out_spec, cross_q_spec, None, None),
        [shaped(*tokens.shape)] * 2,
    )
    (cross_context,) = cross_call(cross_forward_kernel, cross_queries, memory, (), 0)
    after_cross, normed_three = rows_call(
        after_cross_kernel,
        (cross_context, middle, norm_gains, packed, down, up),
        (None, None, None, cross_out_spec, None, None),
        [shaped(*tokens.shape)] * 2,
    )

    def with_partner(rows):
        return jnp.stack([rows, swap(rows)], axis=1).reshape(-1, width)

    out_part, d_rows_part, g_in_up, g_out_down, g_in_down, g_out_up = feed_forward(
        with_partner(normed_three),
        with_partner(cotangent),
        fc_in_half,
        w_fc_out,
        in_up,
        out_down,
        in_down,
        out_up,
    )
    d_rows_part = d_rows_part.reshape(trees, 2, seg_len, width)
    out_part = out_part.reshape(trees, 2, seg_len, width)
    d_rows_other = swap(d_rows_part[:, 1])
    out_other, d_rows_other = lax.optimization_barrier((out_part[:, 1], d_rows_other))
    out_other = swap(out_other)

    pair_maps = [shaped(trees, 1, rank, width)] * 2
    d_after, d_cross_ctx, g_down_seven, g_up_seven = rows_call(
        into_cross_kernel,
        (
            d_rows_part[:, 0],
            d_rows_other,
            after_cross,
            cotangent,
            cross_context,
            norm_gains,
            packed,
            down,
            up,
        ),
        (None,) * 6 + (cross_out_spec, None, None),
        [shaped(*tokens.shape)] * 2 + pair_maps,
    )
    d_cross_q, d_cross_k, d_cross_v = cross_call(
        cross_backward_kernel, cross_queries, memory, (d_cross_ctx,), 2
    )
    out_other, d_cross_q = lax.optimization_barrier((out_other, d_cross_q))
    layer_out = after_cross + out_part[:, 0] + out_other
    d_middle, d_context, g_down_mid, g_up_mid = rows_call(
        into_self_kernel,
        (d_cross_q, d_after, middle, context, norm_gains, packed, packed, down, up),
        (None,) * 5 + (cross_q_spec, self_out_spec, None, None),
        [shaped(*tokens.shape), shaped(slots, trees, seg_len, lanes)]
        + [shaped(trees, 2, rank, width)] * 2,
    )
    d_own_context = lax.all_to_all(d_context, ROWS, split_axis=0, concat_axis=0, tiled=True)
    d_context, d_cross_k = lax.optimization_barrier((d_context, d_cross_k))
    d_encoder, g_down_memory, g_up_memory = memory_back_call(
        encoder, d_cross_k, d_cross_v, packed, down, up
    )
    enc_rows = encoder.shape[1] // slots
    sides = d_encoder.reshape(trees, slots // pairs, pairs, enc_rows, width).transpose(2, 1, 0, 3, 4)
    other_side = lax.dynamic_index_in_dim(sides, 1 - my_y, 0, keepdims=False)
    own_side = lax.dynamic_index_in_dim(sides, my_y, 0, keepdims=False)
    enc_side = own_side + swap(other_side)

    def columns(parts):
        stack = jnp.concatenate(parts, axis=1)
        return stack.reshape(stack.shape[:3] + (slots, lanes)).transpose(3, 0, 1, 2, 4)

    hidden_parts = jnp.stack([g_in_up, g_out_down], axis=1).reshape(
        trees, 2, slots // pairs, 2, rank, -1
    )
    hidden_parts = hidden_parts.transpose(2, 0, 1, 4, 3, 5).reshape(
        slots // pairs, trees, 2, rank, hidden_units // slots
    )
    hidden_all = to_everyone(summed_to_owner(hidden_parts, "z"))
    early = summed_to_owner(
        columns(
            [
                g_down_mid,
                g_down_seven,
                g_up_mid,
                g_up_seven,
                g_in_down[:, None],
                g_out_up[:, None],
            ]
        ),
        ROWS,
    )

    normed_shape = (slots, trees, seg_len, width)
    d_qkv, g_down_part, g_up_qkv = self_call(
        self_backward_kernel,
        depth,
        segment_order,
        parents,
        (qkv, d_own_context, normed_all.reshape(normed_shape), inner_all, up_own),
        [
            slots_spec(qkv.shape),
            slots_spec(d_own_context.shape),
            slots_spec(normed_shape),
            slots_spec(inner_all.shape),
            tree_spec(up_own.shape),
        ],
        [
            shaped(*qkv.shape),
            shaped(trees, 3, rank, width),
            shaped(trees, 3, rank, lanes),
        ],
        [
            slots_spec(qkv.shape),
            tree_spec((trees, 3, rank, width)),
            tree_spec((trees, 3, rank, lanes)),
        ],
        43,
    )
    enc_side, g_down_part = lax.optimization_barrier((enc_side, g_down_part))
    late = summed_to_owner(columns([g_down_part, g_down_memory, g_up_memory]), ROWS)
    grad_encoder = summed_to_owner(enc_side, "z")
    attention_all = to_everyone(jnp.concatenate([late, g_up_qkv, early], axis=1))
    grad_tokens = into_tokens_call(
        d_qkv, qkv_own, tokens, d_middle, norm_gains, down_qkv, up_own
    )

    all_picks = lax.all_gather(adapter_pick, COPIES, axis=0, tiled=True)
    entry = lax.broadcasted_iota(jnp.int32, (adapters, 1), 0)
    tree_index = lax.broadcasted_iota(jnp.int32, (1, all_picks.shape[0]), 1)
    source = jnp.sum(jnp.where(entry == all_picks[None, :], tree_index, 0), axis=1)
    wide = shaped(adapters, projections, rank, width)
    narrow = shaped(adapters, rank, width)
    grad_down, grad_up, grad_in_down, grad_out_up = place_call(
        place_kernel, source, (attention_all,), [wide, wide, narrow, narrow]
    )
    grad_in_up, grad_out_down = place_call(
        place_hidden_kernel, source, (hidden_all,), [shaped(adapters, rank, hidden_units)] * 2
    )
    return (
        layer_out,
        grad_tokens,
        grad_encoder,
        grad_down.swapaxes(2, 3),
        grad_up,
        grad_in_down.swapaxes(1, 2),
        grad_in_up,
        grad_out_down.swapaxes(1, 2),
        grad_out_up,
    )


def placements(rows, copies):
    spread = P(copies, rows, None)
    ins = (
        spread,
        P(copies, None, None),
        spread,
        P(copies),
        P(copies, None),
        P(copies, None),
        P(),
        P(None, rows),
        P(rows, None),
        P(None, rows),
        P(None, rows),
        P(rows, None),
        P(None, rows),
        P(rows, None),
    ) + (P(),) * 6
    return ins, (spread,) * 3 + (P(),) * 6


def solution(mesh):
    copies, rows = mesh.shape["dp"], mesh.shape["seq"]
    general = jax.shard_map(
        shards,
        mesh=mesh,
        in_specs=placements("seq", "dp")[0],
        out_specs=placements("seq", "dp")[1],
        check_vma=False,
    )
    if rows != 8 or copies % 2:
        return general
    fine = jax.sharding.Mesh(
        mesh.devices.reshape(copies // 2, 2, rows // 2, 2), ("x", "c", "z", "y")
    )
    ins, outs = placements(ROWS, COPIES)
    special = jax.shard_map(by_heads, mesh=fine, in_specs=ins, out_specs=outs, check_vma=False)

    def step(*arrays):
        one_each = arrays[0].shape[0] == arrays[14].shape[0]
        return (special if one_each else general)(*arrays)

    return step
```

```python
import functools
import math

import jax
import jax.numpy as jnp
from jax import lax
from jax.experimental import pallas as pl
from jax.experimental.pallas import tpu as pltpu
from jax.sharding import PartitionSpec as P

HEADS = 16
HD = 64


PRECISE = lax.Precision.HIGHEST
ADAPT_SCALE = 2.0
NORM_EPS = 1e-05
MASK_FILL = -1e30


def matmul(left_side, right_side):
    return jnp.dot(left_side, right_side, precision=PRECISE, preferred_element_type=jnp.float32)


def product(formula, first_operand, second_operand):
    return jnp.einsum(
        formula,
        first_operand,
        second_operand,
        precision=PRECISE,
        preferred_element_type=jnp.float32,
    )


def reach_table(segment_order, parents):
    segment_count = parents.shape[-1]
    column = lax.broadcasted_iota(jnp.int32, (segment_count, segment_count), 1)
    identity = (
        lax.broadcasted_iota(jnp.int32, (segment_count, segment_count), 0) == column
    ).astype(jnp.int32)
    parent_hot = (parents[..., :, None] == column).astype(jnp.int32)

    def extend(sweep_index, reach_rows):
        return jnp.minimum(identity + jnp.einsum("gab,gbc->gac", parent_hot, reach_rows), 1)

    initial = jnp.broadcast_to(identity, parent_hot.shape)
    reach_rows = lax.fori_loop(0, segment_count, extend, initial)
    order_hot = (segment_order[..., :, None] == column).astype(jnp.int32)
    return jnp.einsum("gsa,gab,gtb->gst", order_hot, reach_rows, order_hot)


def layer_norm(values, gain_row):
    center = values - jnp.mean(values, -1, keepdims=True)
    inverse = lax.rsqrt(jnp.mean(center * center, -1, keepdims=True) + NORM_EPS)
    normal = center * inverse
    return (normal * gain_row, normal, inverse)


def norm_back(normal, inverse, gain_row, grads):
    scaled = grads * gain_row
    mean_one = jnp.mean(scaled, -1, keepdims=True)
    mean_two = jnp.mean(scaled * normal, -1, keepdims=True)
    return inverse * (scaled - mean_one - normal * mean_two)


def gelu_back(pre_act, d_hidden):

    def activate(values):
        return jax.nn.gelu(values, approximate=True)

    return jax.vjp(activate, pre_act)[1](d_hidden)[0]


def cols_forward(inputs, shard):
    flat_rows = inputs.reshape(-1, inputs.shape[-1])
    result = matmul(flat_rows, lax.all_gather(shard, "seq", axis=1, tiled=True))
    return result.reshape(inputs.shape[:-1] + (result.shape[-1],))


def cols_back(grads, shard):
    flat_grads = grads.reshape(-1, grads.shape[-1])
    result = matmul(flat_grads, lax.all_gather(shard, "seq", axis=1, tiled=True).T)
    return result.reshape(grads.shape[:-1] + (shard.shape[0],))


def rows_forward(inputs, shard):
    flat_rows = inputs.reshape(-1, inputs.shape[-1])
    result = matmul(flat_rows, lax.all_gather(shard, "seq", axis=0, tiled=True))
    return result.reshape(inputs.shape[:-1] + (shard.shape[1],))


def rows_back(grads, shard):
    flat_grads = grads.reshape(-1, grads.shape[-1])
    result = matmul(flat_grads, lax.all_gather(shard, "seq", axis=0, tiled=True).T)
    return result.reshape(grads.shape[:-1] + (result.shape[-1],))


def adapter_apply(inputs, down_map, up_map):
    inner = product("gsd,gdr->gsr", inputs, down_map)
    return (ADAPT_SCALE * product("gsr,gro->gso", inner, up_map), inner)


def adapter_back(inputs, inner, down_map, up_map, grads):
    d_inner = ADAPT_SCALE * product("gso,gro->gsr", grads, up_map)
    grad_up = ADAPT_SCALE * product("gsr,gso->gro", inner, grads)
    grad_down = product("gsd,gsr->gdr", inputs, d_inner)
    return (product("gsr,gdr->gsd", d_inner, down_map), grad_down, grad_up)


def key_mask(my_reach, my_slot, query_index, first_key, key_count, seg_len):
    slot_count = my_reach.shape[1]
    key_index = first_key + lax.broadcasted_iota(jnp.int32, (1, key_count), 1)
    key_slot = key_index // seg_len
    slot_hot = (key_slot[0][:, None] == lax.broadcasted_iota(jnp.int32, (1, slot_count), 1)).astype(
        jnp.int32
    )
    key_allowed = jnp.einsum("gc,nc->gn", my_reach, slot_hot)
    causal_ok = (key_slot != my_slot) | (key_index <= query_index)
    allowed = (key_allowed[:, None, :] > 0) & causal_ok[None]
    return (allowed, jnp.any(key_allowed > 0))


def self_forward(queries, key_rows, value_rows, my_reach, my_slot):
    groups, seg_len, width = queries.shape
    query_heads = queries.reshape(groups, seg_len, HEADS, HD) * HD ** (-0.5)
    query_index = my_slot * seg_len + lax.broadcasted_iota(jnp.int32, (seg_len, 1), 0)
    start_state = (
        jnp.full((groups, HEADS, seg_len), MASK_FILL, jnp.float32),
        jnp.zeros((groups, HEADS, seg_len), jnp.float32),
        jnp.zeros((groups, HEADS, seg_len, HD), jnp.float32),
    )
    key_part = lax.all_gather(key_rows, "seq", axis=1, tiled=True)
    value_part = lax.all_gather(value_rows, "seq", axis=1, tiled=True)
    key_count = key_part.shape[1]
    allowed, any_allowed = key_mask(
        my_reach, my_slot, query_index, jnp.int32(0), key_count, seg_len
    )

    def attend(state):
        peak, mass, accum = state
        key_heads = key_part.reshape(groups, key_count, HEADS, HD)
        value_heads = value_part.reshape(groups, key_count, HEADS, HD)
        scores = product("gshd,gnhd->ghsn", query_heads, key_heads)
        masked = jnp.where(allowed[:, None], scores, MASK_FILL)
        new_peak = jnp.maximum(peak, jnp.max(masked, -1))
        probs = jnp.where(allowed[:, None], jnp.exp(masked - new_peak[..., None]), 0.0)
        mass = jnp.sum(probs, -1)
        accum = product("ghsn,gnhd->ghsd", probs, value_heads)
        return (new_peak, mass, accum)

    peak, mass, accum = lax.cond(any_allowed, attend, lambda state: state, start_state)
    context = (accum / mass[..., None]).transpose(0, 2, 1, 3).reshape(groups, seg_len, width)
    return (context, peak + jnp.log(mass))


def self_backward(queries, key_all, value_all, log_mass, delta, d_context, my_reach, my_slot):
    groups, seg_len, width = queries.shape
    scale = HD ** (-0.5)
    query_heads = queries.reshape(groups, seg_len, HEADS, HD) * scale
    out_heads = d_context.reshape(groups, seg_len, HEADS, HD)
    query_index = my_slot * seg_len + lax.broadcasted_iota(jnp.int32, (seg_len, 1), 0)
    total_keys = key_all.shape[1]
    block_keys = seg_len * math.gcd(total_keys // seg_len, max(1, 512 // seg_len))
    firsts = jnp.arange(total_keys // block_keys, dtype=jnp.int32) * block_keys

    def block_step(state, first_key):
        allowed, any_allowed = key_mask(
            my_reach, my_slot, query_index, first_key, block_keys, seg_len
        )

        def gradients(inner_state):
            key_heads = lax.dynamic_slice_in_dim(key_all, first_key, block_keys, 1).reshape(
                groups, block_keys, HEADS, HD
            )
            value_heads = lax.dynamic_slice_in_dim(value_all, first_key, block_keys, 1).reshape(
                groups, block_keys, HEADS, HD
            )
            scores = product("gshd,gnhd->ghsn", query_heads, key_heads)
            masked = jnp.where(allowed[:, None], scores, MASK_FILL)
            probs = jnp.where(allowed[:, None], jnp.exp(masked - log_mass[..., None]), 0.0)
            d_probs = product("gshd,gnhd->ghsn", out_heads, value_heads)
            d_scores = probs * (d_probs - delta[..., None])
            d_query = inner_state[0] + product("ghsn,gnhd->gshd", d_scores, key_heads)
            d_value_part = product("ghsn,gshd->gnhd", probs, out_heads)
            d_key_part = product("ghsn,gshd->gnhd", d_scores, query_heads)
            d_key_all = lax.dynamic_update_slice_in_dim(
                inner_state[1], d_key_part.reshape(groups, block_keys, width), first_key, 1
            )
            d_value_all = lax.dynamic_update_slice_in_dim(
                inner_state[2], d_value_part.reshape(groups, block_keys, width), first_key, 1
            )
            return (d_query, d_key_all, d_value_all)

        return (lax.cond(any_allowed, gradients, lambda inner_state: inner_state, state), None)

    zero_query = jnp.zeros((groups, seg_len, HEADS, HD), jnp.float32)
    initial = (zero_query, jnp.zeros_like(key_all), jnp.zeros_like(value_all))
    final_state, unused = lax.scan(block_step, initial, firsts)
    d_query = final_state[0].reshape(groups, seg_len, width) * scale
    return (d_query, final_state[1], final_state[2])


def cross_forward(queries, key_rows, value_rows):
    groups, seg_len, width = queries.shape
    enc_rows = key_rows.shape[1]
    query_heads = queries.reshape(groups, seg_len, HEADS, HD) * HD ** (-0.5)
    scores = product("gshd,gehd->ghse", query_heads, key_rows.reshape(groups, enc_rows, HEADS, HD))
    probs = jax.nn.softmax(scores, axis=-1)
    context = product("ghse,gehd->gshd", probs, value_rows.reshape(groups, enc_rows, HEADS, HD))
    return (context.reshape(groups, seg_len, width), probs)


def cross_backward(queries, key_rows, value_rows, probs, d_context):
    groups, seg_len, width = queries.shape
    enc_rows = key_rows.shape[1]
    scale = HD ** (-0.5)
    query_heads = queries.reshape(groups, seg_len, HEADS, HD) * scale
    key_heads = key_rows.reshape(groups, enc_rows, HEADS, HD)
    value_heads = value_rows.reshape(groups, enc_rows, HEADS, HD)
    out_heads = d_context.reshape(groups, seg_len, HEADS, HD)
    d_values = product("ghse,gshd->gehd", probs, out_heads)
    d_probs = product("gshd,gehd->ghse", out_heads, value_heads)
    d_scores = probs * (d_probs - jnp.sum(probs * d_probs, -1, keepdims=True))
    d_queries = product("ghse,gehd->gshd", d_scores, key_heads) * scale
    d_keys = product("ghse,gshd->gehd", d_scores, query_heads)
    return (
        d_queries.reshape(groups, seg_len, width),
        d_keys.reshape(groups, enc_rows, width),
        d_values.reshape(groups, enc_rows, width),
    )


def shards(
    tokens,
    encoder,
    cotangent,
    adapter_pick,
    segment_order,
    parents,
    norm_gains,
    w_qkv,
    w_self_out,
    w_cross_q,
    w_cross_kv,
    w_cross_out,
    w_fc_in,
    w_fc_out,
    attn_down,
    attn_up,
    fc_in_down,
    fc_in_up,
    fc_out_down,
    fc_out_up,
):
    groups, seg_len, width = tokens.shape
    enc_rows = encoder.shape[1]
    my_slot = lax.axis_index("seq")
    reach_rows = reach_table(segment_order, parents)
    my_reach = lax.dynamic_index_in_dim(reach_rows, my_slot, 1, keepdims=False)
    adapter_count = attn_down.shape[0]
    chosen = (
        adapter_pick[:, None] == lax.broadcasted_iota(jnp.int32, (1, adapter_count), 1)
    ).astype(jnp.float32)
    chosen_low = chosen.astype(jnp.bfloat16)

    def select(adapter_table):
        return jnp.einsum(
            "ga,a...->g...", chosen_low, adapter_table, preferred_element_type=jnp.float32
        )

    sel_down = select(attn_down)
    sel_up = select(attn_up)
    in_down = select(fc_in_down)
    in_up = select(fc_in_up)
    out_down = select(fc_out_down)
    out_up = select(fc_out_up)
    normed_one, normal_one, inverse_one = layer_norm(tokens, norm_gains[0])
    inner_qkv = product("gsd,gpdr->gspr", normed_one, sel_down[:, 0:3])
    stacked = cols_forward(normed_one, w_qkv) + ADAPT_SCALE * product(
        "gspr,gpro->gspo", inner_qkv, sel_up[:, 0:3]
    ).reshape(groups, seg_len, 3 * width)
    queries = stacked[..., :width]
    key_rows = stacked[..., width : 2 * width]
    value_rows = stacked[..., 2 * width :]
    context, log_mass = self_forward(queries, key_rows, value_rows, my_reach, my_slot)
    self_term, inner_self = adapter_apply(context, sel_down[:, 3], sel_up[:, 3])
    middle = tokens + rows_forward(context, w_self_out) + self_term
    normed_two, normal_two, inverse_two = layer_norm(middle, norm_gains[1])
    query_term, inner_cross_q = adapter_apply(normed_two, sel_down[:, 4], sel_up[:, 4])
    cross_queries = cols_forward(normed_two, w_cross_q) + query_term
    inner_memory = product("ged,gpdr->gepr", encoder, sel_down[:, 5:7])
    memory = cols_forward(encoder, w_cross_kv) + ADAPT_SCALE * product(
        "gepr,gpro->gepo", inner_memory, sel_up[:, 5:7]
    ).reshape(groups, enc_rows, 2 * width)
    cross_keys = memory[..., :width]
    cross_values = memory[..., width:]
    cross_context, cross_probs = cross_forward(cross_queries, cross_keys, cross_values)
    cross_term, inner_cross_out = adapter_apply(cross_context, sel_down[:, 7], sel_up[:, 7])
    after_cross = middle + rows_forward(cross_context, w_cross_out) + cross_term
    normed_three, normal_three, inverse_three = layer_norm(after_cross, norm_gains[2])
    inner_in = product("gsd,gdr->gsr", normed_three, in_down)
    pre_act = cols_forward(normed_three, w_fc_in) + ADAPT_SCALE * product(
        "gsr,grf->gsf", inner_in, in_up
    )
    hidden = jax.nn.gelu(pre_act, approximate=True)
    inner_out = product("gsf,gfr->gsr", hidden, out_down)
    mlp_out = rows_forward(hidden, w_fc_out) + ADAPT_SCALE * product(
        "gsr,grd->gsd", inner_out, out_up
    )
    layer_out = after_cross + mlp_out
    d_inner_out = ADAPT_SCALE * product("gsd,grd->gsr", cotangent, out_up)
    grad_out_up_tree = ADAPT_SCALE * product("gsr,gsd->grd", inner_out, cotangent)
    d_hidden = rows_back(cotangent, w_fc_out) + product("gsr,gfr->gsf", d_inner_out, out_down)
    grad_out_down_tree = product("gsf,gsr->gfr", hidden, d_inner_out)
    d_pre = gelu_back(pre_act, d_hidden)
    d_inner_in = ADAPT_SCALE * product("gsf,grf->gsr", d_pre, in_up)
    grad_in_up_tree = ADAPT_SCALE * product("gsr,gsf->grf", inner_in, d_pre)
    d_normed_three = cols_back(d_pre, w_fc_in) + product("gsr,gdr->gsd", d_inner_in, in_down)
    grad_in_down_tree = product("gsd,gsr->gdr", normed_three, d_inner_in)
    d_after = cotangent + norm_back(normal_three, inverse_three, norm_gains[2], d_normed_three)
    d_cross_ctx, grad_down_seven, grad_up_seven = adapter_back(
        cross_context, inner_cross_out, sel_down[:, 7], sel_up[:, 7], d_after
    )
    d_cross_ctx = d_cross_ctx + rows_back(d_after, w_cross_out)
    d_cross_q, d_cross_k, d_cross_v = cross_backward(
        cross_queries, cross_keys, cross_values, cross_probs, d_cross_ctx
    )
    d_normed_two, grad_down_four, grad_up_four = adapter_back(
        normed_two, inner_cross_q, sel_down[:, 4], sel_up[:, 4], d_cross_q
    )
    d_normed_two = d_normed_two + cols_back(d_cross_q, w_cross_q)
    d_middle = d_after + norm_back(normal_two, inverse_two, norm_gains[1], d_normed_two)
    d_memory = jnp.concatenate([d_cross_k, d_cross_v], axis=-1)
    d_memory_split = d_memory.reshape(groups, enc_rows, 2, width)
    d_inner_memory = ADAPT_SCALE * product("gepo,gpro->gepr", d_memory_split, sel_up[:, 5:7])
    grad_up_memory = ADAPT_SCALE * product("gepr,gepo->gpro", inner_memory, d_memory_split)
    grad_down_memory = product("ged,gepr->gpdr", encoder, d_inner_memory)
    d_encoder_local = cols_back(d_memory, w_cross_kv) + product(
        "gepr,gpdr->ged", d_inner_memory, sel_down[:, 5:7]
    )
    grad_encoder = lax.psum_scatter(d_encoder_local, "seq", scatter_dimension=1, tiled=True)
    d_context, grad_down_three, grad_up_three = adapter_back(
        context, inner_self, sel_down[:, 3], sel_up[:, 3], d_middle
    )
    d_context = d_context + rows_back(d_middle, w_self_out)
    delta = jnp.sum(
        d_context.reshape(groups, seg_len, HEADS, HD) * context.reshape(groups, seg_len, HEADS, HD),
        -1,
    ).transpose(0, 2, 1)
    key_all, value_all = (
        lax.all_gather(key_rows, "seq", axis=1, tiled=True),
        lax.all_gather(value_rows, "seq", axis=1, tiled=True),
    )
    d_queries, d_key_all, d_value_all = self_backward(
        queries, key_all, value_all, log_mass, delta, d_context, my_reach, my_slot
    )
    d_keys, d_values = (
        lax.psum_scatter(d_key_all, "seq", scatter_dimension=1, tiled=True),
        lax.psum_scatter(d_value_all, "seq", scatter_dimension=1, tiled=True),
    )
    d_stacked = jnp.concatenate([d_queries, d_keys, d_values], axis=-1)
    d_split = d_stacked.reshape(groups, seg_len, 3, width)
    d_inner_qkv = ADAPT_SCALE * product("gspo,gpro->gspr", d_split, sel_up[:, 0:3])
    grad_up_qkv = ADAPT_SCALE * product("gspr,gspo->gpro", inner_qkv, d_split)
    grad_down_qkv = product("gsd,gspr->gpdr", normed_one, d_inner_qkv)
    d_normed_one = cols_back(d_stacked, w_qkv) + product(
        "gspr,gpdr->gsd", d_inner_qkv, sel_down[:, 0:3]
    )
    grad_tokens = d_middle + norm_back(normal_one, inverse_one, norm_gains[0], d_normed_one)
    down_stack = jnp.concatenate(
        [
            grad_down_qkv,
            grad_down_three[:, None],
            grad_down_four[:, None],
            grad_down_memory,
            grad_down_seven[:, None],
        ],
        axis=1,
    )
    up_stack = jnp.concatenate(
        [
            grad_up_qkv,
            grad_up_three[:, None],
            grad_up_four[:, None],
            grad_up_memory,
            grad_up_seven[:, None],
        ],
        axis=1,
    )
    tree_parts = (
        down_stack,
        up_stack,
        grad_in_down_tree,
        grad_in_up_tree,
        grad_out_down_tree,
        grad_out_up_tree,
    )
    shapes = (
        attn_down.shape,
        attn_up.shape,
        fc_in_down.shape,
        fc_in_up.shape,
        fc_out_down.shape,
        fc_out_up.shape,
    )
    local_sums = tuple(
        (product("ga,gx->ax", chosen, part.reshape(groups, -1)).reshape(-1) for part in tree_parts)
    )
    owned = lax.psum_scatter(local_sums, ("dp", "seq"), scatter_dimension=0, tiled=True)
    full_sums = lax.all_gather(owned, ("dp", "seq"), axis=0, tiled=True)
    results = [summed.reshape(shape) for summed, shape in zip(full_sums, shapes)]
    return (
        layer_out,
        grad_tokens,
        grad_encoder,
        results[0],
        results[1],
        results[2],
        results[3],
        results[4],
        results[5],
    )


ROWS = ("z", "y")
COPIES = ("x", "c")
EVERY = ROWS + COPIES
F32 = jnp.float32
BF16 = jnp.bfloat16
MIB = 1 << 20
SWAP = [(0, 1), (1, 0)]
NN = (((1,), (0,)), ((), ()))
NT = (((1,), (1,)), ((), ()))
TN = (((0,), (0,)), ((), ()))


def split(values):
    high = values.astype(BF16)
    return high, (values - high.astype(F32)).astype(BF16)


def dot(left, right, dims=NN):
    return lax.dot_general(left, right, dims, preferred_element_type=F32)


def dot3(left, right, dims=NN):
    (left_high, left_low), (right_high, right_low) = left, right
    return (
        dot(left_high, right_high, dims)
        + dot(left_high, right_low, dims)
        + dot(left_low, right_high, dims)
    )


def dot2(left, right, dims=NN):
    return dot(left[0], right, dims) + dot(left[1], right, dims)


def adapted(rows, down, up):
    inner = dot2(rows, down, NT)
    return dot2(split(ADAPT_SCALE * inner), up), inner


def adapted_back(rows, grads, down, up):
    inner = split(ADAPT_SCALE * dot2(rows, down, NT))
    d_inner = split(ADAPT_SCALE * dot2(grads, up, NT))
    return dot2(d_inner, down), dot3(d_inner, rows, TN), dot3(inner, grads, TN)


def both(parts, where):
    return parts[0][where], parts[1][where]


def vmem(limit):
    return pltpu.CompilerParams(vmem_limit_bytes=limit * MIB)


def lasting(micros):
    return pl.CostEstimate(
        flops=int(micros * 1e9), bytes_accessed=int(micros * 3e6), transcendentals=0
    )


def shaped(*shape):
    return jax.ShapeDtypeStruct(shape, F32)


def whole_spec(shape):
    return pl.BlockSpec(shape, lambda *_: (0,) * len(shape))


def signal(target):
    pl.semaphore_signal(
        pltpu.get_barrier_semaphore(), 1, device_id=target, device_id_type=pl.DeviceIdType.MESH
    )


def greet(z, last, partners, more=0):
    for partner in partners:
        signal(partner)

    @pl.when(z > 0)
    def _():
        signal({"z": z - 1})

    @pl.when(z < last)
    def _():
        signal({"z": z + 1})

    def met():
        lines = (z > 0).astype(jnp.int32) + (z < last).astype(jnp.int32)
        pl.semaphore_wait(pltpu.get_barrier_semaphore(), len(partners) + lines + more)

    return met


def remote(source, target, sem, arrival, device):
    return pltpu.make_async_remote_copy(
        src_ref=source,
        dst_ref=target,
        send_sem=sem,
        recv_sem=arrival,
        device_id=device,
        device_id_type=pl.DeviceIdType.MESH,
    )


def start(copy):
    copy.start()


def wait_send(copy):
    copy.wait_send()


def heads_kernel(
    order_ref,
    parents_ref,
    tokens_ref,
    gains_ref,
    weight_ref,
    shard_ref,
    down_ref,
    up_ref,
    normed_ref,
    inner_ref,
    qkv_ref,
    own_weight_ref,
    packed_ref,
    context_ref,
    own_context_ref,
    rows_ref,
    blocks_ref,
    w_high,
    w_low,
    keep_sem,
    block_sem,
    block_here_sem,
    here_sem,
    across_sem,
    over_first_sem,
    over_second_sem,
    line_sem,
    line_first_sem,
    line_second_sem,
    shard_here_sem,
    plane_sem,
    plane_here_sem,
    core_sem,
    core_here_sem,
    context_sem,
    context_here_sem,
):
    x, c = lax.axis_index("x"), lax.axis_index("c")
    z, y = lax.axis_index("z"), lax.axis_index("y")
    last = lax.axis_size("z") - 1
    trees, seg_len, width = tokens_ref.shape
    lanes = weight_ref.shape[1] // 3
    rank = up_ref.shape[2]
    slots = rows_ref.shape[0]
    mine, facing = 2 * x + c, 2 * (1 - x) + c

    def place(level, side):
        return level * 2 + side

    own = place(z, y)

    def block_move(i):
        block = 3 * own + i
        target, kind = block % slots, block // slots
        source = weight_ref.at[:, i * lanes : (i + 1) * lanes]

        def sent():
            return remote(
                source,
                blocks_ref.at[kind],
                block_sem.at[i],
                block_here_sem.at[kind],
                {"z": target // 2, "y": target % 2},
            )

        def kept():
            return pltpu.make_async_copy(source, blocks_ref.at[kind], block_here_sem.at[kind])

        return target, sent, kept

    half = shard_ref.shape[1] // 2

    def rows_move(slot, sem, device):
        return remote(rows_ref.at[slot], rows_ref.at[slot], sem, here_sem.at[slot], device)

    def shard_move(part, slot, sem, device):
        rows = slice(part * half, (part + 1) * half)
        piece = packed_ref.at[slot, mine, rows]
        source = shard_ref.at[mine, rows] if slot is own else piece
        return remote(source, piece, sem, shard_here_sem.at[part, slot], device)

    first = functools.partial(shard_move, 0)
    second = functools.partial(shard_move, 1)

    def along(move, sems, slot, level, action):
        @pl.when(jnp.logical_and(level <= z, z < last))
        def _():
            action(move(slot, sems.at[0, slot], {"z": z + 1}))

        @pl.when(jnp.logical_and(level >= z, z > 0))
        def _():
            action(move(slot, sems.at[1, slot], {"z": z - 1}))

    def over(move, sems, slot, action):
        action(move(slot, sems.at[slot], {"y": 1 - y}))

    def beside(level):
        return own if level is z else place(level, y)

    def plane_move(part, slot):
        piece = packed_ref.at[slot, mine, part * half : (part + 1) * half]
        return remote(
            piece, piece, plane_sem.at[part, slot], plane_here_sem.at[part, slot], {"x": 1 - x}
        )

    def core_move(part, slot, kind):
        piece = packed_ref.at[slot, facing if kind else mine, part * half : (part + 1) * half]
        index = 2 * part + kind
        return remote(
            piece, piece, core_sem.at[index, slot], core_here_sem.at[index, slot], {"c": 1 - c}
        )

    def levels_at(hop, action):
        if hop == 0:
            action(z)
            return
        for level in (z - hop, z + hop):

            @pl.when(jnp.logical_and(level >= 0, level <= last))
            def _(level=level):
                action(level)

    def peer(step):
        target = (own + step) % slots
        return target, {"z": target // 2, "y": target % 2}

    for step in range(1, slots):
        signal(peer(step)[1])
    signal({"x": 1 - x})
    signal({"c": 1 - c})
    for tree in range(trees):
        normed = layer_norm(tokens_ref[tree], gains_ref[0:1])[0]
        rows_ref[own, tree * seg_len : (tree + 1) * seg_len] = normed
    pl.semaphore_wait(pltpu.get_barrier_semaphore(), slots + 1)
    along(rows_move, line_sem, own, z, start)
    over(rows_move, across_sem, own, start)
    for i in range(3):
        target, sent, kept = block_move(i)

        @pl.when(target != own)
        def _(sent=sent):
            sent().start()

        @pl.when(target == own)
        def _(kept=kept):
            kept().start()

    def start_shards():
        over(second, over_second_sem, own, start)
        along(first, line_first_sem, own, z, start)
        over(first, over_first_sem, own, start)
        along(second, line_second_sem, own, z, start)

    def keep(slot):
        return pltpu.make_async_copy(rows_ref.at[slot], normed_ref.at[slot], keep_sem.at[slot])

    def keep_shard():
        return pltpu.make_async_copy(shard_ref, packed_ref.at[own], keep_sem.at[slots])

    def keep_blocks():
        return pltpu.make_async_copy(blocks_ref, own_weight_ref, keep_sem.at[slots + 1])

    keep_shard().start()

    def take_blocks():
        for kind in range(3):
            block = blocks_ref.at[kind]
            pltpu.make_async_copy(block, block, block_here_sem.at[kind]).wait()
            where = slice(kind * lanes, (kind + 1) * lanes)
            w_high[:, where], w_low[:, where] = split(block[...])
        keep_blocks().start()

    def work(slot):
        keep(slot).start()
        parts = split(rows_ref[slot])
        product = dot3(parts, (w_high[...], w_low[...]))
        for tree in range(trees):
            rows = slice(tree * seg_len, (tree + 1) * seg_len)
            inner = dot2(both(parts, rows), down_ref[tree], NT)
            inner_ref[slot, tree] = inner
            inner_parts = split(ADAPT_SCALE * inner)
            for kind in range(3):
                term = dot2(
                    both(inner_parts, (slice(None), slice(kind * rank, (kind + 1) * rank))),
                    up_ref[tree, kind],
                )
                qkv_ref[slot, kind, tree] = (
                    product[rows, kind * lanes : (kind + 1) * lanes] + term
                )

    def arrived(move, slot):
        move(slot, across_sem.at[0], {"y": 1 - y}).wait_recv()

    def share(part, slot):
        plane_move(part, slot).start()
        core_move(part, slot, 0).start()

    def rows_by_line(level):
        slot = place(level, y)
        arrived(rows_move, slot)
        along(rows_move, line_sem, slot, level, start)
        over(rows_move, across_sem, slot, start)

    def first_by_line(level):
        slot = place(level, y)
        arrived(first, slot)
        along(first, line_first_sem, slot, level, start)
        over(first, over_first_sem, slot, start)
        share(0, slot)

    def second_by_line(level):
        for side in (y, 1 - y):
            slot = place(level, side)
            arrived(second, slot)
            along(second, line_second_sem, slot, level, start)
            share(1, slot)

    def rows_over(level):
        slot = place(level, 1 - y)
        arrived(rows_move, slot)
        work(slot)

    def first_over(level):
        slot = place(level, 1 - y)
        arrived(first, slot)
        share(0, slot)

    def faced(part, slot):
        plane_move(part, slot).wait_recv()
        core_move(part, slot, 1).start()

    def faced_at(hop):
        def act(level):
            if level is not z:
                faced(0, place(level, y))
                faced(1, place(level, y))
            faced(1, place(level, 1 - y))

        levels_at(hop, act)

    def attend_tree(tree):
        def slot_of(segment):
            found = jnp.int32(0)
            for slot in range(1, slots):
                found = jnp.where(order_ref[tree, slot] == segment, slot, found)
            return found

        def attend_slot(slot, carry):
            chain = ancestor_slots(order_ref, parents_ref, slot_of, tree, slot)
            own_context_ref[slot, tree] = attend(
                qkv_ref[slot, 0, tree] * HD ** (-0.5),
                jnp.concatenate([qkv_ref[where, 1, tree] for where, _ in chain], axis=0),
                jnp.concatenate([qkv_ref[where, 2, tree] for where, _ in chain], axis=0),
                chain_mask(chain, seg_len),
            )
            return carry

        lax.fori_loop(0, slots, attend_slot, 0)

    def context_move(step):
        target, device = peer(step)
        return remote(
            own_context_ref.at[target],
            context_ref.at[own],
            context_sem.at[step],
            context_here_sem.at[step],
            device,
        )

    def context_keep():
        return pltpu.make_async_copy(
            own_context_ref.at[own], context_ref.at[own], context_sem.at[0]
        )

    other = place(z, 1 - y)
    levels_at(1, rows_by_line)
    take_blocks()
    work(own)
    levels_at(1, lambda level: work(place(level, y)))
    levels_at(2, rows_by_line)
    start_shards()
    rows_over(z)
    levels_at(2, lambda level: work(place(level, y)))
    for hop in range(3, last + 1):
        levels_at(hop, rows_by_line)
    levels_at(1, rows_over)
    arrived(second, other)
    along(second, line_second_sem, other, z, start)
    share(1, other)
    levels_at(1, first_by_line)
    levels_at(1, second_by_line)
    for hop in range(3, last + 1):
        levels_at(hop, lambda level: work(place(level, y)))
    first_over(z)
    for hop in range(2, last + 1):
        levels_at(hop, rows_over)
    for tree in range(trees):
        attend_tree(tree)
        if tree == 0:
            levels_at(2, first_by_line)
            levels_at(2, second_by_line)
            levels_at(1, first_over)
            faced_at(0)
    context_keep().start()
    for step in range(1, slots):
        context_move(step).start()
    for hop in range(3, last + 1):
        levels_at(hop, first_by_line)
        levels_at(hop, second_by_line)
    faced_at(1)
    for hop in range(2, last + 1):
        levels_at(hop, first_over)
    for hop in range(2, last + 1):
        faced_at(hop)
    for hop in range(last + 1):
        levels_at(hop, lambda level: faced(0, place(level, 1 - y)))

    context_keep().wait()
    for step in range(1, slots):
        context_move(step).wait_send()
        context_move(step).wait_recv()
    keep_shard().wait()
    keep_blocks().wait()
    for i in range(3):
        target, sent, _ = block_move(i)

        @pl.when(target != own)
        def _(sent=sent):
            sent().wait_send()

    def finish(slot):
        for part in range(2):
            plane_move(part, slot).wait_send()
            for kind in range(2):
                core_move(part, slot, kind).wait_recv()
                core_move(part, slot, kind).wait_send()

    def sent_on(level):
        slot = beside(level)
        along(rows_move, line_sem, slot, level, wait_send)
        over(rows_move, across_sem, slot, wait_send)
        along(first, line_first_sem, slot, level, wait_send)
        over(first, over_first_sem, slot, wait_send)
        along(second, line_second_sem, slot, level, wait_send)
        along(second, line_second_sem, place(level, 1 - y), level, wait_send)
        if level is z:
            over(second, over_second_sem, own, wait_send)
        else:
            finish(slot)
        finish(place(level, 1 - y))

    for hop in range(last + 1):
        levels_at(hop, sent_on)
    for slot in range(slots):
        keep(slot).wait()


def heads_call(order, parents, tokens, gains, weight, shard, down, up):
    trees, seg_len, width = tokens.shape
    slots = lax.axis_size(ROWS)
    lanes = weight.shape[1] // 3
    inner = down.shape[1]
    dma = pltpu.SemaphoreType.DMA
    here = pl.BlockSpec(memory_space=pltpu.VMEM)
    there = pl.BlockSpec(memory_space=pl.ANY)
    scalars = pl.BlockSpec(memory_space=pltpu.SMEM)
    return pl.pallas_call(
        heads_kernel,
        out_shape=[
            shaped(slots, trees * seg_len, width),
            shaped(slots, trees, seg_len, inner),
            shaped(slots, 3, trees, seg_len, lanes),
            shaped(3, width, lanes),
            shaped(slots, *shard.shape),
            shaped(slots, trees, seg_len, lanes),
        ],
        in_specs=[scalars, scalars, here, here, there, there, here, here],
        out_specs=[there, here, here, there, there, there],
        scratch_shapes=[
            pltpu.VMEM((slots, trees, seg_len, lanes), F32),
            pltpu.VMEM((slots, trees * seg_len, width), F32),
            pltpu.VMEM((3, width, lanes), F32),
            pltpu.VMEM((width, 3 * lanes), BF16),
            pltpu.VMEM((width, 3 * lanes), BF16),
            dma((slots + 2,)),
            dma((3,)),
            dma((3,)),
        ]
        + [dma((slots,))] * 4
        + [dma((2, slots))] * 6
        + [dma((4, slots))] * 2
        + [dma((slots,))] * 2,
        compiler_params=pltpu.CompilerParams(
            vmem_limit_bytes=48 * MIB, collective_id=0, has_side_effects=True
        ),
        cost_estimate=lasting(180),
    )(order, parents, tokens, gains, weight, shard, down, up)


def ancestor_slots(order_ref, parents_ref, slot_of, tree, slot, depth=4):
    segment = order_ref[tree, slot]
    chain = [(slot, None)]
    there = None
    for _ in range(depth - 1):
        parent = parents_ref[tree, segment]
        there = parent >= 0 if there is None else jnp.logical_and(there, parent >= 0)
        segment = jnp.maximum(parent, 0)
        chain.append((slot_of(segment), there))
    return chain


def fill_slot_of(order_ref, slot_of, tree, slots):
    for slot in range(slots):
        slot_of[order_ref[tree, slot]] = slot


def chain_mask(chain, seg_len):
    row = lax.broadcasted_iota(jnp.int32, (seg_len, seg_len), 0)
    column = lax.broadcasted_iota(jnp.int32, (seg_len, seg_len), 1)
    masks = [(column <= row).astype(jnp.int32)]
    for _, there in chain[1:]:
        masks.append(jnp.full((seg_len, seg_len), there.astype(jnp.int32)))
    mask = jnp.concatenate(masks, axis=1)
    return jnp.concatenate([mask, mask], axis=0) > 0


def stacked_heads(parts):
    lane = lax.broadcasted_iota(jnp.int32, parts[0].shape, 1)
    return tuple(
        jnp.concatenate(
            [jnp.where(lane < HD, part, 0), jnp.where(lane >= HD, part, 0)], axis=0
        ).astype(BF16)
        for part in parts
    )


def beside_heads(stacked):
    count = stacked.shape[0] // 2
    lane = lax.broadcasted_iota(jnp.int32, (count, stacked.shape[1]), 1)
    return jnp.where(lane < HD, stacked[:count], stacked[count:])


def by_lanes(left, right):
    wide = jnp.concatenate(left, axis=1)
    return dot(wide, jnp.concatenate([right[0], right[0]], axis=1), NT) + dot(
        left[0], right[1], NT
    )


def by_rows(left, right, dims):
    width = right[0].shape[1]
    wide = dot(left[0], jnp.concatenate(right, axis=1), dims)
    return wide[:, :width] + wide[:, width:] + dot(left[1], right[0], dims)


def pair_scores(query_parts, key_parts, mask):
    scores = by_lanes(query_parts, key_parts)
    if mask is not None:
        scores = jnp.where(mask, scores, MASK_FILL)
    return jnp.exp(scores - jnp.max(scores, -1, keepdims=True))


def attend(queries, keys, values, mask=None):
    weights = pair_scores(stacked_heads(split(queries)), split(keys), mask)
    mass = jnp.sum(weights, -1, keepdims=True)
    return beside_heads(by_rows(split(weights), split(values), NN) / mass)


def attend_back(queries, keys, values, d_context, mask=None):
    query_parts, out_parts = stacked_heads(split(queries)), stacked_heads(split(d_context))
    key_parts, value_parts = split(keys), split(values)
    weights = pair_scores(query_parts, key_parts, mask)
    weights = weights * (1.0 / jnp.sum(weights, -1, keepdims=True))
    d_weights = by_lanes(out_parts, value_parts)
    shared = jnp.sum(weights * d_weights, -1, keepdims=True)
    score_parts = split(weights * (d_weights - shared))
    return (
        beside_heads(by_rows(score_parts, key_parts, NN)) * HD ** (-0.5),
        by_rows(score_parts, query_parts, TN),
        by_rows(split(weights), out_parts, TN),
    )


def self_backward_kernel(
    order_ref,
    parents_ref,
    qkv_ref,
    d_context_ref,
    normed_ref,
    inner_ref,
    up_ref,
    _,
    __,
    d_qkv_ref,
    g_down_ref,
    g_up_ref,
    slot_of,
):
    tree = pl.program_id(0)
    slots, seg_len, pair = qkv_ref.shape[0], qkv_ref.shape[3], qkv_ref.shape[4]
    rank = up_ref.shape[2]
    fill_slot_of(order_ref, slot_of, tree, slots)
    d_qkv_ref[...] = jnp.zeros_like(d_qkv_ref)

    def one_slot(slot, carry):
        chain = ancestor_slots(order_ref, parents_ref, lambda seg: slot_of[seg], tree, slot)
        keys = jnp.concatenate([qkv_ref[where, 1, 0] for where, _ in chain], axis=0)
        values = jnp.concatenate([qkv_ref[where, 2, 0] for where, _ in chain], axis=0)
        d_queries, d_keys, d_values = attend_back(
            qkv_ref[slot, 0, 0] * HD ** (-0.5),
            keys,
            values,
            d_context_ref[slot, 0],
            mask=chain_mask(chain, seg_len),
        )
        d_qkv_ref[slot, 0, 0] += d_queries
        for entry, (where, _) in enumerate(chain):
            rows = slice(entry * seg_len, (entry + 1) * seg_len)
            d_qkv_ref[where, 1, 0] += d_keys[rows]
            d_qkv_ref[where, 2, 0] += d_values[rows]
        return carry

    lax.fori_loop(0, slots, one_slot, 0)

    inner = split(ADAPT_SCALE * inner_ref[...].reshape(slots * seg_len, 3 * rank))
    d_inner = []
    for kind in range(3):
        grads = split(d_qkv_ref[:, kind, 0].reshape(slots * seg_len, pair))
        ranks = slice(kind * rank, (kind + 1) * rank)
        d_inner.append(dot2(grads, up_ref[0, kind], NT))
        g_up_ref[0, kind] = dot3(both(inner, (slice(None), ranks)), grads, TN)
    high, low = split(ADAPT_SCALE * jnp.concatenate(d_inner, axis=1))
    rows_high, rows_low = split(normed_ref[...].reshape(slots * seg_len, -1))
    wide = dot(jnp.concatenate([high, low], axis=1), rows_high, TN)
    g_down = wide[: 3 * rank] + wide[3 * rank :] + dot(high, rows_low, TN)
    g_down_ref[0] = g_down.reshape(3, rank, -1)


def slots_spec(shape):
    lead = len(shape) - 3
    return pl.BlockSpec(
        shape[:lead] + (1,) + shape[lead + 1 :],
        lambda tree, *_: (0,) * lead + (tree, 0, 0),
    )


def tree_spec(shape):
    return pl.BlockSpec((1,) + shape[1:], lambda tree, *_: (tree,) + (0,) * (len(shape) - 1))


def self_call(kernel, order, parents, operands, in_specs, out_shape, out_specs, micros):
    trees, slots = order.shape
    return pl.pallas_call(
        kernel,
        out_shape=out_shape,
        grid_spec=pltpu.PrefetchScalarGridSpec(
            num_scalar_prefetch=2,
            grid=(trees,),
            in_specs=in_specs,
            out_specs=out_specs,
            scratch_shapes=[pltpu.SMEM((slots,), jnp.int32)],
        ),
        compiler_params=vmem(56),
        cost_estimate=lasting(micros),
    )(order, parents, *operands)


def head_pairs(ref):
    return [slice(2 * pair * HD, 2 * (pair + 1) * HD) for pair in range(ref.shape[2] // (2 * HD))]


def cross_forward_kernel(query_ref, key_ref, value_ref, _, context_ref):
    for lanes in head_pairs(query_ref):
        context_ref[0, :, lanes] = attend(
            query_ref[0, :, lanes] * HD ** (-0.5), key_ref[0, :, lanes], value_ref[0, :, lanes]
        )


def cross_backward_kernel(
    query_ref, key_ref, value_ref, d_context_ref, d_query_ref, d_key_ref, d_value_ref
):
    for lanes in head_pairs(query_ref):
        d_query_ref[0, :, lanes], d_key_ref[0, :, lanes], d_value_ref[0, :, lanes] = attend_back(
            query_ref[0, :, lanes] * HD ** (-0.5),
            key_ref[0, :, lanes],
            value_ref[0, :, lanes],
            d_context_ref[0, :, lanes],
        )


def cross_call(kernel, queries, memory, rest, long_outs, ahead=()):
    trees, seg_len, width = queries.shape
    enc_rows = memory.shape[1]
    lanes = 4 * HD
    steps = width // lanes
    short = pl.BlockSpec((1, seg_len, lanes), lambda tree, step: (tree, 0, step))
    keys = pl.BlockSpec((1, enc_rows, lanes), lambda tree, step: (tree, 0, step))
    values = pl.BlockSpec((1, enc_rows, lanes), lambda tree, step: (tree, 0, steps + step))
    return pl.pallas_call(
        kernel,
        out_shape=[shaped(trees, seg_len, width)] + [shaped(trees, enc_rows, width)] * long_outs,
        grid=(trees, steps),
        in_specs=[short, keys, values]
        + [short] * len(rest)
        + [pl.BlockSpec(memory_space=pl.ANY)] * len(ahead),
        out_specs=[short] + [keys] * long_outs,
        compiler_params=vmem(48),
        cost_estimate=lasting(32 if long_outs else 19),
    )(queries, memory, memory, *rest, *ahead)


def square(ref):
    return ref[...].reshape(-1, ref.shape[-1])


def joined(ref):
    slots, trees = ref.shape[:2]
    return jnp.concatenate(
        [
            jnp.concatenate([ref[slot, tree] for slot in range(slots)], axis=1)
            for tree in range(trees)
        ],
        axis=0,
    )


def rows_of(ref):
    return ref[...].reshape(-1, ref.shape[-1])


def tree_rows(trees, count):
    return [slice(tree * count, (tree + 1) * count) for tree in range(trees)]


def with_adapters(parts, down_ref, up_ref, entry, trees):
    count = parts[0].shape[0] // trees
    return jnp.concatenate(
        [
            adapted(both(parts, rows), down_ref[tree, entry], up_ref[tree, entry])[0]
            for tree, rows in enumerate(tree_rows(trees, count))
        ],
        axis=0,
    )


def with_adapters_back(parts, grads, down_ref, up_ref, entry, trees, g_down_ref, g_up_ref, place):
    count = parts[0].shape[0] // trees
    terms = []
    for tree, rows in enumerate(tree_rows(trees, count)):
        term, g_down_ref[tree, place], g_up_ref[tree, place] = adapted_back(
            both(parts, rows), both(grads, rows), down_ref[tree, entry], up_ref[tree, entry]
        )
        terms.append(term)
    return jnp.concatenate(terms, axis=0)


def after_self_kernel(
    context_ref, tokens_ref, gains_ref, out_ref, query_ref, down_ref, up_ref, middle_ref, cross_ref
):
    trees = tokens_ref.shape[0]
    context = split(joined(context_ref))
    middle = rows_of(tokens_ref) + dot3(context, split(square(out_ref)))
    middle = middle + with_adapters(context, down_ref, up_ref, 3, trees)
    middle_ref[...] = middle.reshape(middle_ref.shape)
    normed = split(layer_norm(middle, gains_ref[1:2])[0])
    queries = dot3(normed, split(square(query_ref)), NT)
    queries = queries + with_adapters(normed, down_ref, up_ref, 4, trees)
    cross_ref[...] = queries.reshape(cross_ref.shape)


def after_cross_kernel(
    context_ref, middle_ref, gains_ref, out_ref, down_ref, up_ref, after_ref, normed_ref
):
    trees = context_ref.shape[0]
    context = split(rows_of(context_ref))
    after = rows_of(middle_ref) + dot3(context, split(square(out_ref)))
    after = after + with_adapters(context, down_ref, up_ref, 7, trees)
    after_ref[...] = after.reshape(after_ref.shape)
    normed = layer_norm(after, gains_ref[2:3])[0]
    normed_ref[...] = normed.reshape(normed_ref.shape)


def into_cross_kernel(
    d_rows_ref,
    after_ref,
    cotangent_ref,
    context_ref,
    gains_ref,
    out_ref,
    down_ref,
    up_ref,
    g_in_up_ref,
    g_out_down_ref,
    d_after_ref,
    d_context_ref,
    g_down_ref,
    g_up_ref,
    hidden_ref,
    other_ref,
    parts_ref,
    swap_sem,
    part_sem,
    part_here_sem,
):
    trees = after_ref.shape[0]
    z, levels = lax.axis_index("z"), lax.axis_size("z")
    partner = {"y": 1 - lax.axis_index("y")}
    signal(partner)
    for step in range(1, levels):
        signal({"z": (z + step) % levels})
    pl.semaphore_wait(pltpu.get_barrier_semaphore(), levels)
    swapped = remote(
        d_rows_ref.at[:, 1], other_ref, swap_sem.at[0], swap_sem.at[1], partner
    )
    swapped.start()

    unit_grads = (g_in_up_ref, g_out_down_ref)

    def part_move(step, which):
        level = (z + step) % levels
        return remote(
            unit_grads[which].at[:, pl.ds(2 * level, 2)],
            parts_ref.at[step - 1, which],
            part_sem.at[step - 1, which],
            part_here_sem.at[step - 1, which],
            {"z": level},
        )

    moves = [(step, which) for step in range(1, levels) for which in range(2)]
    for step, which in moves:
        part_move(step, which).start()
    context = split(rows_of(context_ref))
    weight = split(square(out_ref))
    _, normal, inverse = layer_norm(rows_of(after_ref), gains_ref[2:3])
    for step, which in moves:
        part_move(step, which).wait_recv()
    for which in range(2):
        total = unit_grads[which][:, pl.ds(2 * z, 2)]
        for step in range(1, levels):
            total = total + parts_ref[step - 1, which]
        block = total.shape[3]
        for plane in range(2):
            lanes = slice(plane * block, (plane + 1) * block)
            hidden_ref[:, which, :, lanes] = total[:, plane]
    own_rows = jnp.concatenate([d_rows_ref[tree, 0] for tree in range(trees)], axis=0)
    swapped.wait()
    d_normed = own_rows + rows_of(other_ref)
    d_after = rows_of(cotangent_ref) + norm_back(normal, inverse, gains_ref[2:3], d_normed)
    d_after_ref[...] = d_after.reshape(d_after_ref.shape)
    grads = split(d_after)
    d_context = dot3(grads, weight, NT)
    d_context = d_context + with_adapters_back(
        context, grads, down_ref, up_ref, 7, trees, g_down_ref, g_up_ref, 0
    )
    d_context_ref[...] = d_context.reshape(d_context_ref.shape)
    for step, which in moves:
        part_move(step, which).wait_send()


def into_self_kernel(
    d_query_ref,
    d_after_ref,
    middle_ref,
    context_ref,
    gains_ref,
    query_ref,
    out_ref,
    down_ref,
    up_ref,
    d_middle_ref,
    d_context_ref,
    g_down_ref,
    g_up_ref,
):
    slots, trees, seg_len, lanes = context_ref.shape
    rows, normal, inverse = layer_norm(rows_of(middle_ref), gains_ref[1:2])
    grads = split(rows_of(d_query_ref))
    d_normed = dot3(grads, split(square(query_ref)))
    d_normed = d_normed + with_adapters_back(
        split(rows), grads, down_ref, up_ref, 4, trees, g_down_ref, g_up_ref, 1
    )
    d_middle = rows_of(d_after_ref) + norm_back(normal, inverse, gains_ref[1:2], d_normed)
    d_middle_ref[...] = d_middle.reshape(d_middle_ref.shape)
    grads = split(d_middle)
    context = split(joined(context_ref))
    d_context = dot3(grads, split(square(out_ref)), NT)
    d_context = d_context + with_adapters_back(
        context, grads, down_ref, up_ref, 3, trees, g_down_ref, g_up_ref, 0
    )
    for slot in range(slots):
        for tree in range(trees):
            d_context_ref[slot, tree] = d_context[
                tree * seg_len : (tree + 1) * seg_len, slot * lanes : (slot + 1) * lanes
            ]


def packed_spec(packed, first, count):
    return pl.BlockSpec(
        packed.shape[:2] + (count, packed.shape[3]), lambda *_: (0, 0, first // count, 0)
    )


def rows_call(kernel, operands, specs, out_shape, scratch=(), params=None):
    return pl.pallas_call(
        kernel,
        out_shape=out_shape,
        grid=(1,),
        in_specs=[
            whole_spec(operand.shape) if spec is None else spec
            for operand, spec in zip(operands, specs)
        ],
        out_specs=[whole_spec(out.shape) for out in out_shape],
        scratch_shapes=scratch,
        compiler_params=params or vmem(56),
        cost_estimate=lasting(10),
    )(*operands)


def memory_kernel(encoder_ref, weight_ref, down_ref, up_ref, memory_ref, row_high, row_low, inner):
    trees, rank = down_ref.shape[0], down_ref.shape[2]
    step = pl.program_id(0)
    half = pl.num_programs(0) // 2
    lanes = memory_ref.shape[2]
    count = encoder_ref.shape[1]

    @pl.when(step == 0)
    def _():
        row_high[...], row_low[...] = split(rows_of(encoder_ref))
        for tree, rows in enumerate(tree_rows(trees, count)):
            for kind in range(2):
                parts = (row_high[rows], row_low[rows])
                inner[kind, rows] = jnp.concatenate(
                    split(ADAPT_SCALE * dot2(parts, down_ref[tree, 5 + kind], NT)), axis=1
                )

    result = dot3((row_high[...], row_low[...]), split(square(weight_ref)), NT)
    kind = step // half
    for tree, rows in enumerate(tree_rows(trees, count)):
        up = up_ref[tree, 0]
        term = dot(inner[kind, rows], jnp.concatenate([up, up], axis=0))
        memory_ref[tree] = result[rows] + term


def memory_call(encoder, packed, down, up):
    trees, count, width = encoder.shape
    rank = down.shape[2]
    slots, copies = packed.shape[:2]
    lanes = 2 * width // slots
    half = slots // 2
    return pl.pallas_call(
        memory_kernel,
        out_shape=shaped(trees, count, 2 * width),
        grid=(slots,),
        in_specs=[
            whole_spec(encoder.shape),
            pl.BlockSpec((1, copies, lanes // copies, width), lambda step: (step, 0, 0, 0)),
            whole_spec(down.shape),
            pl.BlockSpec((trees, 1, rank, lanes), lambda step: (0, 5 + step // half, 0, step % half)),
        ],
        out_specs=pl.BlockSpec((trees, count, lanes), lambda step: (0, 0, step)),
        scratch_shapes=[
            pltpu.VMEM((trees * count, width), BF16),
            pltpu.VMEM((trees * count, width), BF16),
            pltpu.VMEM((2, trees * count, 2 * rank), BF16),
        ],
        compiler_params=vmem(56),
        cost_estimate=lasting(22),
    )(encoder, packed, down, up)


def memory_back_kernel(
    encoder_ref,
    d_key_ref,
    d_value_ref,
    weight_ref,
    down_ref,
    up_ref,
    d_encoder_ref,
    g_down_ref,
    g_up_ref,
    row_high,
    row_low,
    inner,
    d_inner,
):
    trees, rank = down_ref.shape[0], down_ref.shape[2]
    step = pl.program_id(0)
    half = pl.num_programs(0) // 2
    count = encoder_ref.shape[1]
    spans = tree_rows(trees, count)

    @pl.when(step == 0)
    def _():
        row_high[...], row_low[...] = split(rows_of(encoder_ref))
        d_encoder_ref[...] = jnp.zeros_like(d_encoder_ref)
        d_inner[...] = jnp.zeros_like(d_inner)
        for tree, rows in enumerate(spans):
            for kind in range(2):
                parts = (row_high[rows], row_low[rows])
                inner[kind, rows] = jnp.concatenate(
                    split(ADAPT_SCALE * dot2(parts, down_ref[tree, 5 + kind], NT)), axis=1
                )

    kind = step // half
    grads = split(jnp.where(kind == 0, rows_of(d_key_ref), rows_of(d_value_ref)))
    d_encoder_ref[...] += dot3(grads, split(square(weight_ref))).reshape(d_encoder_ref.shape)
    for tree, rows in enumerate(spans):
        own = both(grads, rows)
        d_inner[kind, rows] += dot2(own, up_ref[tree, 0], NT)
        high, low = inner[kind, rows, :rank], inner[kind, rows, rank:]
        g_up_ref[tree, 0] = dot3((high, low), own, TN)

    @pl.when(step == 2 * half - 1)
    def _():
        for tree, rows in enumerate(spans):
            parts = (row_high[rows], row_low[rows])
            for kind in range(2):
                own = split(ADAPT_SCALE * d_inner[kind, rows])
                d_encoder_ref[tree] += dot2(own, down_ref[tree, 5 + kind])
                g_down_ref[tree, kind] = dot3(own, parts, TN)


def memory_back_call(encoder, d_keys, d_values, packed, down, up):
    trees, count, width = encoder.shape
    rank = down.shape[2]
    slots, copies = packed.shape[:2]
    lanes = 2 * width // slots
    half = slots // 2
    kind_spec = pl.BlockSpec((trees, 1, rank, lanes), lambda step: (0, step // half, 0, step % half))
    return pl.pallas_call(
        memory_back_kernel,
        out_shape=[
            shaped(trees, count, width),
            shaped(trees, 2, rank, width),
            shaped(trees, 2, rank, width),
        ],
        grid=(slots,),
        in_specs=[
            whole_spec(encoder.shape),
            pl.BlockSpec((trees, count, lanes), lambda step: (0, 0, jnp.minimum(step, half - 1))),
            pl.BlockSpec((trees, count, lanes), lambda step: (0, 0, jnp.maximum(step - half, 0))),
            pl.BlockSpec((1, copies, lanes // copies, width), lambda step: (step, 0, 0, 0)),
            whole_spec(down.shape),
            pl.BlockSpec((trees, 1, rank, lanes), lambda step: (0, 5 + step // half, 0, step % half)),
        ],
        out_specs=[
            whole_spec((trees, count, width)),
            whole_spec((trees, 2, rank, width)),
            kind_spec,
        ],
        scratch_shapes=[
            pltpu.VMEM((trees * count, width), BF16),
            pltpu.VMEM((trees * count, width), BF16),
            pltpu.VMEM((2, trees * count, 2 * rank), BF16),
            pltpu.VMEM((2, trees * count, rank), F32),
        ],
        compiler_params=vmem(56),
        cost_estimate=lasting(31),
    )(encoder, d_keys, d_values, packed, down, up)


def nearest(z, last, turn):
    orders = [
        sorted((level for level in range(last + 1) if level != own), key=lambda level: abs(level - own))
        for own in range(last + 1)
    ]
    level = orders[0][turn]
    for own in range(1, last + 1):
        level = jnp.where(z == own, orders[own][turn], level)
    return level


def feed_forward_kernel(
    rows_ref,
    cot_ref,
    w_in_ref,
    w_out_ref,
    below_ref,
    above_ref,
    in_up_ref,
    out_down_ref,
    in_down_ref,
    out_up_ref,
    out_ref,
    d_rows_ref,
    g_in_up_ref,
    g_out_down_ref,
    g_in_down_ref,
    g_out_up_ref,
    shards_ref,
    w_in_buf,
    row_high,
    row_low,
    cot_high,
    cot_low,
    inner_in,
    d_inner_out,
    inner_in_t,
    d_inner_out_t,
    inner_out,
    d_inner_in,
    own_sem,
    w_in_sem,
    line_sem,
    line_here_sem,
    plane_sem,
    plane_here_sem,
    core_sem,
    core_here_sem,
    near_sem,
):
    trees, rank = in_up_ref.shape[0], in_up_ref.shape[2]
    spans = tree_rows(trees, rows_ref.shape[0] // trees)
    x, c, z = lax.axis_index("x"), lax.axis_index("c"), lax.axis_index("z")
    last = lax.axis_size("z") - 1
    block = shards_ref.shape[2]
    part = block // 2
    levels = [nearest(z, last, turn) for turn in range(last)]

    def piece(level, plane, core):
        return shards_ref.at[level, plane, pl.ds(pl.multiple_of(core * part, part), part)]

    def line_move(turn, target):
        level = levels[turn]
        here = piece(level, x, c)
        return remote(here, here, line_sem.at[turn], line_here_sem.at[level], {"z": target})

    def plane_move(turn):
        here = piece(levels[turn], x, c)
        return remote(here, here, plane_sem.at[turn], plane_here_sem.at[turn], {"x": 1 - x})

    def core_move(turn, kind):
        here = piece(levels[turn], x if kind == 0 else 1 - x, c)
        index = 2 * turn + kind
        return remote(here, here, core_sem.at[index], core_here_sem.at[index], {"c": 1 - c})

    def near_copy(source, level, index):
        return pltpu.make_async_copy(source, piece(level, x, c), near_sem.at[index])

    def near(action):
        @pl.when(z > 0)
        def _():
            action(near_copy(below_ref, z - 1, 0))

        @pl.when(z < last)
        def _():
            action(near_copy(above_ref, z + 1, 1))

    def wait_line(turn):
        @pl.when(jnp.abs(levels[turn] - z) > 1)
        def _():
            line_move(turn, z).wait_recv()

    def passing(turn, action):
        level = levels[turn]

        @pl.when(jnp.logical_and(level < z, z < last))
        def _():
            action(line_move(turn, z + 1))

        @pl.when(jnp.logical_and(level > z, z > 0))
        def _():
            action(line_move(turn, z - 1))

    def relay(turn):
        wait_line(turn)
        passing(turn, lambda copy: copy.start())
        plane_move(turn).start()
        core_move(turn, 0).start()

    def relay_plane(turn):
        plane_move(turn).wait_recv()
        core_move(turn, 1).start()

    order = [(-1, 0), (-1, 1), (0, 0), (1, 0), (0, 1), (2, 0), (1, 1), (2, 1)]

    def chosen(step):
        level, plane = z, x
        for index, (turn, other) in enumerate(order):
            hit = step == index
            level = jnp.where(hit, z if turn < 0 else levels[turn], level)
            plane = jnp.where(hit, 1 - x if other else x, plane)
        return level, plane

    def w_in_copy(step):
        level, plane = chosen(step)
        columns = pl.ds(pl.multiple_of(plane * block, block), block)
        slot = lax.rem(step, 2)
        return pltpu.make_async_copy(
            w_in_ref.at[level, :, columns], w_in_buf.at[slot], w_in_sem.at[slot]
        )

    def own_copy(plane):
        return pltpu.make_async_copy(
            w_out_ref.at[pl.ds(plane * block, block)], shards_ref.at[z, plane], own_sem.at[plane]
        )

    met = greet(z, last, [{"x": 1 - x}, {"c": 1 - c}])
    for plane in range(2):
        own_copy(plane).start()
    w_in_copy(0).start()
    near(start)
    met()
    near(lambda copy: copy.wait())
    relay(0)

    row_high[...], row_low[...] = split(rows_ref[...])
    cot_high[...], cot_low[...] = split(cot_ref[...])
    out_ref[...] = jnp.zeros_like(out_ref)
    d_rows_ref[...] = jnp.zeros_like(d_rows_ref)
    inner_out[...] = jnp.zeros_like(inner_out)
    d_inner_in[...] = jnp.zeros_like(d_inner_in)
    for tree, own in enumerate(spans):
        rows = (row_high[own], row_low[own])
        cots = (cot_high[own], cot_low[own])
        down, up = in_down_ref[tree], out_up_ref[tree]
        inner_in[own] = jnp.concatenate(split(ADAPT_SCALE * dot2(rows, down, NT)), axis=1)
        d_inner_out[own] = jnp.concatenate(split(ADAPT_SCALE * dot2(cots, up, NT)), axis=1)
        inner_in_t[tree] = jnp.concatenate(
            split(ADAPT_SCALE * (dot(down, rows[0], NT) + dot(down, rows[1], NT))), axis=0
        )
        d_inner_out_t[tree] = jnp.concatenate(
            split(ADAPT_SCALE * (dot(up, cots[0], NT) + dot(up, cots[1], NT))), axis=0
        )
    for plane in range(2):
        own_copy(plane).wait()

    def work(step, carry):
        level, plane = chosen(step)
        entry = level * 2 + plane

        @pl.when(step + 1 < len(order))
        def _():
            w_in_copy(step + 1).start()

        @pl.when(step == 2)
        def _():
            core_move(0, 0).wait_recv()
            relay(1)
            relay_plane(0)

        @pl.when(step == 3)
        def _():
            core_move(1, 0).wait_recv()

        @pl.when(step == 4)
        def _():
            core_move(0, 1).wait_recv()

        @pl.when(step == 5)
        def _():
            relay(2)
            relay_plane(1)
            core_move(2, 0).wait_recv()

        @pl.when(step == 6)
        def _():
            core_move(1, 1).wait_recv()

        @pl.when(step == 7)
        def _():
            relay_plane(2)
            core_move(2, 1).wait_recv()

        w_in_copy(step).wait()
        rows = (row_high[...], row_low[...])
        cots = (cot_high[...], cot_low[...])
        w_in = split(w_in_buf[lax.rem(step, 2)])
        w_out = split(shards_ref[level, plane])
        in_up = [in_up_ref[tree, entry] for tree in range(trees)]
        out_down = [out_down_ref[tree, entry] for tree in range(trees)]

        def per_tree(inner, maps):
            return jnp.concatenate(
                [
                    dot(inner[own], jnp.concatenate([maps[tree], maps[tree]], axis=0))
                    for tree, own in enumerate(spans)
                ],
                axis=0,
            )

        pre_act = dot3(rows, w_in) + per_tree(inner_in, in_up)
        root = math.sqrt(2.0 / math.pi)
        squared = pre_act * pre_act
        bend = jnp.tanh(root * (pre_act + 0.044715 * (squared * pre_act)))
        hidden = 0.5 * pre_act * (1.0 + bend)
        slope = 0.5 * (1.0 + bend) + 0.5 * pre_act * (1.0 - bend * bend) * (
            root * (1.0 + 3 * 0.044715 * squared)
        )
        hidden_parts = split(hidden)
        out_ref[...] += dot3(hidden_parts, w_out)
        d_hidden = dot3(cots, w_out, NT) + per_tree(d_inner_out, out_down)
        pre_parts = split(d_hidden * slope)
        d_rows_ref[...] += dot3(pre_parts, w_in, NT)

        for tree, own in enumerate(spans):
            hidden_own = both(hidden_parts, own)
            pre_own = both(pre_parts, own)
            inner_out[own] += dot2(hidden_own, out_down[tree], NT)
            d_inner_in[own] += dot2(pre_own, in_up[tree], NT)
            pair = dot(inner_in_t[tree], pre_own[0])
            g_in_up_ref[tree, entry] = (
                pair[:rank] + pair[rank:] + dot(inner_in_t[tree, :rank], pre_own[1])
            )
            pair = dot(d_inner_out_t[tree], hidden_own[0])
            g_out_down_ref[tree, entry] = (
                pair[:rank] + pair[rank:] + dot(d_inner_out_t[tree, :rank], hidden_own[1])
            )
        return carry

    lax.fori_loop(0, len(order), work, 0)

    for tree, own in enumerate(spans):
        inner = split(ADAPT_SCALE * inner_out[own])
        d_inner = split(ADAPT_SCALE * d_inner_in[own])
        out_ref[own] += dot2(inner, out_up_ref[tree])
        d_rows_ref[own] += dot2(d_inner, in_down_ref[tree])
        g_in_down_ref[tree] = dot3(d_inner, (row_high[own], row_low[own]), TN)
        g_out_up_ref[tree] = dot3(inner, (cot_high[own], cot_low[own]), TN)

    for turn in range(last):
        passing(turn, lambda copy: copy.wait_send())
        plane_move(turn).wait_send()
        core_move(turn, 0).wait_send()
        core_move(turn, 1).wait_send()


def feed_forward(rows, cots, w_in, w_out, near, in_up, out_down, in_down, out_up):
    count, width = rows.shape
    levels, _, units = w_in.shape
    block = units // 2
    trees, entries, rank = in_up.shape[:3]
    dma = pltpu.SemaphoreType.DMA
    here = pl.BlockSpec(memory_space=pltpu.VMEM)
    there = pl.BlockSpec(memory_space=pl.ANY)
    return pl.pallas_call(
        feed_forward_kernel,
        out_shape=[shaped(count, width)] * 2
        + [shaped(*in_up.shape), shaped(*out_down.shape)]
        + [shaped(*in_down.shape), shaped(*out_up.shape)],
        in_specs=[here, here] + [there] * 4 + [here] * 4,
        out_specs=[here] * 6,
        scratch_shapes=[
            pltpu.VMEM((levels, 2, block, width), F32),
            pltpu.VMEM((2, width, block), F32),
        ]
        + [pltpu.VMEM((count, width), BF16)] * 4
        + [pltpu.VMEM((count, 2 * rank), BF16)] * 2
        + [pltpu.VMEM((trees, 2 * rank, count // trees), BF16)] * 2
        + [pltpu.VMEM((count, rank), F32)] * 2
        + [
            dma((2,)),
            dma((2,)),
            dma((levels - 1,)),
            dma((levels,)),
            dma((levels - 1,)),
            dma((levels - 1,)),
            dma((2 * levels - 2,)),
            dma((2 * levels - 2,)),
            dma((2,)),
        ],
        compiler_params=pltpu.CompilerParams(
            vmem_limit_bytes=60 * MIB, collective_id=2, has_side_effects=True
        ),
        cost_estimate=lasting(110),
    )(rows, cots, w_in, w_out, *near, in_up, out_down, in_down, out_up)


def by_distance(z, last, turn):
    orders = [sorted(range(last + 1), key=lambda level: -abs(level - own)) for own in range(last + 1)]
    level = orders[0][turn]
    for own in range(1, last + 1):
        level = jnp.where(z == own, orders[own][turn], level)
    return level


def into_tokens_kernel(
    d_qkv_ref,
    weight_ref,
    tokens_ref,
    d_middle_ref,
    gains_ref,
    down_ref,
    up_ref,
    out_ref,
    own_ref,
    sent_ref,
    across_ref,
    rising_ref,
    falling_ref,
    w_high,
    w_low,
    sent_sem,
    line_sem,
    across_sem,
    rising_sem,
    falling_sem,
):
    z, y = lax.axis_index("z"), lax.axis_index("y")
    last = lax.axis_size("z") - 1
    trees, rank = up_ref.shape[0], up_ref.shape[2]
    seg_len, lanes = d_qkv_ref.shape[3], d_qkv_ref.shape[4]
    met = greet(z, last, [{"y": 1 - y}])
    for kind in range(3):
        where = slice(kind * lanes, (kind + 1) * lanes)
        w_high[:, where], w_low[:, where] = split(weight_ref[kind])
    met()

    def partial(level, side, ref):
        slot = level * 2 + side
        grads = split(
            jnp.concatenate(
                [
                    jnp.concatenate([d_qkv_ref[slot, kind, tree] for kind in range(3)], axis=1)
                    for tree in range(trees)
                ],
                axis=0,
            )
        )
        total = dot3(grads, (w_high[...], w_low[...]), NT)
        for tree, rows in enumerate(tree_rows(trees, seg_len)):
            inner = jnp.concatenate(
                [
                    dot2(
                        both(grads, (rows, slice(kind * lanes, (kind + 1) * lanes))),
                        up_ref[tree, kind],
                        NT,
                    )
                    for kind in range(3)
                ],
                axis=1,
            )
            ref[level, rows] = total[rows] + dot2(split(ADAPT_SCALE * inner), down_ref[tree])

    def move(source, target, level, sem, arrival, device):
        return pltpu.make_async_remote_copy(
            src_ref=source.at[level],
            dst_ref=target.at[level],
            send_sem=sem,
            recv_sem=arrival.at[level],
            device_id=device,
            device_id_type=pl.DeviceIdType.MESH,
        )

    def across(turn, level):
        return move(sent_ref, across_ref, level, sent_sem.at[turn], across_sem, {"y": 1 - y})

    def rising(turn, level):
        return move(own_ref, rising_ref, level, line_sem.at[turn], rising_sem, {"z": z + 1})

    def falling(turn, level):
        return move(own_ref, falling_ref, level, line_sem.at[turn], falling_sem, {"z": z - 1})

    levels = [by_distance(z, last, turn) for turn in range(last + 1)]
    for turn, level in enumerate(levels):
        partial(level, 1 - y, sent_ref)
        across(turn, level).start()
    for level in levels:
        partial(level, y, own_ref)
    for turn, level in enumerate(levels):
        across(turn, level).wait_recv()
        own_ref[level] += across_ref[level]

        @pl.when(jnp.logical_and(level >= z, z > 0))
        def _(level=level):
            rising(0, level).wait_recv()
            own_ref[level] += rising_ref[level]

        @pl.when(jnp.logical_and(level <= z, z < last))
        def _(level=level):
            falling(0, level).wait_recv()
            own_ref[level] += falling_ref[level]

        @pl.when(level > z)
        def _(turn=turn, level=level):
            rising(turn, level).start()

        @pl.when(level < z)
        def _(turn=turn, level=level):
            falling(turn, level).start()

    _, normal, inverse = layer_norm(rows_of(tokens_ref), gains_ref[0:1])
    grad = rows_of(d_middle_ref) + norm_back(normal, inverse, gains_ref[0:1], own_ref[z])
    out_ref[...] = grad.reshape(out_ref.shape)
    for turn, level in enumerate(levels):
        across(turn, level).wait_send()

        @pl.when(level > z)
        def _(turn=turn, level=level):
            rising(turn, level).wait_send()

        @pl.when(level < z)
        def _(turn=turn, level=level):
            falling(turn, level).wait_send()


def into_tokens_call(d_qkv, weight, tokens, d_middle, gains, down, up):
    trees, seg_len, width = tokens.shape
    levels = lax.axis_size("z")
    lanes = weight.shape[2]
    dma = pltpu.SemaphoreType.DMA((levels,))
    here = pl.BlockSpec(memory_space=pltpu.VMEM)
    return pl.pallas_call(
        into_tokens_kernel,
        out_shape=shaped(*tokens.shape),
        in_specs=[here] * 7,
        out_specs=here,
        scratch_shapes=[pltpu.VMEM((levels, trees * seg_len, width), F32)] * 5
        + [pltpu.VMEM((width, 3 * lanes), BF16)] * 2
        + [dma] * 5,
        compiler_params=pltpu.CompilerParams(
            vmem_limit_bytes=56 * MIB, collective_id=1, has_side_effects=True
        ),
        cost_estimate=lasting(110),
    )(d_qkv, weight, tokens, d_middle, gains, down, up)


LATE_DOWN, LATE_UP = (0, 1, 2, 5, 6), (5, 6)
OWN_UP = (0, 1, 2)
EARLY = (3, 4, 7)


def place_kernel(source_ref, parts_ref, down_ref, up_ref, in_down_ref, out_up_ref):
    places = [(down_ref, entry) for entry in LATE_DOWN] + [(up_ref, entry) for entry in LATE_UP]
    places += [(up_ref, entry) for entry in OWN_UP]
    places += [(down_ref, entry) for entry in EARLY] + [(up_ref, entry) for entry in EARLY]
    span = parts_ref.shape[5]
    for owner in range(parts_ref.shape[1]):
        lanes = slice(owner * span, (owner + 1) * span)
        for part, (ref, entry) in enumerate(places):
            ref[0, entry, :, lanes] = parts_ref[0, owner, 0, part]
        in_down_ref[0, :, lanes] = parts_ref[0, owner, 0, len(places)]
        out_up_ref[0, :, lanes] = parts_ref[0, owner, 0, len(places) + 1]


def place_hidden_kernel(source_ref, parts_ref, in_up_ref, out_down_ref):
    for owner in range(parts_ref.shape[1]):
        units = parts_ref.shape[5]
        lanes = slice(owner * units, (owner + 1) * units)
        in_up_ref[0, :, lanes] = parts_ref[0, owner, 0, 0]
        out_down_ref[0, :, lanes] = parts_ref[0, owner, 0, 1]


def place_call(kernel, source, arrays, out_shape):
    def chosen(array):
        groups = array.shape[2]
        return pl.BlockSpec(
            (1, array.shape[1], 1) + array.shape[3:],
            lambda entry, tree: (tree[entry] // groups, 0, tree[entry] % groups, 0, 0, 0),
        )

    return pl.pallas_call(
        kernel,
        out_shape=out_shape,
        grid_spec=pltpu.PrefetchScalarGridSpec(
            num_scalar_prefetch=1,
            grid=(out_shape[0].shape[0],),
            in_specs=[chosen(array) for array in arrays],
            out_specs=[tree_spec(out.shape) for out in out_shape],
        ),
        compiler_params=vmem(48),
        cost_estimate=lasting(9),
    )(source, *arrays)


def my_quarter(shard):
    part = shard.shape[0] // lax.axis_size(COPIES)
    return lax.dynamic_slice_in_dim(shard, lax.axis_index(COPIES) * part, part, 0)


def gather_pair_half(quarter, shape):
    whole = lax.all_gather(quarter, ("z",) + COPIES, axis=0, tiled=True)
    return whole.reshape((-1,) + shape)


def pick(table, adapter_pick):
    return jnp.stack(
        [
            lax.dynamic_index_in_dim(table, adapter_pick[tree], 0, keepdims=False)
            for tree in range(adapter_pick.shape[0])
        ]
    )


def after(array, other):
    return array + 0.0 * other[(0,) * other.ndim]


def swap(array):
    return lax.ppermute(array, "y", SWAP)


def summed_to_owner(parts, axes):
    return jnp.sum(lax.all_to_all(parts, axes, split_axis=0, concat_axis=0, tiled=True), axis=0)


def summed_along_line(parts):
    levels = lax.axis_size("z")
    z = lax.axis_index("z")
    total = lax.dynamic_index_in_dim(parts, z, 0, keepdims=False)
    for other in range(1, levels):
        sent = lax.dynamic_index_in_dim(parts, z ^ other, 0, keepdims=False)
        total = total + lax.ppermute(
            sent, "z", [(level, level ^ other) for level in range(levels)]
        )
    return total


def to_everyone(array):
    everyone = lax.all_gather(array, COPIES + ROWS, axis=0, tiled=False)
    return everyone.reshape((-1, lax.axis_size(ROWS)) + array.shape)


def by_heads(
    tokens,
    encoder,
    cotangent,
    adapter_pick,
    segment_order,
    parents,
    norm_gains,
    w_qkv,
    w_self_out,
    w_cross_q,
    w_cross_kv,
    w_cross_out,
    w_fc_in,
    w_fc_out,
    attn_down,
    attn_up,
    fc_in_down,
    fc_in_up,
    fc_out_down,
    fc_out_up,
):
    trees, seg_len, width = tokens.shape
    slots = lax.axis_size(ROWS)
    copies = lax.axis_size(COPIES)
    adapters, projections, rank = attn_up.shape[:3]
    hidden_units = fc_in_up.shape[2]
    pairs = lax.axis_size("y")
    me, my_y = lax.axis_index(ROWS), lax.axis_index("y")
    lanes = width // slots

    down = pick(attn_down.swapaxes(2, 3), adapter_pick)
    up = pick(attn_up, adapter_pick)
    in_down = pick(fc_in_down.swapaxes(1, 2), adapter_pick)
    out_up = pick(fc_out_up, adapter_pick)

    def half_columns(table):
        picked = pick(table, adapter_pick).reshape(
            trees, rank, slots // pairs, pairs, hidden_units // slots
        )
        half = lax.dynamic_index_in_dim(picked, my_y, 3, keepdims=False)
        return half.reshape(trees, rank, slots, -1).swapaxes(1, 2)

    in_up = half_columns(fc_in_up)
    out_down = half_columns(fc_out_down.swapaxes(1, 2))
    down_qkv = down[:, 0:3].reshape(trees, 3 * rank, width)
    up_own = lax.dynamic_slice_in_dim(up[:, 0:3], me * lanes, lanes, 3)

    shard = jnp.concatenate(
        [
            w.reshape(copies, -1, width)
            for w in (w_cross_kv.T, w_self_out, w_cross_out, w_cross_q.T)
        ],
        axis=1,
    )
    normed_all, inner_all, qkv, qkv_own, packed, context = heads_call(
        segment_order, parents, tokens, norm_gains, w_qkv, shard, down_qkv, up_own
    )
    row = width // (slots * copies)
    self_out_spec = packed_spec(packed, 2 * row, row)
    cross_out_spec = packed_spec(packed, 3 * row, row)
    cross_q_spec = packed_spec(packed, 4 * row, row)

    fc_in_late, qkv = lax.optimization_barrier((my_quarter(w_fc_in), qkv))
    fc_in_half = gather_pair_half(fc_in_late, w_fc_in.shape)
    fc_out_late, context = lax.optimization_barrier((my_quarter(w_fc_out), context))
    levels = range(lax.axis_size("z") - 1)
    fc_out_near = (
        lax.ppermute(fc_out_late, "z", [(level, level + 1) for level in levels]),
        lax.ppermute(fc_out_late, "z", [(level + 1, level) for level in levels]),
    )

    cotangent_other = swap(after(cotangent, context))
    memory = memory_call(encoder, packed, down, up)
    middle, cross_queries = rows_call(
        after_self_kernel,
        (context, tokens, norm_gains, packed, packed, down, up),
        (None, None, None, self_out_spec, cross_q_spec, None, None),
        [shaped(*tokens.shape)] * 2,
    )
    (cross_context,) = cross_call(
        cross_forward_kernel, cross_queries, memory, (), 0, (cotangent_other,)
    )
    after_cross, normed_three = rows_call(
        after_cross_kernel,
        (cross_context, middle, norm_gains, packed, down, up),
        (None, None, None, cross_out_spec, None, None),
        [shaped(*tokens.shape)] * 2,
    )

    all_picks = lax.all_gather(adapter_pick, COPIES, axis=0, tiled=True)
    entry = lax.broadcasted_iota(jnp.int32, (adapters, 1), 0)
    tree_index = lax.broadcasted_iota(jnp.int32, (1, all_picks.shape[0]), 1)
    source = jnp.sum(jnp.where(entry == all_picks[None, :], tree_index, 0), axis=1)
    def paired(own_rows, other_rows):
        return jnp.stack([own_rows, other_rows], axis=1).reshape(-1, width)

    out_part, d_rows_part, g_in_up, g_out_down, g_in_down, g_out_up = feed_forward(
        paired(normed_three, swap(normed_three)),
        paired(cotangent, cotangent_other),
        fc_in_half,
        w_fc_out,
        fc_out_near,
        in_up,
        out_down,
        in_down,
        out_up,
    )
    d_rows_part = d_rows_part.reshape(trees, 2, seg_len, width)
    out_part = out_part.reshape(trees, 2, seg_len, width)

    ahead = pl.BlockSpec(memory_space=pl.ANY)
    pair_maps = [shaped(trees, 1, rank, width)] * 2
    d_after, d_cross_ctx, g_down_seven, g_up_seven, hidden_sums = rows_call(
        into_cross_kernel,
        (
            d_rows_part,
            after_cross,
            cotangent,
            cross_context,
            norm_gains,
            packed,
            down,
            up,
            g_in_up,
            g_out_down,
        ),
        (None,) * 5 + (cross_out_spec,) + (None,) * 4,
        [shaped(*tokens.shape)] * 2
        + pair_maps
        + [shaped(trees, 2, rank, hidden_units // slots)],
        [
            pltpu.VMEM(tokens.shape, F32),
            pltpu.VMEM((len(levels), 2, trees, 2) + g_in_up.shape[2:], F32),
            pltpu.SemaphoreType.DMA((2,)),
            pltpu.SemaphoreType.DMA((len(levels), 2)),
            pltpu.SemaphoreType.DMA((len(levels), 2)),
        ],
        pltpu.CompilerParams(
            vmem_limit_bytes=56 * MIB, collective_id=3, has_side_effects=True
        ),
    )
    def columns(parts):
        stack = jnp.concatenate(parts, axis=1)
        return stack.reshape(stack.shape[:3] + (slots, lanes)).transpose(3, 0, 1, 2, 4)

    d_cross_q, d_cross_k, d_cross_v = cross_call(
        cross_backward_kernel, cross_queries, memory, (d_cross_ctx,), 2
    )
    out_other = swap(after(out_part[:, 1], d_cross_q))
    hidden_all = to_everyone(hidden_sums)
    layer_out = after_cross + out_part[:, 0] + out_other
    d_middle, d_context, g_down_mid, g_up_mid = rows_call(
        into_self_kernel,
        (d_cross_q, d_after, middle, context, norm_gains, packed, packed, down, up),
        (None,) * 5 + (cross_q_spec, self_out_spec, None, None),
        [shaped(*tokens.shape), shaped(slots, trees, seg_len, lanes)]
        + [shaped(trees, 2, rank, width)] * 2,
    )
    d_own_context = lax.all_to_all(d_context, ROWS, split_axis=0, concat_axis=0, tiled=True)
    d_context, d_cross_k = lax.optimization_barrier((d_context, d_cross_k))
    d_encoder, g_down_memory, g_up_memory = memory_back_call(
        encoder, d_cross_k, d_cross_v, packed, down, up
    )
    enc_rows = encoder.shape[1] // slots
    sides = d_encoder.reshape(trees, slots // pairs, pairs, enc_rows, width).transpose(2, 1, 0, 3, 4)
    other_side = lax.dynamic_index_in_dim(sides, 1 - my_y, 0, keepdims=False)
    own_side = lax.dynamic_index_in_dim(sides, my_y, 0, keepdims=False)
    enc_side = own_side + swap(other_side)
    early = summed_to_owner(
        columns(
            [
                g_down_mid,
                g_down_seven,
                g_up_mid,
                g_up_seven,
                g_in_down[:, None],
                g_out_up[:, None],
            ]
        ),
        ROWS,
    )

    grad_in_up, grad_out_down = place_call(
        place_hidden_kernel, source, (hidden_all,), [shaped(adapters, rank, hidden_units)] * 2
    )

    normed_shape = (slots, trees, seg_len, width)
    d_qkv, g_down_part, g_up_qkv = self_call(
        self_backward_kernel,
        segment_order,
        parents,
        (
            qkv,
            d_own_context,
            normed_all.reshape(normed_shape),
            inner_all,
            up_own,
            grad_in_up,
            out_other,
        ),
        [
            slots_spec(qkv.shape),
            slots_spec(d_own_context.shape),
            slots_spec(normed_shape),
            slots_spec(inner_all.shape),
            tree_spec(up_own.shape),
            ahead,
            ahead,
        ],
        [
            shaped(*qkv.shape),
            shaped(trees, 3, rank, width),
            shaped(trees, 3, rank, lanes),
        ],
        [
            slots_spec(qkv.shape),
            tree_spec((trees, 3, rank, width)),
            tree_spec((trees, 3, rank, lanes)),
        ],
        28,
    )
    late = summed_to_owner(columns([g_down_part, g_down_memory, g_up_memory]), ROWS)
    enc_side, late = lax.optimization_barrier((enc_side, late))
    grad_encoder = summed_along_line(enc_side)
    attention_all = to_everyone(jnp.concatenate([late, g_up_qkv, early], axis=1))
    grad_tokens = into_tokens_call(
        d_qkv, qkv_own, tokens, d_middle, norm_gains, down_qkv, up_own
    )
    wide = shaped(adapters, projections, rank, width)
    narrow = shaped(adapters, rank, width)
    grad_down, grad_up, grad_in_down, grad_out_up = place_call(
        place_kernel, source, (attention_all,), [wide, wide, narrow, narrow]
    )
    return (
        layer_out,
        grad_tokens,
        grad_encoder,
        grad_down.swapaxes(2, 3),
        grad_up,
        grad_in_down.swapaxes(1, 2),
        grad_in_up,
        grad_out_down.swapaxes(1, 2),
        grad_out_up,
    )


def placements(rows, copies):
    spread = P(copies, rows, None)
    ins = (
        spread,
        P(copies, None, None),
        spread,
        P(copies),
        P(copies, None),
        P(copies, None),
        P(),
        P(None, rows),
        P(rows, None),
        P(None, rows),
        P(None, rows),
        P(rows, None),
        P(None, rows),
        P(rows, None),
    ) + (P(),) * 6
    return ins, (spread,) * 3 + (P(),) * 6


def solution(mesh):
    copies, rows = mesh.shape["dp"], mesh.shape["seq"]
    general = jax.shard_map(
        shards,
        mesh=mesh,
        in_specs=placements("seq", "dp")[0],
        out_specs=placements("seq", "dp")[1],
        check_vma=False,
    )
    if rows != 8 or copies % 2:
        return general
    fine = jax.sharding.Mesh(
        mesh.devices.reshape(copies // 2, 2, rows // 2, 2), ("x", "c", "z", "y")
    )
    ins, outs = placements(ROWS, COPIES)
    special = jax.shard_map(by_heads, mesh=fine, in_specs=ins, out_specs=outs, check_vma=False)

    def step(*arrays):
        one_each = arrays[0].shape[0] == arrays[14].shape[0]
        return (special if one_each else general)(*arrays)

    return step
```

```python
import functools
import math

import jax
import jax.numpy as jnp
from jax import lax
from jax.experimental import pallas as pl
from jax.experimental.pallas import tpu as pltpu
from jax.sharding import PartitionSpec as P

HEADS = 16
HD = 64


PRECISE = lax.Precision.HIGHEST
ADAPT_SCALE = 2.0
NORM_EPS = 1e-05
MASK_FILL = -1e30


def matmul(left_side, right_side):
    return jnp.dot(left_side, right_side, precision=PRECISE, preferred_element_type=jnp.float32)


def product(formula, first_operand, second_operand):
    return jnp.einsum(
        formula,
        first_operand,
        second_operand,
        precision=PRECISE,
        preferred_element_type=jnp.float32,
    )


def reach_table(segment_order, parents):
    segment_count = parents.shape[-1]
    column = lax.broadcasted_iota(jnp.int32, (segment_count, segment_count), 1)
    identity = (
        lax.broadcasted_iota(jnp.int32, (segment_count, segment_count), 0) == column
    ).astype(jnp.int32)
    parent_hot = (parents[..., :, None] == column).astype(jnp.int32)

    def extend(sweep_index, reach_rows):
        return jnp.minimum(identity + jnp.einsum("gab,gbc->gac", parent_hot, reach_rows), 1)

    initial = jnp.broadcast_to(identity, parent_hot.shape)
    reach_rows = lax.fori_loop(0, segment_count, extend, initial)
    order_hot = (segment_order[..., :, None] == column).astype(jnp.int32)
    return jnp.einsum("gsa,gab,gtb->gst", order_hot, reach_rows, order_hot)


def layer_norm(values, gain_row):
    center = values - jnp.mean(values, -1, keepdims=True)
    inverse = lax.rsqrt(jnp.mean(center * center, -1, keepdims=True) + NORM_EPS)
    normal = center * inverse
    return (normal * gain_row, normal, inverse)


def norm_back(normal, inverse, gain_row, grads):
    scaled = grads * gain_row
    mean_one = jnp.mean(scaled, -1, keepdims=True)
    mean_two = jnp.mean(scaled * normal, -1, keepdims=True)
    return inverse * (scaled - mean_one - normal * mean_two)


def gelu_back(pre_act, d_hidden):

    def activate(values):
        return jax.nn.gelu(values, approximate=True)

    return jax.vjp(activate, pre_act)[1](d_hidden)[0]


def cols_forward(inputs, shard):
    flat_rows = inputs.reshape(-1, inputs.shape[-1])
    result = matmul(flat_rows, lax.all_gather(shard, "seq", axis=1, tiled=True))
    return result.reshape(inputs.shape[:-1] + (result.shape[-1],))


def cols_back(grads, shard):
    flat_grads = grads.reshape(-1, grads.shape[-1])
    result = matmul(flat_grads, lax.all_gather(shard, "seq", axis=1, tiled=True).T)
    return result.reshape(grads.shape[:-1] + (shard.shape[0],))


def rows_forward(inputs, shard):
    flat_rows = inputs.reshape(-1, inputs.shape[-1])
    result = matmul(flat_rows, lax.all_gather(shard, "seq", axis=0, tiled=True))
    return result.reshape(inputs.shape[:-1] + (shard.shape[1],))


def rows_back(grads, shard):
    flat_grads = grads.reshape(-1, grads.shape[-1])
    result = matmul(flat_grads, lax.all_gather(shard, "seq", axis=0, tiled=True).T)
    return result.reshape(grads.shape[:-1] + (result.shape[-1],))


def adapter_apply(inputs, down_map, up_map):
    inner = product("gsd,gdr->gsr", inputs, down_map)
    return (ADAPT_SCALE * product("gsr,gro->gso", inner, up_map), inner)


def adapter_back(inputs, inner, down_map, up_map, grads):
    d_inner = ADAPT_SCALE * product("gso,gro->gsr", grads, up_map)
    grad_up = ADAPT_SCALE * product("gsr,gso->gro", inner, grads)
    grad_down = product("gsd,gsr->gdr", inputs, d_inner)
    return (product("gsr,gdr->gsd", d_inner, down_map), grad_down, grad_up)


def key_mask(my_reach, my_slot, query_index, first_key, key_count, seg_len):
    slot_count = my_reach.shape[1]
    key_index = first_key + lax.broadcasted_iota(jnp.int32, (1, key_count), 1)
    key_slot = key_index // seg_len
    slot_hot = (key_slot[0][:, None] == lax.broadcasted_iota(jnp.int32, (1, slot_count), 1)).astype(
        jnp.int32
    )
    key_allowed = jnp.einsum("gc,nc->gn", my_reach, slot_hot)
    causal_ok = (key_slot != my_slot) | (key_index <= query_index)
    allowed = (key_allowed[:, None, :] > 0) & causal_ok[None]
    return (allowed, jnp.any(key_allowed > 0))


def self_forward(queries, key_rows, value_rows, my_reach, my_slot):
    groups, seg_len, width = queries.shape
    query_heads = queries.reshape(groups, seg_len, HEADS, HD) * HD ** (-0.5)
    query_index = my_slot * seg_len + lax.broadcasted_iota(jnp.int32, (seg_len, 1), 0)
    start_state = (
        jnp.full((groups, HEADS, seg_len), MASK_FILL, jnp.float32),
        jnp.zeros((groups, HEADS, seg_len), jnp.float32),
        jnp.zeros((groups, HEADS, seg_len, HD), jnp.float32),
    )
    key_part = lax.all_gather(key_rows, "seq", axis=1, tiled=True)
    value_part = lax.all_gather(value_rows, "seq", axis=1, tiled=True)
    key_count = key_part.shape[1]
    allowed, any_allowed = key_mask(
        my_reach, my_slot, query_index, jnp.int32(0), key_count, seg_len
    )

    def attend(state):
        peak, mass, accum = state
        key_heads = key_part.reshape(groups, key_count, HEADS, HD)
        value_heads = value_part.reshape(groups, key_count, HEADS, HD)
        scores = product("gshd,gnhd->ghsn", query_heads, key_heads)
        masked = jnp.where(allowed[:, None], scores, MASK_FILL)
        new_peak = jnp.maximum(peak, jnp.max(masked, -1))
        probs = jnp.where(allowed[:, None], jnp.exp(masked - new_peak[..., None]), 0.0)
        mass = jnp.sum(probs, -1)
        accum = product("ghsn,gnhd->ghsd", probs, value_heads)
        return (new_peak, mass, accum)

    peak, mass, accum = lax.cond(any_allowed, attend, lambda state: state, start_state)
    context = (accum / mass[..., None]).transpose(0, 2, 1, 3).reshape(groups, seg_len, width)
    return (context, peak + jnp.log(mass))


def self_backward(queries, key_all, value_all, log_mass, delta, d_context, my_reach, my_slot):
    groups, seg_len, width = queries.shape
    scale = HD ** (-0.5)
    query_heads = queries.reshape(groups, seg_len, HEADS, HD) * scale
    out_heads = d_context.reshape(groups, seg_len, HEADS, HD)
    query_index = my_slot * seg_len + lax.broadcasted_iota(jnp.int32, (seg_len, 1), 0)
    total_keys = key_all.shape[1]
    block_keys = seg_len * math.gcd(total_keys // seg_len, max(1, 512 // seg_len))
    firsts = jnp.arange(total_keys // block_keys, dtype=jnp.int32) * block_keys

    def block_step(state, first_key):
        allowed, any_allowed = key_mask(
            my_reach, my_slot, query_index, first_key, block_keys, seg_len
        )

        def gradients(inner_state):
            key_heads = lax.dynamic_slice_in_dim(key_all, first_key, block_keys, 1).reshape(
                groups, block_keys, HEADS, HD
            )
            value_heads = lax.dynamic_slice_in_dim(value_all, first_key, block_keys, 1).reshape(
                groups, block_keys, HEADS, HD
            )
            scores = product("gshd,gnhd->ghsn", query_heads, key_heads)
            masked = jnp.where(allowed[:, None], scores, MASK_FILL)
            probs = jnp.where(allowed[:, None], jnp.exp(masked - log_mass[..., None]), 0.0)
            d_probs = product("gshd,gnhd->ghsn", out_heads, value_heads)
            d_scores = probs * (d_probs - delta[..., None])
            d_query = inner_state[0] + product("ghsn,gnhd->gshd", d_scores, key_heads)
            d_value_part = product("ghsn,gshd->gnhd", probs, out_heads)
            d_key_part = product("ghsn,gshd->gnhd", d_scores, query_heads)
            d_key_all = lax.dynamic_update_slice_in_dim(
                inner_state[1], d_key_part.reshape(groups, block_keys, width), first_key, 1
            )
            d_value_all = lax.dynamic_update_slice_in_dim(
                inner_state[2], d_value_part.reshape(groups, block_keys, width), first_key, 1
            )
            return (d_query, d_key_all, d_value_all)

        return (lax.cond(any_allowed, gradients, lambda inner_state: inner_state, state), None)

    zero_query = jnp.zeros((groups, seg_len, HEADS, HD), jnp.float32)
    initial = (zero_query, jnp.zeros_like(key_all), jnp.zeros_like(value_all))
    final_state, unused = lax.scan(block_step, initial, firsts)
    d_query = final_state[0].reshape(groups, seg_len, width) * scale
    return (d_query, final_state[1], final_state[2])


def cross_forward(queries, key_rows, value_rows):
    groups, seg_len, width = queries.shape
    enc_rows = key_rows.shape[1]
    query_heads = queries.reshape(groups, seg_len, HEADS, HD) * HD ** (-0.5)
    scores = product("gshd,gehd->ghse", query_heads, key_rows.reshape(groups, enc_rows, HEADS, HD))
    probs = jax.nn.softmax(scores, axis=-1)
    context = product("ghse,gehd->gshd", probs, value_rows.reshape(groups, enc_rows, HEADS, HD))
    return (context.reshape(groups, seg_len, width), probs)


def cross_backward(queries, key_rows, value_rows, probs, d_context):
    groups, seg_len, width = queries.shape
    enc_rows = key_rows.shape[1]
    scale = HD ** (-0.5)
    query_heads = queries.reshape(groups, seg_len, HEADS, HD) * scale
    key_heads = key_rows.reshape(groups, enc_rows, HEADS, HD)
    value_heads = value_rows.reshape(groups, enc_rows, HEADS, HD)
    out_heads = d_context.reshape(groups, seg_len, HEADS, HD)
    d_values = product("ghse,gshd->gehd", probs, out_heads)
    d_probs = product("gshd,gehd->ghse", out_heads, value_heads)
    d_scores = probs * (d_probs - jnp.sum(probs * d_probs, -1, keepdims=True))
    d_queries = product("ghse,gehd->gshd", d_scores, key_heads) * scale
    d_keys = product("ghse,gshd->gehd", d_scores, query_heads)
    return (
        d_queries.reshape(groups, seg_len, width),
        d_keys.reshape(groups, enc_rows, width),
        d_values.reshape(groups, enc_rows, width),
    )


def shards(
    tokens,
    encoder,
    cotangent,
    adapter_pick,
    segment_order,
    parents,
    norm_gains,
    w_qkv,
    w_self_out,
    w_cross_q,
    w_cross_kv,
    w_cross_out,
    w_fc_in,
    w_fc_out,
    attn_down,
    attn_up,
    fc_in_down,
    fc_in_up,
    fc_out_down,
    fc_out_up,
):
    groups, seg_len, width = tokens.shape
    enc_rows = encoder.shape[1]
    my_slot = lax.axis_index("seq")
    reach_rows = reach_table(segment_order, parents)
    my_reach = lax.dynamic_index_in_dim(reach_rows, my_slot, 1, keepdims=False)
    adapter_count = attn_down.shape[0]
    chosen = (
        adapter_pick[:, None] == lax.broadcasted_iota(jnp.int32, (1, adapter_count), 1)
    ).astype(jnp.float32)
    chosen_low = chosen.astype(jnp.bfloat16)

    def select(adapter_table):
        return jnp.einsum(
            "ga,a...->g...", chosen_low, adapter_table, preferred_element_type=jnp.float32
        )

    sel_down = select(attn_down)
    sel_up = select(attn_up)
    in_down = select(fc_in_down)
    in_up = select(fc_in_up)
    out_down = select(fc_out_down)
    out_up = select(fc_out_up)
    normed_one, normal_one, inverse_one = layer_norm(tokens, norm_gains[0])
    inner_qkv = product("gsd,gpdr->gspr", normed_one, sel_down[:, 0:3])
    stacked = cols_forward(normed_one, w_qkv) + ADAPT_SCALE * product(
        "gspr,gpro->gspo", inner_qkv, sel_up[:, 0:3]
    ).reshape(groups, seg_len, 3 * width)
    queries = stacked[..., :width]
    key_rows = stacked[..., width : 2 * width]
    value_rows = stacked[..., 2 * width :]
    context, log_mass = self_forward(queries, key_rows, value_rows, my_reach, my_slot)
    self_term, inner_self = adapter_apply(context, sel_down[:, 3], sel_up[:, 3])
    middle = tokens + rows_forward(context, w_self_out) + self_term
    normed_two, normal_two, inverse_two = layer_norm(middle, norm_gains[1])
    query_term, inner_cross_q = adapter_apply(normed_two, sel_down[:, 4], sel_up[:, 4])
    cross_queries = cols_forward(normed_two, w_cross_q) + query_term
    inner_memory = product("ged,gpdr->gepr", encoder, sel_down[:, 5:7])
    memory = cols_forward(encoder, w_cross_kv) + ADAPT_SCALE * product(
        "gepr,gpro->gepo", inner_memory, sel_up[:, 5:7]
    ).reshape(groups, enc_rows, 2 * width)
    cross_keys = memory[..., :width]
    cross_values = memory[..., width:]
    cross_context, cross_probs = cross_forward(cross_queries, cross_keys, cross_values)
    cross_term, inner_cross_out = adapter_apply(cross_context, sel_down[:, 7], sel_up[:, 7])
    after_cross = middle + rows_forward(cross_context, w_cross_out) + cross_term
    normed_three, normal_three, inverse_three = layer_norm(after_cross, norm_gains[2])
    inner_in = product("gsd,gdr->gsr", normed_three, in_down)
    pre_act = cols_forward(normed_three, w_fc_in) + ADAPT_SCALE * product(
        "gsr,grf->gsf", inner_in, in_up
    )
    hidden = jax.nn.gelu(pre_act, approximate=True)
    inner_out = product("gsf,gfr->gsr", hidden, out_down)
    mlp_out = rows_forward(hidden, w_fc_out) + ADAPT_SCALE * product(
        "gsr,grd->gsd", inner_out, out_up
    )
    layer_out = after_cross + mlp_out
    d_inner_out = ADAPT_SCALE * product("gsd,grd->gsr", cotangent, out_up)
    grad_out_up_tree = ADAPT_SCALE * product("gsr,gsd->grd", inner_out, cotangent)
    d_hidden = rows_back(cotangent, w_fc_out) + product("gsr,gfr->gsf", d_inner_out, out_down)
    grad_out_down_tree = product("gsf,gsr->gfr", hidden, d_inner_out)
    d_pre = gelu_back(pre_act, d_hidden)
    d_inner_in = ADAPT_SCALE * product("gsf,grf->gsr", d_pre, in_up)
    grad_in_up_tree = ADAPT_SCALE * product("gsr,gsf->grf", inner_in, d_pre)
    d_normed_three = cols_back(d_pre, w_fc_in) + product("gsr,gdr->gsd", d_inner_in, in_down)
    grad_in_down_tree = product("gsd,gsr->gdr", normed_three, d_inner_in)
    d_after = cotangent + norm_back(normal_three, inverse_three, norm_gains[2], d_normed_three)
    d_cross_ctx, grad_down_seven, grad_up_seven = adapter_back(
        cross_context, inner_cross_out, sel_down[:, 7], sel_up[:, 7], d_after
    )
    d_cross_ctx = d_cross_ctx + rows_back(d_after, w_cross_out)
    d_cross_q, d_cross_k, d_cross_v = cross_backward(
        cross_queries, cross_keys, cross_values, cross_probs, d_cross_ctx
    )
    d_normed_two, grad_down_four, grad_up_four = adapter_back(
        normed_two, inner_cross_q, sel_down[:, 4], sel_up[:, 4], d_cross_q
    )
    d_normed_two = d_normed_two + cols_back(d_cross_q, w_cross_q)
    d_middle = d_after + norm_back(normal_two, inverse_two, norm_gains[1], d_normed_two)
    d_memory = jnp.concatenate([d_cross_k, d_cross_v], axis=-1)
    d_memory_split = d_memory.reshape(groups, enc_rows, 2, width)
    d_inner_memory = ADAPT_SCALE * product("gepo,gpro->gepr", d_memory_split, sel_up[:, 5:7])
    grad_up_memory = ADAPT_SCALE * product("gepr,gepo->gpro", inner_memory, d_memory_split)
    grad_down_memory = product("ged,gepr->gpdr", encoder, d_inner_memory)
    d_encoder_local = cols_back(d_memory, w_cross_kv) + product(
        "gepr,gpdr->ged", d_inner_memory, sel_down[:, 5:7]
    )
    grad_encoder = lax.psum_scatter(d_encoder_local, "seq", scatter_dimension=1, tiled=True)
    d_context, grad_down_three, grad_up_three = adapter_back(
        context, inner_self, sel_down[:, 3], sel_up[:, 3], d_middle
    )
    d_context = d_context + rows_back(d_middle, w_self_out)
    delta = jnp.sum(
        d_context.reshape(groups, seg_len, HEADS, HD) * context.reshape(groups, seg_len, HEADS, HD),
        -1,
    ).transpose(0, 2, 1)
    key_all, value_all = (
        lax.all_gather(key_rows, "seq", axis=1, tiled=True),
        lax.all_gather(value_rows, "seq", axis=1, tiled=True),
    )
    d_queries, d_key_all, d_value_all = self_backward(
        queries, key_all, value_all, log_mass, delta, d_context, my_reach, my_slot
    )
    d_keys, d_values = (
        lax.psum_scatter(d_key_all, "seq", scatter_dimension=1, tiled=True),
        lax.psum_scatter(d_value_all, "seq", scatter_dimension=1, tiled=True),
    )
    d_stacked = jnp.concatenate([d_queries, d_keys, d_values], axis=-1)
    d_split = d_stacked.reshape(groups, seg_len, 3, width)
    d_inner_qkv = ADAPT_SCALE * product("gspo,gpro->gspr", d_split, sel_up[:, 0:3])
    grad_up_qkv = ADAPT_SCALE * product("gspr,gspo->gpro", inner_qkv, d_split)
    grad_down_qkv = product("gsd,gspr->gpdr", normed_one, d_inner_qkv)
    d_normed_one = cols_back(d_stacked, w_qkv) + product(
        "gspr,gpdr->gsd", d_inner_qkv, sel_down[:, 0:3]
    )
    grad_tokens = d_middle + norm_back(normal_one, inverse_one, norm_gains[0], d_normed_one)
    down_stack = jnp.concatenate(
        [
            grad_down_qkv,
            grad_down_three[:, None],
            grad_down_four[:, None],
            grad_down_memory,
            grad_down_seven[:, None],
        ],
        axis=1,
    )
    up_stack = jnp.concatenate(
        [
            grad_up_qkv,
            grad_up_three[:, None],
            grad_up_four[:, None],
            grad_up_memory,
            grad_up_seven[:, None],
        ],
        axis=1,
    )
    tree_parts = (
        down_stack,
        up_stack,
        grad_in_down_tree,
        grad_in_up_tree,
        grad_out_down_tree,
        grad_out_up_tree,
    )
    shapes = (
        attn_down.shape,
        attn_up.shape,
        fc_in_down.shape,
        fc_in_up.shape,
        fc_out_down.shape,
        fc_out_up.shape,
    )
    local_sums = tuple(
        (product("ga,gx->ax", chosen, part.reshape(groups, -1)).reshape(-1) for part in tree_parts)
    )
    owned = lax.psum_scatter(local_sums, ("dp", "seq"), scatter_dimension=0, tiled=True)
    full_sums = lax.all_gather(owned, ("dp", "seq"), axis=0, tiled=True)
    results = [summed.reshape(shape) for summed, shape in zip(full_sums, shapes)]
    return (
        layer_out,
        grad_tokens,
        grad_encoder,
        results[0],
        results[1],
        results[2],
        results[3],
        results[4],
        results[5],
    )


ROWS = ("z", "y")
COPIES = ("x", "c")
EVERY = ROWS + COPIES
F32 = jnp.float32
BF16 = jnp.bfloat16
MIB = 1 << 20
SWAP = [(0, 1), (1, 0)]
NN = (((1,), (0,)), ((), ()))
NT = (((1,), (1,)), ((), ()))
TN = (((0,), (0,)), ((), ()))


def split(values):
    high = values.astype(BF16)
    return high, (values - high.astype(F32)).astype(BF16)


def dot(left, right, dims=NN):
    return lax.dot_general(left, right, dims, preferred_element_type=F32)


def dot3(left, right, dims=NN):
    (left_high, left_low), (right_high, right_low) = left, right
    return (
        dot(left_high, right_high, dims)
        + dot(left_high, right_low, dims)
        + dot(left_low, right_high, dims)
    )


def dot2(left, right, dims=NN):
    return dot(left[0], right, dims) + dot(left[1], right, dims)


def adapted(rows, down, up):
    inner = dot2(rows, down, NT)
    return dot2(split(ADAPT_SCALE * inner), up), inner


def adapted_back(rows, grads, down, up):
    inner = split(ADAPT_SCALE * dot2(rows, down, NT))
    d_inner = split(ADAPT_SCALE * dot2(grads, up, NT))
    return dot2(d_inner, down), dot3(d_inner, rows, TN), dot3(inner, grads, TN)


def both(parts, where):
    return parts[0][where], parts[1][where]


def vmem(limit):
    return pltpu.CompilerParams(vmem_limit_bytes=limit * MIB)


def lasting(micros):
    return pl.CostEstimate(
        flops=int(micros * 1e9), bytes_accessed=int(micros * 3e6), transcendentals=0
    )


def shaped(*shape):
    return jax.ShapeDtypeStruct(shape, F32)


def whole_spec(shape):
    return pl.BlockSpec(shape, lambda *_: (0,) * len(shape))


def signal(target):
    pl.semaphore_signal(
        pltpu.get_barrier_semaphore(), 1, device_id=target, device_id_type=pl.DeviceIdType.MESH
    )


def greet(z, last, partners, more=0):
    for partner in partners:
        signal(partner)

    @pl.when(z > 0)
    def _():
        signal({"z": z - 1})

    @pl.when(z < last)
    def _():
        signal({"z": z + 1})

    def met():
        lines = (z > 0).astype(jnp.int32) + (z < last).astype(jnp.int32)
        pl.semaphore_wait(pltpu.get_barrier_semaphore(), len(partners) + lines + more)

    return met


def remote(source, target, sem, arrival, device):
    return pltpu.make_async_remote_copy(
        src_ref=source,
        dst_ref=target,
        send_sem=sem,
        recv_sem=arrival,
        device_id=device,
        device_id_type=pl.DeviceIdType.MESH,
    )


def start(copy):
    copy.start()


def wait_send(copy):
    copy.wait_send()


def heads_kernel(
    order_ref,
    parents_ref,
    tokens_ref,
    gains_ref,
    weight_ref,
    shard_ref,
    down_ref,
    up_ref,
    normed_ref,
    inner_ref,
    qkv_ref,
    own_weight_ref,
    packed_ref,
    context_ref,
    own_context_ref,
    rows_ref,
    blocks_ref,
    w_high,
    w_low,
    keep_sem,
    block_sem,
    block_here_sem,
    block_core_sem,
    block_core_here_sem,
    here_sem,
    across_sem,
    over_first_sem,
    over_second_sem,
    line_sem,
    line_first_sem,
    line_second_sem,
    shard_here_sem,
    plane_sem,
    plane_here_sem,
    core_sem,
    core_here_sem,
    context_sem,
    context_here_sem,
):
    x, c = lax.axis_index("x"), lax.axis_index("c")
    z, y = lax.axis_index("z"), lax.axis_index("y")
    last = lax.axis_size("z") - 1
    trees, seg_len, width = tokens_ref.shape
    lanes = weight_ref.shape[1] // 3
    rank = up_ref.shape[2]
    slots = rows_ref.shape[0]
    mine, facing = 2 * x + c, 2 * (1 - x) + c

    def place(level, side):
        return level * 2 + side

    own = place(z, y)

    half = pl.ds(pl.multiple_of(c * (width // 2), width // 2), width // 2)

    def block_move(i):
        block = 3 * own + i
        target, kind = block % slots, block // slots
        source = weight_ref.at[half, i * lanes : (i + 1) * lanes]

        def sent():
            return remote(
                source,
                blocks_ref.at[kind, half],
                block_sem.at[i],
                block_here_sem.at[kind],
                {"z": target // 2, "y": target % 2},
            )

        def kept():
            return pltpu.make_async_copy(
                source, blocks_ref.at[kind, half], block_here_sem.at[kind]
            )

        return target, sent, kept

    def block_across(kind):
        block = blocks_ref.at[kind, half]
        return remote(
            block, block, block_core_sem.at[kind], block_core_here_sem.at[kind], {"c": 1 - c}
        )

    cut = shard_ref.shape[1] * 7 // 80 * 8
    spans = (slice(0, cut), slice(cut, shard_ref.shape[1]))

    def rows_move(slot, sem, device):
        return remote(rows_ref.at[slot], rows_ref.at[slot], sem, here_sem.at[slot], device)

    def shard_move(part, slot, sem, device):
        piece = packed_ref.at[slot, mine, spans[part]]
        source = shard_ref.at[mine, spans[part]] if slot is own else piece
        return remote(source, piece, sem, shard_here_sem.at[part, slot], device)

    first = functools.partial(shard_move, 0)
    second = functools.partial(shard_move, 1)

    def along(move, sems, slot, level, action):
        @pl.when(jnp.logical_and(level <= z, z < last))
        def _():
            action(move(slot, sems.at[0, slot], {"z": z + 1}))

        @pl.when(jnp.logical_and(level >= z, z > 0))
        def _():
            action(move(slot, sems.at[1, slot], {"z": z - 1}))

    def over(move, sems, slot, action):
        action(move(slot, sems.at[slot], {"y": 1 - y}))

    def beside(level):
        return own if level is z else place(level, y)

    def plane_move(part, slot):
        piece = packed_ref.at[slot, mine, spans[part]]
        return remote(
            piece, piece, plane_sem.at[part, slot], plane_here_sem.at[part, slot], {"x": 1 - x}
        )

    def core_move(part, slot, kind):
        piece = packed_ref.at[slot, facing if kind else mine, spans[part]]
        index = 2 * part + kind
        return remote(
            piece, piece, core_sem.at[index, slot], core_here_sem.at[index, slot], {"c": 1 - c}
        )

    def levels_at(hop, action):
        if hop == 0:
            action(z)
            return
        for level in (z - hop, z + hop):

            @pl.when(jnp.logical_and(level >= 0, level <= last))
            def _(level=level):
                action(level)

    def peer(step):
        target = (own + step) % slots
        return target, {"z": target // 2, "y": target % 2}

    for step in range(1, slots):
        signal(peer(step)[1])
    signal({"x": 1 - x})
    signal({"c": 1 - c})
    for tree in range(trees):
        normed = layer_norm(tokens_ref[tree], gains_ref[0:1])[0]
        rows_ref[own, tree * seg_len : (tree + 1) * seg_len] = normed
    pl.semaphore_wait(pltpu.get_barrier_semaphore(), slots + 1)
    along(rows_move, line_sem, own, z, start)
    over(rows_move, across_sem, own, start)
    for i in range(3):
        target, sent, kept = block_move(i)

        @pl.when(target != own)
        def _(sent=sent):
            sent().start()

        @pl.when(target == own)
        def _(kept=kept):
            kept().start()

    def start_shards():
        over(second, over_second_sem, own, start)
        along(first, line_first_sem, own, z, start)
        over(first, over_first_sem, own, start)
        along(second, line_second_sem, own, z, start)

    def keep(slot):
        return pltpu.make_async_copy(rows_ref.at[slot], normed_ref.at[slot], keep_sem.at[slot])

    def keep_shard():
        return pltpu.make_async_copy(shard_ref, packed_ref.at[own], keep_sem.at[slots])

    def keep_blocks():
        return pltpu.make_async_copy(blocks_ref, own_weight_ref, keep_sem.at[slots + 1])

    keep_shard().start()

    def take_blocks():
        for kind in range(3):
            block = blocks_ref.at[kind, half]
            pltpu.make_async_copy(block, block, block_here_sem.at[kind]).wait()
            block_across(kind).start()
        for kind in range(3):
            block_across(kind).wait_recv()
            where = slice(kind * lanes, (kind + 1) * lanes)
            w_high[:, where], w_low[:, where] = split(blocks_ref[kind])
        keep_blocks().start()

    def work(slot):
        keep(slot).start()
        parts = split(rows_ref[slot])
        product = dot3(parts, (w_high[...], w_low[...]))
        for tree in range(trees):
            rows = slice(tree * seg_len, (tree + 1) * seg_len)
            inner = dot2(both(parts, rows), down_ref[tree], NT)
            inner_ref[slot, tree] = inner
            inner_parts = split(ADAPT_SCALE * inner)
            for kind in range(3):
                term = dot2(
                    both(inner_parts, (slice(None), slice(kind * rank, (kind + 1) * rank))),
                    up_ref[tree, kind],
                )
                qkv_ref[slot, kind, tree] = (
                    product[rows, kind * lanes : (kind + 1) * lanes] + term
                )

    def arrived(move, slot):
        move(slot, across_sem.at[0], {"y": 1 - y}).wait_recv()

    def share(part, slot):
        plane_move(part, slot).start()
        core_move(part, slot, 0).start()

    def rows_by_line(level):
        slot = place(level, y)
        arrived(rows_move, slot)
        along(rows_move, line_sem, slot, level, start)
        over(rows_move, across_sem, slot, start)

    def first_by_line(level):
        slot = place(level, y)
        arrived(first, slot)
        along(first, line_first_sem, slot, level, start)
        over(first, over_first_sem, slot, start)
        share(0, slot)

    def second_by_line(level):
        for side in (y, 1 - y):
            slot = place(level, side)
            arrived(second, slot)
            along(second, line_second_sem, slot, level, start)
            share(1, slot)

    def rows_over(level):
        slot = place(level, 1 - y)
        arrived(rows_move, slot)
        work(slot)

    def first_over(level):
        slot = place(level, 1 - y)
        arrived(first, slot)
        share(0, slot)

    def faced(part, slot):
        plane_move(part, slot).wait_recv()
        core_move(part, slot, 1).start()

    def faced_at(hop):
        def act(level):
            if level is not z:
                faced(0, place(level, y))
                faced(1, place(level, y))
            faced(1, place(level, 1 - y))

        levels_at(hop, act)

    def attend_tree(tree):
        def slot_of(segment):
            found = jnp.int32(0)
            for slot in range(1, slots):
                found = jnp.where(order_ref[tree, slot] == segment, slot, found)
            return found

        def attend_slot(slot, carry):
            chain = ancestor_slots(order_ref, parents_ref, slot_of, tree, slot)
            own_context_ref[slot, tree] = attend(
                qkv_ref[slot, 0, tree] * HD ** (-0.5),
                jnp.concatenate([qkv_ref[where, 1, tree] for where, _ in chain], axis=0),
                jnp.concatenate([qkv_ref[where, 2, tree] for where, _ in chain], axis=0),
                chain_mask(chain, seg_len),
            )
            return carry

        lax.fori_loop(0, slots, attend_slot, 0)

    def context_move(step):
        target, device = peer(step)
        return remote(
            own_context_ref.at[target],
            context_ref.at[own],
            context_sem.at[step],
            context_here_sem.at[step],
            device,
        )

    def context_keep():
        return pltpu.make_async_copy(
            own_context_ref.at[own], context_ref.at[own], context_sem.at[0]
        )

    other = place(z, 1 - y)
    levels_at(1, rows_by_line)
    take_blocks()
    work(own)
    levels_at(1, lambda level: work(place(level, y)))
    levels_at(2, rows_by_line)
    start_shards()
    rows_over(z)
    levels_at(2, lambda level: work(place(level, y)))
    for hop in range(3, last + 1):
        levels_at(hop, rows_by_line)
    levels_at(1, rows_over)
    arrived(second, other)
    along(second, line_second_sem, other, z, start)
    share(1, other)
    levels_at(1, first_by_line)
    levels_at(1, second_by_line)
    for hop in range(3, last + 1):
        levels_at(hop, lambda level: work(place(level, y)))
    first_over(z)
    for hop in range(2, last + 1):
        levels_at(hop, rows_over)
    for tree in range(trees):
        attend_tree(tree)
        if tree == 0:
            levels_at(2, first_by_line)
            levels_at(2, second_by_line)
            levels_at(1, first_over)
            faced_at(0)
    context_keep().start()
    for step in range(1, slots):
        context_move(step).start()
    for hop in range(3, last + 1):
        levels_at(hop, first_by_line)
        levels_at(hop, second_by_line)
    faced_at(1)
    for hop in range(2, last + 1):
        levels_at(hop, first_over)
    for hop in range(2, last + 1):
        faced_at(hop)
    for hop in range(last + 1):
        levels_at(hop, lambda level: faced(0, place(level, 1 - y)))

    context_keep().wait()
    for step in range(1, slots):
        context_move(step).wait_send()
        context_move(step).wait_recv()
    keep_shard().wait()
    keep_blocks().wait()
    for i in range(3):
        block_across(i).wait_send()
        target, sent, _ = block_move(i)

        @pl.when(target != own)
        def _(sent=sent):
            sent().wait_send()

    def finish(slot):
        for part in range(2):
            plane_move(part, slot).wait_send()
            for kind in range(2):
                core_move(part, slot, kind).wait_recv()
                core_move(part, slot, kind).wait_send()

    def sent_on(level):
        slot = beside(level)
        along(rows_move, line_sem, slot, level, wait_send)
        over(rows_move, across_sem, slot, wait_send)
        along(first, line_first_sem, slot, level, wait_send)
        over(first, over_first_sem, slot, wait_send)
        along(second, line_second_sem, slot, level, wait_send)
        along(second, line_second_sem, place(level, 1 - y), level, wait_send)
        if level is z:
            over(second, over_second_sem, own, wait_send)
        else:
            finish(slot)
        finish(place(level, 1 - y))

    for hop in range(last + 1):
        levels_at(hop, sent_on)
    for slot in range(slots):
        keep(slot).wait()


def heads_call(order, parents, tokens, gains, weight, shard, down, up):
    trees, seg_len, width = tokens.shape
    slots = lax.axis_size(ROWS)
    lanes = weight.shape[1] // 3
    inner = down.shape[1]
    dma = pltpu.SemaphoreType.DMA
    here = pl.BlockSpec(memory_space=pltpu.VMEM)
    there = pl.BlockSpec(memory_space=pl.ANY)
    scalars = pl.BlockSpec(memory_space=pltpu.SMEM)
    return pl.pallas_call(
        heads_kernel,
        out_shape=[
            shaped(slots, trees * seg_len, width),
            shaped(slots, trees, seg_len, inner),
            shaped(slots, 3, trees, seg_len, lanes),
            shaped(3, width, lanes),
            shaped(slots, *shard.shape),
            shaped(slots, trees, seg_len, lanes),
        ],
        in_specs=[scalars, scalars, here, here, there, there, here, here],
        out_specs=[there, here, here, there, there, there],
        scratch_shapes=[
            pltpu.VMEM((slots, trees, seg_len, lanes), F32),
            pltpu.VMEM((slots, trees * seg_len, width), F32),
            pltpu.VMEM((3, width, lanes), F32),
            pltpu.VMEM((width, 3 * lanes), BF16),
            pltpu.VMEM((width, 3 * lanes), BF16),
            dma((slots + 2,)),
        ]
        + [dma((3,))] * 4
        + [dma((slots,))] * 4
        + [dma((2, slots))] * 6
        + [dma((4, slots))] * 2
        + [dma((slots,))] * 2,
        compiler_params=pltpu.CompilerParams(
            vmem_limit_bytes=48 * MIB, collective_id=0, has_side_effects=True
        ),
        cost_estimate=lasting(180),
    )(order, parents, tokens, gains, weight, shard, down, up)


def ancestor_slots(order_ref, parents_ref, slot_of, tree, slot, depth=4):
    segment = order_ref[tree, slot]
    chain = [(slot, None)]
    there = None
    for _ in range(depth - 1):
        parent = parents_ref[tree, segment]
        there = parent >= 0 if there is None else jnp.logical_and(there, parent >= 0)
        segment = jnp.maximum(parent, 0)
        chain.append((slot_of(segment), there))
    return chain


def fill_slot_of(order_ref, slot_of, tree, slots):
    for slot in range(slots):
        slot_of[order_ref[tree, slot]] = slot


def chain_mask(chain, seg_len):
    row = lax.broadcasted_iota(jnp.int32, (seg_len, seg_len), 0)
    column = lax.broadcasted_iota(jnp.int32, (seg_len, seg_len), 1)
    masks = [(column <= row).astype(jnp.int32)]
    for _, there in chain[1:]:
        masks.append(jnp.full((seg_len, seg_len), there.astype(jnp.int32)))
    mask = jnp.concatenate(masks, axis=1)
    return jnp.concatenate([mask, mask], axis=0) > 0


def stacked_heads(parts):
    lane = lax.broadcasted_iota(jnp.int32, parts[0].shape, 1)
    return tuple(
        jnp.concatenate(
            [jnp.where(lane < HD, part, 0), jnp.where(lane >= HD, part, 0)], axis=0
        ).astype(BF16)
        for part in parts
    )


def beside_heads(stacked):
    count = stacked.shape[0] // 2
    lane = lax.broadcasted_iota(jnp.int32, (count, stacked.shape[1]), 1)
    return jnp.where(lane < HD, stacked[:count], stacked[count:])


def by_lanes(left, right):
    wide = jnp.concatenate(left, axis=1)
    return dot(wide, jnp.concatenate([right[0], right[0]], axis=1), NT) + dot(
        left[0], right[1], NT
    )


def by_rows(left, right, dims):
    width = right[0].shape[1]
    wide = dot(left[0], jnp.concatenate(right, axis=1), dims)
    return wide[:, :width] + wide[:, width:] + dot(left[1], right[0], dims)


def pair_scores(query_parts, key_parts, mask):
    scores = by_lanes(query_parts, key_parts)
    if mask is not None:
        scores = jnp.where(mask, scores, MASK_FILL)
    return jnp.exp(scores - jnp.max(scores, -1, keepdims=True))


def attend(queries, keys, values, mask=None):
    weights = pair_scores(stacked_heads(split(queries)), split(keys), mask)
    mass = jnp.sum(weights, -1, keepdims=True)
    return beside_heads(by_rows(split(weights), split(values), NN) / mass)


def attend_back(queries, keys, values, d_context, mask=None):
    query_parts, out_parts = stacked_heads(split(queries)), stacked_heads(split(d_context))
    key_parts, value_parts = split(keys), split(values)
    weights = pair_scores(query_parts, key_parts, mask)
    weights = weights * (1.0 / jnp.sum(weights, -1, keepdims=True))
    d_weights = by_lanes(out_parts, value_parts)
    shared = jnp.sum(weights * d_weights, -1, keepdims=True)
    score_parts = split(weights * (d_weights - shared))
    return (
        beside_heads(by_rows(score_parts, key_parts, NN)) * HD ** (-0.5),
        by_rows(score_parts, query_parts, TN),
        by_rows(split(weights), out_parts, TN),
    )


def self_backward_kernel(
    order_ref,
    parents_ref,
    qkv_ref,
    d_context_ref,
    normed_ref,
    inner_ref,
    up_ref,
    _,
    d_qkv_ref,
    g_down_ref,
    g_up_ref,
    slot_of,
):
    tree = pl.program_id(0)
    slots, seg_len, pair = qkv_ref.shape[0], qkv_ref.shape[3], qkv_ref.shape[4]
    rank = up_ref.shape[2]
    fill_slot_of(order_ref, slot_of, tree, slots)
    d_qkv_ref[...] = jnp.zeros_like(d_qkv_ref)

    def one_slot(slot, carry):
        chain = ancestor_slots(order_ref, parents_ref, lambda seg: slot_of[seg], tree, slot)
        keys = jnp.concatenate([qkv_ref[where, 1, 0] for where, _ in chain], axis=0)
        values = jnp.concatenate([qkv_ref[where, 2, 0] for where, _ in chain], axis=0)
        d_queries, d_keys, d_values = attend_back(
            qkv_ref[slot, 0, 0] * HD ** (-0.5),
            keys,
            values,
            d_context_ref[slot, 0],
            mask=chain_mask(chain, seg_len),
        )
        d_qkv_ref[slot, 0, 0] += d_queries
        for entry, (where, _) in enumerate(chain):
            rows = slice(entry * seg_len, (entry + 1) * seg_len)
            d_qkv_ref[where, 1, 0] += d_keys[rows]
            d_qkv_ref[where, 2, 0] += d_values[rows]
        return carry

    lax.fori_loop(0, slots, one_slot, 0)

    inner = split(ADAPT_SCALE * inner_ref[...].reshape(slots * seg_len, 3 * rank))
    d_inner = []
    for kind in range(3):
        grads = split(d_qkv_ref[:, kind, 0].reshape(slots * seg_len, pair))
        ranks = slice(kind * rank, (kind + 1) * rank)
        d_inner.append(dot2(grads, up_ref[0, kind], NT))
        g_up_ref[0, kind] = dot3(both(inner, (slice(None), ranks)), grads, TN)
    high, low = split(ADAPT_SCALE * jnp.concatenate(d_inner, axis=1))
    rows_high, rows_low = split(normed_ref[...].reshape(slots * seg_len, -1))
    wide = dot(jnp.concatenate([high, low], axis=1), rows_high, TN)
    g_down = wide[: 3 * rank] + wide[3 * rank :] + dot(high, rows_low, TN)
    g_down_ref[0] = g_down.reshape(3, rank, -1)


def slots_spec(shape):
    lead = len(shape) - 3
    return pl.BlockSpec(
        shape[:lead] + (1,) + shape[lead + 1 :],
        lambda tree, *_: (0,) * lead + (tree, 0, 0),
    )


def tree_spec(shape):
    return pl.BlockSpec((1,) + shape[1:], lambda tree, *_: (tree,) + (0,) * (len(shape) - 1))


def self_call(kernel, order, parents, operands, in_specs, out_shape, out_specs, micros):
    trees, slots = order.shape
    return pl.pallas_call(
        kernel,
        out_shape=out_shape,
        grid_spec=pltpu.PrefetchScalarGridSpec(
            num_scalar_prefetch=2,
            grid=(trees,),
            in_specs=in_specs,
            out_specs=out_specs,
            scratch_shapes=[pltpu.SMEM((slots,), jnp.int32)],
        ),
        compiler_params=vmem(56),
        cost_estimate=lasting(micros),
    )(order, parents, *operands)


def head_pairs(ref):
    return [slice(2 * pair * HD, 2 * (pair + 1) * HD) for pair in range(ref.shape[2] // (2 * HD))]


def cross_forward_kernel(query_ref, key_ref, value_ref, _, context_ref):
    for lanes in head_pairs(query_ref):
        context_ref[0, :, lanes] = attend(
            query_ref[0, :, lanes] * HD ** (-0.5), key_ref[0, :, lanes], value_ref[0, :, lanes]
        )


def cross_backward_kernel(
    query_ref, key_ref, value_ref, d_context_ref, d_query_ref, d_key_ref, d_value_ref
):
    for lanes in head_pairs(query_ref):
        d_query_ref[0, :, lanes], d_key_ref[0, :, lanes], d_value_ref[0, :, lanes] = attend_back(
            query_ref[0, :, lanes] * HD ** (-0.5),
            key_ref[0, :, lanes],
            value_ref[0, :, lanes],
            d_context_ref[0, :, lanes],
        )


def cross_call(kernel, queries, memory, rest, long_outs, ahead=()):
    trees, seg_len, width = queries.shape
    enc_rows = memory.shape[1]
    lanes = 4 * HD
    steps = width // lanes
    short = pl.BlockSpec((1, seg_len, lanes), lambda tree, step: (tree, 0, step))
    keys = pl.BlockSpec((1, enc_rows, lanes), lambda tree, step: (tree, 0, step))
    values = pl.BlockSpec((1, enc_rows, lanes), lambda tree, step: (tree, 0, steps + step))
    return pl.pallas_call(
        kernel,
        out_shape=[shaped(trees, seg_len, width)] + [shaped(trees, enc_rows, width)] * long_outs,
        grid=(trees, steps),
        in_specs=[short, keys, values]
        + [short] * len(rest)
        + [pl.BlockSpec(memory_space=pl.ANY)] * len(ahead),
        out_specs=[short] + [keys] * long_outs,
        compiler_params=vmem(48),
        cost_estimate=lasting(32 if long_outs else 19),
    )(queries, memory, memory, *rest, *ahead)


def square(ref):
    return ref[...].reshape(-1, ref.shape[-1])


def joined(ref):
    slots, trees = ref.shape[:2]
    return jnp.concatenate(
        [
            jnp.concatenate([ref[slot, tree] for slot in range(slots)], axis=1)
            for tree in range(trees)
        ],
        axis=0,
    )


def rows_of(ref):
    return ref[...].reshape(-1, ref.shape[-1])


def tree_rows(trees, count):
    return [slice(tree * count, (tree + 1) * count) for tree in range(trees)]


def with_adapters(parts, down_ref, up_ref, entry, trees):
    count = parts[0].shape[0] // trees
    return jnp.concatenate(
        [
            adapted(both(parts, rows), down_ref[tree, entry], up_ref[tree, entry])[0]
            for tree, rows in enumerate(tree_rows(trees, count))
        ],
        axis=0,
    )


def with_adapters_back(parts, grads, down_ref, up_ref, entry, trees, g_down_ref, g_up_ref, place):
    count = parts[0].shape[0] // trees
    terms = []
    for tree, rows in enumerate(tree_rows(trees, count)):
        term, g_down_ref[tree, place], g_up_ref[tree, place] = adapted_back(
            both(parts, rows), both(grads, rows), down_ref[tree, entry], up_ref[tree, entry]
        )
        terms.append(term)
    return jnp.concatenate(terms, axis=0)


def after_self_kernel(
    context_ref, tokens_ref, gains_ref, out_ref, query_ref, down_ref, up_ref, middle_ref, cross_ref
):
    trees = tokens_ref.shape[0]
    context = split(joined(context_ref))
    middle = rows_of(tokens_ref) + dot3(context, split(square(out_ref)))
    middle = middle + with_adapters(context, down_ref, up_ref, 3, trees)
    middle_ref[...] = middle.reshape(middle_ref.shape)
    normed = split(layer_norm(middle, gains_ref[1:2])[0])
    queries = dot3(normed, split(square(query_ref)), NT)
    queries = queries + with_adapters(normed, down_ref, up_ref, 4, trees)
    cross_ref[...] = queries.reshape(cross_ref.shape)


def after_cross_kernel(
    context_ref, middle_ref, gains_ref, out_ref, down_ref, up_ref, after_ref, normed_ref
):
    trees = context_ref.shape[0]
    context = split(rows_of(context_ref))
    after = rows_of(middle_ref) + dot3(context, split(square(out_ref)))
    after = after + with_adapters(context, down_ref, up_ref, 7, trees)
    after_ref[...] = after.reshape(after_ref.shape)
    normed = layer_norm(after, gains_ref[2:3])[0]
    normed_ref[...] = normed.reshape(normed_ref.shape)


def into_cross_kernel(
    d_rows_ref,
    after_ref,
    cotangent_ref,
    context_ref,
    gains_ref,
    out_ref,
    down_ref,
    up_ref,
    g_in_up_ref,
    g_out_down_ref,
    d_after_ref,
    d_context_ref,
    g_down_ref,
    g_up_ref,
    hidden_ref,
    other_ref,
    parts_ref,
    swap_sem,
    part_sem,
    part_here_sem,
):
    trees = after_ref.shape[0]
    z, levels = lax.axis_index("z"), lax.axis_size("z")
    partner = {"y": 1 - lax.axis_index("y")}
    signal(partner)
    for step in range(1, levels):
        signal({"z": (z + step) % levels})
    pl.semaphore_wait(pltpu.get_barrier_semaphore(), levels)
    swapped = remote(
        d_rows_ref.at[:, 1], other_ref, swap_sem.at[0], swap_sem.at[1], partner
    )
    swapped.start()

    unit_grads = (g_in_up_ref, g_out_down_ref)

    def part_move(step, which):
        level = (z + step) % levels
        return remote(
            unit_grads[which].at[:, pl.ds(2 * level, 2)],
            parts_ref.at[step - 1, which],
            part_sem.at[step - 1, which],
            part_here_sem.at[step - 1, which],
            {"z": level},
        )

    moves = [(step, which) for step in range(1, levels) for which in range(2)]
    for step, which in moves:
        part_move(step, which).start()
    context = split(rows_of(context_ref))
    weight = split(square(out_ref))
    _, normal, inverse = layer_norm(rows_of(after_ref), gains_ref[2:3])
    for step, which in moves:
        part_move(step, which).wait_recv()
    for which in range(2):
        total = unit_grads[which][:, pl.ds(2 * z, 2)]
        for step in range(1, levels):
            total = total + parts_ref[step - 1, which]
        block = total.shape[3]
        for plane in range(2):
            lanes = slice(plane * block, (plane + 1) * block)
            hidden_ref[:, which, :, lanes] = total[:, plane]
    own_rows = jnp.concatenate([d_rows_ref[tree, 0] for tree in range(trees)], axis=0)
    swapped.wait()
    d_normed = own_rows + rows_of(other_ref)
    d_after = rows_of(cotangent_ref) + norm_back(normal, inverse, gains_ref[2:3], d_normed)
    d_after_ref[...] = d_after.reshape(d_after_ref.shape)
    grads = split(d_after)
    d_context = dot3(grads, weight, NT)
    d_context = d_context + with_adapters_back(
        context, grads, down_ref, up_ref, 7, trees, g_down_ref, g_up_ref, 0
    )
    d_context_ref[...] = d_context.reshape(d_context_ref.shape)
    for step, which in moves:
        part_move(step, which).wait_send()


def into_self_kernel(
    d_query_ref,
    d_after_ref,
    middle_ref,
    context_ref,
    gains_ref,
    query_ref,
    out_ref,
    down_ref,
    up_ref,
    d_middle_ref,
    d_context_ref,
    g_down_ref,
    g_up_ref,
):
    slots, trees, seg_len, lanes = context_ref.shape
    rows, normal, inverse = layer_norm(rows_of(middle_ref), gains_ref[1:2])
    grads = split(rows_of(d_query_ref))
    d_normed = dot3(grads, split(square(query_ref)))
    d_normed = d_normed + with_adapters_back(
        split(rows), grads, down_ref, up_ref, 4, trees, g_down_ref, g_up_ref, 1
    )
    d_middle = rows_of(d_after_ref) + norm_back(normal, inverse, gains_ref[1:2], d_normed)
    d_middle_ref[...] = d_middle.reshape(d_middle_ref.shape)
    grads = split(d_middle)
    context = split(joined(context_ref))
    d_context = dot3(grads, split(square(out_ref)), NT)
    d_context = d_context + with_adapters_back(
        context, grads, down_ref, up_ref, 3, trees, g_down_ref, g_up_ref, 0
    )
    for slot in range(slots):
        for tree in range(trees):
            d_context_ref[slot, tree] = d_context[
                tree * seg_len : (tree + 1) * seg_len, slot * lanes : (slot + 1) * lanes
            ]


def packed_spec(packed, first, count):
    return pl.BlockSpec(
        packed.shape[:2] + (count, packed.shape[3]), lambda *_: (0, 0, first // count, 0)
    )


def rows_call(kernel, operands, specs, out_shape, scratch=(), params=None):
    return pl.pallas_call(
        kernel,
        out_shape=out_shape,
        grid=(1,),
        in_specs=[
            whole_spec(operand.shape) if spec is None else spec
            for operand, spec in zip(operands, specs)
        ],
        out_specs=[whole_spec(out.shape) for out in out_shape],
        scratch_shapes=scratch,
        compiler_params=params or vmem(56),
        cost_estimate=lasting(10),
    )(*operands)


def memory_kernel(encoder_ref, weight_ref, down_ref, up_ref, memory_ref, row_high, row_low, inner):
    trees, rank = down_ref.shape[0], down_ref.shape[2]
    step = pl.program_id(0)
    half = pl.num_programs(0) // 2
    lanes = memory_ref.shape[2]
    count = encoder_ref.shape[1]

    @pl.when(step == 0)
    def _():
        row_high[...], row_low[...] = split(rows_of(encoder_ref))
        for tree, rows in enumerate(tree_rows(trees, count)):
            for kind in range(2):
                parts = (row_high[rows], row_low[rows])
                inner[kind, rows] = jnp.concatenate(
                    split(ADAPT_SCALE * dot2(parts, down_ref[tree, 5 + kind], NT)), axis=1
                )

    result = dot3((row_high[...], row_low[...]), split(square(weight_ref)), NT)
    kind = step // half
    for tree, rows in enumerate(tree_rows(trees, count)):
        up = up_ref[tree, 0]
        term = dot(inner[kind, rows], jnp.concatenate([up, up], axis=0))
        memory_ref[tree] = result[rows] + term


def memory_call(encoder, packed, down, up):
    trees, count, width = encoder.shape
    rank = down.shape[2]
    slots, copies = packed.shape[:2]
    lanes = 2 * width // slots
    half = slots // 2
    return pl.pallas_call(
        memory_kernel,
        out_shape=shaped(trees, count, 2 * width),
        grid=(slots,),
        in_specs=[
            whole_spec(encoder.shape),
            pl.BlockSpec((1, copies, lanes // copies, width), lambda step: (step, 0, 0, 0)),
            whole_spec(down.shape),
            pl.BlockSpec((trees, 1, rank, lanes), lambda step: (0, 5 + step // half, 0, step % half)),
        ],
        out_specs=pl.BlockSpec((trees, count, lanes), lambda step: (0, 0, step)),
        scratch_shapes=[
            pltpu.VMEM((trees * count, width), BF16),
            pltpu.VMEM((trees * count, width), BF16),
            pltpu.VMEM((2, trees * count, 2 * rank), BF16),
        ],
        compiler_params=vmem(56),
        cost_estimate=lasting(22),
    )(encoder, packed, down, up)


def memory_back_kernel(
    encoder_ref,
    d_key_ref,
    d_value_ref,
    weight_ref,
    down_ref,
    up_ref,
    d_encoder_ref,
    g_down_ref,
    g_up_ref,
    row_high,
    row_low,
    inner,
    d_inner,
):
    trees, rank = down_ref.shape[0], down_ref.shape[2]
    step = pl.program_id(0)
    half = pl.num_programs(0) // 2
    count = encoder_ref.shape[1]
    spans = tree_rows(trees, count)

    @pl.when(step == 0)
    def _():
        row_high[...], row_low[...] = split(rows_of(encoder_ref))
        d_encoder_ref[...] = jnp.zeros_like(d_encoder_ref)
        d_inner[...] = jnp.zeros_like(d_inner)
        for tree, rows in enumerate(spans):
            for kind in range(2):
                parts = (row_high[rows], row_low[rows])
                inner[kind, rows] = jnp.concatenate(
                    split(ADAPT_SCALE * dot2(parts, down_ref[tree, 5 + kind], NT)), axis=1
                )

    kind = step // half
    grads = split(jnp.where(kind == 0, rows_of(d_key_ref), rows_of(d_value_ref)))
    d_encoder_ref[...] += dot3(grads, split(square(weight_ref))).reshape(d_encoder_ref.shape)
    for tree, rows in enumerate(spans):
        own = both(grads, rows)
        d_inner[kind, rows] += dot2(own, up_ref[tree, 0], NT)
        high, low = inner[kind, rows, :rank], inner[kind, rows, rank:]
        g_up_ref[tree, 0] = dot3((high, low), own, TN)

    @pl.when(step == 2 * half - 1)
    def _():
        for tree, rows in enumerate(spans):
            parts = (row_high[rows], row_low[rows])
            for kind in range(2):
                own = split(ADAPT_SCALE * d_inner[kind, rows])
                d_encoder_ref[tree] += dot2(own, down_ref[tree, 5 + kind])
                g_down_ref[tree, kind] = dot3(own, parts, TN)


def memory_back_call(encoder, d_keys, d_values, packed, down, up):
    trees, count, width = encoder.shape
    rank = down.shape[2]
    slots, copies = packed.shape[:2]
    lanes = 2 * width // slots
    half = slots // 2
    kind_spec = pl.BlockSpec((trees, 1, rank, lanes), lambda step: (0, step // half, 0, step % half))
    return pl.pallas_call(
        memory_back_kernel,
        out_shape=[
            shaped(trees, count, width),
            shaped(trees, 2, rank, width),
            shaped(trees, 2, rank, width),
        ],
        grid=(slots,),
        in_specs=[
            whole_spec(encoder.shape),
            pl.BlockSpec((trees, count, lanes), lambda step: (0, 0, jnp.minimum(step, half - 1))),
            pl.BlockSpec((trees, count, lanes), lambda step: (0, 0, jnp.maximum(step - half, 0))),
            pl.BlockSpec((1, copies, lanes // copies, width), lambda step: (step, 0, 0, 0)),
            whole_spec(down.shape),
            pl.BlockSpec((trees, 1, rank, lanes), lambda step: (0, 5 + step // half, 0, step % half)),
        ],
        out_specs=[
            whole_spec((trees, count, width)),
            whole_spec((trees, 2, rank, width)),
            kind_spec,
        ],
        scratch_shapes=[
            pltpu.VMEM((trees * count, width), BF16),
            pltpu.VMEM((trees * count, width), BF16),
            pltpu.VMEM((2, trees * count, 2 * rank), BF16),
            pltpu.VMEM((2, trees * count, rank), F32),
        ],
        compiler_params=vmem(56),
        cost_estimate=lasting(31),
    )(encoder, d_keys, d_values, packed, down, up)


def nearest(z, last, turn):
    orders = [
        sorted((level for level in range(last + 1) if level != own), key=lambda level: abs(level - own))
        for own in range(last + 1)
    ]
    level = orders[0][turn]
    for own in range(1, last + 1):
        level = jnp.where(z == own, orders[own][turn], level)
    return level


def feed_forward_kernel(
    rows_ref,
    cot_ref,
    w_in_ref,
    w_out_ref,
    below_ref,
    above_ref,
    in_up_ref,
    out_down_ref,
    in_down_ref,
    out_up_ref,
    _,
    out_ref,
    d_rows_ref,
    g_in_up_ref,
    g_out_down_ref,
    g_in_down_ref,
    g_out_up_ref,
    shards_ref,
    w_in_buf,
    row_high,
    row_low,
    cot_high,
    cot_low,
    inner_in,
    d_inner_out,
    inner_in_t,
    d_inner_out_t,
    inner_out,
    d_inner_in,
    own_sem,
    w_in_sem,
    line_sem,
    line_here_sem,
    plane_sem,
    plane_here_sem,
    core_sem,
    core_here_sem,
    near_sem,
):
    trees, rank = in_up_ref.shape[0], in_up_ref.shape[2]
    spans = tree_rows(trees, rows_ref.shape[0] // trees)
    x, c, z = lax.axis_index("x"), lax.axis_index("c"), lax.axis_index("z")
    last = lax.axis_size("z") - 1
    block = shards_ref.shape[2]
    part = block // 2
    levels = [nearest(z, last, turn) for turn in range(last)]

    def piece(level, plane, core):
        return shards_ref.at[level, plane, pl.ds(pl.multiple_of(core * part, part), part)]

    def line_move(turn, target):
        level = levels[turn]
        here = piece(level, x, c)
        return remote(here, here, line_sem.at[turn], line_here_sem.at[level], {"z": target})

    def plane_move(turn):
        here = piece(levels[turn], x, c)
        return remote(here, here, plane_sem.at[turn], plane_here_sem.at[turn], {"x": 1 - x})

    def core_move(turn, kind):
        here = piece(levels[turn], x if kind == 0 else 1 - x, c)
        index = 2 * turn + kind
        return remote(here, here, core_sem.at[index], core_here_sem.at[index], {"c": 1 - c})

    def near_copy(source, level, index):
        return pltpu.make_async_copy(source, piece(level, x, c), near_sem.at[index])

    def near(action):
        @pl.when(z > 0)
        def _():
            action(near_copy(below_ref, z - 1, 0))

        @pl.when(z < last)
        def _():
            action(near_copy(above_ref, z + 1, 1))

    def wait_line(turn):
        @pl.when(jnp.abs(levels[turn] - z) > 1)
        def _():
            line_move(turn, z).wait_recv()

    def passing(turn, action):
        level = levels[turn]

        @pl.when(jnp.logical_and(level < z, z < last))
        def _():
            action(line_move(turn, z + 1))

        @pl.when(jnp.logical_and(level > z, z > 0))
        def _():
            action(line_move(turn, z - 1))

    def relay(turn):
        wait_line(turn)
        passing(turn, lambda copy: copy.start())
        plane_move(turn).start()
        core_move(turn, 0).start()

    def relay_plane(turn):
        plane_move(turn).wait_recv()
        core_move(turn, 1).start()

    order = [(-1, 0), (-1, 1), (0, 0), (1, 0), (0, 1), (2, 0), (1, 1), (2, 1)]

    def chosen(step):
        level, plane = z, x
        for index, (turn, other) in enumerate(order):
            hit = step == index
            level = jnp.where(hit, z if turn < 0 else levels[turn], level)
            plane = jnp.where(hit, 1 - x if other else x, plane)
        return level, plane

    def w_in_copy(step):
        level, plane = chosen(step)
        columns = pl.ds(pl.multiple_of(plane * block, block), block)
        slot = lax.rem(step, 2)
        return pltpu.make_async_copy(
            w_in_ref.at[level, :, columns], w_in_buf.at[slot], w_in_sem.at[slot]
        )

    def own_copy(plane):
        return pltpu.make_async_copy(
            w_out_ref.at[pl.ds(plane * block, block)], shards_ref.at[z, plane], own_sem.at[plane]
        )

    met = greet(z, last, [{"x": 1 - x}, {"c": 1 - c}])
    for plane in range(2):
        own_copy(plane).start()
    w_in_copy(0).start()
    near(start)
    met()
    near(lambda copy: copy.wait())
    relay(0)

    row_high[...], row_low[...] = split(rows_ref[...])
    cot_high[...], cot_low[...] = split(cot_ref[...])
    out_ref[...] = jnp.zeros_like(out_ref)
    d_rows_ref[...] = jnp.zeros_like(d_rows_ref)
    inner_out[...] = jnp.zeros_like(inner_out)
    d_inner_in[...] = jnp.zeros_like(d_inner_in)
    for tree, own in enumerate(spans):
        rows = (row_high[own], row_low[own])
        cots = (cot_high[own], cot_low[own])
        down, up = in_down_ref[tree], out_up_ref[tree]
        inner_in[own] = jnp.concatenate(split(ADAPT_SCALE * dot2(rows, down, NT)), axis=1)
        d_inner_out[own] = jnp.concatenate(split(ADAPT_SCALE * dot2(cots, up, NT)), axis=1)
        inner_in_t[tree] = jnp.concatenate(
            split(ADAPT_SCALE * (dot(down, rows[0], NT) + dot(down, rows[1], NT))), axis=0
        )
        d_inner_out_t[tree] = jnp.concatenate(
            split(ADAPT_SCALE * (dot(up, cots[0], NT) + dot(up, cots[1], NT))), axis=0
        )
    for plane in range(2):
        own_copy(plane).wait()

    def work(step, carry):
        level, plane = chosen(step)
        entry = level * 2 + plane

        @pl.when(step + 1 < len(order))
        def _():
            w_in_copy(step + 1).start()

        @pl.when(step == 2)
        def _():
            core_move(0, 0).wait_recv()
            relay(1)
            relay_plane(0)

        @pl.when(step == 3)
        def _():
            core_move(1, 0).wait_recv()

        @pl.when(step == 4)
        def _():
            core_move(0, 1).wait_recv()

        @pl.when(step == 5)
        def _():
            relay(2)
            relay_plane(1)
            core_move(2, 0).wait_recv()

        @pl.when(step == 6)
        def _():
            core_move(1, 1).wait_recv()

        @pl.when(step == 7)
        def _():
            relay_plane(2)
            core_move(2, 1).wait_recv()

        w_in_copy(step).wait()
        rows = (row_high[...], row_low[...])
        cots = (cot_high[...], cot_low[...])
        w_in = split(w_in_buf[lax.rem(step, 2)])
        w_out = split(shards_ref[level, plane])
        in_up = [in_up_ref[tree, entry] for tree in range(trees)]
        out_down = [out_down_ref[tree, entry] for tree in range(trees)]

        def per_tree(inner, maps):
            return jnp.concatenate(
                [
                    dot(inner[own], jnp.concatenate([maps[tree], maps[tree]], axis=0))
                    for tree, own in enumerate(spans)
                ],
                axis=0,
            )

        pre_act = dot3(rows, w_in) + per_tree(inner_in, in_up)
        root = math.sqrt(2.0 / math.pi)
        squared = pre_act * pre_act
        bend = jnp.tanh(root * (pre_act + 0.044715 * (squared * pre_act)))
        hidden = 0.5 * pre_act * (1.0 + bend)
        slope = 0.5 * (1.0 + bend) + 0.5 * pre_act * (1.0 - bend * bend) * (
            root * (1.0 + 3 * 0.044715 * squared)
        )
        hidden_parts = split(hidden)
        out_ref[...] += dot3(hidden_parts, w_out)
        d_hidden = dot3(cots, w_out, NT) + per_tree(d_inner_out, out_down)
        pre_parts = split(d_hidden * slope)
        d_rows_ref[...] += dot3(pre_parts, w_in, NT)

        for tree, own in enumerate(spans):
            hidden_own = both(hidden_parts, own)
            pre_own = both(pre_parts, own)
            inner_out[own] += dot2(hidden_own, out_down[tree], NT)
            d_inner_in[own] += dot2(pre_own, in_up[tree], NT)
            pair = dot(inner_in_t[tree], pre_own[0])
            g_in_up_ref[tree, entry] = (
                pair[:rank] + pair[rank:] + dot(inner_in_t[tree, :rank], pre_own[1])
            )
            pair = dot(d_inner_out_t[tree], hidden_own[0])
            g_out_down_ref[tree, entry] = (
                pair[:rank] + pair[rank:] + dot(d_inner_out_t[tree, :rank], hidden_own[1])
            )
        return carry

    lax.fori_loop(0, len(order), work, 0)

    for tree, own in enumerate(spans):
        inner = split(ADAPT_SCALE * inner_out[own])
        d_inner = split(ADAPT_SCALE * d_inner_in[own])
        out_ref[own] += dot2(inner, out_up_ref[tree])
        d_rows_ref[own] += dot2(d_inner, in_down_ref[tree])
        g_in_down_ref[tree] = dot3(d_inner, (row_high[own], row_low[own]), TN)
        g_out_up_ref[tree] = dot3(inner, (cot_high[own], cot_low[own]), TN)

    for turn in range(last):
        passing(turn, lambda copy: copy.wait_send())
        plane_move(turn).wait_send()
        core_move(turn, 0).wait_send()
        core_move(turn, 1).wait_send()


def feed_forward(rows, cots, w_in, w_out, near, in_up, out_down, in_down, out_up, ahead):
    count, width = rows.shape
    levels, _, units = w_in.shape
    block = units // 2
    trees, entries, rank = in_up.shape[:3]
    dma = pltpu.SemaphoreType.DMA
    here = pl.BlockSpec(memory_space=pltpu.VMEM)
    there = pl.BlockSpec(memory_space=pl.ANY)
    return pl.pallas_call(
        feed_forward_kernel,
        out_shape=[shaped(count, width)] * 2
        + [shaped(*in_up.shape), shaped(*out_down.shape)]
        + [shaped(*in_down.shape), shaped(*out_up.shape)],
        in_specs=[here, here] + [there] * 4 + [here] * 4 + [there],
        out_specs=[here] * 6,
        scratch_shapes=[
            pltpu.VMEM((levels, 2, block, width), F32),
            pltpu.VMEM((2, width, block), F32),
        ]
        + [pltpu.VMEM((count, width), BF16)] * 4
        + [pltpu.VMEM((count, 2 * rank), BF16)] * 2
        + [pltpu.VMEM((trees, 2 * rank, count // trees), BF16)] * 2
        + [pltpu.VMEM((count, rank), F32)] * 2
        + [
            dma((2,)),
            dma((2,)),
            dma((levels - 1,)),
            dma((levels,)),
            dma((levels - 1,)),
            dma((levels - 1,)),
            dma((2 * levels - 2,)),
            dma((2 * levels - 2,)),
            dma((2,)),
        ],
        compiler_params=pltpu.CompilerParams(
            vmem_limit_bytes=60 * MIB, collective_id=2, has_side_effects=True
        ),
        cost_estimate=lasting(110),
    )(rows, cots, w_in, w_out, *near, in_up, out_down, in_down, out_up, ahead)


def by_distance(z, last, turn):
    orders = [sorted(range(last + 1), key=lambda level: -abs(level - own)) for own in range(last + 1)]
    level = orders[0][turn]
    for own in range(1, last + 1):
        level = jnp.where(z == own, orders[own][turn], level)
    return level


def into_tokens_kernel(
    d_qkv_ref,
    weight_ref,
    tokens_ref,
    d_middle_ref,
    gains_ref,
    down_ref,
    up_ref,
    out_ref,
    own_ref,
    sent_ref,
    across_ref,
    rising_ref,
    falling_ref,
    w_high,
    w_low,
    sent_sem,
    line_sem,
    across_sem,
    rising_sem,
    falling_sem,
):
    z, y = lax.axis_index("z"), lax.axis_index("y")
    last = lax.axis_size("z") - 1
    trees, rank = up_ref.shape[0], up_ref.shape[2]
    seg_len, lanes = d_qkv_ref.shape[3], d_qkv_ref.shape[4]
    met = greet(z, last, [{"y": 1 - y}])
    for kind in range(3):
        where = slice(kind * lanes, (kind + 1) * lanes)
        w_high[:, where], w_low[:, where] = split(weight_ref[kind])
    met()

    def partial(level, side, ref):
        slot = level * 2 + side
        grads = split(
            jnp.concatenate(
                [
                    jnp.concatenate([d_qkv_ref[slot, kind, tree] for kind in range(3)], axis=1)
                    for tree in range(trees)
                ],
                axis=0,
            )
        )
        total = dot3(grads, (w_high[...], w_low[...]), NT)
        for tree, rows in enumerate(tree_rows(trees, seg_len)):
            inner = jnp.concatenate(
                [
                    dot2(
                        both(grads, (rows, slice(kind * lanes, (kind + 1) * lanes))),
                        up_ref[tree, kind],
                        NT,
                    )
                    for kind in range(3)
                ],
                axis=1,
            )
            ref[level, rows] = total[rows] + dot2(split(ADAPT_SCALE * inner), down_ref[tree])

    def move(source, target, level, sem, arrival, device):
        return pltpu.make_async_remote_copy(
            src_ref=source.at[level],
            dst_ref=target.at[level],
            send_sem=sem,
            recv_sem=arrival.at[level],
            device_id=device,
            device_id_type=pl.DeviceIdType.MESH,
        )

    def across(turn, level):
        return move(sent_ref, across_ref, level, sent_sem.at[turn], across_sem, {"y": 1 - y})

    def rising(turn, level):
        return move(own_ref, rising_ref, level, line_sem.at[turn], rising_sem, {"z": z + 1})

    def falling(turn, level):
        return move(own_ref, falling_ref, level, line_sem.at[turn], falling_sem, {"z": z - 1})

    levels = [by_distance(z, last, turn) for turn in range(last + 1)]
    for turn, level in enumerate(levels):
        partial(level, 1 - y, sent_ref)
        across(turn, level).start()
    for level in levels:
        partial(level, y, own_ref)
    for turn, level in enumerate(levels):
        across(turn, level).wait_recv()
        own_ref[level] += across_ref[level]

        @pl.when(jnp.logical_and(level >= z, z > 0))
        def _(level=level):
            rising(0, level).wait_recv()
            own_ref[level] += rising_ref[level]

        @pl.when(jnp.logical_and(level <= z, z < last))
        def _(level=level):
            falling(0, level).wait_recv()
            own_ref[level] += falling_ref[level]

        @pl.when(level > z)
        def _(turn=turn, level=level):
            rising(turn, level).start()

        @pl.when(level < z)
        def _(turn=turn, level=level):
            falling(turn, level).start()

    _, normal, inverse = layer_norm(rows_of(tokens_ref), gains_ref[0:1])
    grad = rows_of(d_middle_ref) + norm_back(normal, inverse, gains_ref[0:1], own_ref[z])
    out_ref[...] = grad.reshape(out_ref.shape)
    for turn, level in enumerate(levels):
        across(turn, level).wait_send()

        @pl.when(level > z)
        def _(turn=turn, level=level):
            rising(turn, level).wait_send()

        @pl.when(level < z)
        def _(turn=turn, level=level):
            falling(turn, level).wait_send()


def into_tokens_call(d_qkv, weight, tokens, d_middle, gains, down, up):
    trees, seg_len, width = tokens.shape
    levels = lax.axis_size("z")
    lanes = weight.shape[2]
    dma = pltpu.SemaphoreType.DMA((levels,))
    here = pl.BlockSpec(memory_space=pltpu.VMEM)
    return pl.pallas_call(
        into_tokens_kernel,
        out_shape=shaped(*tokens.shape),
        in_specs=[here] * 7,
        out_specs=here,
        scratch_shapes=[pltpu.VMEM((levels, trees * seg_len, width), F32)] * 5
        + [pltpu.VMEM((width, 3 * lanes), BF16)] * 2
        + [dma] * 5,
        compiler_params=pltpu.CompilerParams(
            vmem_limit_bytes=56 * MIB, collective_id=1, has_side_effects=True
        ),
        cost_estimate=lasting(110),
    )(d_qkv, weight, tokens, d_middle, gains, down, up)


def place_kernel(source_ref, parts_ref, down_ref, up_ref, in_down_ref, out_up_ref):
    places = [(down_ref, entry) for entry in range(3)] + [(up_ref, entry) for entry in range(3)]
    places += [(down_ref, entry) for entry in range(3, 8)]
    places += [(up_ref, entry) for entry in range(3, 8)]
    span = parts_ref.shape[5]
    for owner in range(parts_ref.shape[1]):
        lanes = slice(owner * span, (owner + 1) * span)
        for part, (ref, entry) in enumerate(places):
            ref[0, entry, :, lanes] = parts_ref[0, owner, 0, part]
        in_down_ref[0, :, lanes] = parts_ref[0, owner, 0, len(places)]
        out_up_ref[0, :, lanes] = parts_ref[0, owner, 0, len(places) + 1]


def place_hidden_kernel(source_ref, parts_ref, _, in_up_ref, out_down_ref):
    for owner in range(parts_ref.shape[1]):
        units = parts_ref.shape[5]
        lanes = slice(owner * units, (owner + 1) * units)
        in_up_ref[0, :, lanes] = parts_ref[0, owner, 0, 0]
        out_down_ref[0, :, lanes] = parts_ref[0, owner, 0, 1]


def place_call(kernel, source, arrays, out_shape, ahead=()):
    def chosen(array):
        groups = array.shape[2]
        return pl.BlockSpec(
            (1, array.shape[1], 1) + array.shape[3:],
            lambda entry, tree: (tree[entry] // groups, 0, tree[entry] % groups, 0, 0, 0),
        )

    return pl.pallas_call(
        kernel,
        out_shape=out_shape,
        grid_spec=pltpu.PrefetchScalarGridSpec(
            num_scalar_prefetch=1,
            grid=(out_shape[0].shape[0],),
            in_specs=[chosen(array) for array in arrays]
            + [pl.BlockSpec(memory_space=pl.ANY)] * len(ahead),
            out_specs=[tree_spec(out.shape) for out in out_shape],
        ),
        compiler_params=vmem(48),
        cost_estimate=lasting(9),
    )(source, *arrays, *ahead)


def my_quarter(shard):
    part = shard.shape[0] // lax.axis_size(COPIES)
    return lax.dynamic_slice_in_dim(shard, lax.axis_index(COPIES) * part, part, 0)


def gather_pair_half(quarter, shape):
    whole = lax.all_gather(quarter, ("z",) + COPIES, axis=0, tiled=True)
    return whole.reshape((-1,) + shape)


def pick(table, adapter_pick):
    return jnp.stack(
        [
            lax.dynamic_index_in_dim(table, adapter_pick[tree], 0, keepdims=False)
            for tree in range(adapter_pick.shape[0])
        ]
    )


def after(array, other):
    return array + 0.0 * other[(0,) * other.ndim]


def swap(array):
    return lax.ppermute(array, "y", SWAP)


def summed_to_owner(parts, axes):
    return jnp.sum(lax.all_to_all(parts, axes, split_axis=0, concat_axis=0, tiled=True), axis=0)


def summed_along_line(parts):
    levels = lax.axis_size("z")
    z = lax.axis_index("z")
    total = lax.dynamic_index_in_dim(parts, z, 0, keepdims=False)
    for other in range(1, levels):
        sent = lax.dynamic_index_in_dim(parts, z ^ other, 0, keepdims=False)
        total = total + lax.ppermute(
            sent, "z", [(level, level ^ other) for level in range(levels)]
        )
    return total


def to_everyone(array):
    everyone = lax.all_gather(array, COPIES + ROWS, axis=0, tiled=False)
    return everyone.reshape((-1, lax.axis_size(ROWS)) + array.shape)


def by_heads(
    tokens,
    encoder,
    cotangent,
    adapter_pick,
    segment_order,
    parents,
    norm_gains,
    w_qkv,
    w_self_out,
    w_cross_q,
    w_cross_kv,
    w_cross_out,
    w_fc_in,
    w_fc_out,
    attn_down,
    attn_up,
    fc_in_down,
    fc_in_up,
    fc_out_down,
    fc_out_up,
):
    trees, seg_len, width = tokens.shape
    slots = lax.axis_size(ROWS)
    copies = lax.axis_size(COPIES)
    adapters, projections, rank = attn_up.shape[:3]
    hidden_units = fc_in_up.shape[2]
    pairs = lax.axis_size("y")
    me, my_y = lax.axis_index(ROWS), lax.axis_index("y")
    lanes = width // slots

    down = pick(attn_down.swapaxes(2, 3), adapter_pick)
    up = pick(attn_up, adapter_pick)
    in_down = pick(fc_in_down.swapaxes(1, 2), adapter_pick)
    out_up = pick(fc_out_up, adapter_pick)

    def half_columns(table):
        picked = pick(table, adapter_pick).reshape(
            trees, rank, slots // pairs, pairs, hidden_units // slots
        )
        half = lax.dynamic_index_in_dim(picked, my_y, 3, keepdims=False)
        return half.reshape(trees, rank, slots, -1).swapaxes(1, 2)

    in_up = half_columns(fc_in_up)
    out_down = half_columns(fc_out_down.swapaxes(1, 2))
    down_qkv = down[:, 0:3].reshape(trees, 3 * rank, width)
    up_own = lax.dynamic_slice_in_dim(up[:, 0:3], me * lanes, lanes, 3)

    shard = jnp.concatenate(
        [
            w.reshape(copies, -1, width)
            for w in (w_cross_kv.T, w_self_out, w_cross_out, w_cross_q.T)
        ],
        axis=1,
    )
    normed_all, inner_all, qkv, qkv_own, packed, context = heads_call(
        segment_order, parents, tokens, norm_gains, w_qkv, shard, down_qkv, up_own
    )
    row = width // (slots * copies)
    self_out_spec = packed_spec(packed, 2 * row, row)
    cross_out_spec = packed_spec(packed, 3 * row, row)
    cross_q_spec = packed_spec(packed, 4 * row, row)

    fc_in_late, qkv = lax.optimization_barrier((my_quarter(w_fc_in), qkv))
    fc_in_half = gather_pair_half(fc_in_late, w_fc_in.shape)
    fc_out_late, context = lax.optimization_barrier((my_quarter(w_fc_out), context))
    levels = range(lax.axis_size("z") - 1)
    fc_out_near = (
        lax.ppermute(fc_out_late, "z", [(level, level + 1) for level in levels]),
        lax.ppermute(fc_out_late, "z", [(level + 1, level) for level in levels]),
    )

    cotangent_other = swap(after(cotangent, context))
    memory = memory_call(encoder, packed, down, up)
    middle, cross_queries = rows_call(
        after_self_kernel,
        (context, tokens, norm_gains, packed, packed, down, up),
        (None, None, None, self_out_spec, cross_q_spec, None, None),
        [shaped(*tokens.shape)] * 2,
    )
    (cross_context,) = cross_call(
        cross_forward_kernel, cross_queries, memory, (), 0, (cotangent_other,)
    )
    after_cross, normed_three = rows_call(
        after_cross_kernel,
        (cross_context, middle, norm_gains, packed, down, up),
        (None, None, None, cross_out_spec, None, None),
        [shaped(*tokens.shape)] * 2,
    )

    all_picks = lax.all_gather(adapter_pick, COPIES, axis=0, tiled=True)
    entry = lax.broadcasted_iota(jnp.int32, (adapters, 1), 0)
    tree_index = lax.broadcasted_iota(jnp.int32, (1, all_picks.shape[0]), 1)
    source = jnp.sum(jnp.where(entry == all_picks[None, :], tree_index, 0), axis=1)
    def paired(own_rows, other_rows):
        return jnp.stack([own_rows, other_rows], axis=1).reshape(-1, width)

    out_part, d_rows_part, g_in_up, g_out_down, g_in_down, g_out_up = feed_forward(
        paired(normed_three, swap(normed_three)),
        paired(cotangent, cotangent_other),
        fc_in_half,
        w_fc_out,
        fc_out_near,
        in_up,
        out_down,
        in_down,
        out_up,
        source,
    )
    d_rows_part = d_rows_part.reshape(trees, 2, seg_len, width)
    out_part = out_part.reshape(trees, 2, seg_len, width)

    ahead = pl.BlockSpec(memory_space=pl.ANY)
    pair_maps = [shaped(trees, 1, rank, width)] * 2
    d_after, d_cross_ctx, g_down_seven, g_up_seven, hidden_sums = rows_call(
        into_cross_kernel,
        (
            d_rows_part,
            after_cross,
            cotangent,
            cross_context,
            norm_gains,
            packed,
            down,
            up,
            g_in_up,
            g_out_down,
        ),
        (None,) * 5 + (cross_out_spec,) + (None,) * 4,
        [shaped(*tokens.shape)] * 2
        + pair_maps
        + [shaped(trees, 2, rank, hidden_units // slots)],
        [
            pltpu.VMEM(tokens.shape, F32),
            pltpu.VMEM((len(levels), 2, trees, 2) + g_in_up.shape[2:], F32),
            pltpu.SemaphoreType.DMA((2,)),
            pltpu.SemaphoreType.DMA((len(levels), 2)),
            pltpu.SemaphoreType.DMA((len(levels), 2)),
        ],
        pltpu.CompilerParams(
            vmem_limit_bytes=56 * MIB, collective_id=3, has_side_effects=True
        ),
    )
    def columns(parts):
        stack = jnp.concatenate(parts, axis=1)
        return stack.reshape(stack.shape[:3] + (slots, lanes)).transpose(3, 0, 1, 2, 4)

    d_cross_q, d_cross_k, d_cross_v = cross_call(
        cross_backward_kernel, cross_queries, memory, (d_cross_ctx,), 2
    )
    out_other = swap(after(out_part[:, 1], d_cross_q))
    hidden_all = to_everyone(hidden_sums)
    layer_out = after_cross + out_part[:, 0] + out_other
    d_middle, d_context, g_down_mid, g_up_mid = rows_call(
        into_self_kernel,
        (d_cross_q, d_after, middle, context, norm_gains, packed, packed, down, up),
        (None,) * 5 + (cross_q_spec, self_out_spec, None, None),
        [shaped(*tokens.shape), shaped(slots, trees, seg_len, lanes)]
        + [shaped(trees, 2, rank, width)] * 2,
    )
    d_own_context = lax.all_to_all(d_context, ROWS, split_axis=0, concat_axis=0, tiled=True)
    d_context, d_cross_k = lax.optimization_barrier((d_context, d_cross_k))
    d_encoder, g_down_memory, g_up_memory = memory_back_call(
        encoder, d_cross_k, d_cross_v, packed, down, up
    )
    enc_rows = encoder.shape[1] // slots
    sides = d_encoder.reshape(trees, slots // pairs, pairs, enc_rows, width).transpose(2, 1, 0, 3, 4)
    other_side = lax.dynamic_index_in_dim(sides, 1 - my_y, 0, keepdims=False)
    own_side = lax.dynamic_index_in_dim(sides, my_y, 0, keepdims=False)
    enc_side = own_side + swap(other_side)
    early = summed_to_owner(
        columns(
            [
                g_down_mid,
                g_down_memory,
                g_down_seven,
                g_up_mid,
                g_up_memory,
                g_up_seven,
                g_in_down[:, None],
                g_out_up[:, None],
            ]
        ),
        ROWS,
    )

    normed_shape = (slots, trees, seg_len, width)
    d_qkv, g_down_part, g_up_qkv = self_call(
        self_backward_kernel,
        segment_order,
        parents,
        (
            qkv,
            d_own_context,
            normed_all.reshape(normed_shape),
            inner_all,
            up_own,
            out_other,
        ),
        [
            slots_spec(qkv.shape),
            slots_spec(d_own_context.shape),
            slots_spec(normed_shape),
            slots_spec(inner_all.shape),
            tree_spec(up_own.shape),
            ahead,
        ],
        [
            shaped(*qkv.shape),
            shaped(trees, 3, rank, width),
            shaped(trees, 3, rank, lanes),
        ],
        [
            slots_spec(qkv.shape),
            tree_spec((trees, 3, rank, width)),
            tree_spec((trees, 3, rank, lanes)),
        ],
        28,
    )
    late = summed_to_owner(columns([after(g_down_part, early)]), ROWS)
    enc_side, late = lax.optimization_barrier((enc_side, late))
    grad_encoder = summed_along_line(enc_side)
    grad_in_up, grad_out_down = place_call(
        place_hidden_kernel, source, (hidden_all,), [shaped(adapters, rank, hidden_units)] * 2,
        (g_down_part,),
    )
    attention_all = to_everyone(
        after(jnp.concatenate([late, g_up_qkv, early], axis=1), grad_in_up)
    )
    grad_tokens = into_tokens_call(
        d_qkv, qkv_own, tokens, d_middle, norm_gains, down_qkv, up_own
    )
    wide = shaped(adapters, projections, rank, width)
    narrow = shaped(adapters, rank, width)
    grad_down, grad_up, grad_in_down, grad_out_up = place_call(
        place_kernel, source, (attention_all,), [wide, wide, narrow, narrow]
    )
    return (
        layer_out,
        grad_tokens,
        grad_encoder,
        grad_down.swapaxes(2, 3),
        grad_up,
        grad_in_down.swapaxes(1, 2),
        grad_in_up,
        grad_out_down.swapaxes(1, 2),
        grad_out_up,
    )


def placements(rows, copies):
    spread = P(copies, rows, None)
    ins = (
        spread,
        P(copies, None, None),
        spread,
        P(copies),
        P(copies, None),
        P(copies, None),
        P(),
        P(None, rows),
        P(rows, None),
        P(None, rows),
        P(None, rows),
        P(rows, None),
        P(None, rows),
        P(rows, None),
    ) + (P(),) * 6
    return ins, (spread,) * 3 + (P(),) * 6


def solution(mesh):
    copies, rows = mesh.shape["dp"], mesh.shape["seq"]
    general = jax.shard_map(
        shards,
        mesh=mesh,
        in_specs=placements("seq", "dp")[0],
        out_specs=placements("seq", "dp")[1],
        check_vma=False,
    )
    if rows != 8 or copies % 2:
        return general
    fine = jax.sharding.Mesh(
        mesh.devices.reshape(copies // 2, 2, rows // 2, 2), ("x", "c", "z", "y")
    )
    ins, outs = placements(ROWS, COPIES)
    special = jax.shard_map(by_heads, mesh=fine, in_specs=ins, out_specs=outs, check_vma=False)

    def step(*arrays):
        one_each = arrays[0].shape[0] == arrays[14].shape[0]
        return (special if one_each else general)(*arrays)

    return step
```

```python
import functools
import math

import jax
import jax.numpy as jnp
from jax import lax
from jax.experimental import pallas as pl
from jax.experimental.pallas import tpu as pltpu
from jax.sharding import PartitionSpec as P

HEADS = 16
HD = 64


PRECISE = lax.Precision.HIGHEST
ADAPT_SCALE = 2.0
NORM_EPS = 1e-05
MASK_FILL = -1e30


def matmul(left_side, right_side):
    return jnp.dot(left_side, right_side, precision=PRECISE, preferred_element_type=jnp.float32)


def product(formula, first_operand, second_operand):
    return jnp.einsum(
        formula,
        first_operand,
        second_operand,
        precision=PRECISE,
        preferred_element_type=jnp.float32,
    )


def reach_table(segment_order, parents):
    segment_count = parents.shape[-1]
    column = lax.broadcasted_iota(jnp.int32, (segment_count, segment_count), 1)
    identity = (
        lax.broadcasted_iota(jnp.int32, (segment_count, segment_count), 0) == column
    ).astype(jnp.int32)
    parent_hot = (parents[..., :, None] == column).astype(jnp.int32)

    def extend(sweep_index, reach_rows):
        return jnp.minimum(identity + jnp.einsum("gab,gbc->gac", parent_hot, reach_rows), 1)

    initial = jnp.broadcast_to(identity, parent_hot.shape)
    reach_rows = lax.fori_loop(0, segment_count, extend, initial)
    order_hot = (segment_order[..., :, None] == column).astype(jnp.int32)
    return jnp.einsum("gsa,gab,gtb->gst", order_hot, reach_rows, order_hot)


def layer_norm(values, gain_row):
    center = values - jnp.mean(values, -1, keepdims=True)
    inverse = lax.rsqrt(jnp.mean(center * center, -1, keepdims=True) + NORM_EPS)
    normal = center * inverse
    return (normal * gain_row, normal, inverse)


def norm_back(normal, inverse, gain_row, grads):
    scaled = grads * gain_row
    mean_one = jnp.mean(scaled, -1, keepdims=True)
    mean_two = jnp.mean(scaled * normal, -1, keepdims=True)
    return inverse * (scaled - mean_one - normal * mean_two)


def gelu_back(pre_act, d_hidden):

    def activate(values):
        return jax.nn.gelu(values, approximate=True)

    return jax.vjp(activate, pre_act)[1](d_hidden)[0]


def cols_forward(inputs, shard):
    flat_rows = inputs.reshape(-1, inputs.shape[-1])
    result = matmul(flat_rows, lax.all_gather(shard, "seq", axis=1, tiled=True))
    return result.reshape(inputs.shape[:-1] + (result.shape[-1],))


def cols_back(grads, shard):
    flat_grads = grads.reshape(-1, grads.shape[-1])
    result = matmul(flat_grads, lax.all_gather(shard, "seq", axis=1, tiled=True).T)
    return result.reshape(grads.shape[:-1] + (shard.shape[0],))


def rows_forward(inputs, shard):
    flat_rows = inputs.reshape(-1, inputs.shape[-1])
    result = matmul(flat_rows, lax.all_gather(shard, "seq", axis=0, tiled=True))
    return result.reshape(inputs.shape[:-1] + (shard.shape[1],))


def rows_back(grads, shard):
    flat_grads = grads.reshape(-1, grads.shape[-1])
    result = matmul(flat_grads, lax.all_gather(shard, "seq", axis=0, tiled=True).T)
    return result.reshape(grads.shape[:-1] + (result.shape[-1],))


def adapter_apply(inputs, down_map, up_map):
    inner = product("gsd,gdr->gsr", inputs, down_map)
    return (ADAPT_SCALE * product("gsr,gro->gso", inner, up_map), inner)


def adapter_back(inputs, inner, down_map, up_map, grads):
    d_inner = ADAPT_SCALE * product("gso,gro->gsr", grads, up_map)
    grad_up = ADAPT_SCALE * product("gsr,gso->gro", inner, grads)
    grad_down = product("gsd,gsr->gdr", inputs, d_inner)
    return (product("gsr,gdr->gsd", d_inner, down_map), grad_down, grad_up)


def key_mask(my_reach, my_slot, query_index, first_key, key_count, seg_len):
    slot_count = my_reach.shape[1]
    key_index = first_key + lax.broadcasted_iota(jnp.int32, (1, key_count), 1)
    key_slot = key_index // seg_len
    slot_hot = (key_slot[0][:, None] == lax.broadcasted_iota(jnp.int32, (1, slot_count), 1)).astype(
        jnp.int32
    )
    key_allowed = jnp.einsum("gc,nc->gn", my_reach, slot_hot)
    causal_ok = (key_slot != my_slot) | (key_index <= query_index)
    allowed = (key_allowed[:, None, :] > 0) & causal_ok[None]
    return (allowed, jnp.any(key_allowed > 0))


def self_forward(queries, key_rows, value_rows, my_reach, my_slot):
    groups, seg_len, width = queries.shape
    query_heads = queries.reshape(groups, seg_len, HEADS, HD) * HD ** (-0.5)
    query_index = my_slot * seg_len + lax.broadcasted_iota(jnp.int32, (seg_len, 1), 0)
    start_state = (
        jnp.full((groups, HEADS, seg_len), MASK_FILL, jnp.float32),
        jnp.zeros((groups, HEADS, seg_len), jnp.float32),
        jnp.zeros((groups, HEADS, seg_len, HD), jnp.float32),
    )
    key_part = lax.all_gather(key_rows, "seq", axis=1, tiled=True)
    value_part = lax.all_gather(value_rows, "seq", axis=1, tiled=True)
    key_count = key_part.shape[1]
    allowed, any_allowed = key_mask(
        my_reach, my_slot, query_index, jnp.int32(0), key_count, seg_len
    )

    def attend(state):
        peak, mass, accum = state
        key_heads = key_part.reshape(groups, key_count, HEADS, HD)
        value_heads = value_part.reshape(groups, key_count, HEADS, HD)
        scores = product("gshd,gnhd->ghsn", query_heads, key_heads)
        masked = jnp.where(allowed[:, None], scores, MASK_FILL)
        new_peak = jnp.maximum(peak, jnp.max(masked, -1))
        probs = jnp.where(allowed[:, None], jnp.exp(masked - new_peak[..., None]), 0.0)
        mass = jnp.sum(probs, -1)
        accum = product("ghsn,gnhd->ghsd", probs, value_heads)
        return (new_peak, mass, accum)

    peak, mass, accum = lax.cond(any_allowed, attend, lambda state: state, start_state)
    context = (accum / mass[..., None]).transpose(0, 2, 1, 3).reshape(groups, seg_len, width)
    return (context, peak + jnp.log(mass))


def self_backward(queries, key_all, value_all, log_mass, delta, d_context, my_reach, my_slot):
    groups, seg_len, width = queries.shape
    scale = HD ** (-0.5)
    query_heads = queries.reshape(groups, seg_len, HEADS, HD) * scale
    out_heads = d_context.reshape(groups, seg_len, HEADS, HD)
    query_index = my_slot * seg_len + lax.broadcasted_iota(jnp.int32, (seg_len, 1), 0)
    total_keys = key_all.shape[1]
    block_keys = seg_len * math.gcd(total_keys // seg_len, max(1, 512 // seg_len))
    firsts = jnp.arange(total_keys // block_keys, dtype=jnp.int32) * block_keys

    def block_step(state, first_key):
        allowed, any_allowed = key_mask(
            my_reach, my_slot, query_index, first_key, block_keys, seg_len
        )

        def gradients(inner_state):
            key_heads = lax.dynamic_slice_in_dim(key_all, first_key, block_keys, 1).reshape(
                groups, block_keys, HEADS, HD
            )
            value_heads = lax.dynamic_slice_in_dim(value_all, first_key, block_keys, 1).reshape(
                groups, block_keys, HEADS, HD
            )
            scores = product("gshd,gnhd->ghsn", query_heads, key_heads)
            masked = jnp.where(allowed[:, None], scores, MASK_FILL)
            probs = jnp.where(allowed[:, None], jnp.exp(masked - log_mass[..., None]), 0.0)
            d_probs = product("gshd,gnhd->ghsn", out_heads, value_heads)
            d_scores = probs * (d_probs - delta[..., None])
            d_query = inner_state[0] + product("ghsn,gnhd->gshd", d_scores, key_heads)
            d_value_part = product("ghsn,gshd->gnhd", probs, out_heads)
            d_key_part = product("ghsn,gshd->gnhd", d_scores, query_heads)
            d_key_all = lax.dynamic_update_slice_in_dim(
                inner_state[1], d_key_part.reshape(groups, block_keys, width), first_key, 1
            )
            d_value_all = lax.dynamic_update_slice_in_dim(
                inner_state[2], d_value_part.reshape(groups, block_keys, width), first_key, 1
            )
            return (d_query, d_key_all, d_value_all)

        return (lax.cond(any_allowed, gradients, lambda inner_state: inner_state, state), None)

    zero_query = jnp.zeros((groups, seg_len, HEADS, HD), jnp.float32)
    initial = (zero_query, jnp.zeros_like(key_all), jnp.zeros_like(value_all))
    final_state, unused = lax.scan(block_step, initial, firsts)
    d_query = final_state[0].reshape(groups, seg_len, width) * scale
    return (d_query, final_state[1], final_state[2])


def cross_forward(queries, key_rows, value_rows):
    groups, seg_len, width = queries.shape
    enc_rows = key_rows.shape[1]
    query_heads = queries.reshape(groups, seg_len, HEADS, HD) * HD ** (-0.5)
    scores = product("gshd,gehd->ghse", query_heads, key_rows.reshape(groups, enc_rows, HEADS, HD))
    probs = jax.nn.softmax(scores, axis=-1)
    context = product("ghse,gehd->gshd", probs, value_rows.reshape(groups, enc_rows, HEADS, HD))
    return (context.reshape(groups, seg_len, width), probs)


def cross_backward(queries, key_rows, value_rows, probs, d_context):
    groups, seg_len, width = queries.shape
    enc_rows = key_rows.shape[1]
    scale = HD ** (-0.5)
    query_heads = queries.reshape(groups, seg_len, HEADS, HD) * scale
    key_heads = key_rows.reshape(groups, enc_rows, HEADS, HD)
    value_heads = value_rows.reshape(groups, enc_rows, HEADS, HD)
    out_heads = d_context.reshape(groups, seg_len, HEADS, HD)
    d_values = product("ghse,gshd->gehd", probs, out_heads)
    d_probs = product("gshd,gehd->ghse", out_heads, value_heads)
    d_scores = probs * (d_probs - jnp.sum(probs * d_probs, -1, keepdims=True))
    d_queries = product("ghse,gehd->gshd", d_scores, key_heads) * scale
    d_keys = product("ghse,gshd->gehd", d_scores, query_heads)
    return (
        d_queries.reshape(groups, seg_len, width),
        d_keys.reshape(groups, enc_rows, width),
        d_values.reshape(groups, enc_rows, width),
    )


def shards(
    tokens,
    encoder,
    cotangent,
    adapter_pick,
    segment_order,
    parents,
    norm_gains,
    w_qkv,
    w_self_out,
    w_cross_q,
    w_cross_kv,
    w_cross_out,
    w_fc_in,
    w_fc_out,
    attn_down,
    attn_up,
    fc_in_down,
    fc_in_up,
    fc_out_down,
    fc_out_up,
):
    groups, seg_len, width = tokens.shape
    enc_rows = encoder.shape[1]
    my_slot = lax.axis_index("seq")
    reach_rows = reach_table(segment_order, parents)
    my_reach = lax.dynamic_index_in_dim(reach_rows, my_slot, 1, keepdims=False)
    adapter_count = attn_down.shape[0]
    chosen = (
        adapter_pick[:, None] == lax.broadcasted_iota(jnp.int32, (1, adapter_count), 1)
    ).astype(jnp.float32)
    chosen_low = chosen.astype(jnp.bfloat16)

    def select(adapter_table):
        return jnp.einsum(
            "ga,a...->g...", chosen_low, adapter_table, preferred_element_type=jnp.float32
        )

    sel_down = select(attn_down)
    sel_up = select(attn_up)
    in_down = select(fc_in_down)
    in_up = select(fc_in_up)
    out_down = select(fc_out_down)
    out_up = select(fc_out_up)
    normed_one, normal_one, inverse_one = layer_norm(tokens, norm_gains[0])
    inner_qkv = product("gsd,gpdr->gspr", normed_one, sel_down[:, 0:3])
    stacked = cols_forward(normed_one, w_qkv) + ADAPT_SCALE * product(
        "gspr,gpro->gspo", inner_qkv, sel_up[:, 0:3]
    ).reshape(groups, seg_len, 3 * width)
    queries = stacked[..., :width]
    key_rows = stacked[..., width : 2 * width]
    value_rows = stacked[..., 2 * width :]
    context, log_mass = self_forward(queries, key_rows, value_rows, my_reach, my_slot)
    self_term, inner_self = adapter_apply(context, sel_down[:, 3], sel_up[:, 3])
    middle = tokens + rows_forward(context, w_self_out) + self_term
    normed_two, normal_two, inverse_two = layer_norm(middle, norm_gains[1])
    query_term, inner_cross_q = adapter_apply(normed_two, sel_down[:, 4], sel_up[:, 4])
    cross_queries = cols_forward(normed_two, w_cross_q) + query_term
    inner_memory = product("ged,gpdr->gepr", encoder, sel_down[:, 5:7])
    memory = cols_forward(encoder, w_cross_kv) + ADAPT_SCALE * product(
        "gepr,gpro->gepo", inner_memory, sel_up[:, 5:7]
    ).reshape(groups, enc_rows, 2 * width)
    cross_keys = memory[..., :width]
    cross_values = memory[..., width:]
    cross_context, cross_probs = cross_forward(cross_queries, cross_keys, cross_values)
    cross_term, inner_cross_out = adapter_apply(cross_context, sel_down[:, 7], sel_up[:, 7])
    after_cross = middle + rows_forward(cross_context, w_cross_out) + cross_term
    normed_three, normal_three, inverse_three = layer_norm(after_cross, norm_gains[2])
    inner_in = product("gsd,gdr->gsr", normed_three, in_down)
    pre_act = cols_forward(normed_three, w_fc_in) + ADAPT_SCALE * product(
        "gsr,grf->gsf", inner_in, in_up
    )
    hidden = jax.nn.gelu(pre_act, approximate=True)
    inner_out = product("gsf,gfr->gsr", hidden, out_down)
    mlp_out = rows_forward(hidden, w_fc_out) + ADAPT_SCALE * product(
        "gsr,grd->gsd", inner_out, out_up
    )
    layer_out = after_cross + mlp_out
    d_inner_out = ADAPT_SCALE * product("gsd,grd->gsr", cotangent, out_up)
    grad_out_up_tree = ADAPT_SCALE * product("gsr,gsd->grd", inner_out, cotangent)
    d_hidden = rows_back(cotangent, w_fc_out) + product("gsr,gfr->gsf", d_inner_out, out_down)
    grad_out_down_tree = product("gsf,gsr->gfr", hidden, d_inner_out)
    d_pre = gelu_back(pre_act, d_hidden)
    d_inner_in = ADAPT_SCALE * product("gsf,grf->gsr", d_pre, in_up)
    grad_in_up_tree = ADAPT_SCALE * product("gsr,gsf->grf", inner_in, d_pre)
    d_normed_three = cols_back(d_pre, w_fc_in) + product("gsr,gdr->gsd", d_inner_in, in_down)
    grad_in_down_tree = product("gsd,gsr->gdr", normed_three, d_inner_in)
    d_after = cotangent + norm_back(normal_three, inverse_three, norm_gains[2], d_normed_three)
    d_cross_ctx, grad_down_seven, grad_up_seven = adapter_back(
        cross_context, inner_cross_out, sel_down[:, 7], sel_up[:, 7], d_after
    )
    d_cross_ctx = d_cross_ctx + rows_back(d_after, w_cross_out)
    d_cross_q, d_cross_k, d_cross_v = cross_backward(
        cross_queries, cross_keys, cross_values, cross_probs, d_cross_ctx
    )
    d_normed_two, grad_down_four, grad_up_four = adapter_back(
        normed_two, inner_cross_q, sel_down[:, 4], sel_up[:, 4], d_cross_q
    )
    d_normed_two = d_normed_two + cols_back(d_cross_q, w_cross_q)
    d_middle = d_after + norm_back(normal_two, inverse_two, norm_gains[1], d_normed_two)
    d_memory = jnp.concatenate([d_cross_k, d_cross_v], axis=-1)
    d_memory_split = d_memory.reshape(groups, enc_rows, 2, width)
    d_inner_memory = ADAPT_SCALE * product("gepo,gpro->gepr", d_memory_split, sel_up[:, 5:7])
    grad_up_memory = ADAPT_SCALE * product("gepr,gepo->gpro", inner_memory, d_memory_split)
    grad_down_memory = product("ged,gepr->gpdr", encoder, d_inner_memory)
    d_encoder_local = cols_back(d_memory, w_cross_kv) + product(
        "gepr,gpdr->ged", d_inner_memory, sel_down[:, 5:7]
    )
    grad_encoder = lax.psum_scatter(d_encoder_local, "seq", scatter_dimension=1, tiled=True)
    d_context, grad_down_three, grad_up_three = adapter_back(
        context, inner_self, sel_down[:, 3], sel_up[:, 3], d_middle
    )
    d_context = d_context + rows_back(d_middle, w_self_out)
    delta = jnp.sum(
        d_context.reshape(groups, seg_len, HEADS, HD) * context.reshape(groups, seg_len, HEADS, HD),
        -1,
    ).transpose(0, 2, 1)
    key_all, value_all = (
        lax.all_gather(key_rows, "seq", axis=1, tiled=True),
        lax.all_gather(value_rows, "seq", axis=1, tiled=True),
    )
    d_queries, d_key_all, d_value_all = self_backward(
        queries, key_all, value_all, log_mass, delta, d_context, my_reach, my_slot
    )
    d_keys, d_values = (
        lax.psum_scatter(d_key_all, "seq", scatter_dimension=1, tiled=True),
        lax.psum_scatter(d_value_all, "seq", scatter_dimension=1, tiled=True),
    )
    d_stacked = jnp.concatenate([d_queries, d_keys, d_values], axis=-1)
    d_split = d_stacked.reshape(groups, seg_len, 3, width)
    d_inner_qkv = ADAPT_SCALE * product("gspo,gpro->gspr", d_split, sel_up[:, 0:3])
    grad_up_qkv = ADAPT_SCALE * product("gspr,gspo->gpro", inner_qkv, d_split)
    grad_down_qkv = product("gsd,gspr->gpdr", normed_one, d_inner_qkv)
    d_normed_one = cols_back(d_stacked, w_qkv) + product(
        "gspr,gpdr->gsd", d_inner_qkv, sel_down[:, 0:3]
    )
    grad_tokens = d_middle + norm_back(normal_one, inverse_one, norm_gains[0], d_normed_one)
    down_stack = jnp.concatenate(
        [
            grad_down_qkv,
            grad_down_three[:, None],
            grad_down_four[:, None],
            grad_down_memory,
            grad_down_seven[:, None],
        ],
        axis=1,
    )
    up_stack = jnp.concatenate(
        [
            grad_up_qkv,
            grad_up_three[:, None],
            grad_up_four[:, None],
            grad_up_memory,
            grad_up_seven[:, None],
        ],
        axis=1,
    )
    tree_parts = (
        down_stack,
        up_stack,
        grad_in_down_tree,
        grad_in_up_tree,
        grad_out_down_tree,
        grad_out_up_tree,
    )
    shapes = (
        attn_down.shape,
        attn_up.shape,
        fc_in_down.shape,
        fc_in_up.shape,
        fc_out_down.shape,
        fc_out_up.shape,
    )
    local_sums = tuple(
        (product("ga,gx->ax", chosen, part.reshape(groups, -1)).reshape(-1) for part in tree_parts)
    )
    owned = lax.psum_scatter(local_sums, ("dp", "seq"), scatter_dimension=0, tiled=True)
    full_sums = lax.all_gather(owned, ("dp", "seq"), axis=0, tiled=True)
    results = [summed.reshape(shape) for summed, shape in zip(full_sums, shapes)]
    return (
        layer_out,
        grad_tokens,
        grad_encoder,
        results[0],
        results[1],
        results[2],
        results[3],
        results[4],
        results[5],
    )


ROWS = ("z", "y")
COPIES = ("x", "c")
EVERY = ROWS + COPIES
F32 = jnp.float32
BF16 = jnp.bfloat16
MIB = 1 << 20
SWAP = [(0, 1), (1, 0)]
NN = (((1,), (0,)), ((), ()))
NT = (((1,), (1,)), ((), ()))
TN = (((0,), (0,)), ((), ()))


def split(values):
    high = values.astype(BF16)
    return high, (values - high.astype(F32)).astype(BF16)


def dot(left, right, dims=NN):
    return lax.dot_general(left, right, dims, preferred_element_type=F32)


def dot3(left, right, dims=NN):
    (left_high, left_low), (right_high, right_low) = left, right
    return (
        dot(left_high, right_high, dims)
        + dot(left_high, right_low, dims)
        + dot(left_low, right_high, dims)
    )


def dot2(left, right, dims=NN):
    return dot(left[0], right, dims) + dot(left[1], right, dims)


def adapted(rows, down, up):
    inner = dot2(rows, down, NT)
    return dot2(split(ADAPT_SCALE * inner), up), inner


def adapted_back(rows, grads, down, up):
    inner = split(ADAPT_SCALE * dot2(rows, down, NT))
    d_inner = split(ADAPT_SCALE * dot2(grads, up, NT))
    return dot2(d_inner, down), dot3(d_inner, rows, TN), dot3(inner, grads, TN)


def both(parts, where):
    return parts[0][where], parts[1][where]


def vmem(limit):
    return pltpu.CompilerParams(vmem_limit_bytes=limit * MIB)


def lasting(micros):
    return pl.CostEstimate(
        flops=int(micros * 1e9), bytes_accessed=int(micros * 3e6), transcendentals=0
    )


def shaped(*shape):
    return jax.ShapeDtypeStruct(shape, F32)


def whole_spec(shape):
    return pl.BlockSpec(shape, lambda *_: (0,) * len(shape))


def signal(target):
    pl.semaphore_signal(
        pltpu.get_barrier_semaphore(), 1, device_id=target, device_id_type=pl.DeviceIdType.MESH
    )


def greet(z, last, partners, more=0):
    for partner in partners:
        signal(partner)

    @pl.when(z > 0)
    def _():
        signal({"z": z - 1})

    @pl.when(z < last)
    def _():
        signal({"z": z + 1})

    def met():
        lines = (z > 0).astype(jnp.int32) + (z < last).astype(jnp.int32)
        pl.semaphore_wait(pltpu.get_barrier_semaphore(), len(partners) + lines + more)

    return met


def remote(source, target, sem, arrival, device):
    return pltpu.make_async_remote_copy(
        src_ref=source,
        dst_ref=target,
        send_sem=sem,
        recv_sem=arrival,
        device_id=device,
        device_id_type=pl.DeviceIdType.MESH,
    )


def start(copy):
    copy.start()


def wait_send(copy):
    copy.wait_send()


def heads_kernel(
    order_ref,
    parents_ref,
    tokens_ref,
    gains_ref,
    weight_ref,
    shard_ref,
    down_ref,
    up_ref,
    quarter_ref,
    normed_ref,
    inner_ref,
    qkv_ref,
    own_weight_ref,
    packed_ref,
    context_ref,
    below_ref,
    above_ref,
    own_context_ref,
    rows_ref,
    blocks_ref,
    w_high,
    w_low,
    keep_sem,
    block_sem,
    block_here_sem,
    block_core_sem,
    block_core_here_sem,
    here_sem,
    across_sem,
    over_first_sem,
    over_second_sem,
    line_sem,
    line_first_sem,
    line_second_sem,
    shard_here_sem,
    plane_sem,
    plane_here_sem,
    core_sem,
    core_here_sem,
    context_sem,
    context_here_sem,
    near_sem,
    near_here_sem,
):
    x, c = lax.axis_index("x"), lax.axis_index("c")
    z, y = lax.axis_index("z"), lax.axis_index("y")
    last = lax.axis_size("z") - 1
    trees, seg_len, width = tokens_ref.shape
    lanes = weight_ref.shape[1] // 3
    rank = up_ref.shape[2]
    slots = rows_ref.shape[0]
    mine, facing = 2 * x + c, 2 * (1 - x) + c

    def place(level, side):
        return level * 2 + side

    own = place(z, y)

    half = pl.ds(pl.multiple_of(c * (width // 2), width // 2), width // 2)

    def block_move(i):
        block = 3 * own + i
        target, kind = block % slots, block // slots
        source = weight_ref.at[half, i * lanes : (i + 1) * lanes]

        def sent():
            return remote(
                source,
                blocks_ref.at[kind, half],
                block_sem.at[i],
                block_here_sem.at[kind],
                {"z": target // 2, "y": target % 2},
            )

        def kept():
            return pltpu.make_async_copy(
                source, blocks_ref.at[kind, half], block_here_sem.at[kind]
            )

        return target, sent, kept

    def block_across(kind):
        block = blocks_ref.at[kind, half]
        return remote(
            block, block, block_core_sem.at[kind], block_core_here_sem.at[kind], {"c": 1 - c}
        )

    cut = shard_ref.shape[1] * 7 // 80 * 8
    spans = (slice(0, cut), slice(cut, shard_ref.shape[1]))

    def rows_move(slot, sem, device):
        return remote(rows_ref.at[slot], rows_ref.at[slot], sem, here_sem.at[slot], device)

    def shard_move(part, slot, sem, device):
        piece = packed_ref.at[slot, mine, spans[part]]
        source = shard_ref.at[mine, spans[part]] if slot is own else piece
        return remote(source, piece, sem, shard_here_sem.at[part, slot], device)

    first = functools.partial(shard_move, 0)
    second = functools.partial(shard_move, 1)

    def along(move, sems, slot, level, action):
        @pl.when(jnp.logical_and(level <= z, z < last))
        def _():
            action(move(slot, sems.at[0, slot], {"z": z + 1}))

        @pl.when(jnp.logical_and(level >= z, z > 0))
        def _():
            action(move(slot, sems.at[1, slot], {"z": z - 1}))

    def over(move, sems, slot, action):
        action(move(slot, sems.at[slot], {"y": 1 - y}))

    def beside(level):
        return own if level is z else place(level, y)

    def plane_move(part, slot):
        piece = packed_ref.at[slot, mine, spans[part]]
        return remote(
            piece, piece, plane_sem.at[part, slot], plane_here_sem.at[part, slot], {"x": 1 - x}
        )

    def core_move(part, slot, kind):
        piece = packed_ref.at[slot, facing if kind else mine, spans[part]]
        index = 2 * part + kind
        return remote(
            piece, piece, core_sem.at[index, slot], core_here_sem.at[index, slot], {"c": 1 - c}
        )

    def levels_at(hop, action):
        if hop == 0:
            action(z)
            return
        for level in (z - hop, z + hop):

            @pl.when(jnp.logical_and(level >= 0, level <= last))
            def _(level=level):
                action(level)

    def peer(step):
        target = (own + step) % slots
        return target, {"z": target // 2, "y": target % 2}

    for step in range(1, slots):
        signal(peer(step)[1])
    signal({"x": 1 - x})
    signal({"c": 1 - c})
    for tree in range(trees):
        normed = layer_norm(tokens_ref[tree], gains_ref[0:1])[0]
        rows_ref[own, tree * seg_len : (tree + 1) * seg_len] = normed
    pl.semaphore_wait(pltpu.get_barrier_semaphore(), slots + 1)
    along(rows_move, line_sem, own, z, start)
    over(rows_move, across_sem, own, start)
    for i in range(3):
        target, sent, kept = block_move(i)

        @pl.when(target != own)
        def _(sent=sent):
            sent().start()

        @pl.when(target == own)
        def _(kept=kept):
            kept().start()

    def start_shards():
        over(second, over_second_sem, own, start)
        along(first, line_first_sem, own, z, start)
        over(first, over_first_sem, own, start)
        along(second, line_second_sem, own, z, start)

    def keep(slot):
        return pltpu.make_async_copy(rows_ref.at[slot], normed_ref.at[slot], keep_sem.at[slot])

    def keep_shard():
        return pltpu.make_async_copy(shard_ref, packed_ref.at[own], keep_sem.at[slots])

    def keep_blocks():
        return pltpu.make_async_copy(blocks_ref, own_weight_ref, keep_sem.at[slots + 1])

    keep_shard().start()

    def take_blocks():
        for kind in range(3):
            block = blocks_ref.at[kind, half]
            pltpu.make_async_copy(block, block, block_here_sem.at[kind]).wait()
            block_across(kind).start()
        for kind in range(3):
            block_across(kind).wait_recv()
            where = slice(kind * lanes, (kind + 1) * lanes)
            w_high[:, where], w_low[:, where] = split(blocks_ref[kind])
        keep_blocks().start()

    def work(slot):
        keep(slot).start()
        parts = split(rows_ref[slot])
        product = dot3(parts, (w_high[...], w_low[...]))
        for tree in range(trees):
            rows = slice(tree * seg_len, (tree + 1) * seg_len)
            inner = dot2(both(parts, rows), down_ref[tree], NT)
            inner_ref[slot, tree] = inner
            inner_parts = split(ADAPT_SCALE * inner)
            for kind in range(3):
                term = dot2(
                    both(inner_parts, (slice(None), slice(kind * rank, (kind + 1) * rank))),
                    up_ref[tree, kind],
                )
                qkv_ref[slot, kind, tree] = (
                    product[rows, kind * lanes : (kind + 1) * lanes] + term
                )

    def arrived(move, slot):
        move(slot, across_sem.at[0], {"y": 1 - y}).wait_recv()

    def share(part, slot):
        plane_move(part, slot).start()
        core_move(part, slot, 0).start()

    def rows_by_line(level):
        slot = place(level, y)
        arrived(rows_move, slot)
        along(rows_move, line_sem, slot, level, start)
        over(rows_move, across_sem, slot, start)

    def first_by_line(level):
        slot = place(level, y)
        arrived(first, slot)
        along(first, line_first_sem, slot, level, start)
        over(first, over_first_sem, slot, start)
        share(0, slot)

    def second_by_line(level):
        for side in (y, 1 - y):
            slot = place(level, side)
            arrived(second, slot)
            along(second, line_second_sem, slot, level, start)
            share(1, slot)

    def rows_over(level):
        slot = place(level, 1 - y)
        arrived(rows_move, slot)
        work(slot)

    def first_over(level):
        slot = place(level, 1 - y)
        arrived(first, slot)
        share(0, slot)

    def faced(part, slot):
        plane_move(part, slot).wait_recv()
        core_move(part, slot, 1).start()

    def faced_at(hop):
        def act(level):
            if level is not z:
                faced(0, place(level, y))
                faced(1, place(level, y))
            faced(1, place(level, 1 - y))

        levels_at(hop, act)

    def attend_tree(tree):
        def slot_of(segment):
            found = jnp.int32(0)
            for slot in range(1, slots):
                found = jnp.where(order_ref[tree, slot] == segment, slot, found)
            return found

        def attend_slot(slot, carry):
            chain = ancestor_slots(order_ref, parents_ref, slot_of, tree, slot)
            own_context_ref[slot, tree] = attend(
                qkv_ref[slot, 0, tree] * HD ** (-0.5),
                jnp.concatenate([qkv_ref[where, 1, tree] for where, _ in chain], axis=0),
                jnp.concatenate([qkv_ref[where, 2, tree] for where, _ in chain], axis=0),
                chain_mask(chain, seg_len),
            )
            return carry

        lax.fori_loop(0, slots, attend_slot, 0)

    def context_move(step):
        target, device = peer(step)
        return remote(
            own_context_ref.at[target],
            context_ref.at[own],
            context_sem.at[step],
            context_here_sem.at[step],
            device,
        )

    def context_keep():
        return pltpu.make_async_copy(
            own_context_ref.at[own], context_ref.at[own], context_sem.at[0]
        )

    other = place(z, 1 - y)
    levels_at(1, rows_by_line)
    take_blocks()
    work(own)
    levels_at(1, lambda level: work(place(level, y)))
    levels_at(2, rows_by_line)
    start_shards()
    rows_over(z)
    levels_at(2, lambda level: work(place(level, y)))
    for hop in range(3, last + 1):
        levels_at(hop, rows_by_line)
    levels_at(1, rows_over)
    arrived(second, other)
    along(second, line_second_sem, other, z, start)
    share(1, other)
    levels_at(1, first_by_line)
    levels_at(1, second_by_line)
    for hop in range(3, last + 1):
        levels_at(hop, lambda level: work(place(level, y)))
    first_over(z)
    for hop in range(2, last + 1):
        levels_at(hop, rows_over)
    for tree in range(trees):
        attend_tree(tree)
        if tree == 0:
            levels_at(2, first_by_line)
            levels_at(2, second_by_line)
            levels_at(1, first_over)
            faced_at(0)
    context_keep().start()
    for step in range(1, slots):
        context_move(step).start()
    for hop in range(3, last + 1):
        levels_at(hop, first_by_line)
        levels_at(hop, second_by_line)

    def to_above():
        return remote(
            quarter_ref, below_ref, near_sem.at[0], near_here_sem.at[0], {"z": z + 1}
        )

    def to_below():
        return remote(
            quarter_ref, above_ref, near_sem.at[1], near_here_sem.at[1], {"z": z - 1}
        )

    @pl.when(z < last)
    def _():
        to_above().start()

    @pl.when(z > 0)
    def _():
        to_below().start()

    faced_at(1)
    for hop in range(2, last + 1):
        levels_at(hop, first_over)
    for hop in range(2, last + 1):
        faced_at(hop)
    for hop in range(last + 1):
        levels_at(hop, lambda level: faced(0, place(level, 1 - y)))

    @pl.when(z < last)
    def _():
        to_above().wait_send()
        to_below().wait_recv()

    @pl.when(z > 0)
    def _():
        to_below().wait_send()
        to_above().wait_recv()

    context_keep().wait()
    for step in range(1, slots):
        context_move(step).wait_send()
        context_move(step).wait_recv()
    keep_shard().wait()
    keep_blocks().wait()
    for i in range(3):
        block_across(i).wait_send()
        target, sent, _ = block_move(i)

        @pl.when(target != own)
        def _(sent=sent):
            sent().wait_send()

    def finish(slot):
        for part in range(2):
            plane_move(part, slot).wait_send()
            for kind in range(2):
                core_move(part, slot, kind).wait_recv()
                core_move(part, slot, kind).wait_send()

    def sent_on(level):
        slot = beside(level)
        along(rows_move, line_sem, slot, level, wait_send)
        over(rows_move, across_sem, slot, wait_send)
        along(first, line_first_sem, slot, level, wait_send)
        over(first, over_first_sem, slot, wait_send)
        along(second, line_second_sem, slot, level, wait_send)
        along(second, line_second_sem, place(level, 1 - y), level, wait_send)
        if level is z:
            over(second, over_second_sem, own, wait_send)
        else:
            finish(slot)
        finish(place(level, 1 - y))

    for hop in range(last + 1):
        levels_at(hop, sent_on)
    for slot in range(slots):
        keep(slot).wait()


def heads_call(order, parents, tokens, gains, weight, shard, down, up, quarter):
    trees, seg_len, width = tokens.shape
    slots = lax.axis_size(ROWS)
    lanes = weight.shape[1] // 3
    inner = down.shape[1]
    dma = pltpu.SemaphoreType.DMA
    here = pl.BlockSpec(memory_space=pltpu.VMEM)
    there = pl.BlockSpec(memory_space=pl.ANY)
    scalars = pl.BlockSpec(memory_space=pltpu.SMEM)
    return pl.pallas_call(
        heads_kernel,
        out_shape=[
            shaped(slots, trees * seg_len, width),
            shaped(slots, trees, seg_len, inner),
            shaped(slots, 3, trees, seg_len, lanes),
            shaped(3, width, lanes),
            shaped(slots, *shard.shape),
            shaped(slots, trees, seg_len, lanes),
            shaped(*quarter.shape),
            shaped(*quarter.shape),
        ],
        in_specs=[scalars, scalars, here, here, there, there, here, here, there],
        out_specs=[there, here, here] + [there] * 5,
        scratch_shapes=[
            pltpu.VMEM((slots, trees, seg_len, lanes), F32),
            pltpu.VMEM((slots, trees * seg_len, width), F32),
            pltpu.VMEM((3, width, lanes), F32),
            pltpu.VMEM((width, 3 * lanes), BF16),
            pltpu.VMEM((width, 3 * lanes), BF16),
            dma((slots + 2,)),
        ]
        + [dma((3,))] * 4
        + [dma((slots,))] * 4
        + [dma((2, slots))] * 6
        + [dma((4, slots))] * 2
        + [dma((slots,))] * 2
        + [dma((2,))] * 2,
        compiler_params=pltpu.CompilerParams(
            vmem_limit_bytes=48 * MIB, collective_id=0, has_side_effects=True
        ),
        cost_estimate=lasting(180),
    )(order, parents, tokens, gains, weight, shard, down, up, quarter)


def ancestor_slots(order_ref, parents_ref, slot_of, tree, slot, depth=4):
    segment = order_ref[tree, slot]
    chain = [(slot, None)]
    there = None
    for _ in range(depth - 1):
        parent = parents_ref[tree, segment]
        there = parent >= 0 if there is None else jnp.logical_and(there, parent >= 0)
        segment = jnp.maximum(parent, 0)
        chain.append((slot_of(segment), there))
    return chain


def fill_slot_of(order_ref, slot_of, tree, slots):
    for slot in range(slots):
        slot_of[order_ref[tree, slot]] = slot


def chain_mask(chain, seg_len):
    row = lax.broadcasted_iota(jnp.int32, (seg_len, seg_len), 0)
    column = lax.broadcasted_iota(jnp.int32, (seg_len, seg_len), 1)
    masks = [(column <= row).astype(jnp.int32)]
    for _, there in chain[1:]:
        masks.append(jnp.full((seg_len, seg_len), there.astype(jnp.int32)))
    mask = jnp.concatenate(masks, axis=1)
    return jnp.concatenate([mask, mask], axis=0) > 0


def stacked_heads(parts):
    lane = lax.broadcasted_iota(jnp.int32, parts[0].shape, 1)
    return tuple(
        jnp.concatenate(
            [jnp.where(lane < HD, part, 0), jnp.where(lane >= HD, part, 0)], axis=0
        ).astype(BF16)
        for part in parts
    )


def beside_heads(stacked):
    count = stacked.shape[0] // 2
    lane = lax.broadcasted_iota(jnp.int32, (count, stacked.shape[1]), 1)
    return jnp.where(lane < HD, stacked[:count], stacked[count:])


def by_lanes(left, right):
    wide = jnp.concatenate(left, axis=1)
    return dot(wide, jnp.concatenate([right[0], right[0]], axis=1), NT) + dot(
        left[0], right[1], NT
    )


def by_rows(left, right, dims):
    width = right[0].shape[1]
    wide = dot(left[0], jnp.concatenate(right, axis=1), dims)
    return wide[:, :width] + wide[:, width:] + dot(left[1], right[0], dims)


def pair_scores(query_parts, key_parts, mask):
    scores = by_lanes(query_parts, key_parts)
    if mask is not None:
        scores = jnp.where(mask, scores, MASK_FILL)
    return jnp.exp(scores - jnp.max(scores, -1, keepdims=True))


def attend(queries, keys, values, mask=None):
    weights = pair_scores(stacked_heads(split(queries)), split(keys), mask)
    mass = jnp.sum(weights, -1, keepdims=True)
    return beside_heads(by_rows(split(weights), split(values), NN) / mass)


def attend_back(queries, keys, values, d_context, mask=None):
    query_parts, out_parts = stacked_heads(split(queries)), stacked_heads(split(d_context))
    key_parts, value_parts = split(keys), split(values)
    weights = pair_scores(query_parts, key_parts, mask)
    weights = weights * (1.0 / jnp.sum(weights, -1, keepdims=True))
    d_weights = by_lanes(out_parts, value_parts)
    shared = jnp.sum(weights * d_weights, -1, keepdims=True)
    score_parts = split(weights * (d_weights - shared))
    return (
        beside_heads(by_rows(score_parts, key_parts, NN)) * HD ** (-0.5),
        by_rows(score_parts, query_parts, TN),
        by_rows(split(weights), out_parts, TN),
    )


def self_backward_kernel(
    order_ref,
    parents_ref,
    qkv_ref,
    d_context_ref,
    normed_ref,
    inner_ref,
    up_ref,
    _,
    d_qkv_ref,
    g_down_ref,
    g_up_ref,
    slot_of,
):
    tree = pl.program_id(0)
    slots, seg_len, pair = qkv_ref.shape[0], qkv_ref.shape[3], qkv_ref.shape[4]
    rank = up_ref.shape[2]
    fill_slot_of(order_ref, slot_of, tree, slots)
    d_qkv_ref[...] = jnp.zeros_like(d_qkv_ref)

    def one_slot(slot, carry):
        chain = ancestor_slots(order_ref, parents_ref, lambda seg: slot_of[seg], tree, slot)
        keys = jnp.concatenate([qkv_ref[where, 1, 0] for where, _ in chain], axis=0)
        values = jnp.concatenate([qkv_ref[where, 2, 0] for where, _ in chain], axis=0)
        d_queries, d_keys, d_values = attend_back(
            qkv_ref[slot, 0, 0] * HD ** (-0.5),
            keys,
            values,
            d_context_ref[slot, 0],
            mask=chain_mask(chain, seg_len),
        )
        d_qkv_ref[slot, 0, 0] += d_queries
        for entry, (where, _) in enumerate(chain):
            rows = slice(entry * seg_len, (entry + 1) * seg_len)
            d_qkv_ref[where, 1, 0] += d_keys[rows]
            d_qkv_ref[where, 2, 0] += d_values[rows]
        return carry

    lax.fori_loop(0, slots, one_slot, 0)

    inner = split(ADAPT_SCALE * inner_ref[...].reshape(slots * seg_len, 3 * rank))
    d_inner = []
    for kind in range(3):
        grads = split(d_qkv_ref[:, kind, 0].reshape(slots * seg_len, pair))
        ranks = slice(kind * rank, (kind + 1) * rank)
        d_inner.append(dot2(grads, up_ref[0, kind], NT))
        g_up_ref[0, kind] = dot3(both(inner, (slice(None), ranks)), grads, TN)
    high, low = split(ADAPT_SCALE * jnp.concatenate(d_inner, axis=1))
    rows_high, rows_low = split(normed_ref[...].reshape(slots * seg_len, -1))
    wide = dot(jnp.concatenate([high, low], axis=1), rows_high, TN)
    g_down = wide[: 3 * rank] + wide[3 * rank :] + dot(high, rows_low, TN)
    g_down_ref[0] = g_down.reshape(3, rank, -1)


def slots_spec(shape):
    lead = len(shape) - 3
    return pl.BlockSpec(
        shape[:lead] + (1,) + shape[lead + 1 :],
        lambda tree, *_: (0,) * lead + (tree, 0, 0),
    )


def tree_spec(shape):
    return pl.BlockSpec((1,) + shape[1:], lambda tree, *_: (tree,) + (0,) * (len(shape) - 1))


def self_call(kernel, order, parents, operands, in_specs, out_shape, out_specs, micros):
    trees, slots = order.shape
    return pl.pallas_call(
        kernel,
        out_shape=out_shape,
        grid_spec=pltpu.PrefetchScalarGridSpec(
            num_scalar_prefetch=2,
            grid=(trees,),
            in_specs=in_specs,
            out_specs=out_specs,
            scratch_shapes=[pltpu.SMEM((slots,), jnp.int32)],
        ),
        compiler_params=vmem(56),
        cost_estimate=lasting(micros),
    )(order, parents, *operands)


def head_pairs(ref):
    return [slice(2 * pair * HD, 2 * (pair + 1) * HD) for pair in range(ref.shape[2] // (2 * HD))]


def cross_forward_kernel(query_ref, key_ref, value_ref, _, context_ref):
    for lanes in head_pairs(query_ref):
        context_ref[0, :, lanes] = attend(
            query_ref[0, :, lanes] * HD ** (-0.5), key_ref[0, :, lanes], value_ref[0, :, lanes]
        )


def cross_backward_kernel(
    query_ref, key_ref, value_ref, d_context_ref, d_query_ref, d_key_ref, d_value_ref
):
    for lanes in head_pairs(query_ref):
        d_query_ref[0, :, lanes], d_key_ref[0, :, lanes], d_value_ref[0, :, lanes] = attend_back(
            query_ref[0, :, lanes] * HD ** (-0.5),
            key_ref[0, :, lanes],
            value_ref[0, :, lanes],
            d_context_ref[0, :, lanes],
        )


def cross_call(kernel, queries, memory, rest, long_outs, ahead=()):
    trees, seg_len, width = queries.shape
    enc_rows = memory.shape[1]
    lanes = 4 * HD
    steps = width // lanes
    short = pl.BlockSpec((1, seg_len, lanes), lambda tree, step: (tree, 0, step))
    keys = pl.BlockSpec((1, enc_rows, lanes), lambda tree, step: (tree, 0, step))
    values = pl.BlockSpec((1, enc_rows, lanes), lambda tree, step: (tree, 0, steps + step))
    return pl.pallas_call(
        kernel,
        out_shape=[shaped(trees, seg_len, width)] + [shaped(trees, enc_rows, width)] * long_outs,
        grid=(trees, steps),
        in_specs=[short, keys, values]
        + [short] * len(rest)
        + [pl.BlockSpec(memory_space=pl.ANY)] * len(ahead),
        out_specs=[short] + [keys] * long_outs,
        compiler_params=vmem(48),
        cost_estimate=lasting(32 if long_outs else 19),
    )(queries, memory, memory, *rest, *ahead)


def square(ref):
    return ref[...].reshape(-1, ref.shape[-1])


def joined(ref):
    slots, trees = ref.shape[:2]
    return jnp.concatenate(
        [
            jnp.concatenate([ref[slot, tree] for slot in range(slots)], axis=1)
            for tree in range(trees)
        ],
        axis=0,
    )


def rows_of(ref):
    return ref[...].reshape(-1, ref.shape[-1])


def tree_rows(trees, count):
    return [slice(tree * count, (tree + 1) * count) for tree in range(trees)]


def with_adapters(parts, down_ref, up_ref, entry, trees):
    count = parts[0].shape[0] // trees
    return jnp.concatenate(
        [
            adapted(both(parts, rows), down_ref[tree, entry], up_ref[tree, entry])[0]
            for tree, rows in enumerate(tree_rows(trees, count))
        ],
        axis=0,
    )


def with_adapters_back(parts, grads, down_ref, up_ref, entry, trees, g_down_ref, g_up_ref, place):
    count = parts[0].shape[0] // trees
    terms = []
    for tree, rows in enumerate(tree_rows(trees, count)):
        term, g_down_ref[tree, place], g_up_ref[tree, place] = adapted_back(
            both(parts, rows), both(grads, rows), down_ref[tree, entry], up_ref[tree, entry]
        )
        terms.append(term)
    return jnp.concatenate(terms, axis=0)


def after_self_kernel(
    context_ref, tokens_ref, gains_ref, out_ref, query_ref, down_ref, up_ref, middle_ref, cross_ref
):
    trees = tokens_ref.shape[0]
    context = split(joined(context_ref))
    middle = rows_of(tokens_ref) + dot3(context, split(square(out_ref)))
    middle = middle + with_adapters(context, down_ref, up_ref, 3, trees)
    middle_ref[...] = middle.reshape(middle_ref.shape)
    normed = split(layer_norm(middle, gains_ref[1:2])[0])
    queries = dot3(normed, split(square(query_ref)), NT)
    queries = queries + with_adapters(normed, down_ref, up_ref, 4, trees)
    cross_ref[...] = queries.reshape(cross_ref.shape)


def after_cross_kernel(
    context_ref, middle_ref, gains_ref, out_ref, down_ref, up_ref, after_ref, normed_ref
):
    trees = context_ref.shape[0]
    context = split(rows_of(context_ref))
    after = rows_of(middle_ref) + dot3(context, split(square(out_ref)))
    after = after + with_adapters(context, down_ref, up_ref, 7, trees)
    after_ref[...] = after.reshape(after_ref.shape)
    normed = layer_norm(after, gains_ref[2:3])[0]
    normed_ref[...] = normed.reshape(normed_ref.shape)


def into_cross_kernel(
    d_rows_ref,
    after_ref,
    cotangent_ref,
    context_ref,
    gains_ref,
    out_ref,
    down_ref,
    up_ref,
    g_in_up_ref,
    g_out_down_ref,
    d_after_ref,
    d_context_ref,
    g_down_ref,
    g_up_ref,
    hidden_ref,
    other_ref,
    parts_ref,
    swap_sem,
    part_sem,
    part_here_sem,
):
    trees = after_ref.shape[0]
    z, levels = lax.axis_index("z"), lax.axis_size("z")
    partner = {"y": 1 - lax.axis_index("y")}
    signal(partner)
    for step in range(1, levels):
        signal({"z": (z + step) % levels})
    pl.semaphore_wait(pltpu.get_barrier_semaphore(), levels)
    swapped = remote(
        d_rows_ref.at[:, 1], other_ref, swap_sem.at[0], swap_sem.at[1], partner
    )
    swapped.start()

    unit_grads = (g_in_up_ref, g_out_down_ref)

    def part_move(step, which):
        level = (z + step) % levels
        return remote(
            unit_grads[which].at[:, pl.ds(2 * level, 2)],
            parts_ref.at[step - 1, which],
            part_sem.at[step - 1, which],
            part_here_sem.at[step - 1, which],
            {"z": level},
        )

    moves = [(step, which) for step in range(1, levels) for which in range(2)]
    for step, which in moves:
        part_move(step, which).start()
    context = split(rows_of(context_ref))
    weight = split(square(out_ref))
    _, normal, inverse = layer_norm(rows_of(after_ref), gains_ref[2:3])
    for step, which in moves:
        part_move(step, which).wait_recv()
    for which in range(2):
        total = unit_grads[which][:, pl.ds(2 * z, 2)]
        for step in range(1, levels):
            total = total + parts_ref[step - 1, which]
        block = total.shape[3]
        for plane in range(2):
            lanes = slice(plane * block, (plane + 1) * block)
            hidden_ref[:, which, :, lanes] = total[:, plane]
    own_rows = jnp.concatenate([d_rows_ref[tree, 0] for tree in range(trees)], axis=0)
    swapped.wait()
    d_normed = own_rows + rows_of(other_ref)
    d_after = rows_of(cotangent_ref) + norm_back(normal, inverse, gains_ref[2:3], d_normed)
    d_after_ref[...] = d_after.reshape(d_after_ref.shape)
    grads = split(d_after)
    d_context = dot3(grads, weight, NT)
    d_context = d_context + with_adapters_back(
        context, grads, down_ref, up_ref, 7, trees, g_down_ref, g_up_ref, 0
    )
    d_context_ref[...] = d_context.reshape(d_context_ref.shape)
    for step, which in moves:
        part_move(step, which).wait_send()


def into_self_kernel(
    d_query_ref,
    d_after_ref,
    middle_ref,
    context_ref,
    gains_ref,
    query_ref,
    out_ref,
    down_ref,
    up_ref,
    d_middle_ref,
    d_context_ref,
    g_down_ref,
    g_up_ref,
):
    slots, trees, seg_len, lanes = context_ref.shape
    rows, normal, inverse = layer_norm(rows_of(middle_ref), gains_ref[1:2])
    grads = split(rows_of(d_query_ref))
    d_normed = dot3(grads, split(square(query_ref)))
    d_normed = d_normed + with_adapters_back(
        split(rows), grads, down_ref, up_ref, 4, trees, g_down_ref, g_up_ref, 1
    )
    d_middle = rows_of(d_after_ref) + norm_back(normal, inverse, gains_ref[1:2], d_normed)
    d_middle_ref[...] = d_middle.reshape(d_middle_ref.shape)
    grads = split(d_middle)
    context = split(joined(context_ref))
    d_context = dot3(grads, split(square(out_ref)), NT)
    d_context = d_context + with_adapters_back(
        context, grads, down_ref, up_ref, 3, trees, g_down_ref, g_up_ref, 0
    )
    for slot in range(slots):
        for tree in range(trees):
            d_context_ref[slot, tree] = d_context[
                tree * seg_len : (tree + 1) * seg_len, slot * lanes : (slot + 1) * lanes
            ]


def packed_spec(packed, first, count):
    return pl.BlockSpec(
        packed.shape[:2] + (count, packed.shape[3]), lambda *_: (0, 0, first // count, 0)
    )


def rows_call(kernel, operands, specs, out_shape, scratch=(), params=None):
    return pl.pallas_call(
        kernel,
        out_shape=out_shape,
        grid=(1,),
        in_specs=[
            whole_spec(operand.shape) if spec is None else spec
            for operand, spec in zip(operands, specs)
        ],
        out_specs=[whole_spec(out.shape) for out in out_shape],
        scratch_shapes=scratch,
        compiler_params=params or vmem(56),
        cost_estimate=lasting(10),
    )(*operands)


def memory_kernel(encoder_ref, weight_ref, down_ref, up_ref, memory_ref, row_high, row_low, inner):
    trees, rank = down_ref.shape[0], down_ref.shape[2]
    step = pl.program_id(0)
    half = pl.num_programs(0) // 2
    lanes = memory_ref.shape[2]
    count = encoder_ref.shape[1]

    @pl.when(step == 0)
    def _():
        row_high[...], row_low[...] = split(rows_of(encoder_ref))
        for tree, rows in enumerate(tree_rows(trees, count)):
            for kind in range(2):
                parts = (row_high[rows], row_low[rows])
                inner[kind, rows] = jnp.concatenate(
                    split(ADAPT_SCALE * dot2(parts, down_ref[tree, 5 + kind], NT)), axis=1
                )

    result = dot3((row_high[...], row_low[...]), split(square(weight_ref)), NT)
    kind = step // half
    for tree, rows in enumerate(tree_rows(trees, count)):
        up = up_ref[tree, 0]
        term = dot(inner[kind, rows], jnp.concatenate([up, up], axis=0))
        memory_ref[tree] = result[rows] + term


def memory_call(encoder, packed, down, up):
    trees, count, width = encoder.shape
    rank = down.shape[2]
    slots, copies = packed.shape[:2]
    lanes = 2 * width // slots
    half = slots // 2
    return pl.pallas_call(
        memory_kernel,
        out_shape=shaped(trees, count, 2 * width),
        grid=(slots,),
        in_specs=[
            whole_spec(encoder.shape),
            pl.BlockSpec((1, copies, lanes // copies, width), lambda step: (step, 0, 0, 0)),
            whole_spec(down.shape),
            pl.BlockSpec((trees, 1, rank, lanes), lambda step: (0, 5 + step // half, 0, step % half)),
        ],
        out_specs=pl.BlockSpec((trees, count, lanes), lambda step: (0, 0, step)),
        scratch_shapes=[
            pltpu.VMEM((trees * count, width), BF16),
            pltpu.VMEM((trees * count, width), BF16),
            pltpu.VMEM((2, trees * count, 2 * rank), BF16),
        ],
        compiler_params=vmem(56),
        cost_estimate=lasting(22),
    )(encoder, packed, down, up)


def memory_back_kernel(
    encoder_ref,
    d_key_ref,
    d_value_ref,
    weight_ref,
    down_ref,
    up_ref,
    d_encoder_ref,
    g_down_ref,
    g_up_ref,
    row_high,
    row_low,
    inner,
    d_inner,
):
    trees, rank = down_ref.shape[0], down_ref.shape[2]
    step = pl.program_id(0)
    half = pl.num_programs(0) // 2
    count = encoder_ref.shape[1]
    spans = tree_rows(trees, count)

    @pl.when(step == 0)
    def _():
        row_high[...], row_low[...] = split(rows_of(encoder_ref))
        d_encoder_ref[...] = jnp.zeros_like(d_encoder_ref)
        d_inner[...] = jnp.zeros_like(d_inner)
        for tree, rows in enumerate(spans):
            for kind in range(2):
                parts = (row_high[rows], row_low[rows])
                inner[kind, rows] = jnp.concatenate(
                    split(ADAPT_SCALE * dot2(parts, down_ref[tree, 5 + kind], NT)), axis=1
                )

    kind = step // half
    grads = split(jnp.where(kind == 0, rows_of(d_key_ref), rows_of(d_value_ref)))
    d_encoder_ref[...] += dot3(grads, split(square(weight_ref))).reshape(d_encoder_ref.shape)
    for tree, rows in enumerate(spans):
        own = both(grads, rows)
        d_inner[kind, rows] += dot2(own, up_ref[tree, 0], NT)
        high, low = inner[kind, rows, :rank], inner[kind, rows, rank:]
        g_up_ref[tree, 0] = dot3((high, low), own, TN)

    @pl.when(step == 2 * half - 1)
    def _():
        for tree, rows in enumerate(spans):
            parts = (row_high[rows], row_low[rows])
            for kind in range(2):
                own = split(ADAPT_SCALE * d_inner[kind, rows])
                d_encoder_ref[tree] += dot2(own, down_ref[tree, 5 + kind])
                g_down_ref[tree, kind] = dot3(own, parts, TN)


def memory_back_call(encoder, d_keys, d_values, packed, down, up):
    trees, count, width = encoder.shape
    rank = down.shape[2]
    slots, copies = packed.shape[:2]
    lanes = 2 * width // slots
    half = slots // 2
    kind_spec = pl.BlockSpec((trees, 1, rank, lanes), lambda step: (0, step // half, 0, step % half))
    return pl.pallas_call(
        memory_back_kernel,
        out_shape=[
            shaped(trees, count, width),
            shaped(trees, 2, rank, width),
            shaped(trees, 2, rank, width),
        ],
        grid=(slots,),
        in_specs=[
            whole_spec(encoder.shape),
            pl.BlockSpec((trees, count, lanes), lambda step: (0, 0, jnp.minimum(step, half - 1))),
            pl.BlockSpec((trees, count, lanes), lambda step: (0, 0, jnp.maximum(step - half, 0))),
            pl.BlockSpec((1, copies, lanes // copies, width), lambda step: (step, 0, 0, 0)),
            whole_spec(down.shape),
            pl.BlockSpec((trees, 1, rank, lanes), lambda step: (0, 5 + step // half, 0, step % half)),
        ],
        out_specs=[
            whole_spec((trees, count, width)),
            whole_spec((trees, 2, rank, width)),
            kind_spec,
        ],
        scratch_shapes=[
            pltpu.VMEM((trees * count, width), BF16),
            pltpu.VMEM((trees * count, width), BF16),
            pltpu.VMEM((2, trees * count, 2 * rank), BF16),
            pltpu.VMEM((2, trees * count, rank), F32),
        ],
        compiler_params=vmem(56),
        cost_estimate=lasting(31),
    )(encoder, d_keys, d_values, packed, down, up)


def nearest(z, last, turn):
    orders = [
        sorted((level for level in range(last + 1) if level != own), key=lambda level: abs(level - own))
        for own in range(last + 1)
    ]
    level = orders[0][turn]
    for own in range(1, last + 1):
        level = jnp.where(z == own, orders[own][turn], level)
    return level


def feed_forward_kernel(
    rows_ref,
    cot_ref,
    w_in_ref,
    w_out_ref,
    below_ref,
    above_ref,
    in_up_ref,
    out_down_ref,
    in_down_ref,
    out_up_ref,
    _,
    out_ref,
    d_rows_ref,
    g_in_up_ref,
    g_out_down_ref,
    g_in_down_ref,
    g_out_up_ref,
    shards_ref,
    w_in_buf,
    row_high,
    row_low,
    cot_high,
    cot_low,
    inner_in,
    d_inner_out,
    inner_in_t,
    d_inner_out_t,
    inner_out,
    d_inner_in,
    own_sem,
    w_in_sem,
    line_sem,
    line_here_sem,
    plane_sem,
    plane_here_sem,
    core_sem,
    core_here_sem,
    near_sem,
):
    trees, rank = in_up_ref.shape[0], in_up_ref.shape[2]
    spans = tree_rows(trees, rows_ref.shape[0] // trees)
    x, c, z = lax.axis_index("x"), lax.axis_index("c"), lax.axis_index("z")
    last = lax.axis_size("z") - 1
    block = shards_ref.shape[2]
    part = block // 2
    levels = [nearest(z, last, turn) for turn in range(last)]

    def piece(level, plane, core):
        return shards_ref.at[level, plane, pl.ds(pl.multiple_of(core * part, part), part)]

    def line_move(turn, target):
        level = levels[turn]
        here = piece(level, x, c)
        return remote(here, here, line_sem.at[turn], line_here_sem.at[level], {"z": target})

    def plane_move(turn):
        here = piece(levels[turn], x, c)
        return remote(here, here, plane_sem.at[turn], plane_here_sem.at[turn], {"x": 1 - x})

    def core_move(turn, kind):
        here = piece(levels[turn], x if kind == 0 else 1 - x, c)
        index = 2 * turn + kind
        return remote(here, here, core_sem.at[index], core_here_sem.at[index], {"c": 1 - c})

    def near_copy(source, level, index):
        return pltpu.make_async_copy(source, piece(level, x, c), near_sem.at[index])

    def near(action):
        @pl.when(z > 0)
        def _():
            action(near_copy(below_ref, z - 1, 0))

        @pl.when(z < last)
        def _():
            action(near_copy(above_ref, z + 1, 1))

    def wait_line(turn):
        @pl.when(jnp.abs(levels[turn] - z) > 1)
        def _():
            line_move(turn, z).wait_recv()

    def passing(turn, action):
        level = levels[turn]

        @pl.when(jnp.logical_and(level < z, z < last))
        def _():
            action(line_move(turn, z + 1))

        @pl.when(jnp.logical_and(level > z, z > 0))
        def _():
            action(line_move(turn, z - 1))

    def relay(turn):
        wait_line(turn)
        passing(turn, lambda copy: copy.start())
        plane_move(turn).start()
        core_move(turn, 0).start()

    def relay_plane(turn):
        plane_move(turn).wait_recv()
        core_move(turn, 1).start()

    order = [(-1, 0), (-1, 1), (0, 0), (1, 0), (0, 1), (2, 0), (1, 1), (2, 1)]

    def chosen(step):
        level, plane = z, x
        for index, (turn, other) in enumerate(order):
            hit = step == index
            level = jnp.where(hit, z if turn < 0 else levels[turn], level)
            plane = jnp.where(hit, 1 - x if other else x, plane)
        return level, plane

    def w_in_copy(step):
        level, plane = chosen(step)
        columns = pl.ds(pl.multiple_of(plane * block, block), block)
        slot = lax.rem(step, 2)
        return pltpu.make_async_copy(
            w_in_ref.at[level, :, columns], w_in_buf.at[slot], w_in_sem.at[slot]
        )

    def own_copy(plane):
        return pltpu.make_async_copy(
            w_out_ref.at[pl.ds(plane * block, block)], shards_ref.at[z, plane], own_sem.at[plane]
        )

    met = greet(z, last, [{"x": 1 - x}, {"c": 1 - c}])
    for plane in range(2):
        own_copy(plane).start()
    w_in_copy(0).start()
    near(start)
    met()
    near(lambda copy: copy.wait())
    relay(0)

    row_high[...], row_low[...] = split(rows_ref[...])
    cot_high[...], cot_low[...] = split(cot_ref[...])
    out_ref[...] = jnp.zeros_like(out_ref)
    d_rows_ref[...] = jnp.zeros_like(d_rows_ref)
    inner_out[...] = jnp.zeros_like(inner_out)
    d_inner_in[...] = jnp.zeros_like(d_inner_in)
    for tree, own in enumerate(spans):
        rows = (row_high[own], row_low[own])
        cots = (cot_high[own], cot_low[own])
        down, up = in_down_ref[tree], out_up_ref[tree]
        inner_in[own] = jnp.concatenate(split(ADAPT_SCALE * dot2(rows, down, NT)), axis=1)
        d_inner_out[own] = jnp.concatenate(split(ADAPT_SCALE * dot2(cots, up, NT)), axis=1)
        inner_in_t[tree] = jnp.concatenate(
            split(ADAPT_SCALE * (dot(down, rows[0], NT) + dot(down, rows[1], NT))), axis=0
        )
        d_inner_out_t[tree] = jnp.concatenate(
            split(ADAPT_SCALE * (dot(up, cots[0], NT) + dot(up, cots[1], NT))), axis=0
        )
    for plane in range(2):
        own_copy(plane).wait()

    def work(step, carry):
        level, plane = chosen(step)
        entry = level * 2 + plane

        @pl.when(step + 1 < len(order))
        def _():
            w_in_copy(step + 1).start()

        @pl.when(step == 2)
        def _():
            core_move(0, 0).wait_recv()
            relay(1)
            relay_plane(0)

        @pl.when(step == 3)
        def _():
            core_move(1, 0).wait_recv()

        @pl.when(step == 4)
        def _():
            core_move(0, 1).wait_recv()

        @pl.when(step == 5)
        def _():
            relay(2)
            relay_plane(1)
            core_move(2, 0).wait_recv()

        @pl.when(step == 6)
        def _():
            core_move(1, 1).wait_recv()

        @pl.when(step == 7)
        def _():
            relay_plane(2)
            core_move(2, 1).wait_recv()

        w_in_copy(step).wait()
        rows = (row_high[...], row_low[...])
        cots = (cot_high[...], cot_low[...])
        w_in = split(w_in_buf[lax.rem(step, 2)])
        w_out = split(shards_ref[level, plane])
        in_up = [in_up_ref[tree, entry] for tree in range(trees)]
        out_down = [out_down_ref[tree, entry] for tree in range(trees)]

        def per_tree(inner, maps):
            return jnp.concatenate(
                [
                    dot(inner[own], jnp.concatenate([maps[tree], maps[tree]], axis=0))
                    for tree, own in enumerate(spans)
                ],
                axis=0,
            )

        pre_act = dot3(rows, w_in) + per_tree(inner_in, in_up)
        root = math.sqrt(2.0 / math.pi)
        squared = pre_act * pre_act
        bend = jnp.tanh(root * (pre_act + 0.044715 * (squared * pre_act)))
        hidden = 0.5 * pre_act * (1.0 + bend)
        slope = 0.5 * (1.0 + bend) + 0.5 * pre_act * (1.0 - bend * bend) * (
            root * (1.0 + 3 * 0.044715 * squared)
        )
        hidden_parts = split(hidden)
        out_ref[...] += dot3(hidden_parts, w_out)
        d_hidden = dot3(cots, w_out, NT) + per_tree(d_inner_out, out_down)
        pre_parts = split(d_hidden * slope)
        d_rows_ref[...] += dot3(pre_parts, w_in, NT)

        for tree, own in enumerate(spans):
            hidden_own = both(hidden_parts, own)
            pre_own = both(pre_parts, own)
            inner_out[own] += dot2(hidden_own, out_down[tree], NT)
            d_inner_in[own] += dot2(pre_own, in_up[tree], NT)
            pair = dot(inner_in_t[tree], pre_own[0])
            g_in_up_ref[tree, entry] = (
                pair[:rank] + pair[rank:] + dot(inner_in_t[tree, :rank], pre_own[1])
            )
            pair = dot(d_inner_out_t[tree], hidden_own[0])
            g_out_down_ref[tree, entry] = (
                pair[:rank] + pair[rank:] + dot(d_inner_out_t[tree, :rank], hidden_own[1])
            )
        return carry

    lax.fori_loop(0, len(order), work, 0)

    for tree, own in enumerate(spans):
        inner = split(ADAPT_SCALE * inner_out[own])
        d_inner = split(ADAPT_SCALE * d_inner_in[own])
        out_ref[own] += dot2(inner, out_up_ref[tree])
        d_rows_ref[own] += dot2(d_inner, in_down_ref[tree])
        g_in_down_ref[tree] = dot3(d_inner, (row_high[own], row_low[own]), TN)
        g_out_up_ref[tree] = dot3(inner, (cot_high[own], cot_low[own]), TN)

    for turn in range(last):
        passing(turn, lambda copy: copy.wait_send())
        plane_move(turn).wait_send()
        core_move(turn, 0).wait_send()
        core_move(turn, 1).wait_send()


def feed_forward(rows, cots, w_in, w_out, near, in_up, out_down, in_down, out_up, ahead):
    count, width = rows.shape
    levels, _, units = w_in.shape
    block = units // 2
    trees, entries, rank = in_up.shape[:3]
    dma = pltpu.SemaphoreType.DMA
    here = pl.BlockSpec(memory_space=pltpu.VMEM)
    there = pl.BlockSpec(memory_space=pl.ANY)
    return pl.pallas_call(
        feed_forward_kernel,
        out_shape=[shaped(count, width)] * 2
        + [shaped(*in_up.shape), shaped(*out_down.shape)]
        + [shaped(*in_down.shape), shaped(*out_up.shape)],
        in_specs=[here, here] + [there] * 4 + [here] * 4 + [there],
        out_specs=[here] * 6,
        scratch_shapes=[
            pltpu.VMEM((levels, 2, block, width), F32),
            pltpu.VMEM((2, width, block), F32),
        ]
        + [pltpu.VMEM((count, width), BF16)] * 4
        + [pltpu.VMEM((count, 2 * rank), BF16)] * 2
        + [pltpu.VMEM((trees, 2 * rank, count // trees), BF16)] * 2
        + [pltpu.VMEM((count, rank), F32)] * 2
        + [
            dma((2,)),
            dma((2,)),
            dma((levels - 1,)),
            dma((levels,)),
            dma((levels - 1,)),
            dma((levels - 1,)),
            dma((2 * levels - 2,)),
            dma((2 * levels - 2,)),
            dma((2,)),
        ],
        compiler_params=pltpu.CompilerParams(
            vmem_limit_bytes=60 * MIB, collective_id=2, has_side_effects=True
        ),
        cost_estimate=lasting(110),
    )(rows, cots, w_in, w_out, *near, in_up, out_down, in_down, out_up, ahead)


def by_distance(z, last, turn):
    orders = [sorted(range(last + 1), key=lambda level: -abs(level - own)) for own in range(last + 1)]
    level = orders[0][turn]
    for own in range(1, last + 1):
        level = jnp.where(z == own, orders[own][turn], level)
    return level


def into_tokens_kernel(
    d_qkv_ref,
    weight_ref,
    tokens_ref,
    d_middle_ref,
    gains_ref,
    down_ref,
    up_ref,
    out_ref,
    own_ref,
    sent_ref,
    across_ref,
    rising_ref,
    falling_ref,
    w_high,
    w_low,
    sent_sem,
    line_sem,
    across_sem,
    rising_sem,
    falling_sem,
):
    z, y = lax.axis_index("z"), lax.axis_index("y")
    last = lax.axis_size("z") - 1
    trees, rank = up_ref.shape[0], up_ref.shape[2]
    seg_len, lanes = d_qkv_ref.shape[3], d_qkv_ref.shape[4]
    met = greet(z, last, [{"y": 1 - y}])
    for kind in range(3):
        where = slice(kind * lanes, (kind + 1) * lanes)
        w_high[:, where], w_low[:, where] = split(weight_ref[kind])
    met()

    def partial(level, side, ref):
        slot = level * 2 + side
        grads = split(
            jnp.concatenate(
                [
                    jnp.concatenate([d_qkv_ref[slot, kind, tree] for kind in range(3)], axis=1)
                    for tree in range(trees)
                ],
                axis=0,
            )
        )
        total = dot3(grads, (w_high[...], w_low[...]), NT)
        for tree, rows in enumerate(tree_rows(trees, seg_len)):
            inner = jnp.concatenate(
                [
                    dot2(
                        both(grads, (rows, slice(kind * lanes, (kind + 1) * lanes))),
                        up_ref[tree, kind],
                        NT,
                    )
                    for kind in range(3)
                ],
                axis=1,
            )
            ref[level, rows] = total[rows] + dot2(split(ADAPT_SCALE * inner), down_ref[tree])

    def move(source, target, level, sem, arrival, device):
        return pltpu.make_async_remote_copy(
            src_ref=source.at[level],
            dst_ref=target.at[level],
            send_sem=sem,
            recv_sem=arrival.at[level],
            device_id=device,
            device_id_type=pl.DeviceIdType.MESH,
        )

    def across(turn, level):
        return move(sent_ref, across_ref, level, sent_sem.at[turn], across_sem, {"y": 1 - y})

    def rising(turn, level):
        return move(own_ref, rising_ref, level, line_sem.at[turn], rising_sem, {"z": z + 1})

    def falling(turn, level):
        return move(own_ref, falling_ref, level, line_sem.at[turn], falling_sem, {"z": z - 1})

    levels = [by_distance(z, last, turn) for turn in range(last + 1)]
    for turn, level in enumerate(levels):
        partial(level, 1 - y, sent_ref)
        across(turn, level).start()
    for level in levels:
        partial(level, y, own_ref)
    for turn, level in enumerate(levels):
        across(turn, level).wait_recv()
        own_ref[level] += across_ref[level]

        @pl.when(jnp.logical_and(level >= z, z > 0))
        def _(level=level):
            rising(0, level).wait_recv()
            own_ref[level] += rising_ref[level]

        @pl.when(jnp.logical_and(level <= z, z < last))
        def _(level=level):
            falling(0, level).wait_recv()
            own_ref[level] += falling_ref[level]

        @pl.when(level > z)
        def _(turn=turn, level=level):
            rising(turn, level).start()

        @pl.when(level < z)
        def _(turn=turn, level=level):
            falling(turn, level).start()

    _, normal, inverse = layer_norm(rows_of(tokens_ref), gains_ref[0:1])
    grad = rows_of(d_middle_ref) + norm_back(normal, inverse, gains_ref[0:1], own_ref[z])
    out_ref[...] = grad.reshape(out_ref.shape)
    for turn, level in enumerate(levels):
        across(turn, level).wait_send()

        @pl.when(level > z)
        def _(turn=turn, level=level):
            rising(turn, level).wait_send()

        @pl.when(level < z)
        def _(turn=turn, level=level):
            falling(turn, level).wait_send()


def into_tokens_call(d_qkv, weight, tokens, d_middle, gains, down, up):
    trees, seg_len, width = tokens.shape
    levels = lax.axis_size("z")
    lanes = weight.shape[2]
    dma = pltpu.SemaphoreType.DMA((levels,))
    here = pl.BlockSpec(memory_space=pltpu.VMEM)
    return pl.pallas_call(
        into_tokens_kernel,
        out_shape=shaped(*tokens.shape),
        in_specs=[here] * 7,
        out_specs=here,
        scratch_shapes=[pltpu.VMEM((levels, trees * seg_len, width), F32)] * 5
        + [pltpu.VMEM((width, 3 * lanes), BF16)] * 2
        + [dma] * 5,
        compiler_params=pltpu.CompilerParams(
            vmem_limit_bytes=56 * MIB, collective_id=1, has_side_effects=True
        ),
        cost_estimate=lasting(110),
    )(d_qkv, weight, tokens, d_middle, gains, down, up)


def place_kernel(source_ref, parts_ref, down_ref, up_ref, in_down_ref, out_up_ref):
    places = [(down_ref, entry) for entry in range(3)] + [(up_ref, entry) for entry in range(3)]
    places += [(down_ref, entry) for entry in range(3, 8)]
    places += [(up_ref, entry) for entry in range(3, 8)]
    span = parts_ref.shape[5]
    for owner in range(parts_ref.shape[1]):
        lanes = slice(owner * span, (owner + 1) * span)
        for part, (ref, entry) in enumerate(places):
            ref[0, entry, :, lanes] = parts_ref[0, owner, 0, part]
        in_down_ref[0, :, lanes] = parts_ref[0, owner, 0, len(places)]
        out_up_ref[0, :, lanes] = parts_ref[0, owner, 0, len(places) + 1]


def place_hidden_kernel(source_ref, parts_ref, _, in_up_ref, out_down_ref):
    for owner in range(parts_ref.shape[1]):
        units = parts_ref.shape[5]
        lanes = slice(owner * units, (owner + 1) * units)
        in_up_ref[0, :, lanes] = parts_ref[0, owner, 0, 0]
        out_down_ref[0, :, lanes] = parts_ref[0, owner, 0, 1]


def place_call(kernel, source, arrays, out_shape, ahead=()):
    def chosen(array):
        groups = array.shape[2]
        return pl.BlockSpec(
            (1, array.shape[1], 1) + array.shape[3:],
            lambda entry, tree: (tree[entry] // groups, 0, tree[entry] % groups, 0, 0, 0),
        )

    return pl.pallas_call(
        kernel,
        out_shape=out_shape,
        grid_spec=pltpu.PrefetchScalarGridSpec(
            num_scalar_prefetch=1,
            grid=(out_shape[0].shape[0],),
            in_specs=[chosen(array) for array in arrays]
            + [pl.BlockSpec(memory_space=pl.ANY)] * len(ahead),
            out_specs=[tree_spec(out.shape) for out in out_shape],
        ),
        compiler_params=vmem(48),
        cost_estimate=lasting(9),
    )(source, *arrays, *ahead)


def my_quarter(shard):
    part = shard.shape[0] // lax.axis_size(COPIES)
    return lax.dynamic_slice_in_dim(shard, lax.axis_index(COPIES) * part, part, 0)


def gather_pair_half(quarter, shape):
    whole = lax.all_gather(quarter, ("z",) + COPIES, axis=0, tiled=True)
    return whole.reshape((-1,) + shape)


def pick(table, adapter_pick):
    return jnp.stack(
        [
            lax.dynamic_index_in_dim(table, adapter_pick[tree], 0, keepdims=False)
            for tree in range(adapter_pick.shape[0])
        ]
    )


def after(array, other):
    return array + 0.0 * other[(0,) * other.ndim]


def swap(array):
    return lax.ppermute(array, "y", SWAP)


def summed_to_owner(parts, axes):
    return jnp.sum(lax.all_to_all(parts, axes, split_axis=0, concat_axis=0, tiled=True), axis=0)


def summed_along_line(parts):
    levels = lax.axis_size("z")
    z = lax.axis_index("z")
    total = lax.dynamic_index_in_dim(parts, z, 0, keepdims=False)
    for other in range(1, levels):
        sent = lax.dynamic_index_in_dim(parts, z ^ other, 0, keepdims=False)
        total = total + lax.ppermute(
            sent, "z", [(level, level ^ other) for level in range(levels)]
        )
    return total


def to_everyone(array):
    everyone = lax.all_gather(array, COPIES + ROWS, axis=0, tiled=False)
    return everyone.reshape((-1, lax.axis_size(ROWS)) + array.shape)


def by_heads(
    tokens,
    encoder,
    cotangent,
    adapter_pick,
    segment_order,
    parents,
    norm_gains,
    w_qkv,
    w_self_out,
    w_cross_q,
    w_cross_kv,
    w_cross_out,
    w_fc_in,
    w_fc_out,
    attn_down,
    attn_up,
    fc_in_down,
    fc_in_up,
    fc_out_down,
    fc_out_up,
):
    trees, seg_len, width = tokens.shape
    slots = lax.axis_size(ROWS)
    copies = lax.axis_size(COPIES)
    adapters, projections, rank = attn_up.shape[:3]
    hidden_units = fc_in_up.shape[2]
    pairs = lax.axis_size("y")
    me, my_y = lax.axis_index(ROWS), lax.axis_index("y")
    lanes = width // slots

    down = pick(attn_down.swapaxes(2, 3), adapter_pick)
    up = pick(attn_up, adapter_pick)
    in_down = pick(fc_in_down.swapaxes(1, 2), adapter_pick)
    out_up = pick(fc_out_up, adapter_pick)

    def half_columns(table):
        picked = pick(table, adapter_pick).reshape(
            trees, rank, slots // pairs, pairs, hidden_units // slots
        )
        half = lax.dynamic_index_in_dim(picked, my_y, 3, keepdims=False)
        return half.reshape(trees, rank, slots, -1).swapaxes(1, 2)

    in_up = half_columns(fc_in_up)
    out_down = half_columns(fc_out_down.swapaxes(1, 2))
    down_qkv = down[:, 0:3].reshape(trees, 3 * rank, width)
    up_own = lax.dynamic_slice_in_dim(up[:, 0:3], me * lanes, lanes, 3)

    shard = jnp.concatenate(
        [
            w.reshape(copies, -1, width)
            for w in (w_cross_kv.T, w_self_out, w_cross_out, w_cross_q.T)
        ],
        axis=1,
    )
    normed_all, inner_all, qkv, qkv_own, packed, context, *fc_out_near = heads_call(
        segment_order,
        parents,
        tokens,
        norm_gains,
        w_qkv,
        shard,
        down_qkv,
        up_own,
        my_quarter(w_fc_out),
    )
    row = width // (slots * copies)
    self_out_spec = packed_spec(packed, 2 * row, row)
    cross_out_spec = packed_spec(packed, 3 * row, row)
    cross_q_spec = packed_spec(packed, 4 * row, row)

    fc_in_late, qkv = lax.optimization_barrier((my_quarter(w_fc_in), qkv))
    fc_in_half = gather_pair_half(fc_in_late, w_fc_in.shape)
    levels = range(lax.axis_size("z") - 1)
    cotangent_other = swap(after(cotangent, context))
    memory = memory_call(encoder, packed, down, up)
    middle, cross_queries = rows_call(
        after_self_kernel,
        (context, tokens, norm_gains, packed, packed, down, up),
        (None, None, None, self_out_spec, cross_q_spec, None, None),
        [shaped(*tokens.shape)] * 2,
    )
    (cross_context,) = cross_call(
        cross_forward_kernel, cross_queries, memory, (), 0, (cotangent_other,)
    )
    after_cross, normed_three = rows_call(
        after_cross_kernel,
        (cross_context, middle, norm_gains, packed, down, up),
        (None, None, None, cross_out_spec, None, None),
        [shaped(*tokens.shape)] * 2,
    )

    all_picks = lax.all_gather(adapter_pick, COPIES, axis=0, tiled=True)
    entry = lax.broadcasted_iota(jnp.int32, (adapters, 1), 0)
    tree_index = lax.broadcasted_iota(jnp.int32, (1, all_picks.shape[0]), 1)
    source = jnp.sum(jnp.where(entry == all_picks[None, :], tree_index, 0), axis=1)
    def paired(own_rows, other_rows):
        return jnp.stack([own_rows, other_rows], axis=1).reshape(-1, width)

    out_part, d_rows_part, g_in_up, g_out_down, g_in_down, g_out_up = feed_forward(
        paired(normed_three, swap(normed_three)),
        paired(cotangent, cotangent_other),
        fc_in_half,
        w_fc_out,
        fc_out_near,
        in_up,
        out_down,
        in_down,
        out_up,
        source,
    )
    d_rows_part = d_rows_part.reshape(trees, 2, seg_len, width)
    out_part = out_part.reshape(trees, 2, seg_len, width)

    ahead = pl.BlockSpec(memory_space=pl.ANY)
    pair_maps = [shaped(trees, 1, rank, width)] * 2
    d_after, d_cross_ctx, g_down_seven, g_up_seven, hidden_sums = rows_call(
        into_cross_kernel,
        (
            d_rows_part,
            after_cross,
            cotangent,
            cross_context,
            norm_gains,
            packed,
            down,
            up,
            g_in_up,
            g_out_down,
        ),
        (None,) * 5 + (cross_out_spec,) + (None,) * 4,
        [shaped(*tokens.shape)] * 2
        + pair_maps
        + [shaped(trees, 2, rank, hidden_units // slots)],
        [
            pltpu.VMEM(tokens.shape, F32),
            pltpu.VMEM((len(levels), 2, trees, 2) + g_in_up.shape[2:], F32),
            pltpu.SemaphoreType.DMA((2,)),
            pltpu.SemaphoreType.DMA((len(levels), 2)),
            pltpu.SemaphoreType.DMA((len(levels), 2)),
        ],
        pltpu.CompilerParams(
            vmem_limit_bytes=56 * MIB, collective_id=3, has_side_effects=True
        ),
    )
    def columns(parts):
        stack = jnp.concatenate(parts, axis=1)
        return stack.reshape(stack.shape[:3] + (slots, lanes)).transpose(3, 0, 1, 2, 4)

    d_cross_q, d_cross_k, d_cross_v = cross_call(
        cross_backward_kernel, cross_queries, memory, (d_cross_ctx,), 2
    )
    out_other = swap(after(out_part[:, 1], d_cross_q))
    hidden_all = to_everyone(hidden_sums)
    layer_out = after_cross + out_part[:, 0] + out_other
    d_middle, d_context, g_down_mid, g_up_mid = rows_call(
        into_self_kernel,
        (d_cross_q, d_after, middle, context, norm_gains, packed, packed, down, up),
        (None,) * 5 + (cross_q_spec, self_out_spec, None, None),
        [shaped(*tokens.shape), shaped(slots, trees, seg_len, lanes)]
        + [shaped(trees, 2, rank, width)] * 2,
    )
    d_own_context = lax.all_to_all(d_context, ROWS, split_axis=0, concat_axis=0, tiled=True)
    d_context, d_cross_k = lax.optimization_barrier((d_context, d_cross_k))
    d_encoder, g_down_memory, g_up_memory = memory_back_call(
        encoder, d_cross_k, d_cross_v, packed, down, up
    )
    enc_rows = encoder.shape[1] // slots
    sides = d_encoder.reshape(trees, slots // pairs, pairs, enc_rows, width).transpose(2, 1, 0, 3, 4)
    other_side = lax.dynamic_index_in_dim(sides, 1 - my_y, 0, keepdims=False)
    own_side = lax.dynamic_index_in_dim(sides, my_y, 0, keepdims=False)
    enc_side = own_side + swap(other_side)
    early = summed_to_owner(
        columns(
            [
                g_down_mid,
                g_down_memory,
                g_down_seven,
                g_up_mid,
                g_up_memory,
                g_up_seven,
                g_in_down[:, None],
                g_out_up[:, None],
            ]
        ),
        ROWS,
    )

    normed_shape = (slots, trees, seg_len, width)
    d_qkv, g_down_part, g_up_qkv = self_call(
        self_backward_kernel,
        segment_order,
        parents,
        (
            qkv,
            d_own_context,
            normed_all.reshape(normed_shape),
            inner_all,
            up_own,
            out_other,
        ),
        [
            slots_spec(qkv.shape),
            slots_spec(d_own_context.shape),
            slots_spec(normed_shape),
            slots_spec(inner_all.shape),
            tree_spec(up_own.shape),
            ahead,
        ],
        [
            shaped(*qkv.shape),
            shaped(trees, 3, rank, width),
            shaped(trees, 3, rank, lanes),
        ],
        [
            slots_spec(qkv.shape),
            tree_spec((trees, 3, rank, width)),
            tree_spec((trees, 3, rank, lanes)),
        ],
        28,
    )
    late = summed_to_owner(columns([after(g_down_part, early)]), ROWS)
    enc_side, late = lax.optimization_barrier((enc_side, late))
    grad_encoder = summed_along_line(enc_side)
    grad_in_up, grad_out_down = place_call(
        place_hidden_kernel, source, (hidden_all,), [shaped(adapters, rank, hidden_units)] * 2,
        (g_down_part,),
    )
    attention_all = to_everyone(
        after(jnp.concatenate([late, g_up_qkv, early], axis=1), grad_in_up)
    )
    grad_tokens = into_tokens_call(
        d_qkv, qkv_own, tokens, d_middle, norm_gains, down_qkv, up_own
    )
    wide = shaped(adapters, projections, rank, width)
    narrow = shaped(adapters, rank, width)
    grad_down, grad_up, grad_in_down, grad_out_up = place_call(
        place_kernel, source, (attention_all,), [wide, wide, narrow, narrow]
    )
    return (
        layer_out,
        grad_tokens,
        grad_encoder,
        grad_down.swapaxes(2, 3),
        grad_up,
        grad_in_down.swapaxes(1, 2),
        grad_in_up,
        grad_out_down.swapaxes(1, 2),
        grad_out_up,
    )


def placements(rows, copies):
    spread = P(copies, rows, None)
    ins = (
        spread,
        P(copies, None, None),
        spread,
        P(copies),
        P(copies, None),
        P(copies, None),
        P(),
        P(None, rows),
        P(rows, None),
        P(None, rows),
        P(None, rows),
        P(rows, None),
        P(None, rows),
        P(rows, None),
    ) + (P(),) * 6
    return ins, (spread,) * 3 + (P(),) * 6


def solution(mesh):
    copies, rows = mesh.shape["dp"], mesh.shape["seq"]
    general = jax.shard_map(
        shards,
        mesh=mesh,
        in_specs=placements("seq", "dp")[0],
        out_specs=placements("seq", "dp")[1],
        check_vma=False,
    )
    if rows != 8 or copies % 2:
        return general
    fine = jax.sharding.Mesh(
        mesh.devices.reshape(copies // 2, 2, rows // 2, 2), ("x", "c", "z", "y")
    )
    ins, outs = placements(ROWS, COPIES)
    special = jax.shard_map(by_heads, mesh=fine, in_specs=ins, out_specs=outs, check_vma=False)

    def step(*arrays):
        one_each = arrays[0].shape[0] == arrays[14].shape[0]
        return (special if one_each else general)(*arrays)

    return step
```
